32 devices in a mesh: section: 2 (over core), batch: 16 (over z, y, x).
Axes of the slice: x: 2, y: 2, z: 4, core: 2. Of those that a mesh axis runs over, the one named last changes fastest.
Arguments:
- x_q: bfloat16 [32, 32, 768], P('batch'), may hold values from -6 to 6
- x_p: bfloat16 [96, 128, 768], P('batch'), may hold values from -6 to 6
- len_q: int32 [32], P('batch'), may hold values from 4 to 32
- len_p: int32 [96], P('batch'), may hold values from 20 to 128
- cot_q: bfloat16 [32, 32, 768], P('batch'), may hold values from -6 to 6
- cot_p: bfloat16 [96, 128, 768], P('batch'), may hold values from -6 to 6
- positive: int32 [32], replicated, may hold values from 0 to 95, as said below
- micro: int32 [32], replicated, may hold values from 0 to 1, as said below
- w_qkv: bfloat16 [2, 2, 768, 2304], P('section'), may hold values from -0.21875 to 0.21875
- w_out: bfloat16 [2, 2, 768, 768], P('section'), may hold values from -0.875 to 0.875
- w_up: bfloat16 [2, 2, 768, 3072], P('section'), may hold values from -0.21875 to 0.21875
- w_down: bfloat16 [2, 2, 3072, 768], P('section'), may hold values from -0.109375 to 0.109375
- norm_gain: float32 [2, 2, 2, 768], P('section'), may hold values from 0.5 to 1.5
- biases: float32 [2, 2, 6, 768], P('section'), may hold values from -1.8 to 1.8
- b_up: float32 [2, 2, 3072], P('section'), may hold values from -1.8 to 1.8
Outputs:
- hidden_q: bfloat16 [2, 32, 32, 768], P('section', 'batch')
- hidden_p: bfloat16 [2, 96, 128, 768], P('section', 'batch')
- grad_q: float32 [2, 32, 32, 768], P('section', 'batch')
- grad_p: float32 [2, 96, 128, 768], P('section', 'batch')
- query_loss: float32 [32], P('batch')
- g_qkv: float32 [2, 2, 768, 2304], P('section', None, 'batch')
- g_out: float32 [2, 2, 768, 768], P('section', None, 'batch')
- g_up: float32 [2, 2, 768, 3072], P('section', None, 'batch')
- g_down: float32 [2, 2, 3072, 768], P('section', None, 'batch')
- g_gain: float32 [2, 2, 2, 768], P('section', None, None, 'batch')
- g_bias: float32 [2, 2, 6, 768], P('section', None, None, 'batch')
- g_bup: float32 [2, 2, 3072], P('section', None, 'batch')
- g_qbias: float32 [2, 2, 768], P('section', None, 'batch')
The draws below stay inside these ranges and needn't reach their ends.
Inputs may be any that keep to these rules, and one draw needn't show every extreme that they name: positive[q] is one of 3 q, 3 q + 1, 3 q + 2: a query's own passage and its two hard negatives. Each aligned block of 2 queries (the queries of one index of batch) holds exactly 1 query of each micro-batch.
All inputs are finite; a program needn't handle non-finite values.
Results may differ from the reference program's by a relative error of at most 0.02.
Values may be sent and summed in bfloat16 or wider, within the bound.
No kernel may reach another device: no remote copies, remote signals or barrier semaphores. Data moves between devices by JAX's collectives and lax.ppermute only.
A program may use at most 448 MiB of HBM per device.

```python
import math
import jax
import jax.numpy as jnp
from jax import lax

D = 768
HEADS = 12
HEAD_DIM = 64
FF = 3072
LQ = 32
LP = 128
MICRO = 2
Q_DEV = 2
NQ = 32
NP = 96
N_SECTION = 2


def draw_positive(key, part):
    key = jax.random.fold_in(key, 7)
    offset = jax.random.randint(key, (NQ,), 0, 3)
    return (3 * jnp.arange(NQ) + offset).astype(jnp.int32)


def draw_micro(key, part):
    key = jax.random.fold_in(key, 11)
    blocks = NQ // Q_DEV
    scores = jax.random.randint(key, (blocks, Q_DEV), 0, 1 << 20)
    distinct = scores * Q_DEV + jnp.arange(Q_DEV, dtype=jnp.int32)[None, :]
    order = jnp.argsort(distinct, axis=1)
    return (order % MICRO).reshape(NQ).astype(jnp.int32)


def with_ends(array, rng, least, largest):
    shape = array.shape
    index_at = [jax.random.randint(jax.random.fold_in(rng, axis), (), 0, shape[axis]) for axis in range(len(shape))]
    array = array.at[tuple(index_at)].set(least)
    longest = shape.index(max(shape))
    index_at[longest] = (index_at[longest] + 1) % shape[longest]
    return array.at[tuple(index_at)].set(largest)


def levels(own_key, extent, pieces, least, top_value):
    def one(axis_at, blocks):
        steps = jax.random.uniform(jax.random.fold_in(jax.random.fold_in(own_key, 6), axis_at), (blocks,), jnp.float32, least / len(pieces), top_value / len(pieces))
        return jnp.repeat(jnp.exp(steps), extent[axis_at] // blocks).reshape((-1,) + (1,) * (len(extent) - axis_at - 1))

    level = one(*pieces[0])
    for cut in pieces[1:]:
        level = level * one(*cut)
    return level


def gaussian(stream_key, dims, deviation, bound, split=(), kind=jnp.bfloat16):
    result = deviation * jax.random.normal(stream_key, dims, jnp.float32)
    if split:
        result = result * levels(stream_key, dims, split, -0.22, 0.18)
    return jnp.clip(result, -bound, bound).astype(kind)


def setup_inputs(seed: int = 0) -> dict:
    splits = jax.random.split(jax.random.key(seed), 16)
    return {
        "x_q": gaussian(splits[0], (NQ, LQ, D), 1.0, 6.0, ((0, 16),)),
        "x_p": gaussian(splits[1], (NP, LP, D), 1.0, 6.0, ((0, 16),)),
        "len_q": with_ends(jax.random.randint(splits[2], (NQ,), min(4, LQ // 2), LQ + 1), jax.random.fold_in(splits[2], 1), min(4, LQ // 2), LQ).astype(jnp.int32),
        "len_p": with_ends(jax.random.randint(splits[3], (NP,), min(20, LP // 2), LP + 1), jax.random.fold_in(splits[3], 1), min(20, LP // 2), LP).astype(jnp.int32),
        "cot_q": gaussian(splits[4], (NQ, LQ, D), 1.0, 6.0, ((0, 16),)),
        "cot_p": gaussian(splits[5], (NP, LP, D), 1.0, 6.0, ((0, 16),)),
        "positive": draw_positive(jax.random.fold_in(splits[15], 71), 0),
        "micro": draw_micro(jax.random.fold_in(splits[15], 71), 0),
        "w_qkv": gaussian(splits[8], (N_SECTION, 2, D, 3 * D), D ** -0.5, 0.21875, ((0, 2),)),
        "w_out": gaussian(splits[9], (N_SECTION, 2, D, D), (D // 16) ** -0.5, 0.875, ((0, 2),)),
        "w_up": gaussian(splits[10], (N_SECTION, 2, D, FF), D ** -0.5, 0.21875, ((0, 2),)),
        "w_down": gaussian(splits[11], (N_SECTION, 2, FF, D), FF ** -0.5, 0.109375, ((0, 2),)),
        "norm_gain": jnp.clip(1.0 + 0.1 * jax.random.normal(splits[12], (N_SECTION, 2, 2, D), jnp.float32), 0.5, 1.5),
        "biases": gaussian(splits[13], (N_SECTION, 2, 6, D), 0.3, 1.8, ((0, 2),), jnp.float32),
        "b_up": gaussian(splits[14], (N_SECTION, 2, FF), 0.3, 1.8, ((0, 2),), jnp.float32),
    }


@jax.custom_vjp
def low(v):
    return lax.optimization_barrier(v.astype(jnp.bfloat16)).astype(jnp.float32)

@jax.custom_vjp
def low_back(v):
    return v

def low_keep(v):
    return (low(v), None)

def low_pass(kept, grad):
    return (grad,)

def back_keep(v):
    return (v, None)

def back_low(kept, grad):
    return (low(grad),)
low.defvjp(low_keep, low_pass)
low_back.defvjp(back_keep, back_low)
PRECISE = lax.Precision.HIGHEST
NORM_EPS = 1e-05
SQRT_HALF = 0.7071067811865476
MASK_FILL = -1e+30
LOGIT_GAIN = 2.5

def round_both(values):
    return low_back(low(values))

def norm_rows(values, scale_gain, shift_bias):
    center = values - lax.optimization_barrier(jnp.mean(values, axis=-1, keepdims=True))
    spread = lax.optimization_barrier(jnp.mean(center * center, axis=-1, keepdims=True))
    return center * lax.rsqrt(spread + NORM_EPS) * scale_gain + shift_bias

def gelu_exact(values):
    return 0.5 * values * (1.0 + jax.scipy.special.erf(values * SQRT_HALF))

def encoder_block(params, block_rows, lengths):
    w_qkv, w_out, w_up, w_down, norm_gains, biases, b_up = params
    seq_count, seq_slots, model_width = block_rows.shape
    flat_rows = block_rows.reshape(seq_count * seq_slots, model_width)
    projected = jnp.dot(flat_rows, w_qkv, precision=PRECISE)
    shape_heads = (seq_count, seq_slots, HEADS, HEAD_DIM)
    query_rows = round_both(projected[:, :model_width] + biases[0]).reshape(shape_heads)
    key_rows = round_both(projected[:, model_width:2 * model_width]).reshape(shape_heads)
    value_rows = round_both(projected[:, 2 * model_width:] + biases[1]).reshape(shape_heads)
    scores = jnp.einsum('nqhd,nkhd->nhqk', query_rows, key_rows, precision=PRECISE)
    scores = low_back(scores * HEAD_DIM ** (-0.5))
    valid_keys = jnp.arange(seq_slots)[None, :] < lengths[:, None]
    scores = jnp.where(valid_keys[:, None, None, :], scores, MASK_FILL)
    exponent = jnp.exp(scores - lax.optimization_barrier(jnp.max(scores, axis=-1, keepdims=True)))
    soft_weights = exponent / lax.optimization_barrier(jnp.sum(exponent, axis=-1, keepdims=True))
    mixed_rows = jnp.einsum('nhqk,nkhd->nqhd', low(soft_weights), value_rows, precision=PRECISE)
    mixed_rows = round_both(mixed_rows.reshape(seq_count * seq_slots, model_width))
    branch_out = low_back(jnp.dot(mixed_rows, w_out, precision=PRECISE) + biases[2])
    first_norm = norm_rows(flat_rows + branch_out, norm_gains[0], biases[3])
    hidden = low_back(jnp.dot(low(first_norm), w_up, precision=PRECISE) + b_up)
    active = low(gelu_exact(hidden))
    branch_ffn = low_back(jnp.dot(active, w_down, precision=PRECISE) + biases[4])
    output = norm_rows(first_norm + branch_ffn, norm_gains[1], biases[5])
    return output.reshape(block_rows.shape)

def tower_layer(params, block_rows, lengths, group_size):
    groups = block_rows.shape[0] // group_size

    def one_group(group_pair):
        return encoder_block(params, group_pair[0], group_pair[1])
    stacked = lax.map(jax.checkpoint(one_group), (block_rows.reshape((groups, group_size) + block_rows.shape[1:]), lengths.reshape(groups, group_size)))
    return stacked.reshape(block_rows.shape)

def reference(x_q, x_p, len_q, len_p, cot_q, cot_p, positive, micro, w_qkv, w_out, w_up, w_down, norm_gain, biases, b_up):
    group_q = math.gcd(NQ, 128)
    group_p = math.gcd(NP, 32)
    valid_q = (jnp.arange(LQ)[None, :] < len_q[:, None]).astype(jnp.float32)[:, :, None]
    valid_p = (jnp.arange(LP)[None, :] < len_p[:, None]).astype(jnp.float32)[:, :, None]
    same_group = micro[:, None] == jnp.repeat(micro, 3)[None, :]
    target = jnp.arange(NP)[None, :] == positive[:, None]
    cot_qf = cot_q.astype(jnp.float32)
    cot_pf = cot_p.astype(jnp.float32)

    def forward(mat_qkv, mat_out, mat_up, mat_down, gains, bias_rows, bias_up, rows_q, rows_p, shift_q, shift_p):

        def params(layer, tower_id):
            return (mat_qkv[layer, tower_id], mat_out[layer, tower_id], mat_up[layer, tower_id], mat_down[layer, tower_id], gains[layer, tower_id], bias_rows[layer, tower_id], bias_up[layer, tower_id])
        mid_q = tower_layer(params(0, 0), rows_q, len_q, group_q)
        mid_p = tower_layer(params(0, 1), rows_p, len_p, group_p)
        sent_q = low_back(low(mid_q) + shift_q)
        sent_p = low_back(low(mid_p) + shift_p)
        top_q = tower_layer(params(1, 0), sent_q, len_q, group_q)
        top_p = tower_layer(params(1, 1), sent_p, len_p, group_p)
        cls_q = low(top_q[:, 0, :])
        cls_p = low(top_p[:, 0, :])
        logits = jnp.dot(cls_q, cls_p.T, precision=PRECISE) * (LOGIT_GAIN * D ** (-0.5))
        logits = jnp.where(same_group, logits, MASK_FILL)
        row_top = lax.optimization_barrier(jnp.max(logits, axis=-1, keepdims=True))
        log_total = row_top[:, 0] + jnp.log(lax.optimization_barrier(jnp.sum(jnp.exp(logits - row_top), axis=-1)))
        query_loss = log_total - lax.optimization_barrier(jnp.sum(jnp.where(target, logits, 0.0), axis=-1))
        objective = jnp.sum(top_q * cot_qf * valid_q) + jnp.sum(top_p * cot_pf * valid_p) + jnp.sum(query_loss)
        return (objective, (low(mid_q), top_q, low(mid_p), top_p, query_loss))
    primals = (w_qkv.astype(jnp.float32), w_out.astype(jnp.float32), w_up.astype(jnp.float32), w_down.astype(jnp.float32), norm_gain, biases, b_up, x_q.astype(jnp.float32), x_p.astype(jnp.float32), jnp.zeros(x_q.shape, jnp.float32), jnp.zeros(x_p.shape, jnp.float32))
    objective, pullback, kept = jax.vjp(forward, *primals, has_aux=True)
    grads = pullback(jnp.ones((), jnp.float32))
    hidden_q = jnp.stack([kept[0], kept[1]]).astype(jnp.bfloat16)
    hidden_p = jnp.stack([kept[2], kept[3]]).astype(jnp.bfloat16)
    grad_q = jnp.stack([grads[7], grads[9]])
    grad_p = jnp.stack([grads[8], grads[10]])
    return (hidden_q, hidden_p, grad_q, grad_p, kept[4], grads[0], grads[1], grads[2], grads[3], grads[4], grads[5], grads[6], grads[5][:, :, 0, :])
```

```python
from functools import partial

import jax
import jax.numpy as jnp
from jax import lax
from jax.sharding import PartitionSpec as P

HEADS = 12
HEAD_DIM = 64


NORM_EPS = 1e-05
SQRT_HALF = 0.7071067811865476
ROOT_TAU_INV = 0.3989422804014327
MASK_FILL = -1e30
LOGIT_GAIN = 2.5
PRECISE = lax.Precision.HIGHEST


def core_swap(block):
    return lax.ppermute(block, "section", [(0, 1), (1, 0)])


def flip_swap(block, bit):
    size = lax.axis_size("batch")
    return lax.ppermute(block, "batch", [(i, i ^ bit) for i in range(size)])


def outer_sum(left, right):
    return lax.dot_general(
        left, right, (((0,), (0,)), ((), ())), preferred_element_type=jnp.float32
    )


def times_transposed(left, right):
    return lax.dot_general(
        left, right, (((1,), (1,)), ((), ())), preferred_element_type=jnp.float32
    )


def norm_rows(values, scale_gain, shift_bias):
    center = values - jnp.mean(values, axis=-1, keepdims=True)
    inverse = lax.rsqrt(jnp.mean(center * center, axis=-1, keepdims=True) + NORM_EPS)
    normed = center * inverse
    return (normed * scale_gain + shift_bias, normed, inverse)


def norm_back(upstream, normed, inverse, scale_gain):
    scaled = upstream * scale_gain
    return inverse * (
        scaled
        - jnp.mean(scaled, axis=-1, keepdims=True)
        - normed * jnp.mean(scaled * normed, axis=-1, keepdims=True)
    )


def gelu_value(values):
    return 0.5 * values * (1.0 + jax.scipy.special.erf(values * SQRT_HALF))


def gelu_slope(values):
    return (
        0.5 * (1.0 + jax.scipy.special.erf(values * SQRT_HALF))
        + values * jnp.exp(-0.5 * values * values) * ROOT_TAU_INV
    )


def soft_scores(query_rows, key_rows, lengths):
    scores = jnp.einsum(
        "nqhd,nkhd->nhqk", query_rows, key_rows, preferred_element_type=jnp.float32
    ) * HEAD_DIM ** (-0.5)
    valid_keys = jnp.arange(scores.shape[-1])[None, :] < lengths[:, None]
    scores = jnp.where(valid_keys[:, None, None, :], scores, MASK_FILL)
    exponent = jnp.exp(scores - jnp.max(scores, axis=-1, keepdims=True))
    return exponent / jnp.sum(exponent, axis=-1, keepdims=True)


def block_forward(weights, block_rows, lengths):
    w_qkv, w_out, w_up, w_down, norm_gains, biases, b_up = weights
    seq_count, seq_slots, model_width = block_rows.shape
    flat_rows = block_rows.reshape(seq_count * seq_slots, model_width)
    projected = jnp.dot(flat_rows, w_qkv, preferred_element_type=jnp.float32)
    shape_heads = (seq_count, seq_slots, HEADS, HEAD_DIM)
    query_rows = (projected[:, :model_width] + biases[0]).astype(jnp.bfloat16).reshape(shape_heads)
    key_rows = projected[:, model_width : 2 * model_width].astype(jnp.bfloat16).reshape(shape_heads)
    value_rows = (
        (projected[:, 2 * model_width :] + biases[1]).astype(jnp.bfloat16).reshape(shape_heads)
    )
    soft_weights = soft_scores(query_rows, key_rows, lengths)
    mixed_rows = jnp.einsum(
        "nhqk,nkhd->nqhd",
        soft_weights.astype(jnp.bfloat16),
        value_rows,
        preferred_element_type=jnp.float32,
    )
    mixed_rows = mixed_rows.reshape(flat_rows.shape).astype(jnp.bfloat16)
    summed = flat_rows.astype(jnp.float32) + (
        jnp.dot(mixed_rows, w_out, preferred_element_type=jnp.float32) + biases[2]
    )
    first_norm, first_hat, first_inv = norm_rows(summed, norm_gains[0], biases[3])
    first_low = first_norm.astype(jnp.bfloat16)
    hidden = jnp.dot(first_low, w_up, preferred_element_type=jnp.float32) + b_up
    active = gelu_value(hidden).astype(jnp.bfloat16)
    second = first_norm + (jnp.dot(active, w_down, preferred_element_type=jnp.float32) + biases[4])
    output, out_hat, out_inv = norm_rows(second, norm_gains[1], biases[5])
    kept_values = (
        flat_rows,
        query_rows,
        key_rows,
        value_rows,
        soft_weights,
        mixed_rows,
        first_hat,
        first_inv,
        first_low,
        hidden,
        active,
        out_hat,
        out_inv,
    )
    return (output.reshape(block_rows.shape), kept_values)


def block_backward(weights, kept_values, upstream):
    w_qkv, w_out, w_up, w_down, norm_gains, biases, b_up = weights
    (
        flat_rows,
        query_rows,
        key_rows,
        value_rows,
        soft_weights,
        mixed_rows,
        first_hat,
        first_inv,
        first_low,
        hidden,
        active,
        out_hat,
        out_inv,
    ) = kept_values
    grad_rows = upstream.reshape(flat_rows.shape)
    d_gain_out = jnp.sum(grad_rows * out_hat, axis=0)
    d_shift_out = jnp.sum(grad_rows, axis=0)
    d_second = norm_back(grad_rows, out_hat, out_inv, norm_gains[1])
    d_branch_ffn = d_second.astype(jnp.bfloat16)
    d_bias_ffn = jnp.sum(d_branch_ffn.astype(jnp.float32), axis=0)
    d_hidden = (times_transposed(d_branch_ffn, w_down) * gelu_slope(hidden)).astype(jnp.bfloat16)
    d_bias_up = jnp.sum(d_hidden.astype(jnp.float32), axis=0)
    d_first = d_second + times_transposed(d_hidden, w_up)
    d_gain_first = jnp.sum(d_first * first_hat, axis=0)
    d_shift_first = jnp.sum(d_first, axis=0)
    d_summed = norm_back(d_first, first_hat, first_inv, norm_gains[0])
    d_branch = d_summed.astype(jnp.bfloat16)
    d_bias_out = jnp.sum(d_branch.astype(jnp.float32), axis=0)
    d_mixed = times_transposed(d_branch, w_out).astype(jnp.bfloat16).reshape(query_rows.shape)
    d_soft = jnp.einsum("nqhd,nkhd->nhqk", d_mixed, value_rows, preferred_element_type=jnp.float32)
    d_value = jnp.einsum(
        "nhqk,nqhd->nkhd",
        soft_weights.astype(jnp.bfloat16),
        d_mixed,
        preferred_element_type=jnp.float32,
    )
    d_scores = (
        soft_weights * (d_soft - jnp.sum(d_soft * soft_weights, axis=-1, keepdims=True))
    ).astype(jnp.bfloat16)
    head_scale = HEAD_DIM ** (-0.5)
    d_query = (
        jnp.einsum("nhqk,nkhd->nqhd", d_scores, key_rows, preferred_element_type=jnp.float32)
        * head_scale
    )
    d_key = (
        jnp.einsum("nhqk,nqhd->nkhd", d_scores, query_rows, preferred_element_type=jnp.float32)
        * head_scale
    )
    d_proj = jnp.concatenate(
        [
            member.astype(jnp.bfloat16).reshape(flat_rows.shape)
            for member in (d_query, d_key, d_value)
        ],
        axis=1,
    )
    model_width = flat_rows.shape[1]
    d_bias_query = jnp.sum(d_proj[:, :model_width].astype(jnp.float32), axis=0)
    d_bias_value = jnp.sum(d_proj[:, 2 * model_width :].astype(jnp.float32), axis=0)
    d_input = d_summed + times_transposed(d_proj, w_qkv)
    pairs = (
        (flat_rows, d_proj),
        (mixed_rows, d_branch),
        (first_low, d_hidden),
        (active, d_branch_ffn),
    )
    vectors = (
        jnp.stack([d_gain_first, d_gain_out]),
        jnp.stack(
            [d_bias_query, d_bias_value, d_bias_out, d_shift_first, d_bias_ffn, d_shift_out]
        ),
        d_bias_up[None],
    )
    return d_input, pairs, vectors


def outer_low(left, right):
    return outer_sum(left, right).astype(jnp.bfloat16)


def seed_grad(cotangent, lengths, cls_grad):
    valid_rows = (jnp.arange(cotangent.shape[1])[None, :] < lengths[:, None]).astype(jnp.float32)
    grad_rows = cotangent.astype(jnp.float32) * valid_rows[:, :, None]
    return grad_rows.at[:, 0, :].add(cls_grad)


def pick(flag, yes, no):
    return jax.tree.map(lambda a, b: jnp.where(flag, a, b), yes, no)


def pick_bit(grid, axis, index):
    return lax.dynamic_index_in_dim(grid, index, axis, keepdims=False)


def own_bit(bit):
    return (lax.axis_index("batch") // bit) % 2


def scatter_sum(grid, bits, left):
    left = list(left)
    for bit in bits:
        axis = left.index(bit)
        mine = own_bit(bit)
        sent = pick_bit(grid, axis, 1 - mine)
        kept = pick_bit(grid, axis, mine)
        arrived = flip_swap(sent, bit)
        total = kept.astype(jnp.float32) + arrived.astype(jnp.float32)
        left.remove(bit)
        grid = total if not left else total.astype(grid.dtype)
    return grid


def all_bits(size):
    bits = [1 << i for i in range(size.bit_length() - 1)]
    return bits[::-1]


def to_grid(array, size):
    bits = all_bits(size)
    return array.reshape((2,) * len(bits) + (array.shape[0] // size,) + array.shape[1:])


def three_orders(size):
    bits = all_bits(size)[::-1]
    if size == 16:
        return [1, 2, 4, 8], [2, 1, 4, 8], [4, 1, 2, 8]
    third = len(bits) // 3
    return [bits[i * third :] + bits[: i * third] for i in range(3)]


def gather_all(block, size):
    if size != 16:
        for bit in all_bits(size)[::-1]:
            block = jnp.concatenate([block, flip_swap(block, bit)], 0)
        return block
    block = jnp.concatenate([block] + [flip_swap(block, k) for k in (1, 2, 3)], 0)
    return jnp.concatenate([block] + [flip_swap(block, k) for k in (4, 8, 12)], 0)


def vector_grid(vectors, size):
    return jnp.concatenate(
        [
            jnp.swapaxes(item.reshape(item.shape[0], size, -1), 0, 1).reshape(size, -1)
            for item in vectors
        ],
        axis=1,
    )


def contrast(own_cls, micro, positive, query_count, batch_index, batch_size):
    width = own_cls.shape[1]
    chip_rows = own_cls.shape[0]
    gathered = gather_all(own_cls, batch_size).reshape(batch_size, chip_rows, width)
    all_q = gathered[:, :query_count].reshape(-1, width)
    all_p = gathered[:, query_count:].reshape(-1, width)
    blocks = jnp.arange(batch_size, dtype=jnp.int32) ^ batch_index
    query_ids = (
        blocks[:, None] * query_count + jnp.arange(query_count, dtype=jnp.int32)[None, :]
    ).reshape(-1)
    passage_ids = (
        3 * query_ids[:, None] + jnp.arange(3, dtype=jnp.int32)[None, :]
    ).reshape(-1)
    labels = jnp.take(micro, query_ids)
    wanted = jnp.take(positive, query_ids)
    logit_scale = LOGIT_GAIN * width ** (-0.5)
    logits = times_transposed(all_q, all_p) * logit_scale
    same_group = labels[:, None] == jnp.repeat(labels, 3)[None, :]
    logits = jnp.where(same_group, logits, MASK_FILL)
    row_top = jnp.max(logits, axis=-1, keepdims=True)
    exponent = jnp.exp(logits - row_top)
    totals = jnp.sum(exponent, axis=-1, keepdims=True)
    target = passage_ids[None, :] == wanted[:, None]
    loss_all = (
        row_top[:, 0] + jnp.log(totals[:, 0]) - jnp.sum(jnp.where(target, logits, 0.0), axis=-1)
    )
    coefficient = (exponent / totals - target.astype(jnp.float32)) * logit_scale
    passage_count = 3 * query_count
    d_cls_q = jnp.dot(coefficient[:query_count], all_p.astype(jnp.float32), precision=PRECISE)
    d_cls_p = lax.dot_general(
        coefficient[:, :passage_count],
        all_q.astype(jnp.float32),
        (((0,), (0,)), ((), ())),
        precision=PRECISE,
    )
    return loss_all[:query_count], d_cls_q, d_cls_p


def shards(
    x_q,
    x_p,
    len_q,
    len_p,
    cot_q,
    cot_p,
    positive,
    micro,
    w_qkv,
    w_out,
    w_up,
    w_down,
    norm_gain,
    biases,
    b_up,
):
    core = lax.axis_index("section")
    is_first = core == 0
    batch_index = lax.axis_index("batch")
    size = lax.axis_size("batch")
    bits = all_bits(size)
    own_sets = (w_qkv, w_out, w_up, w_down, norm_gain, biases, b_up)
    own_q = tuple(member[0, 0] for member in own_sets)
    own_p = tuple(member[0, 1] for member in own_sets)
    other_p = tuple(core_swap(member) for member in own_p)
    layers_p = (pick(is_first, own_p, other_p), pick(is_first, other_p, own_p))
    query_count = x_q.shape[0]
    half_count = x_p.shape[0] // 2

    def own_half(array):
        return lax.dynamic_slice_in_dim(array, core * half_count, half_count, 0)

    rows_p, lens_p, cots_p = own_half(x_p), own_half(len_p), own_half(cot_p)

    early_q, early_kept_q = block_forward(own_q, x_q, len_q)
    mid_q = early_q.astype(jnp.bfloat16)
    late_q, late_kept_q = block_forward(own_q, core_swap(mid_q), len_q)
    mid_p, early_kept_p = block_forward(layers_p[0], rows_p, lens_p)
    mid_p = mid_p.astype(jnp.bfloat16)
    top_p, late_kept_p = block_forward(layers_p[1], mid_p, lens_p)
    top_low_p = top_p.astype(jnp.bfloat16)

    cls_rows = jnp.concatenate([late_q[:, 0, :].astype(jnp.bfloat16), top_low_p[:, 0, :]], 0)
    cls_other = core_swap(cls_rows)
    cls_chip = jnp.concatenate(
        [
            jnp.where(is_first, cls_other[:query_count], cls_rows[:query_count]),
            jnp.where(is_first, cls_rows[query_count:], cls_other[query_count:]),
            jnp.where(is_first, cls_other[query_count:], cls_rows[query_count:]),
        ],
        0,
    )
    loss_own, d_cls_q, d_cls_p = contrast(
        cls_chip, micro, positive, query_count, batch_index, size
    )

    late_grad_q, late_pairs_q, late_vec_q = block_backward(
        own_q, late_kept_q, seed_grad(cot_q, len_q, d_cls_q)
    )
    late_sent_q = late_grad_q.astype(jnp.bfloat16)
    early_grad_q, early_pairs_q, early_vec_q = block_backward(
        own_q, early_kept_q, core_swap(late_sent_q).astype(jnp.float32)
    )
    pairs_q = pick(is_first, early_pairs_q, late_pairs_q)
    vec_q = pick(is_first, early_vec_q, late_vec_q)

    late_grad_p, late_pairs_p, late_vec_p = block_backward(
        layers_p[1], late_kept_p, seed_grad(cots_p, lens_p, own_half(d_cls_p))
    )
    late_sent_p = late_grad_p.astype(jnp.bfloat16).astype(jnp.float32)
    early_grad_p, early_pairs_p, early_vec_p = block_backward(
        layers_p[0], early_kept_p, late_sent_p
    )

    def passage_sums(pairs):
        g_qkv, g_out, g_up, g_down = (outer_low(left, right) for left, right in pairs)

        def halves(array):
            width = array.shape[1] // 2
            keep = lax.dynamic_slice_in_dim(array, core * width, width, 1)
            send = lax.dynamic_slice_in_dim(array, (1 - core) * width, width, 1)
            return keep, send

        results = []
        chunks = ((g_down,), (g_up,), (g_qkv, g_out))
        for chunk, order in zip(chunks, three_orders(size)):
            parts = [halves(array) for array in chunk]
            keep = jnp.concatenate([part[0] for part in parts], 1)
            send = jnp.concatenate([part[1] for part in parts], 1)
            total = (keep.astype(jnp.float32) + core_swap(send).astype(jnp.float32)).astype(
                jnp.bfloat16
            )
            results.append(scatter_sum(to_grid(total, size), order, bits))
        return results

    late_sums = passage_sums(late_pairs_p)
    early_sums = passage_sums(early_pairs_p)

    lefts = [left for left, _ in pairs_q]
    rights = jnp.concatenate([right for _, right in pairs_q], 1)
    rows = rights.shape[0]
    grids = [
        left.reshape((rows,) + (2,) * len(bits) + (left.shape[1] // size,)) for left in lefts
    ]
    left_bits = list(bits)
    for bit in (1, 2):
        axis = 1 + left_bits.index(bit)
        mine = own_bit(bit)
        kept = [pick_bit(grid, axis, mine) for grid in grids]
        sent = [pick_bit(grid, axis, 1 - mine) for grid in grids]
        left_bits.remove(bit)
        packed = jnp.concatenate([item.reshape(rows, -1) for item in sent] + [rights], 1)
        arrived = flip_swap(packed, bit)
        rows = 2 * rows
        grown = []
        offset = 0
        for item in kept:
            flat = item.reshape(rows // 2, -1)
            part = arrived[:, offset : offset + flat.shape[1]]
            offset += flat.shape[1]
            grown.append(jnp.concatenate([flat, part], 0).reshape((rows,) + item.shape[1:]))
        grids = grown
        rights = jnp.concatenate([rights, arrived[:, offset:]], 0)
    query_sums = []
    offset = 0
    for grid, (_, right) in zip(grids, pairs_q):
        width = right.shape[1]
        product = outer_low(grid.reshape(rows, -1), rights[:, offset : offset + width])
        offset += width
        query_sums.append(
            product.reshape((2,) * len(left_bits) + (grid.shape[-1], width))
        )
    wide = jnp.concatenate(query_sums[:3], -1)
    wide = scatter_sum(wide, left_bits[::-1], left_bits)
    down_q = scatter_sum(query_sums[3], left_bits[::-1], left_bits)
    model = down_q.shape[1]
    qkv_q, out_q, up_q = wide[:, : 3 * model], wide[:, 3 * model : 4 * model], wide[:, 4 * model :]

    early_line, late_line = vector_grid(early_vec_p, size), vector_grid(late_vec_p, size)
    line_p = jnp.where(is_first, early_line, late_line) + core_swap(
        jnp.where(is_first, late_line, early_line)
    )
    lines = jnp.concatenate([vector_grid(vec_q, size), line_p], 1)
    lines = scatter_sum(to_grid(lines, size), bits[::-1], bits)[0]
    lines = lines.reshape(2, -1)
    blk = model // size
    g_gain = lines[:, : 2 * blk].reshape(2, 2, blk)
    g_bias = lines[:, 2 * blk : 8 * blk].reshape(2, 6, blk)
    g_bup = lines[:, 8 * blk :]

    def own_layer(early, late):
        other = core_swap(jnp.where(is_first, late, early))
        own = jnp.where(is_first, early, late)
        return jnp.where(is_first, own, other), jnp.where(is_first, other, own)

    def join(early, late, axis):
        return jnp.concatenate(own_layer(early, late), axis)

    down_p = join(early_sums[0], late_sums[0], 1)
    up_p = join(early_sums[1], late_sums[1], 1)
    first, second = own_layer(early_sums[2], late_sums[2])
    cut = 3 * model // 2
    qkv_p = jnp.concatenate([first[:, :cut], second[:, :cut]], 1)
    out_p = jnp.concatenate([first[:, cut:], second[:, cut:]], 1)
    hidden_p = join(mid_p, top_low_p, 0)
    grad_p = join(early_grad_p.reshape(mid_p.shape), late_sent_p.reshape(mid_p.shape), 0)
    hidden_q = jnp.where(is_first, mid_q, late_q.astype(jnp.bfloat16))
    grad_q = jnp.where(is_first, early_grad_q, late_sent_q.astype(jnp.float32))
    return (
        hidden_q[None],
        hidden_p[None],
        grad_q.reshape(x_q.shape)[None],
        grad_p[None],
        loss_own,
        jnp.stack([qkv_q, qkv_p])[None],
        jnp.stack([out_q, out_p])[None],
        jnp.stack([up_q, up_p])[None],
        jnp.stack([down_q, down_p])[None],
        g_gain[None],
        g_bias[None],
        g_bup[None],
        g_bias[None, :, 0, :],
    )


def solution(mesh):
    return jax.shard_map(
        shards,
        mesh=mesh,
        in_specs=(
            P("batch", None, None),
            P("batch", None, None),
            P("batch"),
            P("batch"),
            P("batch", None, None),
            P("batch", None, None),
            P(),
            P(),
            P("section", None, None, None),
            P("section", None, None, None),
            P("section", None, None, None),
            P("section", None, None, None),
            P("section", None, None, None),
            P("section", None, None, None),
            P("section", None, None),
        ),
        out_specs=(
            P("section", "batch", None, None),
            P("section", "batch", None, None),
            P("section", "batch", None, None),
            P("section", "batch", None, None),
            P("batch"),
            P("section", None, "batch", None),
            P("section", None, "batch", None),
            P("section", None, "batch", None),
            P("section", None, "batch", None),
            P("section", None, None, "batch"),
            P("section", None, None, "batch"),
            P("section", None, "batch"),
            P("section", None, "batch"),
        ),
        check_vma=False,
    )
```

```python
import jax
import jax.numpy as jnp
from jax import lax
from jax.experimental import pallas as pl
from jax.experimental.pallas import tpu as pltpu
from jax.sharding import PartitionSpec as P

HEADS = 12
HEAD_DIM = 64


NORM_EPS = 1e-05
SQRT_HALF = 0.7071067811865476
ROOT_TAU_INV = 0.3989422804014327
MASK_FILL = -1e30
LOGIT_GAIN = 2.5
PRECISE = lax.Precision.HIGHEST


def core_swap(block):
    return lax.ppermute(block, "section", [(0, 1), (1, 0)])


def flip_swap(block, bit):
    size = lax.axis_size("batch")
    return lax.ppermute(block, "batch", [(i, i ^ bit) for i in range(size)])


F32 = jnp.float32
LOW = jnp.bfloat16
VMEM_LIMIT = 58 * 1024 * 1024
BLOCKS = 16
IS_FIRST, CORE, PLACES, Z_PLACES, X_BIT, Y_BIT, LENGTHS = 0, 1, 2, 50, 54, 55, 56
ORDERS = ((1, 2, 4, 8), (2, 1, 4, 8), (4, 1, 2, 8))


def mm(left, right):
    return lax.dot_general(left, right, (((1,), (0,)), ((), ())), preferred_element_type=F32)


def mm_nt(left, right):
    return lax.dot_general(left, right, (((1,), (1,)), ((), ())), preferred_element_type=F32)


def mm_tn(left, right):
    return lax.dot_general(left, right, (((0,), (0,)), ((), ())), preferred_element_type=F32)


def row_mean(values):
    return jnp.sum(values, axis=-1, keepdims=True) * (1.0 / values.shape[-1])


def normed_rows(values):
    center = values - row_mean(values)
    inverse = lax.rsqrt(row_mean(center * center) + NORM_EPS)
    return center * inverse, inverse


def norm_pull(upstream, normed, inverse, gain):
    scaled = upstream * gain
    return inverse * (scaled - row_mean(scaled) - normed * row_mean(scaled * normed))


def col_sum(values):
    return jnp.sum(values, axis=0, keepdims=True)


class Moves:
    def __init__(self, sems):
        self.sems = sems
        self.used = 0
        self.open = []

    def slot(self):
        self.used += 1
        return self.sems.at[self.used - 1]

    def fetch(self, source, target):
        copy = pltpu.make_async_copy(source, target, self.slot())
        copy.start()
        return copy

    def fetch_either(self, flag, first, second, target):
        sem = self.slot()
        copy = pltpu.make_async_copy(first, target, sem)
        if second is None:
            copy.start()
            return copy
        other = pltpu.make_async_copy(second, target, sem)

        @pl.when(flag)
        def _():
            copy.start()

        @pl.when(jnp.logical_not(flag))
        def _():
            other.start()

        return copy

    def store(self, source, target):
        self.open.append(self.fetch(source, target))

    def drain(self):
        for copy in self.open:
            copy.wait()


class Tower:
    def __init__(self, index, info, weights, others, small, small_other, seqs, slots, first_len):
        self.index = index
        self.info = info
        self.weights = weights
        self.others = others
        self.small = small
        self.small_other = small_other
        self.seqs = seqs
        self.slots = slots
        self.first_len = first_len
        self.count = seqs * slots
        self.width = weights[1].shape[-1]
        self.wide = weights[2].shape[-1]
        self.group = self.count if self.count <= 128 else slots
        self.shared = others is not None

    def given(self, which):
        own = [self.weights[at] for at in which]
        return own + ([self.others[at] for at in which] if self.shared else [])

    def given_small(self):
        return list(self.small) + ([self.small_other] if self.shared else [])

    def use_own(self, info, layer):
        return info[IS_FIRST] == (1 if layer == 0 else 0)

    def lengths_at(self, info):
        return self.first_len + (info[CORE] * self.seqs if self.shared else 0)

    def row_start(self, info):
        return pl.multiple_of(info[CORE] * self.count, self.count) if self.shared else 0

    def small_rows(self, refs, flag):
        own = [refs[0][0, self.index], refs[1][0, self.index]]
        if self.shared:
            other = refs[3]
            own = [
                jnp.where(flag, own[0], other[0:2, :]),
                jnp.where(flag, own[1], other[2:8, :]),
            ]
        return own

    def hidden_bias(self, refs, flag, step, tile):
        own = refs[2][0, self.index : self.index + 1, step * tile : (step + 1) * tile]
        if self.shared:
            own = jnp.where(flag, own, refs[3][8 + step : 9 + step, :])
        return own


ANYWHERE = pl.BlockSpec(memory_space=pl.ANY)
SCALARS = pl.BlockSpec(memory_space=pltpu.SMEM)
INSIDE = pl.BlockSpec(memory_space=pltpu.VMEM)


def call_kernel(kernel, name, inputs, outs, scratch, copies, flops, after):
    count = len(inputs)
    extra = len(after)

    def body(*refs):
        refs = list(refs)
        kernel(
            refs[:count],
            refs[count + extra : count + extra + len(outs)],
            refs[count + extra + len(outs) : -1],
            Moves(refs[-1]),
        )

    return pl.pallas_call(
        body,
        out_shape=[jax.ShapeDtypeStruct(shape, kind) for shape, kind in outs],
        in_specs=[spec for spec, _ in inputs] + [ANYWHERE] * extra,
        out_specs=[ANYWHERE] * len(outs),
        scratch_shapes=[pltpu.VMEM(shape, kind) for shape, kind in scratch]
        + [pltpu.SemaphoreType.DMA((copies,))],
        compiler_params=pltpu.CompilerParams(vmem_limit_bytes=VMEM_LIMIT),
        cost_estimate=pl.CostEstimate(
            flops=flops, bytes_accessed=flops // 64, transcendentals=0
        ),
        name=name,
    )(*[array for _, array in inputs], *after)


def pair_masks(dtype):
    lanes = lax.broadcasted_iota(jnp.int32, (1, 128), 1)
    low = jnp.where(lanes < HEAD_DIM, 1.0, 0.0)
    return low.astype(dtype), (1.0 - low).astype(dtype)


def stacked_pair(block, low, high):
    return jnp.concatenate([block * low, block * high], axis=0)


def joined_pair(stacked, group):
    lanes = lax.broadcasted_iota(jnp.int32, (1, 128), 1)
    return jnp.where(lanes < HEAD_DIM, stacked[:group], stacked[group:])


def pair_softmax(query_stack, key_block, valid):
    scores = mm_nt(query_stack, key_block) * HEAD_DIM ** (-0.5)
    scores = jnp.where(valid, scores, MASK_FILL)
    exponent = jnp.exp(scores - jnp.max(scores, axis=-1, keepdims=True))
    return exponent * (1.0 / jnp.sum(exponent, axis=-1, keepdims=True))


def valid_keys(info, first_len, group, slots):
    rows = lax.broadcasted_iota(jnp.int32, (2 * group, group), 0)
    keys = lax.broadcasted_iota(jnp.int32, (2 * group, group), 1)
    seqs = group // slots
    if seqs == 1:
        return keys < info[first_len]
    rows = jnp.where(rows >= group, rows - group, rows)
    valid = None
    for j in range(seqs):
        low = j * slots
        inside = (
            (rows >= low)
            & (rows < low + slots)
            & (keys >= low)
            & (keys < low + info[first_len + j])
        )
        valid = inside if valid is None else valid | inside
    return valid


def forward_layer(tower, layer, rows, whole_rows, after=()):
    count, width, wide, group = tower.count, tower.width, tower.wide, tower.group
    tile = width

    def kernel(ins, outs, scratch, moves):
        info, x_any = ins[0], ins[1]
        weights = ins[2:6]
        others = ins[6:10] if tower.shared else [None] * 4
        smalls = ins[10:] if tower.shared else ins[6:]
        out_any, qkv_any, mix_any, low_any, act_any, slope_any, hat1_any, hat2_any, inv_any = outs
        x_v, w_qkv, w_out, w_up, w_down, acc_v = scratch[:6]
        out_v, qkv_v, mix_v, low_v, act_v, slope_v, hat1_v, hat2_v, inv_v = scratch[6:]
        use_own = tower.use_own(info, layer)
        if whole_rows:
            x_any = x_any.at[pl.ds(tower.row_start(info), count)]
        arrived = [moves.fetch(x_any, x_v)]
        for own, other, target in zip(weights, others, (w_qkv, w_out, w_up, w_down)):
            arrived.append(
                moves.fetch_either(use_own, own.at[0, tower.index], other, target)
            )
        gains, bias = tower.small_rows(smalls, use_own)
        arrived[0].wait()
        arrived[1].wait()
        x = x_v[...]
        for part in range(3):
            block = mm(x, w_qkv[:, part * width : (part + 1) * width])
            if part == 0:
                block = block + bias[0:1, :]
            if part == 2:
                block = block + bias[1:2, :]
            qkv_v[:, part * width : (part + 1) * width] = block.astype(LOW)
        moves.store(qkv_v, qkv_any)

        def one_group(g, carry):
            at = pl.ds(pl.multiple_of(g * group, group), group)
            valid = valid_keys(
                info, tower.lengths_at(info) + g * (group // tower.slots), group, tower.slots
            )
            low, high = pair_masks(LOW)
            for pair in range(width // 128):
                lane = pair * 128
                q2 = qkv_v[at, lane : lane + 128]
                k2 = qkv_v[at, width + lane : width + lane + 128]
                v2 = qkv_v[at, 2 * width + lane : 2 * width + lane + 128]
                soft = pair_softmax(stacked_pair(q2, low, high), k2, valid)
                mixed = joined_pair(mm(soft.astype(LOW), v2), group)
                mix_v[at, lane : lane + 128] = mixed.astype(LOW)
            return carry

        lax.fori_loop(0, count // group, one_group, 0)
        moves.store(mix_v, mix_any)
        arrived[2].wait()
        summed = x.astype(F32) + (mm(mix_v[...], w_out[...]) + bias[2:3, :])
        hat, inverse = normed_rows(summed)
        hat1_v[...] = hat
        inv_v[0] = jnp.broadcast_to(inverse, (count, 128))
        moves.store(hat1_v, hat1_any)
        first = hat * gains[0:1, :] + bias[3:4, :]
        low_v[...] = first.astype(LOW)
        moves.store(low_v, low_any)
        acc_v[...] = first + bias[4:5, :]
        arrived[3].wait()
        arrived[4].wait()
        for step in range(wide // tile):
            cols = slice(step * tile, (step + 1) * tile)
            hidden = mm(low_v[...], w_up[:, cols]) + tower.hidden_bias(
                smalls, use_own, step, tile
            )
            cdf = 0.5 * (1.0 + lax.erf(hidden * SQRT_HALF))
            act_v[:, cols] = (hidden * cdf).astype(LOW)
            slope_v[:, cols] = (
                cdf + hidden * (jnp.exp(-0.5 * hidden * hidden) * ROOT_TAU_INV)
            ).astype(LOW)
            acc_v[...] += mm(act_v[:, cols], w_down[cols, :])
        moves.store(act_v, act_any)
        moves.store(slope_v, slope_any)
        hat, inverse = normed_rows(acc_v[...])
        hat2_v[...] = hat
        moves.store(hat2_v, hat2_any)
        inv_v[1] = jnp.broadcast_to(inverse, (count, 128))
        moves.store(inv_v, inv_any)
        out_v[...] = (hat * gains[1:2, :] + bias[5:6, :]).astype(LOW)
        moves.store(out_v, out_any)
        moves.drain()

    outs = [
        ((count, width), LOW),
        ((count, 3 * width), LOW),
        ((count, width), LOW),
        ((count, width), LOW),
        ((count, wide), LOW),
        ((count, wide), LOW),
        ((count, width), F32),
        ((count, width), F32),
        ((2, count, 128), F32),
    ]
    scratch = [
        ((count, width), LOW),
        ((width, 3 * width), LOW),
        ((width, width), LOW),
        ((width, wide), LOW),
        ((wide, width), LOW),
        ((count, width), F32),
    ]
    inputs = [(SCALARS, tower.info), (ANYWHERE, rows)]
    inputs += [(ANYWHERE, array) for array in tower.given((0, 1, 2, 3))]
    inputs += [(INSIDE, array) for array in tower.given_small()]
    return call_kernel(
        kernel,
        "layer_forward",
        inputs,
        outs,
        scratch + outs,
        5 + len(outs),
        2 * max(count, 256) * (4 * width * width + 2 * width * wide),
        list(after),
    )


def place_rows(target, block, info, first, size, column=None):
    for piece in range(block.shape[0] // size):
        at = pl.multiple_of(info[first + piece] * size, size)
        rows = block[piece * size : (piece + 1) * size].astype(LOW)
        if column is None:
            target[pl.ds(at, size), :] = rows
        else:
            target[pl.ds(at, size), pl.ds(column[0], column[1])] = rows


def backward_wide(tower, layer, upstream, first_rows, kept, with_sums, after=()):
    act, slope, low, hat2, inverse = kept
    count, width, wide = tower.count, tower.width, tower.wide
    tile = width
    steps = wide // tile
    half = width // 2
    seeded = first_rows is not None

    def kernel(ins, outs, scratch, moves):
        ins = list(ins)
        info, up_any = ins.pop(0), ins.pop(0)
        first_ref = ins.pop(0) if seeded else None
        own_w = [ins.pop(0) for _ in range(2)]
        other_w = [ins.pop(0) for _ in range(2)] if tower.shared else [None] * 2
        act_any, slope_any, low_any, hat_any, inv_any = (ins.pop(0) for _ in range(5))
        smalls = ins
        w_up, w_down, up_v, act_v, slope_v, low_v, hat_v, inv_v = scratch[:8]
        da_any, df_any, dh_any, vec_any = outs[:4]
        da_v, df_v, dh_v, vec_v = scratch[8:12]
        if with_sums:
            down_send, down_keep, up_send, up_keep = scratch[12:]
        use_own = tower.use_own(info, layer)
        core_at = info[CORE]
        if seeded:
            up_any = up_any.at[pl.ds(tower.row_start(info), count)]
        got = [
            moves.fetch(up_any, up_v),
            moves.fetch(hat_any, hat_v),
            moves.fetch(inv_any.at[1], inv_v),
            moves.fetch_either(use_own, own_w[1].at[0, tower.index], other_w[1], w_down),
            moves.fetch(slope_any, slope_v),
            moves.fetch_either(use_own, own_w[0].at[0, tower.index], other_w[0], w_up),
            moves.fetch(low_any, low_v),
            moves.fetch(act_any, act_v),
        ]
        gains, _ = tower.small_rows(smalls, use_own)
        for copy in got[:3]:
            copy.wait()
        upward = up_v[...].astype(F32)
        if seeded:
            row_at = lax.broadcasted_iota(jnp.int32, (count, 1), 0)
            lengths = tower.lengths_at(info)
            seen = jnp.zeros((count, 1), F32)
            for seq in range(tower.seqs):
                start = seq * tower.slots
                inside_seq = (row_at >= start) & (row_at < start + info[lengths + seq])
                seen = jnp.where(inside_seq, 1.0, seen)
            upward = upward * seen
            for seq in range(tower.seqs):
                upward = upward + jnp.where(
                    row_at == seq * tower.slots, first_ref[seq : seq + 1, :], 0.0
                )
        hat = hat_v[...]
        vec_v[0:1, :] = col_sum(upward * hat)
        vec_v[1:2, :] = col_sum(upward)
        d_second = norm_pull(upward, hat, inv_v[:, 0:1], gains[1:2, :])
        d_low = d_second.astype(LOW)
        df_v[...] = d_low
        vec_v[2:3, :] = col_sum(d_low.astype(F32))
        vec_v[7:8, :] = jnp.zeros((1, width), F32)
        moves.store(df_v, df_any)
        da_v[...] = d_second
        for copy in got[3:]:
            copy.wait()
        if with_sums:
            df_send = df_v[:, pl.ds(pl.multiple_of((1 - core_at) * half, 128), half)]
            df_keep = df_v[:, pl.ds(pl.multiple_of(core_at * half, 128), half)]
        for step in range(steps):
            at = lax.rem(step + (1 - core_at) * (steps // 2), steps)
            cols = pl.ds(pl.multiple_of(at * tile, tile), tile)
            w_rows = w_down[cols, :]
            d_hidden = (mm_nt(df_v[...], w_rows) * slope_v[:, cols].astype(F32)).astype(LOW)
            dh_v[:, cols] = d_hidden
            vec_v[pl.ds(3 + at, 1), :] = col_sum(d_hidden.astype(F32))
            da_v[...] += mm_nt(d_hidden, w_up[:, cols])
            if with_sums:
                product = mm_tn(low_v[...], d_hidden)
                target = up_send if step < steps // 2 else up_keep
                place_rows(
                    target,
                    product,
                    info,
                    PLACES + BLOCKS,
                    width // BLOCKS,
                    ((step % (steps // 2)) * tile, tile),
                )
                if step == steps // 2 - 1:
                    moves.store(up_send, outs[6])
                left = act_v[:, cols]
                piece = wide // BLOCKS
                per = tile // piece
                place_rows(down_send, mm_tn(left, df_send), info, PLACES + at * per, piece)
                place_rows(down_keep, mm_tn(left, df_keep), info, PLACES + at * per, piece)
        if with_sums:
            moves.store(down_send, outs[4])
            moves.store(down_keep, outs[5])
            moves.store(up_keep, outs[7])
        moves.store(da_v, da_any)
        moves.store(dh_v, dh_any)
        moves.store(vec_v, vec_any)
        moves.drain()

    outs = [
        ((count, width), F32),
        ((count, width), LOW),
        ((count, wide), LOW),
        ((8, width), F32),
    ]
    if with_sums:
        outs += [((wide, half), LOW)] * 2 + [((width, wide // 2), LOW)] * 2
    scratch = [
        ((width, wide), LOW),
        ((wide, width), LOW),
        ((count, width), upstream.dtype),
        ((count, wide), LOW),
        ((count, wide), LOW),
        ((count, width), LOW),
        ((count, width), F32),
        ((count, 128), F32),
    ]
    inputs = [(SCALARS, tower.info), (ANYWHERE, upstream)]
    if seeded:
        inputs.append((INSIDE, first_rows))
    inputs += [(ANYWHERE, array) for array in tower.given((2, 3))]
    inputs += [(ANYWHERE, array) for array in (act, slope, low, hat2, inverse)]
    inputs += [(INSIDE, array) for array in tower.given_small()]
    return call_kernel(
        kernel,
        "backward_wide",
        inputs,
        outs,
        scratch + outs,
        8 + len(outs),
        2 * max(count, 256) * width * wide * (4 if with_sums else 2),
        list(after),
    )


def backward_attention(tower, layer, rows, whole_rows, d_first, kept, with_sums, low_out, after=()):
    qkv, mixed, hat1, inverse = kept
    count, width, group = tower.count, tower.width, tower.group
    half = width // 2
    out_type = LOW if low_out else F32

    def kernel(ins, outs, scratch, moves):
        ins = list(ins)
        info, da_any = ins.pop(0), ins.pop(0)
        own_w = [ins.pop(0) for _ in range(2)]
        other_w = [ins.pop(0) for _ in range(2)] if tower.shared else [None] * 2
        x_any, qkv_any, mix_any, hat_any, inv_any = (ins.pop(0) for _ in range(5))
        smalls = ins
        dx_any, dz_any, dp_any, vec_any = outs[:4]
        w_qkv, w_out, da_v, x_v, qkv_v, mix_v, hat_v, inv_v, dmix_v, du_v = scratch[:10]
        dx_v, dz_v, dp_v, vec_v = scratch[10:14]
        use_own = tower.use_own(info, layer)
        core_at = info[CORE]
        if whole_rows:
            x_any = x_any.at[pl.ds(tower.row_start(info), count)]
        got = [
            moves.fetch(da_any, da_v),
            moves.fetch(hat_any, hat_v),
            moves.fetch(inv_any.at[0], inv_v),
            moves.fetch_either(use_own, own_w[1].at[0, tower.index], other_w[1], w_out),
            moves.fetch(qkv_any, qkv_v),
            moves.fetch(mix_any, mix_v),
            moves.fetch(x_any, x_v),
            moves.fetch_either(use_own, own_w[0].at[0, tower.index], other_w[0], w_qkv),
        ]
        gains, _ = tower.small_rows(smalls, use_own)
        for copy in got[:3]:
            copy.wait()
        upward = da_v[...]
        hat = hat_v[...]
        vec_v[0:1, :] = col_sum(upward * hat)
        vec_v[1:2, :] = col_sum(upward)
        d_summed = norm_pull(upward, hat, inv_v[:, 0:1], gains[0:1, :])
        du_v[...] = d_summed
        d_low = d_summed.astype(LOW)
        dz_v[...] = d_low
        vec_v[2:3, :] = col_sum(d_low.astype(F32))
        vec_v[5:8, :] = jnp.zeros((3, width), F32)
        moves.store(dz_v, dz_any)
        got[3].wait()
        dmix_v[...] = mm_nt(d_low, w_out[...]).astype(LOW)
        got[4].wait()

        def one_group(g, carry):
            at = pl.ds(pl.multiple_of(g * group, group), group)
            valid = valid_keys(
                info, tower.lengths_at(info) + g * (group // tower.slots), group, tower.slots
            )
            low, high = pair_masks(LOW)
            scale = HEAD_DIM ** (-0.5)
            for pair in range(width // 128):
                lane = pair * 128
                q2 = qkv_v[at, lane : lane + 128]
                k2 = qkv_v[at, width + lane : width + lane + 128]
                v2 = qkv_v[at, 2 * width + lane : 2 * width + lane + 128]
                query_stack = stacked_pair(q2, low, high)
                soft = pair_softmax(query_stack, k2, valid)
                d_stack = stacked_pair(dmix_v[at, lane : lane + 128], low, high)
                d_soft = mm_nt(d_stack, v2)
                total = jnp.sum(d_soft * soft, axis=-1, keepdims=True)
                d_scores = (soft * (d_soft - total)).astype(LOW)
                dp_v[at, lane : lane + 128] = (
                    joined_pair(mm(d_scores, k2), group) * scale
                ).astype(LOW)
                dp_v[at, width + lane : width + lane + 128] = (
                    mm_tn(d_scores, query_stack) * scale
                ).astype(LOW)
                dp_v[at, 2 * width + lane : 2 * width + lane + 128] = mm_tn(
                    soft.astype(LOW), d_stack
                ).astype(LOW)
            return carry

        lax.fori_loop(0, count // group, one_group, 0)
        vec_v[3:4, :] = col_sum(dp_v[:, :width].astype(F32))
        vec_v[4:5, :] = col_sum(dp_v[:, 2 * width :].astype(F32))
        moves.store(dp_v, dp_any)
        for copy in got[5:]:
            copy.wait()
        if with_sums:
            send, keep = scratch[14:]
            wide_half = 3 * half
            piece = width // BLOCKS
            first = PLACES + 2 * BLOCKS
            for target, side, to in ((send, 1 - core_at, outs[4]), (keep, core_at, outs[5])):
                for third in range(3):
                    cols = pl.ds(pl.multiple_of(side * wide_half + third * half, 128), half)
                    product = mm_tn(x_v[...], dp_v[:, cols])
                    place_rows(target, product, info, first, piece, (third * half, half))
                cols = pl.ds(pl.multiple_of(side * half, 128), half)
                product = mm_tn(mix_v[...], dz_v[:, cols])
                place_rows(target, product, info, first, piece, (wide_half, half))
                moves.store(target, to)
        d_input = du_v[...]
        for part in range(3):
            cols = slice(part * width, (part + 1) * width)
            d_input = d_input + mm_nt(dp_v[:, cols], w_qkv[:, cols])
        dx_v[...] = d_input.astype(out_type)
        moves.store(dx_v, dx_any)
        moves.store(vec_v, vec_any)
        moves.drain()

    outs = [
        ((count, width), out_type),
        ((count, width), LOW),
        ((count, 3 * width), LOW),
        ((8, width), F32),
    ]
    if with_sums:
        outs += [((width, 4 * half), LOW)] * 2
    scratch = [
        ((width, 3 * width), LOW),
        ((width, width), LOW),
        ((count, width), F32),
        ((count, width), LOW),
        ((count, 3 * width), LOW),
        ((count, width), LOW),
        ((count, width), F32),
        ((count, 128), F32),
        ((count, width), LOW),
        ((count, width), F32),
    ]
    inputs = [(SCALARS, tower.info), (ANYWHERE, d_first)]
    inputs += [(ANYWHERE, array) for array in tower.given((0, 1))]
    inputs += [(ANYWHERE, array) for array in (rows, qkv, mixed, hat1, inverse)]
    inputs += [(INSIDE, array) for array in tower.given_small()]
    return call_kernel(
        kernel,
        "backward_attention",
        inputs,
        outs,
        scratch + outs,
        8 + len(outs),
        2 * max(count, 256) * 4 * width * width * (2 if with_sums else 1),
        list(after),
    )


def block_chooser(rows, columns, valid, size, bit):
    at = lax.broadcasted_iota(jnp.int32, (1, columns), 1)
    piece = jnp.floor((at.astype(F32) + 0.5) * (1.0 / size)).astype(jnp.int32)
    wanted = jnp.where(at < valid, at + (piece + bit) * size, -1)
    row_at = lax.broadcasted_iota(jnp.int32, (rows, columns), 0)
    return jnp.where(row_at == wanted, 1.0, 0.0).astype(LOW)


def pack_first(info, early, late, width, after=()):
    count = early[0].shape[0]
    wide = early[3].shape[1]
    half = width // 2
    lefts = 3 * half + wide // 2
    rights = sum(array.shape[1] for array in early[4:])

    def kernel(ins, outs, scratch, moves):
        info_ref = ins[0]
        first, second = ins[1:9], ins[9:17]
        held, keep, send = scratch[:8], scratch[8], scratch[9]
        flag = info_ref[IS_FIRST] == 1
        got = [moves.fetch_either(flag, a, b, to) for a, b, to in zip(first, second, held)]
        mine = info_ref[X_BIT]
        choose = []
        for size in (width // BLOCKS, wide // BLOCKS):
            choose.append(
                [block_chooser(width, half, half, size, bit) for bit in (mine, 1 - mine)]
            )
        for copy in got:
            copy.wait()
        for target, which in ((keep, 0), (send, 1)):
            for part in range(3):
                target[:, part * half : (part + 1) * half] = mm(
                    held[part][...], choose[0][which]
                ).astype(LOW)
            for part in range(wide // width):
                at = (3 + part) * half
                target[:, at : at + half] = mm(
                    held[3][:, part * width : (part + 1) * width], choose[1][which]
                ).astype(LOW)
        at = lefts
        for part in held[4:]:
            send[:, at : at + part.shape[1]] = part[...]
            at += part.shape[1]
        moves.store(keep, outs[0])
        moves.store(send, outs[1])
        moves.drain()

    outs = [((count, lefts), LOW), ((count, lefts + rights), LOW)]
    inputs = [(SCALARS, info)] + [(ANYWHERE, array) for array in tuple(early) + tuple(late)]
    scratch = [(array.shape, LOW) for array in early]
    return call_kernel(
        kernel, "pack_first", inputs, outs, scratch + outs, 10, 1 << 28, list(after)
    )


def pack_second(info, keep, send, arrived, width, after=()):
    count, lefts = keep.shape
    rights = send.shape[1] - lefts
    half, quarter = width // 2, width // 4
    third = 256
    groups = lefts // half - 3
    packed = 3 * third + groups * quarter

    def kernel(ins, outs, scratch, moves):
        info_ref, keep_any, send_any, arrived_any = ins
        keep_v, send_v, arrived_v, keep2, send2 = scratch
        got = [
            moves.fetch(keep_any, keep_v),
            moves.fetch(send_any, send_v),
            moves.fetch(arrived_any, arrived_v),
        ]
        mine = info_ref[Y_BIT]
        narrow = [
            block_chooser(half, third, quarter, width // BLOCKS, bit) for bit in (mine, 1 - mine)
        ]
        broad = [
            block_chooser(2 * half, 2 * quarter, 2 * quarter, quarter, bit)
            for bit in (mine, 1 - mine)
        ]
        for copy in got:
            copy.wait()
        for target, which in ((keep2, 0), (send2, 1)):
            for source, row in ((keep_v, 0), (arrived_v, count)):
                rows = slice(row, row + count)
                for part in range(3):
                    target[rows, part * third : (part + 1) * third] = mm(
                        source[:, part * half : (part + 1) * half], narrow[which]
                    ).astype(LOW)
                for part in range(groups // 2):
                    at = 3 * third + 2 * part * quarter
                    begin = (3 + 2 * part) * half
                    target[rows, at : at + 2 * quarter] = mm(
                        source[:, begin : begin + 2 * half], broad[which]
                    ).astype(LOW)
        send2[:count, packed:] = send_v[:, lefts:]
        send2[count:, packed:] = arrived_v[:, lefts:]
        moves.store(keep2, outs[0])
        moves.store(send2, outs[1])
        moves.drain()

    outs = [((2 * count, packed), LOW), ((2 * count, packed + rights), LOW)]
    inputs = [(SCALARS, info)] + [(ANYWHERE, array) for array in (keep, send, arrived)]
    scratch = [(array.shape, LOW) for array in (keep, send, arrived)]
    return call_kernel(
        kernel, "pack_second", inputs, outs, scratch + outs, 5, 1 << 28, list(after)
    )


def query_products(info, keep, send, arrived, width, wide, after=()):
    count, packed = keep.shape
    third = 256
    piece = width // BLOCKS
    columns = 3 * width + width + wide + (wide // width) * width

    def kernel(ins, outs, scratch, moves):
        info_ref, keep_any, send_any, arrived_any = ins
        left_v, right_v, result = scratch
        total = right_v.shape[1]
        got = [
            moves.fetch(keep_any, left_v.at[:count]),
            moves.fetch(arrived_any.at[:, :packed], left_v.at[pl.ds(count, count)]),
            moves.fetch(send_any.at[:, packed:], right_v.at[:count]),
            moves.fetch(arrived_any.at[:, packed:], right_v.at[pl.ds(count, count)]),
        ]
        for copy in got:
            copy.wait()
        at = 0
        for part, cols in enumerate((3 * width, width, wide)):
            left = left_v[:, part * third : (part + 1) * third]
            for begin in range(0, cols, width):
                product = mm_tn(left, right_v[:, at + begin : at + begin + width])
                for z in range(4):
                    row = pl.multiple_of(info_ref[Z_PLACES + z] * piece, piece)
                    result[pl.ds(row, piece), at + begin : at + begin + width] = product[
                        z * piece : (z + 1) * piece
                    ].astype(LOW)
            at += cols
        product = mm_tn(left_v[:, 3 * third :], right_v[:, at:])
        per = wide // width
        for z in range(4):
            row = pl.multiple_of(info_ref[Z_PLACES + z] * piece, piece)
            for part in range(per):
                begin = (z * per + part) * piece
                result[pl.ds(row, piece), at + part * width : at + (part + 1) * width] = product[
                    begin : begin + piece
                ].astype(LOW)
        moves.store(result.at[pl.ds(2 * piece, 2 * piece)], outs[0])
        moves.store(result.at[pl.ds(0, 2 * piece)], outs[1])
        moves.drain()

    outs = [((2 * piece, columns), LOW)] * 2
    inputs = [(SCALARS, info)] + [(ANYWHERE, array) for array in (keep, send, arrived)]
    scratch = [
        ((2 * count, packed), LOW),
        ((2 * count, send.shape[1] - packed), LOW),
        ((4 * piece, columns), LOW),
    ]
    return call_kernel(
        kernel, "query_products", inputs, outs, scratch, 6, 1 << 30, list(after)
    )


def pick_bit(grid, axis, index):
    return lax.dynamic_index_in_dim(grid, index, axis, keepdims=False)


def own_bit(bit):
    return (lax.axis_index("batch") // bit) % 2


def scatter_sum(grid, bits, left):
    left = list(left)
    for bit in bits:
        axis = left.index(bit)
        mine = own_bit(bit)
        sent = pick_bit(grid, axis, 1 - mine)
        kept = pick_bit(grid, axis, mine)
        arrived = flip_swap(sent, bit)
        total = kept.astype(jnp.float32) + arrived.astype(jnp.float32)
        left.remove(bit)
        grid = total if not left else total.astype(grid.dtype)
    return grid


def all_bits(size):
    bits = [1 << i for i in range(size.bit_length() - 1)]
    return bits[::-1]


def to_grid(array, size):
    bits = all_bits(size)
    return array.reshape((2,) * len(bits) + (array.shape[0] // size,) + array.shape[1:])


def gather_all(block, size):
    if size != 16:
        for bit in all_bits(size)[::-1]:
            block = jnp.concatenate([block, flip_swap(block, bit)], 0)
        return block
    block = jnp.concatenate([block] + [flip_swap(block, k) for k in (1, 2, 3)], 0)
    return jnp.concatenate([block] + [flip_swap(block, k) for k in (4, 8, 12)], 0)


def contrast(own_cls, micro, positive, query_count, batch_index, batch_size):
    width = own_cls.shape[1]
    chip_rows = own_cls.shape[0]
    gathered = gather_all(own_cls, batch_size).reshape(batch_size, chip_rows, width)
    all_q = gathered[:, :query_count].reshape(-1, width)
    all_p = gathered[:, query_count:].reshape(-1, width)
    blocks = jnp.arange(batch_size, dtype=jnp.int32) ^ batch_index
    query_ids = (
        blocks[:, None] * query_count + jnp.arange(query_count, dtype=jnp.int32)[None, :]
    ).reshape(-1)
    passage_ids = (
        3 * query_ids[:, None] + jnp.arange(3, dtype=jnp.int32)[None, :]
    ).reshape(-1)
    labels = jnp.take(micro, query_ids)
    wanted = jnp.take(positive, query_ids)
    logit_scale = LOGIT_GAIN * width ** (-0.5)
    logits = mm_nt(all_q, all_p) * logit_scale
    same_group = labels[:, None] == jnp.repeat(labels, 3)[None, :]
    logits = jnp.where(same_group, logits, MASK_FILL)
    row_top = jnp.max(logits, axis=-1, keepdims=True)
    exponent = jnp.exp(logits - row_top)
    totals = jnp.sum(exponent, axis=-1, keepdims=True)
    target = passage_ids[None, :] == wanted[:, None]
    loss_all = (
        row_top[:, 0] + jnp.log(totals[:, 0]) - jnp.sum(jnp.where(target, logits, 0.0), axis=-1)
    )
    coefficient = (exponent / totals - target.astype(jnp.float32)) * logit_scale
    passage_count = 3 * query_count
    d_cls_q = jnp.dot(coefficient[:query_count], all_p.astype(jnp.float32), precision=PRECISE)
    d_cls_p = lax.dot_general(
        coefficient[:, :passage_count],
        all_q.astype(jnp.float32),
        (((0,), (0,)), ((), ())),
        precision=PRECISE,
    )
    return loss_all[:query_count], d_cls_q, d_cls_p


def integers(core, index, size, len_q, len_p):
    blocks = jnp.arange(BLOCKS, dtype=jnp.int32)
    own = index // (size // BLOCKS)
    relative = blocks ^ own
    places = [
        sum(((relative // bit) % 2) * (8 >> at) for at, bit in enumerate(order))
        for order in ORDERS
    ]
    depth = jnp.arange(4, dtype=jnp.int32) ^ (own // 4)
    z_places = (depth % 2) * 2 + depth // 2
    few = jnp.stack([1 - core, core])
    ends = jnp.stack([own % 2, (own // 2) % 2])
    return jnp.concatenate([few, *places, z_places, ends, len_q, len_p]).astype(jnp.int32)


def two_halves(first, second):
    cut = first.shape[0] // 2

    def added(low, high):
        return (first[low:high].astype(F32) + second[low:high].astype(F32)).astype(LOW)

    return added(cut, 2 * cut), added(0, cut)


class Chain:
    def __init__(self, send, keep, order, size, over_core=True):
        self.order = list(order)
        self.size = size
        self.scale = size // BLOCKS
        self.keep = keep
        self.sent = send
        if over_core:
            self.arrived = core_swap(send)
        else:
            self.arrived = self.swap(send)

    def swap(self, block):
        return flip_swap(block, self.order.pop(0) * self.scale)

    def step(self):
        self.sent, self.keep = two_halves(self.keep, self.arrived)
        self.arrived = self.swap(self.sent)
        return self.sent

    def result(self):
        while self.order:
            self.step()
        total = self.keep.astype(F32) + self.arrived.astype(F32)
        return total

    def rest(self, total):
        if self.scale == 1:
            return total
        left = all_bits(self.scale)
        return scatter_sum(to_grid(total.astype(LOW), self.scale), left, left)


def shards(
    x_q,
    x_p,
    len_q,
    len_p,
    cot_q,
    cot_p,
    positive,
    micro,
    w_qkv,
    w_out,
    w_up,
    w_down,
    norm_gain,
    biases,
    b_up,
):
    core = lax.axis_index("section")
    is_first = core == 0
    batch_index = lax.axis_index("batch")
    size = lax.axis_size("batch")
    bits = all_bits(size)
    query_count, slots_q, model = x_q.shape
    half_count = x_p.shape[0] // 2
    slots_p = x_p.shape[1]
    wide = w_up.shape[-1]
    info = integers(core, batch_index, size, len_q, len_p)
    weights = (w_qkv, w_out, w_up, w_down)
    smalls = (norm_gain, biases, b_up)
    other_p = tuple(core_swap(member[0, 1]) for member in weights)
    small_other = core_swap(
        jnp.concatenate([norm_gain[0, 1], biases[0, 1], b_up[0, 1].reshape(-1, model)], 0)
    )
    tower_q = Tower(0, info, weights, None, smalls, None, query_count, slots_q, LENGTHS)
    tower_p = Tower(
        1, info, weights, other_p, smalls, small_other, half_count, slots_p, LENGTHS + query_count
    )
    flat_q = x_q.reshape(-1, model)
    flat_p = x_p.reshape(-1, model)
    cots_q = cot_q.reshape(-1, model)
    cots_p = cot_p.reshape(-1, model)

    early_q = forward_layer(tower_q, 0, flat_q, True)
    mid_q = early_q[0]
    arrived_q = core_swap(mid_q)
    late_q = forward_layer(tower_q, 1, arrived_q, True)
    early_p = forward_layer(tower_p, 0, flat_p, True, (late_q[0],))
    mid_p = early_p[0]
    late_p = forward_layer(tower_p, 1, mid_p, False)
    top_q, top_p = late_q[0], late_p[0]

    cls_rows = jnp.concatenate([top_q[::slots_q], top_p[::slots_p]], 0)
    cls_other = core_swap(cls_rows)
    cls_chip = jnp.concatenate(
        [
            jnp.where(is_first, cls_other[:query_count], cls_rows[:query_count]),
            jnp.where(is_first, cls_rows[query_count:], cls_other[query_count:]),
            jnp.where(is_first, cls_other[query_count:], cls_rows[query_count:]),
        ],
        0,
    )
    loss_own, d_cls_q, d_cls_p = contrast(
        cls_chip, micro, positive, query_count, batch_index, size
    )
    d_own_p = lax.dynamic_slice_in_dim(d_cls_p, core * half_count, half_count, 0)

    def wide_kept(kept):
        return kept[4], kept[5], kept[3], kept[7], kept[8]

    def narrow_kept(kept):
        return kept[1], kept[2], kept[6], kept[8]

    def factors(rows, kept, wide_back, narrow_back):
        return (
            rows,
            kept[2],
            kept[3],
            kept[4],
            narrow_back[2],
            narrow_back[1],
            wide_back[2],
            wide_back[1],
        )

    late_wide_p = backward_wide(tower_p, 1, cots_p, d_own_p, wide_kept(late_p), True)
    down1 = Chain(late_wide_p[4], late_wide_p[5], ORDERS[0], size)
    up1 = Chain(late_wide_p[6], late_wide_p[7], ORDERS[1], size)

    late_wide_q = backward_wide(
        tower_q, 1, cots_q, d_cls_q, wide_kept(late_q), False, (late_wide_p[0],)
    )
    after = (down1.step(), up1.step())
    late_back_q = backward_attention(
        tower_q, 1, arrived_q, True, late_wide_q[0], narrow_kept(late_q), False, True, after
    )
    late_sent_q = late_back_q[0]
    grad_mid_q = core_swap(late_sent_q)
    late_back_p = backward_attention(
        tower_p, 1, mid_p, False, late_wide_p[0], narrow_kept(late_p), True, True, (late_sent_q,)
    )
    late_sent_p = late_back_p[0]
    rest1 = Chain(late_back_p[4], late_back_p[5], ORDERS[2], size)
    after = (down1.step(), up1.step(), late_sent_p)
    early_wide_q = backward_wide(
        tower_q, 0, grad_mid_q, None, wide_kept(early_q), False, after
    )
    after = (rest1.step(),)
    early_back_q = backward_attention(
        tower_q, 0, flat_q, True, early_wide_q[0], narrow_kept(early_q), False, False, after
    )
    keep, send = pack_first(
        info,
        factors(flat_q, early_q, early_wide_q, early_back_q),
        factors(arrived_q, late_q, late_wide_q, late_back_q),
        model,
    )
    gather_bits = [bit * (size // BLOCKS) for bit in (1, 2)]
    arrived = flip_swap(send, gather_bits[0])
    after = (down1.step(), up1.step(), send)
    early_wide_p = backward_wide(
        tower_p, 0, late_sent_p, None, wide_kept(early_p), True, after
    )
    down0 = Chain(early_wide_p[4], early_wide_p[5], ORDERS[0], size)
    up0 = Chain(early_wide_p[6], early_wide_p[7], ORDERS[1], size)
    after = (rest1.step(), down1.step(), up1.step())
    keep, send = pack_second(info, keep, send, arrived, model)
    arrived = flip_swap(send, gather_bits[1])
    early_back_p = backward_attention(
        tower_p,
        0,
        flat_p,
        True,
        early_wide_p[0],
        narrow_kept(early_p),
        True,
        False,
        after + (send,),
    )
    early_grad_p = early_back_p[0]
    rest0 = Chain(early_back_p[4], early_back_p[5], ORDERS[2], size)
    send, keep = query_products(info, keep, send, arrived, model, wide)
    query = Chain(send, keep, (4, 8), size, False)

    late_sums = [chain.rest(chain.result()) for chain in (down1, up1, rest1)]
    early_sums = [chain.rest(chain.result()) for chain in (down0, up0, rest0)]
    total_q = query.result()
    at = 4 * model + wide
    down_q = jnp.concatenate(
        [total_q[:, at + part * model : at + (part + 1) * model] for part in range(wide // model)],
        0,
    )
    down_q = query.rest(down_q)
    narrow_q = query.rest(total_q[:, :at])
    qkv_q = narrow_q[:, : 3 * model]
    out_q = narrow_q[:, 3 * model : 4 * model]
    up_q = narrow_q[:, 4 * model :]

    early_vec_p = jnp.concatenate([early_wide_p[3], early_back_p[3]], 0)
    late_vec_p = jnp.concatenate([late_wide_p[3], late_back_p[3]], 0)
    vec_p = jnp.where(is_first, early_vec_p, late_vec_p) + core_swap(
        jnp.where(is_first, late_vec_p, early_vec_p)
    )
    vec_q = jnp.where(
        is_first,
        jnp.concatenate([early_wide_q[3], early_back_q[3]], 0),
        jnp.concatenate([late_wide_q[3], late_back_q[3]], 0),
    )
    vecs = jnp.stack([vec_q, vec_p])
    narrow = jnp.concatenate([vecs[:, 0:3], vecs[:, 8:13]], 1)
    narrow = jnp.moveaxis(narrow.reshape(2, 8, size, -1), 2, 0)
    blk = narrow.shape[-1]
    wide_v = jnp.moveaxis(vecs[:, 3:7].reshape(2, size, 1, -1), 1, 0)
    lines = jnp.concatenate(
        [narrow.reshape(size, 2, 8 * blk), wide_v.reshape(size, 2, -1)], 2
    ).reshape(size, -1)
    lines = scatter_sum(to_grid(lines, size), bits[::-1], bits)[0].reshape(2, -1)
    eight = lines[:, : 8 * blk].reshape(2, 8, blk)
    g_gain = jnp.stack([eight[:, 3], eight[:, 0]], 1)
    g_bias = jnp.stack([eight[:, at] for at in (6, 7, 5, 4, 2, 1)], 1)
    g_bup = lines[:, 8 * blk :]

    def own_layer(early, late):
        other = core_swap(jnp.where(is_first, late, early))
        own = jnp.where(is_first, early, late)
        return jnp.where(is_first, own, other), jnp.where(is_first, other, own)

    def join(early, late, axis):
        return jnp.concatenate(own_layer(early, late), axis)

    down_p = join(early_sums[0], late_sums[0], 1)
    up_p = join(early_sums[1], late_sums[1], 1)
    first, second = own_layer(early_sums[2], late_sums[2])
    cut = 3 * model // 2
    qkv_p = jnp.concatenate([first[:, :cut], second[:, :cut]], 1)
    out_p = jnp.concatenate([first[:, cut:], second[:, cut:]], 1)
    hidden_p = join(mid_p, top_p, 0).reshape(x_p.shape)
    grad_p = join(early_grad_p, late_sent_p.astype(F32), 0).reshape(x_p.shape)
    hidden_q = jnp.where(is_first, mid_q, top_q).reshape(x_q.shape)
    grad_q = jnp.where(is_first, early_back_q[0], late_sent_q.astype(F32)).reshape(x_q.shape)
    return (
        hidden_q[None],
        hidden_p[None],
        grad_q[None],
        grad_p[None],
        loss_own,
        jnp.stack([qkv_q, qkv_p])[None],
        jnp.stack([out_q, out_p])[None],
        jnp.stack([up_q, up_p])[None],
        jnp.stack([down_q, down_p])[None],
        g_gain[None],
        g_bias[None],
        g_bup[None],
        g_bias[None, :, 0, :],
    )


def solution(mesh):
    return jax.shard_map(
        shards,
        mesh=mesh,
        in_specs=(
            P("batch", None, None),
            P("batch", None, None),
            P("batch"),
            P("batch"),
            P("batch", None, None),
            P("batch", None, None),
            P(),
            P(),
            P("section", None, None, None),
            P("section", None, None, None),
            P("section", None, None, None),
            P("section", None, None, None),
            P("section", None, None, None),
            P("section", None, None, None),
            P("section", None, None),
        ),
        out_specs=(
            P("section", "batch", None, None),
            P("section", "batch", None, None),
            P("section", "batch", None, None),
            P("section", "batch", None, None),
            P("batch"),
            P("section", None, "batch", None),
            P("section", None, "batch", None),
            P("section", None, "batch", None),
            P("section", None, "batch", None),
            P("section", None, None, "batch"),
            P("section", None, None, "batch"),
            P("section", None, "batch"),
            P("section", None, "batch"),
        ),
        check_vma=False,
    )
```

```python
import jax
import jax.numpy as jnp
from jax import lax
from jax.experimental import pallas as pl
from jax.experimental.pallas import tpu as pltpu
from jax.sharding import PartitionSpec as P

HEADS = 12
HEAD_DIM = 64


NORM_EPS = 1e-05
SQRT_HALF = 0.7071067811865476
ROOT_TAU_INV = 0.3989422804014327
MASK_FILL = -1e30
LOGIT_GAIN = 2.5
PRECISE = lax.Precision.HIGHEST


def core_swap(block):
    return lax.ppermute(block, "section", [(0, 1), (1, 0)])


def flip_swap(block, bit):
    size = lax.axis_size("batch")
    return lax.ppermute(block, "batch", [(i, i ^ bit) for i in range(size)])


F32 = jnp.float32
LOW = jnp.bfloat16
VMEM_LIMIT = 58 * 1024 * 1024
BLOCKS = 16
COST = 1 << 30
IS_FIRST, CORE, PLACES, Z_PLACES, X_BIT, Y_BIT, LENGTHS = 0, 1, 2, 98, 102, 103, 104
ORDERS = (
    (1, 2, 4, 8),
    (2, 4, 1, 8),
    (4, 1, 2, 8),
    (1, 2, 4, 8),
    (4, 1, 2, 8),
    (4, 1, 2, 8),
)


def mm(left, right):
    return lax.dot_general(left, right, (((1,), (0,)), ((), ())), preferred_element_type=F32)


def mm_nt(left, right):
    return lax.dot_general(left, right, (((1,), (1,)), ((), ())), preferred_element_type=F32)


def mm_tn(left, right):
    return lax.dot_general(left, right, (((0,), (0,)), ((), ())), preferred_element_type=F32)


def row_mean(values):
    return jnp.sum(values, axis=-1, keepdims=True) * (1.0 / values.shape[-1])


def normed_rows(values):
    center = values - row_mean(values)
    inverse = lax.rsqrt(row_mean(center * center) + NORM_EPS)
    return center * inverse, inverse


def norm_pull(upstream, normed, inverse, gain):
    scaled = upstream * gain
    return inverse * (scaled - row_mean(scaled) - normed * row_mean(scaled * normed))


def col_sum(values):
    return jnp.sum(values, axis=0, keepdims=True)


class Moves:
    def __init__(self, sems):
        self.sems = sems
        self.used = 0
        self.open = []

    def slot(self):
        self.used += 1
        return self.sems.at[self.used - 1]

    def fetch(self, source, target):
        copy = pltpu.make_async_copy(source, target, self.slot())
        copy.start()
        return copy

    def fetch_either(self, flag, first, second, target):
        sem = self.slot()
        copy = pltpu.make_async_copy(first, target, sem)
        if second is None:
            copy.start()
            return copy
        other = pltpu.make_async_copy(second, target, sem)

        @pl.when(flag)
        def _():
            copy.start()

        @pl.when(jnp.logical_not(flag))
        def _():
            other.start()

        return copy

    def store(self, source, target):
        self.open.append(self.fetch(source, target))

    def drain(self):
        for copy in self.open:
            copy.wait()


class Tower:
    def __init__(self, index, info, weights, others, small, small_other, seqs, slots, first_len):
        self.index = index
        self.info = info
        self.weights = weights
        self.others = others
        self.small = small
        self.small_other = small_other
        self.seqs = seqs
        self.slots = slots
        self.first_len = first_len
        self.count = seqs * slots
        self.width = weights[1].shape[-1]
        self.wide = weights[2].shape[-1]
        self.group = self.count if self.count <= 128 else slots
        self.shared = others is not None

    def given(self, which):
        own = [self.weights[at] for at in which]
        return own + ([self.others[at] for at in which] if self.shared else [])

    def given_small(self):
        return list(self.small) + ([self.small_other] if self.shared else [])

    def use_own(self, info, layer):
        return info[IS_FIRST] == (1 if layer == 0 else 0)

    def lengths_at(self, info):
        return self.first_len + (info[CORE] * self.seqs if self.shared else 0)

    def row_start(self, info):
        return pl.multiple_of(info[CORE] * self.count, self.count) if self.shared else 0

    def small_rows(self, refs, flag):
        own = [refs[0][0, self.index], refs[1][0, self.index]]
        if self.shared:
            other = refs[3]
            own = [
                jnp.where(flag, own[0], other[0:2, :]),
                jnp.where(flag, own[1], other[2:8, :]),
            ]
        return own

    def hidden_bias(self, refs, flag, step, tile):
        own = refs[2][0, self.index : self.index + 1, step * tile : (step + 1) * tile]
        if self.shared:
            own = jnp.where(flag, own, refs[3][8 + step : 9 + step, :])
        return own


ANYWHERE = pl.BlockSpec(memory_space=pl.ANY)
SCALARS = pl.BlockSpec(memory_space=pltpu.SMEM)
INSIDE = pl.BlockSpec(memory_space=pltpu.VMEM)


def call_kernel(kernel, name, inputs, outs, scratch, copies, micros, after, through=()):
    count = len(inputs)
    given = list(after) + list(through)
    extra = len(given)

    def body(*refs):
        refs = list(refs)
        kernel(
            refs[:count],
            refs[count + extra : count + extra + len(outs)],
            refs[count + extra + len(outs) + len(through) : -1],
            Moves(refs[-1]),
        )

    return pl.pallas_call(
        body,
        out_shape=[jax.ShapeDtypeStruct(shape, kind) for shape, kind in outs]
        + [jax.ShapeDtypeStruct(array.shape, array.dtype) for array in through],
        in_specs=[spec for spec, _ in inputs] + [ANYWHERE] * extra,
        out_specs=[ANYWHERE] * (len(outs) + len(through)),
        input_output_aliases={
            count + len(after) + at: len(outs) + at for at in range(len(through))
        },
        scratch_shapes=[pltpu.VMEM(shape, kind) for shape, kind in scratch]
        + [pltpu.SemaphoreType.DMA((copies,))],
        compiler_params=pltpu.CompilerParams(vmem_limit_bytes=VMEM_LIMIT),
        cost_estimate=pl.CostEstimate(
            flops=int(COST * micros) + 1024, bytes_accessed=1024, transcendentals=0
        ),
        name=name,
    )(*[array for _, array in inputs], *given)


def pair_masks(dtype):
    lanes = lax.broadcasted_iota(jnp.int32, (1, 128), 1)
    low = jnp.where(lanes < HEAD_DIM, 1.0, 0.0)
    return low.astype(dtype), (1.0 - low).astype(dtype)


def stacked_pair(block, low, high):
    return jnp.concatenate([block * low, block * high], axis=0)


def joined_pair(stacked, group):
    lanes = lax.broadcasted_iota(jnp.int32, (1, 128), 1)
    return jnp.where(lanes < HEAD_DIM, stacked[:group], stacked[group:])


def pair_softmax(query_stack, key_block, valid):
    scores = mm_nt(key_block, query_stack) * HEAD_DIM ** (-0.5)
    scores = jnp.where(valid, scores, MASK_FILL)
    exponent = jnp.exp(scores - jnp.max(scores, axis=0, keepdims=True))
    return exponent * (1.0 / jnp.sum(exponent, axis=0, keepdims=True))


def valid_keys(info, first_len, group, slots):
    keys = lax.broadcasted_iota(jnp.int32, (group, 2 * group), 0)
    queries = lax.broadcasted_iota(jnp.int32, (group, 2 * group), 1)
    seqs = group // slots
    if seqs == 1:
        return keys < info[first_len]
    queries = jnp.where(queries >= group, queries - group, queries)
    valid = None
    for j in range(seqs):
        low = j * slots
        inside = (
            (queries >= low)
            & (queries < low + slots)
            & (keys >= low)
            & (keys < low + info[first_len + j])
        )
        valid = inside if valid is None else valid | inside
    return valid


def weight_shapes(tower):
    width, steps = tower.width, tower.wide // tower.width
    return [
        ((3, width, width), LOW),
        ((width, width), LOW),
        ((steps, width, width), LOW),
        ((steps, width, width), LOW),
    ]


def fetch_narrow(tower, flag, own, other, targets, moves, order=(0, 1, 2, 3)):
    width = tower.width
    got = {}
    for part in order:
        if part == 3:
            got[3] = moves.fetch_either(flag, own[1].at[0, tower.index], other[1], targets[1])
            continue
        cols = pl.ds(part * width, width)
        second = other[0].at[:, cols] if tower.shared else None
        got[part] = moves.fetch_either(
            flag, own[0].at[0, tower.index, :, cols], second, targets[0].at[part]
        )
    return got


def fetch_step(tower, flag, own, other, targets, moves, step, at):
    width = tower.width
    part = pl.ds(pl.multiple_of(at * width, width), width)
    up, down = (other[0].at[:, part], other[1].at[part]) if tower.shared else (None, None)
    return (
        moves.fetch_either(flag, own[1].at[0, tower.index, part], down, targets[1].at[step]),
        moves.fetch_either(flag, own[0].at[0, tower.index, :, part], up, targets[0].at[step]),
    )


def kept_scratch(tower):
    count, width, wide = tower.count, tower.width, tower.wide
    steps = wide // width
    return [
        ((count, width), LOW),
        ((count, 3 * width), LOW),
        ((count, width), LOW),
        ((count, width), LOW),
        ((steps, count, width), LOW),
        ((steps, count, width), LOW),
        ((count, width), LOW),
        ((count, width), LOW),
        ((2, count, 128), F32),
        ((width // 128, count, 2 * tower.group), LOW),
    ]


OUTPUT, LEFTS, PROJECTED, SLOPE, HAT1, HAT2, INVERSES, SOFT = range(8)


def kept_shapes(tower, inner):
    count, width, wide = tower.count, tower.width, tower.wide
    steps = wide // width
    return [
        ((count, width), LOW),
        ((count, 2 * width + wide + (width if inner else 0)), LOW),
        ((count, 3 * width), LOW),
        ((steps, count, width), LOW),
        ((count, width), LOW),
        ((count, width), LOW),
        ((2, count, 128), F32),
        ((width // 128, count, 2 * tower.group), LOW),
    ]


def forward_body(tower, layer, info, x_v, got, weights, smalls, acc_v, kept, outs, moves):
    count, width, group = tower.count, tower.width, tower.group
    w_qkv, w_out, w_up, w_down = weights
    out_v, qkv_v, mix_v, low_v, act_v, slope_v, hat1_v, hat2_v, inv_v, soft_v = kept
    use_own = tower.use_own(info, layer)
    gains, bias = tower.small_rows(smalls, use_own)
    x = x_v[...]
    for part in range(3):
        got[part].wait()
        block = mm(x, w_qkv[part])
        if part == 0:
            block = block + bias[0:1, :]
        if part == 2:
            block = block + bias[1:2, :]
        qkv_v[:, part * width : (part + 1) * width] = block.astype(LOW)
    moves.store(qkv_v, outs[PROJECTED])
    low, high = pair_masks(LOW)
    for g in range(count // group):
        at = slice(g * group, (g + 1) * group)
        valid = valid_keys(
            info, tower.lengths_at(info) + g * (group // tower.slots), group, tower.slots
        )
        for pair in range(width // 128):
            lane = pair * 128
            q2 = qkv_v[at, lane : lane + 128]
            k2 = qkv_v[at, width + lane : width + lane + 128]
            v2 = qkv_v[at, 2 * width + lane : 2 * width + lane + 128]
            soft = pair_softmax(stacked_pair(q2, low, high), k2, valid).astype(LOW)
            soft_v[pair, at, :] = soft
            mix_v[at, lane : lane + 128] = joined_pair(mm_tn(soft, v2), group).astype(LOW)
    moves.store(soft_v, outs[SOFT])
    moves.store(mix_v, outs[LEFTS].at[:, pl.ds(0, width)])
    got[3].wait()
    summed = x.astype(F32) + (mm(mix_v[...], w_out[...]) + bias[2:3, :])
    hat, inverse = normed_rows(summed)
    hat1_v[...] = hat.astype(LOW)
    inv_v[0] = jnp.broadcast_to(inverse, (count, 128))
    moves.store(hat1_v, outs[HAT1])
    first = hat * gains[0:1, :] + bias[3:4, :]
    low_v[...] = first.astype(LOW)
    moves.store(low_v, outs[LEFTS].at[:, pl.ds(width, width)])
    acc_v[...] = first + bias[4:5, :]
    for step in range(tower.wide // width):
        for copy in got[4 + step]:
            copy.wait()
        hidden = mm(low_v[...], w_up[step]) + tower.hidden_bias(smalls, use_own, step, width)
        cdf = 0.5 * (1.0 + lax.erf(hidden * SQRT_HALF))
        act = (hidden * cdf).astype(LOW)
        act_v[step] = act
        slope_v[step] = (
            cdf + hidden * (jnp.exp(-0.5 * hidden * hidden) * ROOT_TAU_INV)
        ).astype(LOW)
        moves.store(act_v.at[step], outs[LEFTS].at[:, pl.ds((2 + step) * width, width)])
        moves.store(slope_v.at[step], outs[SLOPE].at[step])
        acc_v[...] += mm(act, w_down[step])
    hat, inverse = normed_rows(acc_v[...])
    hat2_v[...] = hat.astype(LOW)
    moves.store(hat2_v, outs[HAT2])
    inv_v[1] = jnp.broadcast_to(inverse, (count, 128))
    moves.store(inv_v, outs[INVERSES])
    out_v[...] = (hat * gains[1:2, :] + bias[5:6, :]).astype(LOW)
    moves.store(out_v, outs[OUTPUT])


def forward_layers(tower, layers, rows, whole_rows, after=(), cost=0):
    count, width = tower.count, tower.width
    steps = tower.wide // width
    shapes = [kept_shapes(tower, at > 0) for at in range(len(layers))]
    kinds = len(shapes[0])
    held = kept_scratch(tower)

    def kernel(ins, outs, scratch, moves):
        info, x_any = ins[0], ins[1]
        own = ins[2:6]
        other = ins[6:10] if tower.shared else [None] * 4
        smalls = ins[10:] if tower.shared else ins[6:]
        x_v, acc_v = scratch[:2]
        if whole_rows:
            x_any = x_any.at[pl.ds(tower.row_start(info), count)]
        x_got = moves.fetch(x_any, x_v)
        weights, got = [], []
        for at, layer in enumerate(layers):
            targets = scratch[2 + 4 * at : 6 + 4 * at]
            flag = tower.use_own(info, layer)
            arrivals = fetch_narrow(tower, flag, own[:2], other[:2], targets[:2], moves)
            for step in range(steps):
                arrivals[4 + step] = fetch_step(
                    tower, flag, own[2:], other[2:], targets[2:], moves, step, step
                )
            weights.append(targets)
            got.append(arrivals)
        x_got.wait()
        for at, layer in enumerate(layers):
            begin = 2 + 4 * len(layers) + len(held) * at
            kept = scratch[begin : begin + len(held)]
            forward_body(
                tower,
                layer,
                info,
                x_v,
                got[at],
                weights[at],
                smalls,
                acc_v,
                kept,
                outs[kinds * at : kinds * (at + 1)],
                moves,
            )
            x_v = kept[0]
            if at + 1 < len(layers):
                inner = outs[kinds * (at + 1) + LEFTS]
                moves.store(x_v, inner.at[:, pl.ds(2 * width + tower.wide, width)])
        moves.drain()

    outs = [shape for layer_shapes in shapes for shape in layer_shapes]
    scratch = [((count, width), LOW), ((count, width), F32)] + weight_shapes(tower) * len(layers)
    inputs = [(SCALARS, tower.info), (ANYWHERE, rows)]
    inputs += [(ANYWHERE, array) for array in tower.given((0, 1, 2, 3))]
    inputs += [(INSIDE, array) for array in tower.given_small()]
    results = call_kernel(
        kernel,
        "layer_forward",
        inputs,
        outs,
        scratch + held * len(layers),
        1 + len(layers) * (4 + 2 * steps + 9 + 2 * steps),
        cost,
        list(after),
    )
    return [results[kinds * at : kinds * (at + 1)] for at in range(len(layers))]


def place_rows(target, block, info, first, size, columns):
    for piece in range(block.shape[0] // size):
        at = pl.multiple_of(info[first + piece] * size, size)
        target[pl.ds(at, size), columns] = block[piece * size : (piece + 1) * size].astype(LOW)


def wide_scratch(tower, upstream):
    count, width = tower.count, tower.width
    steps = tower.wide // width
    return weight_shapes(tower)[2:] + [
        ((count, width), upstream.dtype),
        ((count, width), LOW),
        ((count, 128), F32),
        ((steps, count, width), LOW),
        ((count, width), F32),
        ((count, width), LOW),
        ((steps, count, width), LOW),
        ((8, width), F32),
    ]


def store_sides(source, side_width, outs, column, core_at, moves):
    for side, to in ((1 - core_at, outs[0]), (core_at, outs[1])):
        lanes = pl.ds(pl.multiple_of(side * side_width, 128), side_width)
        moves.store(source.at[:, lanes], to.at[:, pl.ds(column, side_width)])


def wide_body(tower, layer, info, ins, first_ref, smalls, scratch, outs, moves):
    count, width = tower.count, tower.width
    steps = tower.wide // width
    up_any, own, other, slope_any, hat_any, inv_any = ins
    w_up, w_down, up_v, hat_v, inv_v, slope_v, da_v, df_v, dh_v, vec_v = scratch
    use_own = tower.use_own(info, layer)
    core_at = info[CORE]
    if first_ref is not None:
        up_any = up_any.at[pl.ds(tower.row_start(info), count)]
    first_got = [
        moves.fetch(up_any, up_v),
        moves.fetch(hat_any, hat_v),
        moves.fetch(inv_any.at[1], inv_v),
    ]
    got = []
    tiles = list(range(steps))
    if tower.shared:
        tiles = [lax.rem(step + (1 - core_at) * (steps // 2), steps) for step in range(steps)]
    for step, at in enumerate(tiles):
        pieces = [moves.fetch(slope_any.at[at], slope_v.at[step])]
        pieces += fetch_step(tower, use_own, own, other, (w_up, w_down), moves, step, at)
        got.append(pieces)
    gains, _ = tower.small_rows(smalls, use_own)
    for copy in first_got:
        copy.wait()
    upward = up_v[...].astype(F32)
    if first_ref is not None:
        row_at = lax.broadcasted_iota(jnp.int32, (count, 1), 0)
        lengths = tower.lengths_at(info)
        seen = jnp.zeros((count, 1), F32)
        for seq in range(tower.seqs):
            start = seq * tower.slots
            inside_seq = (row_at >= start) & (row_at < start + info[lengths + seq])
            seen = jnp.where(inside_seq, 1.0, seen)
        upward = upward * seen
        for seq in range(tower.seqs):
            upward = upward + jnp.where(
                row_at == seq * tower.slots, first_ref[seq : seq + 1, :], 0.0
            )
    hat = hat_v[...].astype(F32)
    vec_v[0:1, :] = col_sum(upward * hat)
    vec_v[1:2, :] = col_sum(upward)
    d_second = norm_pull(upward, hat, inv_v[:, 0:1], gains[1:2, :])
    d_low = d_second.astype(LOW)
    df_v[...] = d_low
    vec_v[2:3, :] = col_sum(d_low.astype(F32))
    vec_v[7:8, :] = jnp.zeros((1, width), F32)
    da_v[...] = d_second
    vec_out, df_out, dh_out = outs
    if tower.shared:
        store_sides(df_v, width // 2, df_out, tower.wide // 2, core_at, moves)
    else:
        moves.store(df_v, df_out[0])
    for step, at in enumerate(tiles):
        for copy in got[step]:
            copy.wait()
        d_hidden = (mm_nt(df_v[...], w_down[step]) * slope_v[step].astype(F32)).astype(LOW)
        vec_v[pl.ds(3 + at, 1), :] = col_sum(d_hidden.astype(F32))
        dh_v[step] = d_hidden
        da_v[...] += mm_nt(d_hidden, w_up[step])
        if tower.shared:
            side, place = divmod(step, steps // 2)
            moves.store(dh_v.at[step], dh_out[side].at[:, pl.ds(place * width, width)])
        else:
            moves.store(dh_v.at[step], dh_out[0].at[step])
    moves.store(vec_v, vec_out)


def narrow_scratch(tower, out_type):
    count, width = tower.count, tower.width
    return weight_shapes(tower)[:2] + [
        ((count, width), LOW),
        ((count, 128), F32),
        ((count, 3 * width), LOW),
        ((width // 128, count, 2 * tower.group), LOW),
        ((count, width), LOW),
        ((count, 3 * width), LOW),
        ((count, width), LOW),
        ((count, width), F32),
        ((count, width), out_type),
        ((8, width), F32),
    ]


def narrow_fetch(tower, layer, info, ins, scratch, moves):
    own, other, qkv_any, hat_any, inv_any, soft_any = ins
    w_qkv, w_out, hat_v, inv_v, qkv_v, soft_v = scratch[:6]
    use_own = tower.use_own(info, layer)
    got = {"hat": [moves.fetch(hat_any, hat_v), moves.fetch(inv_any.at[0], inv_v)]}
    weights = fetch_narrow(tower, use_own, own, other, (w_qkv, w_out), moves, (3,))
    got["heads"] = [moves.fetch(qkv_any, qkv_v), moves.fetch(soft_any, soft_v)]
    weights.update(fetch_narrow(tower, use_own, own, other, (w_qkv, w_out), moves, (0, 1, 2)))
    got["weights"] = weights
    return got


def narrow_body(tower, layer, info, got, da_v, smalls, scratch, outs, moves):
    count, width, group = tower.count, tower.width, tower.group
    w_qkv, w_out, hat_v, inv_v, qkv_v, soft_v, dz_v, dp_v, dmix_v, du_v, dx_v, vec_v = scratch
    use_own = tower.use_own(info, layer)
    core_at = info[CORE]
    dx_out, vec_out, dz_out, dp_out = outs
    gains, _ = tower.small_rows(smalls, use_own)
    for copy in got["hat"]:
        copy.wait()
    upward = da_v[...]
    hat = hat_v[...].astype(F32)
    vec_v[0:1, :] = col_sum(upward * hat)
    vec_v[1:2, :] = col_sum(upward)
    d_summed = norm_pull(upward, hat, inv_v[:, 0:1], gains[0:1, :])
    du_v[...] = d_summed
    d_low = d_summed.astype(LOW)
    dz_v[...] = d_low
    vec_v[2:3, :] = col_sum(d_low.astype(F32))
    vec_v[5:8, :] = jnp.zeros((3, width), F32)
    if tower.shared:
        store_sides(dz_v, width // 2, dz_out, tower.wide // 2 + 2 * width, core_at, moves)
    else:
        moves.store(dz_v, dz_out[0])
    got["weights"][3].wait()
    dmix_v[...] = mm_nt(d_low, w_out[...]).astype(LOW)
    for copy in got["heads"]:
        copy.wait()
    low, high = pair_masks(LOW)
    scale = HEAD_DIM ** (-0.5)
    for g in range(count // group):
        at = slice(g * group, (g + 1) * group)
        for pair in range(width // 128):
            lane = pair * 128
            q2 = qkv_v[at, lane : lane + 128]
            k2 = qkv_v[at, width + lane : width + lane + 128]
            v2 = qkv_v[at, 2 * width + lane : 2 * width + lane + 128]
            soft = soft_v[pair, at, :]
            d_stack = stacked_pair(dmix_v[at, lane : lane + 128], low, high)
            d_soft = mm_nt(v2, d_stack)
            soft_wide = soft.astype(F32)
            total = jnp.sum(d_soft * soft_wide, axis=0, keepdims=True)
            d_scores = (soft_wide * (d_soft - total)).astype(LOW)
            dp_v[at, lane : lane + 128] = (
                joined_pair(mm_tn(d_scores, k2), group) * scale
            ).astype(LOW)
            dp_v[at, width + lane : width + lane + 128] = (
                mm(d_scores, stacked_pair(q2, low, high)) * scale
            ).astype(LOW)
            dp_v[at, 2 * width + lane : 2 * width + lane + 128] = mm(soft, d_stack).astype(LOW)
    vec_v[3:4, :] = col_sum(dp_v[:, :width].astype(F32))
    vec_v[4:5, :] = col_sum(dp_v[:, 2 * width :].astype(F32))
    moves.store(vec_v, vec_out)
    if tower.shared:
        store_sides(dp_v, 3 * width // 2, dp_out, (tower.wide + width) // 2, core_at, moves)
    else:
        moves.store(dp_v, dp_out[0])
    d_input = du_v[...]
    for part in range(3):
        got["weights"][part].wait()
        d_input = d_input + mm_nt(dp_v[:, part * width : (part + 1) * width], w_qkv[part])
    dx_v[...] = d_input.astype(dx_v.dtype)
    moves.store(dx_v, dx_out)


def backward_layer(
    tower, layer, upstream, first_rows, kept, low_out, after=(), cost=0, through=()
):
    count, width, wide = tower.count, tower.width, tower.wide
    steps = wide // width
    seeded = first_rows is not None
    out_type = LOW if low_out else F32
    wide_shapes = wide_scratch(tower, upstream)

    def kernel(ins, outs, scratch, moves):
        ins = list(ins)
        info, up_any = ins.pop(0), ins.pop(0)
        first_ref = ins.pop(0) if seeded else None
        own = [ins.pop(0) for _ in range(4)]
        other = [ins.pop(0) for _ in range(4)] if tower.shared else [None] * 4
        slope_any, hat2_any, inv_any, qkv_any, hat1_any, soft_any = (
            ins.pop(0) for _ in range(6)
        )
        first, second = scratch[: len(wide_shapes)], scratch[len(wide_shapes) :]
        dx, vec1, vec2 = outs[:3]
        df, dh, dz, dp = [outs[3:]] * 4 if tower.shared else [outs[at : at + 1] for at in range(3, 7)]
        wide_body(
            tower,
            layer,
            info,
            (up_any, own[2:], other[2:], slope_any, hat2_any, inv_any),
            first_ref,
            ins,
            first,
            (vec1, df, dh),
            moves,
        )
        given = (own[:2], other[:2], qkv_any, hat1_any, inv_any, soft_any)
        got = narrow_fetch(tower, layer, info, given, second, moves)
        narrow_body(
            tower, layer, info, got, first[6], ins, second, (dx, vec2, dz, dp), moves
        )
        moves.drain()

    outs = [((count, width), out_type), ((8, width), F32), ((8, width), F32)]
    if tower.shared:
        outs += [((count, (5 * width + wide) // 2), LOW)] * 2
    else:
        outs += [((count, width), LOW), ((steps, count, width), LOW)]
        outs += [((count, width), LOW), ((count, 3 * width), LOW)]
    inputs = [(SCALARS, tower.info), (ANYWHERE, upstream)]
    if seeded:
        inputs.append((INSIDE, first_rows))
    inputs += [(ANYWHERE, array) for array in tower.given((0, 1, 2, 3))]
    inputs += [(ANYWHERE, kept[at]) for at in (SLOPE, HAT2, INVERSES, PROJECTED, HAT1, SOFT)]
    inputs += [(INSIDE, array) for array in tower.given_small()]
    return call_kernel(
        kernel,
        "backward_layer",
        inputs,
        outs,
        wide_shapes + narrow_scratch(tower, out_type),
        3 + 3 * steps + 8 + 3 + steps + 6,
        cost,
        list(after),
        through,
    )


def place_rows(target, block, info, first, size, columns):
    for piece in range(block.shape[0] // size):
        at = pl.multiple_of(info[first + piece] * size, size)
        target[pl.ds(at, size), columns] = block[piece * size : (piece + 1) * size].astype(LOW)


def passage_products(tower, layer, rows, lefts, other_lefts, rights, other_rights, after=(), cost=0):
    count, width, wide = tower.count, tower.width, tower.wide
    steps = wide // width
    half = width // 2
    piece = width // BLOCKS
    places = PLACES + 3 * BLOCKS * layer
    whole = rows is not None

    def kernel(ins, outs, scratch, moves):
        ins = list(ins)
        info = ins.pop(0)
        x_any = ins.pop(0) if whole else None
        left, other_left, right, other_right = ins
        low_v, dh_v, act_v, df_v, x_v, dp_v, mix_v, dz_v, g_down, g_up, g_rest = scratch
        above, below = pl.ds(0, count), pl.ds(count, count)

        def both(sources, column, target):
            columns = pl.ds(column, target.shape[1])
            return [
                moves.fetch(sources[0].at[:, columns], target.at[above]),
                moves.fetch(sources[1].at[:, columns], target.at[below]),
            ]

        lefts_of = (left, other_left)
        rights_of = (right, other_right)
        got_low = both(lefts_of, width, low_v)
        got_dh = [both(rights_of, at * width, dh_v.at[at]) for at in range(steps // 2)]
        got_df = both(rights_of, wide // 2, df_v)
        got_act = [both(lefts_of, (2 + at) * width, act_v.at[at]) for at in range(steps)]
        if whole:
            start = tower.row_start(info)
            other_start = pl.multiple_of(count - start, count)
            got_x = [
                moves.fetch(x_any.at[pl.ds(start, count)], x_v.at[above]),
                moves.fetch(x_any.at[pl.ds(other_start, count)], x_v.at[below]),
            ]
        else:
            got_x = both(lefts_of, 2 * width + wide, x_v)
        got_x += both(rights_of, wide // 2 + half, dp_v)
        got_mix = both(lefts_of, 0, mix_v) + both(rights_of, wide // 2 + 2 * width, dz_v)

        def ready(copies):
            for copy in copies:
                copy.wait()

        def send(source, at):
            cut = source.shape[0] // 2
            moves.store(source.at[pl.ds(cut, cut)], outs[2 * at])
            moves.store(source.at[pl.ds(0, cut)], outs[2 * at + 1])

        ready(got_low)
        for at in range(steps // 2):
            ready(got_dh[at])
            columns = slice(at * width, (at + 1) * width)
            place_rows(
                g_up, mm_tn(low_v[...], dh_v[at]), info, places + BLOCKS, piece, columns
            )
        send(g_up, 1)
        ready(got_df)
        parts = wide // width
        for at in range(steps):
            ready(got_act[at])
            product = mm_tn(act_v[at], df_v[...])
            for block in range(width // piece):
                index, part = divmod(at * (width // piece) + block, parts)
                to = pl.multiple_of(info[places + index] * piece, piece)
                g_down[pl.ds(to, piece), part * half : (part + 1) * half] = product[
                    block * piece : (block + 1) * piece
                ].astype(LOW)
        send(g_down, 0)
        ready(got_x)
        for part in range(3):
            columns = slice(part * half, (part + 1) * half)
            product = mm_tn(x_v[...], dp_v[:, columns])
            place_rows(g_rest, product, info, places + 2 * BLOCKS, piece, columns)
        ready(got_mix)
        product = mm_tn(mix_v[...], dz_v[...])
        place_rows(g_rest, product, info, places + 2 * BLOCKS, piece, slice(3 * half, 4 * half))
        send(g_rest, 2)
        moves.drain()

    outs = [((half, 4 * half), LOW)] * 6
    scratch = [
        ((2 * count, width), LOW),
        ((steps // 2, 2 * count, width), LOW),
        ((steps, 2 * count, width), LOW),
        ((2 * count, half), LOW),
        ((2 * count, width), LOW),
        ((2 * count, 3 * half), LOW),
        ((2 * count, width), LOW),
        ((2 * count, half), LOW),
        ((width, wide // 2), LOW),
        ((width, wide // 2), LOW),
        ((width, 4 * half), LOW),
    ]
    arrays = [rows] if whole else []
    arrays += [lefts, other_lefts, rights, other_rights]
    inputs = [(SCALARS, tower.info)] + [(ANYWHERE, array) for array in arrays]
    return call_kernel(
        kernel,
        "passage_products",
        inputs,
        outs,
        scratch,
        2 * (1 + steps // 2 + 1 + steps + 4) + 6,
        cost,
        list(after),
    )


def block_chooser(rows, columns, valid, size, bit):
    at = lax.broadcasted_iota(jnp.int32, (1, columns), 1)
    piece = jnp.floor((at.astype(F32) + 0.5) * (1.0 / size)).astype(jnp.int32)
    wanted = jnp.where(at < valid, at + (piece + bit) * size, -1)
    row_at = lax.broadcasted_iota(jnp.int32, (rows, columns), 0)
    return jnp.where(row_at == wanted, 1.0, 0.0).astype(LOW)


def pack_first(info, early, late, after=(), cost=0):
    count, width = early[0].shape
    steps = early[2].shape[0]
    half = width // 2
    piece = width // BLOCKS
    lefts = (2 * half, (1 + steps) * half)
    rights = (4 * width, (steps + 1) * width)

    def kernel(ins, outs, scratch, moves):
        info_ref = ins[0]
        first, second = ins[1:7], ins[7:13]
        x_v, left_v, dh_v, df_v, dz_v, dp_v = scratch[:6]
        results = scratch[6:]
        flag = info_ref[IS_FIRST] == 1
        got = [moves.fetch_either(flag, a, b, to) for a, b, to in zip(first, second, scratch)]
        bits = [(info_ref[at], 1 - info_ref[at]) for at in (X_BIT, Y_BIT)]
        for copy in got:
            copy.wait()
        for which in range(2):
            first_to, second_to = results[which], results[2 + which]
            choose = block_chooser(width, half, half, piece, bits[0][which])
            first_to[:, :half] = mm(x_v[...], choose).astype(LOW)
            first_to[:, half : 2 * half] = mm(left_v[:, :width], choose).astype(LOW)
            choose = block_chooser(width, half, half, 2 * piece, bits[1][which])
            second_to[:, :half] = mm(left_v[:, width : 2 * width], choose).astype(LOW)
            for step in range(steps):
                start = (2 + step) * width + bits[1][which] * half
                second_to[:, (1 + step) * half : (2 + step) * half] = left_v[
                    :, pl.ds(pl.multiple_of(start, 128), half)
                ]
        send_a, send_b = results[1], results[3]
        send_a[:, lefts[0] : lefts[0] + 3 * width] = dp_v[...]
        send_a[:, lefts[0] + 3 * width :] = dz_v[...]
        for step in range(steps):
            begin = lefts[1] + step * width
            send_b[:, begin : begin + width] = dh_v[step]
        send_b[:, lefts[1] + steps * width :] = df_v[...]
        for at in range(4):
            moves.store(results[at], outs[at])
        moves.drain()

    outs = []
    for left, right in zip(lefts, rights):
        outs += [((count, left), LOW), ((count, left + right), LOW)]
    inputs = [(SCALARS, info)] + [(ANYWHERE, array) for array in tuple(early) + tuple(late)]
    scratch = [(array.shape, LOW) for array in early]
    return call_kernel(
        kernel, "pack_first", inputs, outs, scratch + outs, 12, cost, list(after)
    )


def pack_second(info, keeps, sends, arrivals, width, after=(), cost=0):
    count = keeps[0].shape[0]
    half, quarter, third = width // 2, width // 4, 256
    piece = width // BLOCKS
    steps = keeps[1].shape[1] // half - 1
    lefts = [keep.shape[1] for keep in keeps]
    rights = [send.shape[1] - left for send, left in zip(sends, lefts)]
    packed = (2 * third, third + steps * quarter)

    def kernel(ins, outs, scratch, moves):
        info_ref = ins[0]
        got = [moves.fetch(source, to) for source, to in zip(ins[1:], scratch)]
        bits = [(info_ref[at], 1 - info_ref[at]) for at in (Y_BIT, X_BIT)]
        for copy in got:
            copy.wait()
        for lot in range(2):
            keep_v, send_v, arrived_v = scratch[lot], scratch[2 + lot], scratch[4 + lot]
            for which in range(2):
                target = scratch[6 + 2 * lot + which]
                narrow = block_chooser(half, third, quarter, piece, bits[lot][which])
                for source, row in ((keep_v, 0), (arrived_v, count)):
                    rows = slice(row, row + count)
                    for part in range(2 - lot):
                        target[rows, part * third : (part + 1) * third] = mm(
                            source[:, part * half : (part + 1) * half], narrow
                        ).astype(LOW)
                    if lot == 0:
                        continue
                    broad = block_chooser(2 * half, half, half, quarter, bits[lot][which])
                    for part in range(steps // 2):
                        begin = (1 + 2 * part) * half
                        at = third + part * half
                        target[rows, at : at + half] = mm(
                            source[:, begin : begin + 2 * half], broad
                        ).astype(LOW)
            send2 = scratch[6 + 2 * lot + 1]
            send2[:count, packed[lot] :] = send_v[:, lefts[lot] :]
            send2[count:, packed[lot] :] = arrived_v[:, lefts[lot] :]
        for at in range(4):
            moves.store(scratch[6 + at], outs[at])
        moves.drain()

    outs = []
    for left, right in zip(packed, rights):
        outs += [((2 * count, left), LOW), ((2 * count, left + right), LOW)]
    arrays = tuple(keeps) + tuple(sends) + tuple(arrivals)
    inputs = [(SCALARS, info)] + [(ANYWHERE, array) for array in arrays]
    scratch = [(array.shape, LOW) for array in arrays]
    return call_kernel(
        kernel, "pack_second", inputs, outs, scratch + outs, 10, cost, list(after)
    )


def query_products(info, keeps, sends, arrivals, width, wide, after=(), cost=0):
    count = keeps[0].shape[0]
    third = 256
    piece = width // BLOCKS
    packed = [keep.shape[1] for keep in keeps]
    rights = [send.shape[1] - left for send, left in zip(sends, packed)]
    columns = 4 * width + 2 * wide

    def kernel(ins, outs, scratch, moves):
        info_ref = ins[0]
        keep_any, send_any, arrived_any = ins[1:3], ins[3:5], ins[5:7]
        left_v, right_v, result = scratch[0:2], scratch[2:4], scratch[4]
        got = []
        for lot in range(2):
            cut = packed[lot]
            below = pl.ds(count, count)
            got.append(
                [
                    moves.fetch(keep_any[lot], left_v[lot].at[pl.ds(0, count)]),
                    moves.fetch(arrived_any[lot].at[:, pl.ds(0, cut)], left_v[lot].at[below]),
                    moves.fetch(
                        send_any[lot].at[:, pl.ds(cut, rights[lot])],
                        right_v[lot].at[pl.ds(0, count)],
                    ),
                    moves.fetch(
                        arrived_any[lot].at[:, pl.ds(cut, rights[lot])], right_v[lot].at[below]
                    ),
                ]
            )

        def place(z, rows, columns_at):
            row = pl.multiple_of(info_ref[Z_PLACES + z] * piece, piece)
            result[pl.ds(row, piece), columns_at : columns_at + width] = rows.astype(LOW)

        at = 0
        for lot, part, cols, begin in (
            (0, 0, 3 * width, 0),
            (0, 1, width, 3 * width),
            (1, 0, wide, 0),
        ):
            if part == 0:
                for copy in got[lot]:
                    copy.wait()
            left = left_v[lot][:, part * third : (part + 1) * third]
            for block in range(cols // width):
                cut = begin + block * width
                product = mm_tn(left, right_v[lot][:, cut : cut + width])
                for z in range(4):
                    place(z, product[z * piece : (z + 1) * piece], at + block * width)
            at += cols
        product = mm_tn(left_v[1][:, third:], right_v[1][:, wide:])
        per = wide // width
        for z in range(4):
            for part in range(per):
                begin = (z * per + part) * piece
                place(z, product[begin : begin + piece], at + part * width)
        moves.store(result.at[pl.ds(2 * piece, 2 * piece)], outs[0])
        moves.store(result.at[pl.ds(0, 2 * piece)], outs[1])
        moves.drain()

    outs = [((2 * piece, columns), LOW)] * 2
    arrays = tuple(keeps) + tuple(sends) + tuple(arrivals)
    inputs = [(SCALARS, info)] + [(ANYWHERE, array) for array in arrays]
    scratch = [((2 * count, cut), LOW) for cut in packed]
    scratch += [((2 * count, cut), LOW) for cut in rights]
    scratch += [((4 * piece, columns), LOW)]
    return call_kernel(
        kernel, "query_products", inputs, outs, scratch, 10, cost, list(after)
    )


def take_in(items, after=(), cost=0, through=()):
    def kernel(ins, outs, scratch, moves):
        ins, scratch = list(ins), list(scratch)
        taken = []
        for pairs, last in items:
            got = []
            for _ in pairs:
                held = [scratch.pop(0), scratch.pop(0)]
                got.append((held, [moves.fetch(ins.pop(0), to) for to in held]))
            taken.append((got, [scratch.pop(0) for _ in range(1 if last else 2)]))
        out_at = 0
        for (got, results), (_, last) in zip(taken, items):
            for held, copies in got:
                for copy in copies:
                    copy.wait()
            for which, result in enumerate(results):
                part_rows = result.shape[0]
                start = 0 if last else (1 - which) * part_rows
                column = 0
                for (keep_v, arrived_v), _ in got:
                    columns = keep_v.shape[1]
                    chunk = 48 if columns <= 1536 and part_rows % 48 == 0 else 16

                    def one(step, carry, keep_v=keep_v, arrived_v=arrived_v, column=column):
                        to = pl.ds(pl.multiple_of(step * chunk, 16), chunk)
                        of = pl.ds(pl.multiple_of(start + step * chunk, 16), chunk)
                        total = keep_v[of, :].astype(F32) + arrived_v[of, :].astype(F32)
                        result[to, column : column + keep_v.shape[1]] = total.astype(result.dtype)
                        return carry

                    lax.fori_loop(0, part_rows // chunk, one, 0)
                    column += columns
                moves.store(result, outs[out_at])
                out_at += 1
        moves.drain()

    outs, scratch = [], []
    for pairs, last in items:
        rows = pairs[0][0].shape[0]
        columns = sum(keep.shape[1] for keep, _ in pairs)
        kind = pairs[0][0].dtype
        mine = [((rows, columns), F32)] if last else [((rows // 2, columns), kind)] * 2
        outs += mine
        for keep, arrived in pairs:
            scratch += [(keep.shape, kind), (arrived.shape, kind)]
        scratch += mine
    inputs = [(ANYWHERE, array) for pairs, _ in items for pair in pairs for array in pair]
    return call_kernel(
        kernel, "take_in", inputs, outs, scratch, len(inputs) + len(outs), cost, list(after), through
    )


class Chain:
    def __init__(self, send, keep, order, scale):
        self.order = list(order)
        self.scale = scale
        self.keep = keep
        self.total = None
        self.arrived = self.swap(send)

    def swap(self, block):
        return flip_swap(block, self.order.pop(0) * self.scale)


def play_round(groups, after=(), cost=0, through=()):
    items = [
        ([(chain.keep, chain.arrived) for chain in group], not group[0].order) for group in groups
    ]
    results = list(take_in(items, after, cost, through))
    seen = []
    for group in groups:
        chain = group[0]
        assert all(other.order == chain.order for other in group)
        if not chain.order:
            chain.total = results.pop(0)
            seen.append(chain.total)
            continue
        sent, chain.keep = results.pop(0), results.pop(0)
        chain.arrived = chain.swap(sent)
        seen.append(sent)
    return tuple(seen + results)


def pick_bit(grid, axis, index):
    return lax.dynamic_index_in_dim(grid, index, axis, keepdims=False)


def own_bit(bit):
    return (lax.axis_index("batch") // bit) % 2


def scatter_sum(grid, bits, left):
    left = list(left)
    for bit in bits:
        axis = left.index(bit)
        mine = own_bit(bit)
        sent = pick_bit(grid, axis, 1 - mine)
        kept = pick_bit(grid, axis, mine)
        arrived = flip_swap(sent, bit)
        total = kept.astype(jnp.float32) + arrived.astype(jnp.float32)
        left.remove(bit)
        grid = total if not left else total.astype(grid.dtype)
    return grid


def all_bits(size):
    bits = [1 << i for i in range(size.bit_length() - 1)]
    return bits[::-1]


def to_grid(array, size):
    bits = all_bits(size)
    return array.reshape((2,) * len(bits) + (array.shape[0] // size,) + array.shape[1:])


def gather_all(block, size):
    if size != 16:
        for bit in all_bits(size)[::-1]:
            block = jnp.concatenate([block, flip_swap(block, bit)], 0)
        return block
    block = jnp.concatenate([block] + [flip_swap(block, k) for k in (1, 2, 3)], 0)
    return jnp.concatenate([block] + [flip_swap(block, k) for k in (4, 8, 12)], 0)


def contrast(own_cls, micro, positive, query_count, batch_index, batch_size):
    width = own_cls.shape[1]
    chip_rows = own_cls.shape[0]
    gathered = gather_all(own_cls, batch_size).reshape(batch_size, chip_rows, width)
    all_q = gathered[:, :query_count].reshape(-1, width)
    all_p = gathered[:, query_count:].reshape(-1, width)
    blocks = jnp.arange(batch_size, dtype=jnp.int32) ^ batch_index
    query_ids = (
        blocks[:, None] * query_count + jnp.arange(query_count, dtype=jnp.int32)[None, :]
    ).reshape(-1)
    passage_ids = (
        3 * query_ids[:, None] + jnp.arange(3, dtype=jnp.int32)[None, :]
    ).reshape(-1)
    labels = jnp.take(micro, query_ids)
    wanted = jnp.take(positive, query_ids)
    logit_scale = LOGIT_GAIN * width ** (-0.5)
    logits = mm_nt(all_q, all_p) * logit_scale
    same_group = labels[:, None] == jnp.repeat(labels, 3)[None, :]
    logits = jnp.where(same_group, logits, MASK_FILL)
    row_top = jnp.max(logits, axis=-1, keepdims=True)
    exponent = jnp.exp(logits - row_top)
    totals = jnp.sum(exponent, axis=-1, keepdims=True)
    target = passage_ids[None, :] == wanted[:, None]
    loss_all = (
        row_top[:, 0] + jnp.log(totals[:, 0]) - jnp.sum(jnp.where(target, logits, 0.0), axis=-1)
    )
    coefficient = (exponent / totals - target.astype(jnp.float32)) * logit_scale
    passage_count = 3 * query_count
    d_cls_q = jnp.dot(coefficient[:query_count], all_p.astype(jnp.float32), precision=PRECISE)
    d_cls_p = lax.dot_general(
        coefficient[:, :passage_count],
        all_q.astype(jnp.float32),
        (((0,), (0,)), ((), ())),
        precision=PRECISE,
    )
    return loss_all[:query_count], d_cls_q, d_cls_p


def integers(core, index, size, len_q, len_p):
    blocks = jnp.arange(BLOCKS, dtype=jnp.int32)
    own = index // (size // BLOCKS)
    relative = blocks ^ own
    places = [
        sum(((relative // bit) % 2) * (8 >> at) for at, bit in enumerate(order))
        for order in ORDERS
    ]
    depth = jnp.arange(4, dtype=jnp.int32) ^ (own // 4)
    z_places = (depth % 2) * 2 + depth // 2
    few = jnp.stack([1 - core, core])
    ends = jnp.stack([own % 2, (own // 2) % 2])
    return jnp.concatenate([few, *places, z_places, ends, len_q, len_p]).astype(jnp.int32)


def shards(
    x_q,
    x_p,
    len_q,
    len_p,
    cot_q,
    cot_p,
    positive,
    micro,
    w_qkv,
    w_out,
    w_up,
    w_down,
    norm_gain,
    biases,
    b_up,
):
    core = lax.axis_index("section")
    is_first = core == 0
    batch_index = lax.axis_index("batch")
    size = lax.axis_size("batch")
    bits = all_bits(size)
    query_count, slots_q, model = x_q.shape
    half_count = x_p.shape[0] // 2
    slots_p = x_p.shape[1]
    wide = w_up.shape[-1]
    info = integers(core, batch_index, size, len_q, len_p)
    weights = (w_qkv, w_out, w_up, w_down)
    smalls = (norm_gain, biases, b_up)
    other_p = tuple(core_swap(member[0, 1]) for member in weights)
    small_other = core_swap(
        jnp.concatenate([norm_gain[0, 1], biases[0, 1], b_up[0, 1].reshape(-1, model)], 0)
    )
    tower_q = Tower(0, info, weights, None, smalls, None, query_count, slots_q, LENGTHS)
    tower_p = Tower(
        1, info, weights, other_p, smalls, small_other, half_count, slots_p, LENGTHS + query_count
    )
    flat_q = x_q.reshape(-1, model)
    flat_p = x_p.reshape(-1, model)
    cots_q = cot_q.reshape(-1, model)
    cots_p = cot_p.reshape(-1, model)

    (early_q,) = forward_layers(tower_q, (0,), flat_q, True)
    mid_q = early_q[OUTPUT]
    arrived_q = core_swap(mid_q)
    (late_q,) = forward_layers(tower_q, (1,), arrived_q, True)
    early_p, late_p = forward_layers(tower_p, (0, 1), flat_p, True, (late_q[OUTPUT],))
    mid_p = early_p[OUTPUT]
    top_q, top_p = late_q[OUTPUT], late_p[OUTPUT]

    cls_rows = jnp.concatenate([top_q[::slots_q], top_p[::slots_p]], 0)
    cls_other = core_swap(cls_rows)
    cls_chip = jnp.concatenate(
        [
            jnp.where(is_first, cls_other[:query_count], cls_rows[:query_count]),
            jnp.where(is_first, cls_rows[query_count:], cls_other[query_count:]),
            jnp.where(is_first, cls_other[query_count:], cls_rows[query_count:]),
        ],
        0,
    )
    loss_own, d_cls_q, d_cls_p = contrast(
        cls_chip, micro, positive, query_count, batch_index, size
    )
    d_own_p = lax.dynamic_slice_in_dim(d_cls_p, core * half_count, half_count, 0)

    def factors(rows, kept, back):
        return (rows, kept[LEFTS], back[4], back[3], back[5], back[6])

    scale = size // BLOCKS

    def passage_chains(layer, rows, lefts, other_lefts, back, other_rights, after, cost):
        products = passage_products(
            tower_p, layer, rows, lefts, other_lefts, back[4], other_rights, after, cost
        )
        return [
            Chain(products[2 * at], products[2 * at + 1], ORDERS[3 * layer + at], scale)
            for at in range(3)
        ], (products[0],)

    def vector_halves(*parts):
        early_q, late_q, early, late = (
            jnp.concatenate(parts[at : at + 2], 0) for at in (0, 2, 4, 6)
        )
        vec_p = jnp.where(is_first, early, late) + core_swap(jnp.where(is_first, late, early))
        vec_q = jnp.where(is_first, early_q, late_q)
        vecs = jnp.stack([vec_q, vec_p])
        narrow = jnp.concatenate([vecs[:, 0:3], vecs[:, 8:13]], 1)
        narrow = jnp.moveaxis(narrow.reshape(2, 8, size, -1), 2, 0).reshape(size, 2, -1)
        broad = jnp.moveaxis(vecs[:, 3:7].reshape(2, size, -1), 1, 0)
        lines = jnp.concatenate([narrow, broad], 2).reshape(BLOCKS, -1)
        lines = jnp.pad(lines, ((0, 0), (0, 16 * 128 - lines.shape[1])))
        place = info[PLACES : PLACES + BLOCKS]
        chosen = (place[None, :] == jnp.arange(BLOCKS)[:, None]).astype(F32)
        lines = jnp.dot(chosen, lines, precision=PRECISE).reshape(BLOCKS * 16, 128)
        return lines[BLOCKS * 8 :], lines[: BLOCKS * 8]

    late_back_q = backward_layer(
        tower_q, 1, cots_q, d_cls_q, late_q, True, cost=0
    )
    late_sent_q = late_back_q[0]
    grad_mid_q = core_swap(late_sent_q)
    early_back_q = backward_layer(
        tower_q,
        0,
        grad_mid_q,
        None,
        early_q,
        False,
        cost=0,
        through=(late_p[LEFTS], early_p[LEFTS], jnp.where(is_first, top_p, mid_p)),
    )
    *early_back_q, late_left, early_left, hidden_sent = early_back_q
    late_left_other, early_left_other = core_swap(late_left), core_swap(early_left)
    hidden_other = core_swap(hidden_sent)
    packs = pack_first(
        info,
        factors(flat_q, early_q, early_back_q),
        factors(arrived_q, late_q, late_back_q),
        cost=0,
    )
    keeps, sends = packs[0::2], packs[1::2]
    arrivals = [flip_swap(sends[0], scale), flip_swap(sends[1], 2 * scale)]
    late_back_p = backward_layer(
        tower_p, 1, cots_p, d_own_p, late_p, True, tuple(sends), cost=0
    )
    late_sent_p = late_back_p[0]
    late_other = core_swap(late_back_p[3])
    packs = pack_second(
        info,
        keeps,
        sends,
        arrivals,
        model,
        (late_sent_p, late_left_other, early_left_other, hidden_other),
        cost=40,
    )
    keeps, sends = packs[0::2], packs[1::2]
    arrivals = [flip_swap(sends[0], 2 * scale), flip_swap(sends[1], scale)]
    (down1, up1, rest1), seen = passage_chains(
        1, None, late_left, late_left_other, late_back_p, late_other, tuple(sends), 0
    )
    early_back_p = backward_layer(
        tower_p, 0, late_sent_p, None, early_p, False, seen, cost=0
    )
    early_grad_p = early_back_p[0]
    early_other = core_swap(early_back_p[3])
    send, keep = query_products(
        info, keeps, sends, arrivals, model, wide, (early_grad_p,), cost=40
    )
    query = Chain(send, keep, (4, 8), scale)
    (down0, up0, rest0), seen = passage_chains(
        0, flat_p, early_left, early_left_other, early_back_p, early_other, (send,), 0
    )
    passed = play_round(
        [[up1, rest1]],
        seen,
        40,
        (
            early_grad_p,
            early_back_q[1],
            early_back_q[2],
            late_back_q[1],
            late_back_q[2],
            early_back_p[1],
            early_back_p[2],
            late_back_p[1],
            late_back_p[2],
        ),
    )
    seen, early_grad_p, parts = passed[:-9], passed[-9], passed[-8:]
    early_grad_other = core_swap(jnp.where(is_first, late_sent_p.astype(F32), early_grad_p))
    vector = Chain(*vector_halves(*parts), (1, 2, 4, 8), scale)
    for groups, cost in (
        ([[down0], [up0], [query], [down1]], 40),
        ([[up1], [rest0], [vector]], 40),
        ([[down0], [up0], [down1]], 40),
        ([[rest0], [vector]], 40),
        ([[down1, up1], [query]], 40),
        ([[down0, up0, rest0], [vector]], 40),
        ([[down1], [vector]], 40),
        ([[down0]], 0),
    ):
        seen = play_round(groups, seen, cost)

    def whole(total):
        if scale == 1:
            return total
        left = all_bits(scale)
        return scatter_sum(to_grid(total.astype(LOW), scale), left, left)

    def parted(total, column):
        parts = wide // model
        step = total.shape[1] // parts if column is None else model // 2
        begin = 0 if column is None else column
        return jnp.concatenate(
            [total[:, begin + part * step : begin + (part + 1) * step] for part in range(parts)], 0
        )

    def layer_sums(total):
        cut = 2 * model
        return whole(parted(total, 0)), whole(total[:, cut : 2 * cut]), whole(total[:, 2 * cut :])

    late_sums = layer_sums(down1.total)
    early_sums = layer_sums(down0.total)
    total_q = query.total
    at = 4 * model + wide
    down_q = whole(parted(total_q[:, at:], None))
    narrow_q = whole(total_q[:, :at])
    qkv_q = narrow_q[:, : 3 * model]
    out_q = narrow_q[:, 3 * model : 4 * model]
    up_q = narrow_q[:, 4 * model :]

    blk = model // size
    lines = vector.total.reshape(-1)[: 12 * (model // BLOCKS) * 2]
    if scale > 1:
        left = all_bits(scale)
        lines = scatter_sum(to_grid(lines.reshape(scale, 1, -1), scale), left, left)
    lines = lines.reshape(2, -1)
    eight = lines[:, : 8 * blk].reshape(2, 8, blk)
    g_gain = jnp.stack([eight[:, 3], eight[:, 0]], 1)
    g_bias = jnp.stack([eight[:, at] for at in (6, 7, 5, 4, 2, 1)], 1)
    g_bup = lines[:, 8 * blk :]

    def own_layer(early, late):
        other = core_swap(jnp.where(is_first, late, early))
        own = jnp.where(is_first, early, late)
        return jnp.where(is_first, own, other), jnp.where(is_first, other, own)

    def join(early, late, axis):
        return jnp.concatenate(own_layer(early, late), axis)

    down_p = join(early_sums[0], late_sums[0], 1)
    up_p = join(early_sums[1], late_sums[1], 1)
    first, second = own_layer(early_sums[2], late_sums[2])
    cut = 3 * model // 2
    qkv_p = jnp.concatenate([first[:, :cut], second[:, :cut]], 1)
    out_p = jnp.concatenate([first[:, cut:], second[:, cut:]], 1)
    pairs = (
        jnp.where(is_first, mid_p, hidden_other),
        jnp.where(is_first, hidden_other, top_p),
    )
    hidden_p = jnp.concatenate(pairs, 0).reshape(x_p.shape)
    pairs = (
        jnp.where(is_first, early_grad_p, early_grad_other),
        jnp.where(is_first, early_grad_other, late_sent_p.astype(F32)),
    )
    grad_p = jnp.concatenate(pairs, 0).reshape(x_p.shape)
    hidden_q = jnp.where(is_first, mid_q, top_q).reshape(x_q.shape)
    grad_q = jnp.where(is_first, early_back_q[0], late_sent_q.astype(F32)).reshape(x_q.shape)
    return (
        hidden_q[None],
        hidden_p[None],
        grad_q[None],
        grad_p[None],
        loss_own,
        jnp.stack([qkv_q, qkv_p])[None],
        jnp.stack([out_q, out_p])[None],
        jnp.stack([up_q, up_p])[None],
        jnp.stack([down_q, down_p])[None],
        g_gain[None],
        g_bias[None],
        g_bup[None],
        g_bias[None, :, 0, :],
    )


def solution(mesh):
    return jax.shard_map(
        shards,
        mesh=mesh,
        in_specs=(
            P("batch", None, None),
            P("batch", None, None),
            P("batch"),
            P("batch"),
            P("batch", None, None),
            P("batch", None, None),
            P(),
            P(),
            P("section", None, None, None),
            P("section", None, None, None),
            P("section", None, None, None),
            P("section", None, None, None),
            P("section", None, None, None),
            P("section", None, None, None),
            P("section", None, None),
        ),
        out_specs=(
            P("section", "batch", None, None),
            P("section", "batch", None, None),
            P("section", "batch", None, None),
            P("section", "batch", None, None),
            P("batch"),
            P("section", None, "batch", None),
            P("section", None, "batch", None),
            P("section", None, "batch", None),
            P("section", None, "batch", None),
            P("section", None, None, "batch"),
            P("section", None, None, "batch"),
            P("section", None, "batch"),
            P("section", None, "batch"),
        ),
        check_vma=False,
    )
```

```python
import jax
import jax.numpy as jnp
from jax import lax
from jax.experimental import pallas as pl
from jax.experimental.pallas import tpu as pltpu
from jax.sharding import PartitionSpec as P

HEADS = 12
HEAD_DIM = 64


NORM_EPS = 1e-05
SQRT_HALF = 0.7071067811865476
ROOT_TAU_INV = 0.3989422804014327
MASK_FILL = -1e30
LOGIT_GAIN = 2.5
PRECISE = lax.Precision.HIGHEST


def core_swap(block):
    return lax.ppermute(block, "section", [(0, 1), (1, 0)])


def flip_swap(block, bit):
    size = lax.axis_size("batch")
    return lax.ppermute(block, "batch", [(i, i ^ bit) for i in range(size)])


F32 = jnp.float32
LOW = jnp.bfloat16
VMEM_LIMIT = 58 * 1024 * 1024
BLOCKS = 16
COST = 1 << 30
IS_FIRST, CORE, PLACES, Z_PLACES, X_BIT, Y_BIT, LENGTHS = 0, 1, 2, 98, 102, 103, 104
ORDERS = (
    (1, 2, 4, 8),
    (2, 1, 4, 8),
    (2, 1, 4, 8),
    (1, 2, 4, 8),
    (2, 1, 4, 8),
    (2, 1, 4, 8),
)

LAYOUTS = (((0, 0), (1, 0), (0, 1536), (1, 1536)), ((0, 0), (1, 0), (0, 1536), (1, 1536)))


def mm(left, right):
    return lax.dot_general(left, right, (((1,), (0,)), ((), ())), preferred_element_type=F32)


def mm_nt(left, right):
    return lax.dot_general(left, right, (((1,), (1,)), ((), ())), preferred_element_type=F32)


def mm_tn(left, right):
    return lax.dot_general(left, right, (((0,), (0,)), ((), ())), preferred_element_type=F32)


def row_mean(values):
    return jnp.sum(values, axis=-1, keepdims=True) * (1.0 / values.shape[-1])


def normed_rows(values):
    center = values - row_mean(values)
    inverse = lax.rsqrt(row_mean(center * center) + NORM_EPS)
    return center * inverse, inverse


def norm_pull(upstream, normed, inverse, gain):
    scaled = upstream * gain
    return inverse * (scaled - row_mean(scaled) - normed * row_mean(scaled * normed))


def col_sum(values):
    return jnp.sum(values, axis=0, keepdims=True)


class Moves:
    def __init__(self, sems):
        self.sems = sems
        self.used = 0
        self.open = []

    def slot(self):
        self.used += 1
        return self.sems.at[self.used - 1]

    def fetch(self, source, target):
        copy = pltpu.make_async_copy(source, target, self.slot())
        copy.start()
        return copy

    def fetch_either(self, flag, first, second, target):
        sem = self.slot()
        copy = pltpu.make_async_copy(first, target, sem)
        if second is None:
            copy.start()
            return copy
        other = pltpu.make_async_copy(second, target, sem)

        @pl.when(flag)
        def _():
            copy.start()

        @pl.when(jnp.logical_not(flag))
        def _():
            other.start()

        return copy

    def store(self, source, target):
        self.open.append(self.fetch(source, target))

    def drain(self):
        for copy in self.open:
            copy.wait()


class Tower:
    def __init__(self, index, info, weights, others, small, small_other, seqs, slots, first_len):
        self.index = index
        self.info = info
        self.weights = weights
        self.others = others
        self.small = small
        self.small_other = small_other
        self.seqs = seqs
        self.slots = slots
        self.first_len = first_len
        self.count = seqs * slots
        self.width = weights[1].shape[-1]
        self.wide = weights[2].shape[-1]
        self.group = self.count if self.count <= 128 else slots
        self.shared = others is not None

    def given(self, which):
        own = [self.weights[at] for at in which]
        return own + ([self.others[at] for at in which] if self.shared else [])

    def given_small(self):
        return list(self.small) + ([self.small_other] if self.shared else [])

    def use_own(self, info, layer):
        return info[IS_FIRST] == (1 if layer == 0 else 0)

    def lengths_at(self, info):
        return self.first_len + (info[CORE] * self.seqs if self.shared else 0)

    def row_start(self, info):
        return pl.multiple_of(info[CORE] * self.count, self.count) if self.shared else 0

    def small_rows(self, refs, flag):
        own = [refs[0][0, self.index], refs[1][0, self.index]]
        if self.shared:
            other = refs[3]
            own = [
                jnp.where(flag, own[0], other[0:2, :]),
                jnp.where(flag, own[1], other[2:8, :]),
            ]
        return own

    def hidden_bias(self, refs, flag, step, tile):
        own = refs[2][0, self.index : self.index + 1, step * tile : (step + 1) * tile]
        if self.shared:
            own = jnp.where(flag, own, refs[3][8 + step : 9 + step, :])
        return own


ANYWHERE = pl.BlockSpec(memory_space=pl.ANY)
SCALARS = pl.BlockSpec(memory_space=pltpu.SMEM)
INSIDE = pl.BlockSpec(memory_space=pltpu.VMEM)


def call_kernel(kernel, name, inputs, outs, scratch, copies, micros, after, through=()):
    count = len(inputs)
    given = list(after) + list(through)
    extra = len(given)

    def body(*refs):
        refs = list(refs)
        kernel(
            refs[:count],
            refs[count + extra : count + extra + len(outs)],
            refs[count + extra + len(outs) + len(through) : -1],
            Moves(refs[-1]),
        )

    return pl.pallas_call(
        body,
        out_shape=[jax.ShapeDtypeStruct(shape, kind) for shape, kind in outs]
        + [jax.ShapeDtypeStruct(array.shape, array.dtype) for array in through],
        in_specs=[spec for spec, _ in inputs] + [ANYWHERE] * extra,
        out_specs=[ANYWHERE] * (len(outs) + len(through)),
        input_output_aliases={
            count + len(after) + at: len(outs) + at for at in range(len(through))
        },
        scratch_shapes=[pltpu.VMEM(shape, kind) for shape, kind in scratch]
        + [pltpu.SemaphoreType.DMA((copies,))],
        compiler_params=pltpu.CompilerParams(vmem_limit_bytes=VMEM_LIMIT),
        cost_estimate=pl.CostEstimate(
            flops=int(COST * micros) + 1024, bytes_accessed=1024, transcendentals=0
        ),
        name=name,
    )(*[array for _, array in inputs], *given)


def pair_masks(dtype):
    lanes = lax.broadcasted_iota(jnp.int32, (1, 128), 1)
    low = jnp.where(lanes < HEAD_DIM, 1.0, 0.0)
    return low.astype(dtype), (1.0 - low).astype(dtype)


def stacked_pair(block, low, high):
    return jnp.concatenate([block * low, block * high], axis=0)


def joined_pair(stacked, group):
    lanes = lax.broadcasted_iota(jnp.int32, (1, 128), 1)
    return jnp.where(lanes < HEAD_DIM, stacked[:group], stacked[group:])


def pair_softmax(query_stack, key_block, valid):
    scores = mm_nt(key_block, query_stack) * HEAD_DIM ** (-0.5)
    scores = jnp.where(valid, scores, MASK_FILL)
    exponent = jnp.exp(scores - jnp.max(scores, axis=0, keepdims=True))
    return exponent * (1.0 / jnp.sum(exponent, axis=0, keepdims=True))


def valid_keys(info, first_len, group, slots):
    keys = lax.broadcasted_iota(jnp.int32, (group, 2 * group), 0)
    queries = lax.broadcasted_iota(jnp.int32, (group, 2 * group), 1)
    seqs = group // slots
    if seqs == 1:
        return keys < info[first_len]
    queries = jnp.where(queries >= group, queries - group, queries)
    valid = None
    for j in range(seqs):
        low = j * slots
        inside = (
            (queries >= low)
            & (queries < low + slots)
            & (keys >= low)
            & (keys < low + info[first_len + j])
        )
        valid = inside if valid is None else valid | inside
    return valid


def weight_shapes(tower):
    width, steps = tower.width, tower.wide // tower.width
    return [
        ((3, width, width), LOW),
        ((width, width), LOW),
        ((steps, width, width), LOW),
        ((steps, width, width), LOW),
    ]


def fetch_narrow(tower, flag, own, other, targets, moves, order=(0, 1, 2, 3)):
    width = tower.width
    got = {}
    for part in order:
        if part == 3:
            got[3] = moves.fetch_either(flag, own[1].at[0, tower.index], other[1], targets[1])
            continue
        cols = pl.ds(part * width, width)
        second = other[0].at[:, cols] if tower.shared else None
        got[part] = moves.fetch_either(
            flag, own[0].at[0, tower.index, :, cols], second, targets[0].at[part]
        )
    return got


def fetch_step(tower, flag, own, other, targets, moves, step, at):
    width = tower.width
    part = pl.ds(pl.multiple_of(at * width, width), width)
    up, down = (other[0].at[:, part], other[1].at[part]) if tower.shared else (None, None)
    return (
        moves.fetch_either(flag, own[1].at[0, tower.index, part], down, targets[1].at[step]),
        moves.fetch_either(flag, own[0].at[0, tower.index, :, part], up, targets[0].at[step]),
    )


def kept_scratch(tower):
    count, width, wide = tower.count, tower.width, tower.wide
    steps = wide // width
    return [
        ((count, width), LOW),
        ((count, 3 * width), LOW),
        ((count, width), LOW),
        ((count, width), LOW),
        ((steps, count, width), LOW),
        ((steps, count, width), LOW),
        ((count, width), LOW),
        ((count, width), LOW),
        ((2, count, 128), F32),
        ((width // 128, count, 2 * tower.group), LOW),
    ]


OUTPUT, LEFTS, PROJECTED, SLOPE, HAT1, HAT2, INVERSES, SOFT = range(8)


def kept_shapes(tower, inner):
    count, width, wide = tower.count, tower.width, tower.wide
    steps = wide // width
    return [
        ((count, width), LOW),
        ((count, 2 * width + wide + (width if inner else 0)), LOW),
        ((count, 3 * width), LOW),
        ((steps, count, width), LOW),
        ((count, width), LOW),
        ((count, width), LOW),
        ((2, count, 128), F32),
        ((width // 128, count, 2 * tower.group), LOW),
    ]


def forward_body(tower, layer, info, x_v, got, weights, smalls, acc_v, kept, outs, moves):
    count, width, group = tower.count, tower.width, tower.group
    w_qkv, w_out, w_up, w_down = weights
    out_v, qkv_v, mix_v, low_v, act_v, slope_v, hat1_v, hat2_v, inv_v, soft_v = kept
    use_own = tower.use_own(info, layer)
    gains, bias = tower.small_rows(smalls, use_own)
    x = x_v[...]
    for part in range(3):
        got[part].wait()
        block = mm(x, w_qkv[part])
        if part == 0:
            block = block + bias[0:1, :]
        if part == 2:
            block = block + bias[1:2, :]
        qkv_v[:, part * width : (part + 1) * width] = block.astype(LOW)
    moves.store(qkv_v, outs[PROJECTED])
    low, high = pair_masks(LOW)
    for g in range(count // group):
        at = slice(g * group, (g + 1) * group)
        valid = valid_keys(
            info, tower.lengths_at(info) + g * (group // tower.slots), group, tower.slots
        )
        for pair in range(width // 128):
            lane = pair * 128
            q2 = qkv_v[at, lane : lane + 128]
            k2 = qkv_v[at, width + lane : width + lane + 128]
            v2 = qkv_v[at, 2 * width + lane : 2 * width + lane + 128]
            soft = pair_softmax(stacked_pair(q2, low, high), k2, valid).astype(LOW)
            soft_v[pair, at, :] = soft
            mix_v[at, lane : lane + 128] = joined_pair(mm_tn(soft, v2), group).astype(LOW)
    moves.store(soft_v, outs[SOFT])
    moves.store(mix_v, outs[LEFTS].at[:, pl.ds(0, width)])
    got[3].wait()
    summed = x.astype(F32) + (mm(mix_v[...], w_out[...]) + bias[2:3, :])
    hat, inverse = normed_rows(summed)
    hat1_v[...] = hat.astype(LOW)
    inv_v[0] = jnp.broadcast_to(inverse, (count, 128))
    moves.store(hat1_v, outs[HAT1])
    first = hat * gains[0:1, :] + bias[3:4, :]
    low_v[...] = first.astype(LOW)
    moves.store(low_v, outs[LEFTS].at[:, pl.ds(width, width)])
    acc_v[...] = first + bias[4:5, :]
    for step in range(tower.wide // width):
        for copy in got[4 + step]:
            copy.wait()
        hidden = mm(low_v[...], w_up[step]) + tower.hidden_bias(smalls, use_own, step, width)
        cdf = 0.5 * (1.0 + lax.erf(hidden * SQRT_HALF))
        act = (hidden * cdf).astype(LOW)
        act_v[step] = act
        slope_v[step] = (
            cdf + hidden * (jnp.exp(-0.5 * hidden * hidden) * ROOT_TAU_INV)
        ).astype(LOW)
        moves.store(act_v.at[step], outs[LEFTS].at[:, pl.ds((2 + step) * width, width)])
        moves.store(slope_v.at[step], outs[SLOPE].at[step])
        acc_v[...] += mm(act, w_down[step])
    hat, inverse = normed_rows(acc_v[...])
    hat2_v[...] = hat.astype(LOW)
    moves.store(hat2_v, outs[HAT2])
    inv_v[1] = jnp.broadcast_to(inverse, (count, 128))
    moves.store(inv_v, outs[INVERSES])
    out_v[...] = (hat * gains[1:2, :] + bias[5:6, :]).astype(LOW)
    moves.store(out_v, outs[OUTPUT])


def forward_layers(tower, layers, rows, whole_rows, after=(), cost=0):
    count, width = tower.count, tower.width
    steps = tower.wide // width
    shapes = [kept_shapes(tower, at > 0) for at in range(len(layers))]
    kinds = len(shapes[0])
    held = kept_scratch(tower)

    def kernel(ins, outs, scratch, moves):
        info, x_any = ins[0], ins[1]
        own = ins[2:6]
        other = ins[6:10] if tower.shared else [None] * 4
        smalls = ins[10:] if tower.shared else ins[6:]
        x_v, acc_v = scratch[:2]
        if whole_rows:
            x_any = x_any.at[pl.ds(tower.row_start(info), count)]
        x_got = moves.fetch(x_any, x_v)
        weights, got = [], []
        for at, layer in enumerate(layers):
            targets = scratch[2 + 4 * at : 6 + 4 * at]
            flag = tower.use_own(info, layer)
            arrivals = fetch_narrow(tower, flag, own[:2], other[:2], targets[:2], moves)
            for step in range(steps):
                arrivals[4 + step] = fetch_step(
                    tower, flag, own[2:], other[2:], targets[2:], moves, step, step
                )
            weights.append(targets)
            got.append(arrivals)
        x_got.wait()
        for at, layer in enumerate(layers):
            begin = 2 + 4 * len(layers) + len(held) * at
            kept = scratch[begin : begin + len(held)]
            forward_body(
                tower,
                layer,
                info,
                x_v,
                got[at],
                weights[at],
                smalls,
                acc_v,
                kept,
                outs[kinds * at : kinds * (at + 1)],
                moves,
            )
            x_v = kept[0]
            if at + 1 < len(layers):
                inner = outs[kinds * (at + 1) + LEFTS]
                moves.store(x_v, inner.at[:, pl.ds(2 * width + tower.wide, width)])
        moves.drain()

    outs = [shape for layer_shapes in shapes for shape in layer_shapes]
    scratch = [((count, width), LOW), ((count, width), F32)] + weight_shapes(tower) * len(layers)
    inputs = [(SCALARS, tower.info), (ANYWHERE, rows)]
    inputs += [(ANYWHERE, array) for array in tower.given((0, 1, 2, 3))]
    inputs += [(INSIDE, array) for array in tower.given_small()]
    results = call_kernel(
        kernel,
        "layer_forward",
        inputs,
        outs,
        scratch + held * len(layers),
        1 + len(layers) * (4 + 2 * steps + 9 + 2 * steps),
        cost,
        list(after),
    )
    return [results[kinds * at : kinds * (at + 1)] for at in range(len(layers))]


def place_rows(target, block, info, first, size, columns):
    for piece in range(block.shape[0] // size):
        at = pl.multiple_of(info[first + piece] * size, size)
        target[pl.ds(at, size), columns] = block[piece * size : (piece + 1) * size].astype(LOW)


def wide_scratch(tower, upstream):
    count, width = tower.count, tower.width
    steps = tower.wide // width
    return weight_shapes(tower)[2:] + [
        ((count, width), upstream.dtype),
        ((count, width), LOW),
        ((count, 128), F32),
        ((steps, count, width), LOW),
        ((count, width), F32),
        ((count, width), LOW),
        ((steps, count, width), LOW),
        ((8, width), F32),
    ]


def store_sides(source, side_width, outs, column, core_at, moves):
    for side, to in ((1 - core_at, outs[0]), (core_at, outs[1])):
        lanes = pl.ds(pl.multiple_of(side * side_width, 128), side_width)
        moves.store(source.at[:, lanes], to.at[:, pl.ds(column, side_width)])


def wide_tiles(tower, info):
    steps = tower.wide // tower.width
    if not tower.shared:
        return list(range(steps))
    return [lax.rem(step + (1 - info[CORE]) * (steps // 2), steps) for step in range(steps)]


def wide_fetch(tower, layer, info, ins, seeded, scratch, moves):
    up_any, own, other, slope_any, hat_any, inv_any = ins
    w_up, w_down, up_v, hat_v, inv_v, slope_v = scratch[:6]
    use_own = tower.use_own(info, layer)
    if seeded:
        up_any = up_any.at[pl.ds(tower.row_start(info), tower.count)]
    first_got = [
        moves.fetch(up_any, up_v),
        moves.fetch(hat_any, hat_v),
        moves.fetch(inv_any.at[1], inv_v),
    ]
    got = []
    for step, at in enumerate(wide_tiles(tower, info)):
        pieces = [moves.fetch(slope_any.at[at], slope_v.at[step])]
        pieces += fetch_step(tower, use_own, own, other, (w_up, w_down), moves, step, at)
        got.append(pieces)
    return first_got, got


def wide_body(tower, layer, info, fetched, first_ref, smalls, scratch, outs, moves):
    count, width = tower.count, tower.width
    steps = tower.wide // width
    w_up, w_down, up_v, hat_v, inv_v, slope_v, da_v, df_v, dh_v, vec_v = scratch
    use_own = tower.use_own(info, layer)
    core_at = info[CORE]
    first_got, got = fetched
    tiles = wide_tiles(tower, info)
    gains, _ = tower.small_rows(smalls, use_own)
    for copy in first_got:
        copy.wait()
    upward = up_v[...].astype(F32)
    if first_ref is not None:
        row_at = lax.broadcasted_iota(jnp.int32, (count, 1), 0)
        lengths = tower.lengths_at(info)
        first_seq = lengths - tower.first_len
        seen = jnp.zeros((count, 1), F32)
        for seq in range(tower.seqs):
            start = seq * tower.slots
            inside_seq = (row_at >= start) & (row_at < start + info[lengths + seq])
            seen = jnp.where(inside_seq, 1.0, seen)
        upward = upward * seen
        for seq in range(tower.seqs):
            upward = upward + jnp.where(
                row_at == seq * tower.slots, first_ref[pl.ds(first_seq + seq, 1), :], 0.0
            )
    hat = hat_v[...].astype(F32)
    vec_v[0:1, :] = col_sum(upward * hat)
    vec_v[1:2, :] = col_sum(upward)
    d_second = norm_pull(upward, hat, inv_v[:, 0:1], gains[1:2, :])
    d_low = d_second.astype(LOW)
    df_v[...] = d_low
    vec_v[2:3, :] = col_sum(d_low.astype(F32))
    vec_v[7:8, :] = jnp.zeros((1, width), F32)
    da_v[...] = d_second
    vec_out, df_out, dh_out = outs
    if tower.shared:
        store_sides(df_v, width // 2, df_out, tower.wide // 2, core_at, moves)
    else:
        moves.store(df_v, df_out[0])
    for step, at in enumerate(tiles):
        for copy in got[step]:
            copy.wait()
        d_hidden = (mm_nt(df_v[...], w_down[step]) * slope_v[step].astype(F32)).astype(LOW)
        vec_v[pl.ds(3 + at, 1), :] = col_sum(d_hidden.astype(F32))
        dh_v[step] = d_hidden
        da_v[...] += mm_nt(d_hidden, w_up[step])
        if tower.shared:
            side, place = divmod(step, steps // 2)
            moves.store(dh_v.at[step], dh_out[side].at[:, pl.ds(place * width, width)])
        else:
            moves.store(dh_v.at[step], dh_out[0].at[step])
    moves.store(vec_v, vec_out)


def narrow_scratch(tower, out_type):
    count, width = tower.count, tower.width
    return weight_shapes(tower)[:2] + [
        ((count, width), LOW),
        ((count, 128), F32),
        ((count, 3 * width), LOW),
        ((width // 128, count, 2 * tower.group), LOW),
        ((count, width), LOW),
        ((count, 3 * width), LOW),
        ((count, width), LOW),
        ((count, width), F32),
        ((count, width), out_type),
        ((8, width), F32),
    ]


def narrow_fetch(tower, layer, info, ins, scratch, moves):
    own, other, qkv_any, hat_any, inv_any, soft_any = ins
    w_qkv, w_out, hat_v, inv_v, qkv_v, soft_v = scratch[:6]
    use_own = tower.use_own(info, layer)
    got = {"hat": [moves.fetch(hat_any, hat_v), moves.fetch(inv_any.at[0], inv_v)]}
    weights = fetch_narrow(tower, use_own, own, other, (w_qkv, w_out), moves, (3,))
    got["heads"] = [moves.fetch(qkv_any, qkv_v), moves.fetch(soft_any, soft_v)]
    weights.update(fetch_narrow(tower, use_own, own, other, (w_qkv, w_out), moves, (0, 1, 2)))
    got["weights"] = weights
    return got


def narrow_body(tower, layer, info, got, da_v, smalls, scratch, outs, moves):
    count, width, group = tower.count, tower.width, tower.group
    w_qkv, w_out, hat_v, inv_v, qkv_v, soft_v, dz_v, dp_v, dmix_v, du_v, dx_v, vec_v = scratch
    use_own = tower.use_own(info, layer)
    core_at = info[CORE]
    dx_out, vec_out, dz_out, dp_out = outs
    gains, _ = tower.small_rows(smalls, use_own)
    for copy in got["hat"]:
        copy.wait()
    upward = da_v[...]
    hat = hat_v[...].astype(F32)
    vec_v[0:1, :] = col_sum(upward * hat)
    vec_v[1:2, :] = col_sum(upward)
    d_summed = norm_pull(upward, hat, inv_v[:, 0:1], gains[0:1, :])
    du_v[...] = d_summed
    d_low = d_summed.astype(LOW)
    dz_v[...] = d_low
    vec_v[2:3, :] = col_sum(d_low.astype(F32))
    vec_v[5:8, :] = jnp.zeros((3, width), F32)
    if tower.shared:
        store_sides(dz_v, width // 2, dz_out, tower.wide // 2 + 2 * width, core_at, moves)
    else:
        moves.store(dz_v, dz_out[0])
    got["weights"][3].wait()
    dmix_v[...] = mm_nt(d_low, w_out[...]).astype(LOW)
    for copy in got["heads"]:
        copy.wait()
    low, high = pair_masks(LOW)
    scale = HEAD_DIM ** (-0.5)
    for g in range(count // group):
        at = slice(g * group, (g + 1) * group)
        for pair in range(width // 128):
            lane = pair * 128
            q2 = qkv_v[at, lane : lane + 128]
            k2 = qkv_v[at, width + lane : width + lane + 128]
            v2 = qkv_v[at, 2 * width + lane : 2 * width + lane + 128]
            soft = soft_v[pair, at, :]
            d_stack = stacked_pair(dmix_v[at, lane : lane + 128], low, high)
            d_soft = mm_nt(v2, d_stack)
            soft_wide = soft.astype(F32)
            total = jnp.sum(d_soft * soft_wide, axis=0, keepdims=True)
            d_scores = (soft_wide * (d_soft - total)).astype(LOW)
            dp_v[at, lane : lane + 128] = (
                joined_pair(mm_tn(d_scores, k2), group) * scale
            ).astype(LOW)
            dp_v[at, width + lane : width + lane + 128] = (
                mm(d_scores, stacked_pair(q2, low, high)) * scale
            ).astype(LOW)
            dp_v[at, 2 * width + lane : 2 * width + lane + 128] = mm(soft, d_stack).astype(LOW)
    vec_v[3:4, :] = col_sum(dp_v[:, :width].astype(F32))
    vec_v[4:5, :] = col_sum(dp_v[:, 2 * width :].astype(F32))
    moves.store(vec_v, vec_out)
    if tower.shared:
        store_sides(dp_v, 3 * width // 2, dp_out, (tower.wide + width) // 2, core_at, moves)
    else:
        moves.store(dp_v, dp_out[0])
    d_input = du_v[...]
    for part in range(3):
        got["weights"][part].wait()
        d_input = d_input + mm_nt(dp_v[:, part * width : (part + 1) * width], w_qkv[part])
    dx_v[...] = d_input.astype(dx_v.dtype)
    moves.store(dx_v, dx_out)


def backward_layer(
    tower, layer, upstream, first_rows, kept, low_out, after=(), cost=0, through=()
):
    count, width, wide = tower.count, tower.width, tower.wide
    steps = wide // width
    seeded = first_rows is not None
    out_type = LOW if low_out else F32
    wide_shapes = wide_scratch(tower, upstream)

    def kernel(ins, outs, scratch, moves):
        ins = list(ins)
        info, up_any = ins.pop(0), ins.pop(0)
        first_ref = ins.pop(0) if seeded else None
        own = [ins.pop(0) for _ in range(4)]
        other = [ins.pop(0) for _ in range(4)] if tower.shared else [None] * 4
        slope_any, hat2_any, inv_any, qkv_any, hat1_any, soft_any = (
            ins.pop(0) for _ in range(6)
        )
        first, second = scratch[: len(wide_shapes)], scratch[len(wide_shapes) :]
        dx, vec1, vec2 = outs[:3]
        df, dh, dz, dp = [outs[3:]] * 4 if tower.shared else [outs[at : at + 1] for at in range(3, 7)]
        given = (up_any, own[2:], other[2:], slope_any, hat2_any, inv_any)
        wide_got = wide_fetch(tower, layer, info, given, seeded, first, moves)
        given = (own[:2], other[:2], qkv_any, hat1_any, inv_any, soft_any)
        got = narrow_fetch(tower, layer, info, given, second, moves)
        wide_body(
            tower, layer, info, wide_got, first_ref, ins, first, (vec1, df, dh), moves
        )
        narrow_body(
            tower, layer, info, got, first[6], ins, second, (dx, vec2, dz, dp), moves
        )
        moves.drain()

    outs = [((count, width), out_type), ((8, width), F32), ((8, width), F32)]
    if tower.shared:
        outs += [((count, (5 * width + wide) // 2), LOW)] * 2
    else:
        outs += [((count, width), LOW), ((steps, count, width), LOW)]
        outs += [((count, width), LOW), ((count, 3 * width), LOW)]
    inputs = [(SCALARS, tower.info), (ANYWHERE, upstream)]
    if seeded:
        inputs.append((INSIDE, first_rows))
    inputs += [(ANYWHERE, array) for array in tower.given((0, 1, 2, 3))]
    inputs += [(ANYWHERE, kept[at]) for at in (SLOPE, HAT2, INVERSES, PROJECTED, HAT1, SOFT)]
    inputs += [(INSIDE, array) for array in tower.given_small()]
    return call_kernel(
        kernel,
        "backward_layer",
        inputs,
        outs,
        wide_shapes + narrow_scratch(tower, out_type),
        3 + 3 * steps + 8 + 3 + steps + 6,
        cost,
        list(after),
        through,
    )


def place_rows(target, block, info, first, size, columns):
    for piece in range(block.shape[0] // size):
        at = pl.multiple_of(info[first + piece] * size, size)
        target[pl.ds(at, size), columns] = block[piece * size : (piece + 1) * size].astype(LOW)


def passage_products(tower, layer, rows, lefts, other_lefts, rights, other_rights, after=(), cost=0):
    count, width, wide = tower.count, tower.width, tower.wide
    steps = wide // width
    half = width // 2
    piece = width // BLOCKS
    layout = LAYOUTS[layer]
    chunks = 1 + max(chunk for chunk, _ in layout)
    widths = [
        max(column + (wide // 2 if at < 2 else width) for at, (to, column) in enumerate(layout) if to == chunk)
        for chunk in range(chunks)
    ]
    whole = rows is not None

    def kernel(ins, outs, scratch, moves):
        ins = list(ins)
        info = ins.pop(0)
        x_any = ins.pop(0) if whole else None
        left, other_left, right, other_right = ins
        low_v, dh_v, act_v, df_v, x_v, dp_v, mix_v, dz_v = scratch[:8]
        grads = scratch[8:]
        above, below = pl.ds(0, count), pl.ds(count, count)

        def both(sources, column, target):
            columns = pl.ds(column, target.shape[1])
            return [
                moves.fetch(sources[0].at[:, columns], target.at[above]),
                moves.fetch(sources[1].at[:, columns], target.at[below]),
            ]

        lefts_of = (left, other_left)
        rights_of = (right, other_right)
        got_low = both(lefts_of, width, low_v)
        got_dh = [both(rights_of, at * width, dh_v.at[at]) for at in range(steps // 2)]
        got_df = both(rights_of, wide // 2, df_v)
        got_act = [both(lefts_of, (2 + at) * width, act_v.at[at]) for at in range(steps)]
        if whole:
            start = tower.row_start(info)
            other_start = pl.multiple_of(count - start, count)
            got_x = [
                moves.fetch(x_any.at[pl.ds(start, count)], x_v.at[above]),
                moves.fetch(x_any.at[pl.ds(other_start, count)], x_v.at[below]),
            ]
        else:
            got_x = both(lefts_of, 2 * width + wide, x_v)
        got_x += both(rights_of, wide // 2 + half, dp_v)
        got_mix = both(lefts_of, 0, mix_v) + both(rights_of, wide // 2 + 2 * width, dz_v)

        def ready(copies):
            for copy in copies:
                copy.wait()

        def target(part):
            chunk, column = layout[part]
            return grads[chunk], column, PLACES + BLOCKS * (3 * layer + chunk)

        def send(part):
            source, column, _ = target(part)
            cut = source.shape[0] // 2
            columns = pl.ds(column, wide // 2 if part < 2 else width)
            to = 2 * layout[part][0]
            moves.store(source.at[pl.ds(cut, cut), columns], outs[to].at[:, columns])
            moves.store(source.at[pl.ds(0, cut), columns], outs[to + 1].at[:, columns])

        ready(got_low)
        for at in range(steps // 2):
            ready(got_dh[at])
            to, column, first = target(1)
            columns = slice(column + at * width, column + (at + 1) * width)
            place_rows(to, mm_tn(low_v[...], dh_v[at]), info, first, piece, columns)
        send(1)
        ready(got_df)
        parts = wide // width
        for at in range(steps):
            ready(got_act[at])
            product = mm_tn(act_v[at], df_v[...])
            for block in range(width // piece):
                index, part = divmod(at * (width // piece) + block, parts)
                to, column, first = target(0)
                rows_to = pl.ds(pl.multiple_of(info[first + index] * piece, piece), piece)
                column += part * half
                to[rows_to, column : column + half] = product[
                    block * piece : (block + 1) * piece
                ].astype(LOW)
        send(0)
        ready(got_x)
        for part in range(4):
            if part == 3:
                ready(got_mix)
                product = mm_tn(mix_v[...], dz_v[...])
            else:
                product = mm_tn(x_v[...], dp_v[:, part * half : (part + 1) * half])
            to, column, first = target(2 + part // 2)
            column += part % 2 * half
            place_rows(to, product, info, first, piece, slice(column, column + half))
            if part % 2:
                send(2 + part // 2)
        moves.drain()

    outs = [((half, columns), LOW) for columns in widths for _ in range(2)]
    scratch = [
        ((2 * count, width), LOW),
        ((steps // 2, 2 * count, width), LOW),
        ((steps, 2 * count, width), LOW),
        ((2 * count, half), LOW),
        ((2 * count, width), LOW),
        ((2 * count, 3 * half), LOW),
        ((2 * count, width), LOW),
        ((2 * count, half), LOW),
    ] + [((width, columns), LOW) for columns in widths]
    arrays = [rows] if whole else []
    arrays += [lefts, other_lefts, rights, other_rights]
    inputs = [(SCALARS, tower.info)] + [(ANYWHERE, array) for array in arrays]
    return call_kernel(
        kernel,
        "passage_products",
        inputs,
        outs,
        scratch,
        2 * (1 + steps // 2 + 1 + steps + 4) + 8,
        cost,
        list(after),
    )


def block_chooser(rows, columns, valid, size, bit):
    at = lax.broadcasted_iota(jnp.int32, (1, columns), 1)
    piece = jnp.floor((at.astype(F32) + 0.5) * (1.0 / size)).astype(jnp.int32)
    wanted = jnp.where(at < valid, at + (piece + bit) * size, -1)
    row_at = lax.broadcasted_iota(jnp.int32, (rows, columns), 0)
    return jnp.where(row_at == wanted, 1.0, 0.0).astype(LOW)


def pack_first(info, early, late, after=(), cost=0):
    count, width = early[0].shape
    steps = early[2].shape[0]
    wide = steps * width
    half = width // 2
    piece = width // BLOCKS
    keeps = (half + 3 * half, 2 * wide // 2)
    wholes = (2 * width, 2 * width)

    def kernel(ins, outs, scratch, moves):
        info_ref = ins[0]
        first, second = ins[1:7], ins[7:13]
        x_v, left_v, dh_v, df_v, dz_v, dp_v = scratch[:6]
        results = scratch[6:]
        flag = info_ref[IS_FIRST] == 1
        got = [moves.fetch_either(flag, a, b, to) for a, b, to in zip(first, second, scratch)]
        bits = [(info_ref[at], 1 - info_ref[at]) for at in (X_BIT, Y_BIT)]
        for copy in got:
            copy.wait()

        def lanes(bit, size):
            return pl.ds(pl.multiple_of(bit * size, 128), size)

        for which in range(2):
            first_to, second_to = results[which], results[2 + which]
            bit = bits[0][which]
            choose = block_chooser(width, half, half, piece, bit)
            first_to[:, :half] = mm(left_v[:, :width], choose).astype(LOW)
            first_to[:, half : 4 * half] = dp_v[:, lanes(bit, 3 * half)]
            bit = bits[1][which]
            for step in range(steps):
                start = (2 + step) * width + bit * half
                second_to[:, step * half : (step + 1) * half] = left_v[
                    :, pl.ds(pl.multiple_of(start, 128), half)
                ]
            for step in range(steps // 2):
                begin = wide // 2 + step * width
                second_to[:, begin : begin + width] = dh_v[bit * (steps // 2) + step]
        results[1][:, keeps[0] : keeps[0] + width] = x_v[...]
        results[1][:, keeps[0] + width :] = dz_v[...]
        results[3][:, keeps[1] : keeps[1] + width] = left_v[:, width : 2 * width]
        results[3][:, keeps[1] + width :] = df_v[...]
        for at in range(4):
            moves.store(results[at], outs[at])
        moves.drain()

    outs = []
    for keep, rest in zip(keeps, wholes):
        outs += [((count, keep), LOW), ((count, keep + rest), LOW)]
    inputs = [(SCALARS, info)] + [(ANYWHERE, array) for array in tuple(early) + tuple(late)]
    scratch = [(array.shape, LOW) for array in early]
    return call_kernel(
        kernel, "pack_first", inputs, outs, scratch + outs, 12, cost, list(after)
    )


def pack_second(info, keeps, sends, arrivals, width, after=(), cost=0):
    count = keeps[0].shape[0]
    wide = keeps[1].shape[1]
    half, quarter, third = width // 2, width // 4, 256
    piece = width // BLOCKS
    chosen = (third + half, half + wide // 4)
    wholes = (3 * half + width, wide // 2 + width)

    def kernel(ins, outs, scratch, moves):
        info_ref = ins[0]
        got = [moves.fetch(source, to) for source, to in zip(ins[1:], scratch)]
        bits = [(info_ref[at], 1 - info_ref[at]) for at in (Y_BIT, X_BIT)]
        for copy in got:
            copy.wait()
        for lot in range(2):
            keep_v, send_v, arrived_v = scratch[lot], scratch[2 + lot], scratch[4 + lot]
            cut = keep_v.shape[1]
            sources = (
                (slice(0, count), keep_v, send_v),
                (slice(count, 2 * count), arrived_v, arrived_v),
            )
            for which in range(2):
                target = scratch[6 + 2 * lot + which]
                bit = bits[lot][which]
                for rows, halved, whole in sources:
                    if lot == 0:
                        choose = block_chooser(half, third, quarter, piece, bit)
                        target[rows, :third] = mm(halved[:, :half], choose).astype(LOW)
                        choose = block_chooser(width, half, half, 2 * piece, bit)
                        target[rows, third:chosen[0]] = mm(
                            whole[:, cut : cut + width], choose
                        ).astype(LOW)
                        continue
                    choose = block_chooser(width, half, half, piece, bit)
                    target[rows, :half] = mm(whole[:, cut : cut + width], choose).astype(LOW)
                    choose = block_chooser(2 * half, half, half, quarter, bit)
                    for part in range(wide // 2 // width):
                        target[rows, half + part * half : half + (part + 1) * half] = mm(
                            halved[:, part * width : (part + 1) * width], choose
                        ).astype(LOW)
            target = scratch[6 + 2 * lot + 1]
            begin = chosen[lot]
            first = half if lot == 0 else wide // 2
            for rows, halved, whole in sources:
                target[rows, begin : begin + cut - first] = halved[:, first:cut]
                target[rows, begin + cut - first :] = whole[:, cut + width :]
        for at in range(4):
            moves.store(scratch[6 + at], outs[at])
        moves.drain()

    outs = []
    for left, right in zip(chosen, wholes):
        outs += [((2 * count, left), LOW), ((2 * count, left + right), LOW)]
    arrays = tuple(keeps) + tuple(sends) + tuple(arrivals)
    inputs = [(SCALARS, info)] + [(ANYWHERE, array) for array in arrays]
    scratch = [(array.shape, LOW) for array in arrays]
    return call_kernel(
        kernel, "pack_second", inputs, outs, scratch + outs, 10, cost, list(after)
    )


def query_products(info, keeps, sends, arrivals, width, wide, after=(), cost=0):
    count = keeps[0].shape[0]
    half, third = width // 2, 256
    piece = width // BLOCKS
    packed = [keep.shape[1] for keep in keeps]
    rights = [send.shape[1] - left for send, left in zip(sends, packed)]
    columns = 4 * width + 2 * wide

    def kernel(ins, outs, scratch, moves):
        info_ref = ins[0]
        keep_any, send_any, arrived_any = ins[1:3], ins[3:5], ins[5:7]
        left_v, right_v, result = scratch[0:2], scratch[2:4], scratch[4]
        got = []
        for lot in range(2):
            cut = packed[lot]
            below = pl.ds(count, count)
            got.append(
                [
                    moves.fetch(keep_any[lot], left_v[lot].at[pl.ds(0, count)]),
                    moves.fetch(arrived_any[lot].at[:, pl.ds(0, cut)], left_v[lot].at[below]),
                    moves.fetch(
                        send_any[lot].at[:, pl.ds(cut, rights[lot])],
                        right_v[lot].at[pl.ds(0, count)],
                    ),
                    moves.fetch(
                        arrived_any[lot].at[:, pl.ds(cut, rights[lot])], right_v[lot].at[below]
                    ),
                ]
            )

        def place(z, rows, column):
            row = pl.multiple_of(info_ref[Z_PLACES + z] * piece, piece)
            result[pl.ds(row, piece), column : column + rows.shape[1]] = rows.astype(LOW)

        for copy in got[0]:
            copy.wait()
        for part in range(3):
            product = mm_tn(
                left_v[0][:, third:], right_v[0][:, part * half : (part + 1) * half]
            )
            for block in range(8):
                z, bit = divmod(block, 2)
                place(
                    z,
                    product[block * piece : (block + 1) * piece],
                    bit * 3 * half + part * half,
                )
        product = mm_tn(left_v[0][:, :third], right_v[0][:, 3 * half :])
        for z in range(4):
            place(z, product[z * piece : (z + 1) * piece], 3 * width)
        for copy in got[1]:
            copy.wait()
        at = 4 * width
        for part in range(wide // 2 // width):
            product = mm_tn(
                left_v[1][:, :half], right_v[1][:, part * width : (part + 1) * width]
            )
            for block in range(8):
                z, bit = divmod(block, 2)
                place(
                    z,
                    product[block * piece : (block + 1) * piece],
                    at + bit * (wide // 2) + part * width,
                )
        at += wide
        product = mm_tn(left_v[1][:, half:], right_v[1][:, wide // 2 :])
        per = wide // width
        for z in range(4):
            for part in range(per):
                begin = (z * per + part) * piece
                place(z, product[begin : begin + piece], at + part * width)
        moves.store(result.at[pl.ds(2 * piece, 2 * piece)], outs[0])
        moves.store(result.at[pl.ds(0, 2 * piece)], outs[1])
        moves.drain()

    outs = [((2 * piece, columns), LOW)] * 2
    arrays = tuple(keeps) + tuple(sends) + tuple(arrivals)
    inputs = [(SCALARS, info)] + [(ANYWHERE, array) for array in arrays]
    scratch = [((2 * count, cut), LOW) for cut in packed]
    scratch += [((2 * count, cut), LOW) for cut in rights]
    scratch += [((4 * piece, columns), LOW)]
    return call_kernel(
        kernel, "query_products", inputs, outs, scratch, 10, cost, list(after)
    )


PIECE_ROWS = 32


def vector_pieces(info, first, parts, wide, after=()):
    width = parts[0].shape[1]
    cut = width // BLOCKS
    big = wide // BLOCKS

    def kernel(ins, outs, scratch, moves):
        info_ref = ins[0]
        refs = ins[1:]
        early = info_ref[IS_FIRST] == 1
        for target in scratch:
            target[...] = jnp.zeros_like(target)

        def lay(target, tower_at, wide_rows, narrow_rows):
            eight = jnp.concatenate([wide_rows[0:3], narrow_rows[0:5]], axis=0)
            for block in range(BLOCKS):
                at = info_ref[PLACES + first + block] * PIECE_ROWS + 16 * tower_at
                at = pl.multiple_of(at, 16)
                target[pl.ds(at, 8), 0:cut] = eight[:, block * cut : (block + 1) * cut]
                row, column = divmod(block * big, width)
                bias = wide_rows[3 + row : 4 + row, column : column + big]
                target[pl.ds(at + 8, 1), 0:128] = bias[:, 0:128]
                target[pl.ds(at + 9, 1), 0 : big - 128] = bias[:, 128:big]

        send, keep = scratch
        eq1, eq2, lq1, lq2, ep1, ep2, lp1, lp2 = (ref[...] for ref in refs)
        lay(keep, 0, jnp.where(early, eq1, lq1), jnp.where(early, eq2, lq2))
        lay(keep, 1, jnp.where(early, ep1, lp1), jnp.where(early, ep2, lp2))
        lay(send, 1, jnp.where(early, lp1, ep1), jnp.where(early, lp2, ep2))
        moves.store(send, outs[0])
        moves.store(keep, outs[1])
        moves.drain()

    outs = [((BLOCKS * PIECE_ROWS, 128), F32)] * 2
    inputs = [(SCALARS, info)] + [(INSIDE, array) for array in parts]
    return call_kernel(kernel, "vector_pieces", inputs, outs, outs, 2, 0, list(after))


def take_in(items, after=(), cost=0, through=()):
    def kernel(ins, outs, scratch, moves):
        ins, scratch = list(ins), list(scratch)
        taken = []
        for pairs, last in items:
            got = []
            for _ in pairs:
                held = [scratch.pop(0), scratch.pop(0)]
                got.append((held, [moves.fetch(ins.pop(0), to) for to in held]))
            taken.append((got, [scratch.pop(0) for _ in range(1 if last else 2)]))
        out_at = 0
        for (got, results), (_, last) in zip(taken, items):
            for held, copies in got:
                for copy in copies:
                    copy.wait()
            for which, result in enumerate(results):
                part_rows = result.shape[0]
                start = 0 if last else (1 - which) * part_rows
                column = 0
                for (keep_v, arrived_v), _ in got:
                    columns = keep_v.shape[1]
                    chunk = 48 if columns <= 1536 and part_rows % 48 == 0 else 16

                    def one(step, carry, keep_v=keep_v, arrived_v=arrived_v, column=column):
                        to = pl.ds(pl.multiple_of(step * chunk, 16), chunk)
                        of = pl.ds(pl.multiple_of(start + step * chunk, 16), chunk)
                        total = keep_v[of, :].astype(F32) + arrived_v[of, :].astype(F32)
                        result[to, column : column + keep_v.shape[1]] = total.astype(result.dtype)
                        return carry

                    lax.fori_loop(0, part_rows // chunk, one, 0)
                    column += columns
                moves.store(result, outs[out_at])
                out_at += 1
        moves.drain()

    outs, scratch = [], []
    for pairs, last in items:
        rows = pairs[0][0].shape[0]
        columns = sum(keep.shape[1] for keep, _ in pairs)
        kind = pairs[0][0].dtype
        mine = [((rows, columns), F32)] if last else [((rows // 2, columns), kind)] * 2
        outs += mine
        for keep, arrived in pairs:
            scratch += [(keep.shape, kind), (arrived.shape, kind)]
        scratch += mine
    inputs = [(ANYWHERE, array) for pairs, _ in items for pair in pairs for array in pair]
    return call_kernel(
        kernel, "take_in", inputs, outs, scratch, len(inputs) + len(outs), cost, list(after), through
    )


class Chain:
    def __init__(self, send, keep, order, scale, from_core=False):
        self.order = list(order)
        self.scale = scale
        self.keep = keep
        self.total = None
        self.arrived = core_swap(send) if from_core else self.swap(send)

    def swap(self, block):
        return flip_swap(block, self.order.pop(0) * self.scale)


def play_round(groups, after=(), cost=0, through=()):
    items = [
        ([(chain.keep, chain.arrived) for chain in group], not group[0].order) for group in groups
    ]
    results = list(take_in(items, after, cost, through))
    seen = []
    for group in groups:
        chain = group[0]
        assert all(other.order == chain.order for other in group)
        if not chain.order:
            chain.total = results.pop(0)
            seen.append(chain.total)
            continue
        sent, chain.keep = results.pop(0), results.pop(0)
        chain.arrived = chain.swap(sent)
        seen.append(sent)
    return tuple(seen + results)


def last_round(info, chain, other_total, vector, after=(), cost=0):
    rows, columns = other_total.shape
    v_rows = vector.keep.shape[0]

    def kernel(ins, outs, scratch, moves):
        info_ref = ins[0]
        first_v, second_v, late_v, v1, v2, own_v, send_v, sum_v = scratch
        got = [moves.fetch(source, to) for source, to in zip(ins[1:], scratch)]
        for copy in got[3:]:
            copy.wait()
        sum_v[...] = v1[...] + v2[...]
        moves.store(sum_v, outs[2])
        for copy in got[:3]:
            copy.wait()
        flag = info_ref[IS_FIRST] == 1
        for row in range(0, rows, 16):
            part = slice(row, row + 16)
            early = first_v[part, :].astype(F32) + second_v[part, :].astype(F32)
            late = late_v[part, :]
            send_v[part, :] = jnp.where(flag, late, early)
            own_v[part, :] = jnp.where(flag, early, late)
        moves.store(send_v, outs[1])
        moves.store(own_v, outs[0])
        moves.drain()

    outs = [((rows, columns), F32)] * 2 + [((v_rows, 128), F32)]
    arrays = (chain.keep, chain.arrived, other_total, vector.keep, vector.arrived)
    inputs = [(SCALARS, info)] + [(ANYWHERE, array) for array in arrays]
    scratch = [(array.shape, array.dtype) for array in arrays]
    return call_kernel(
        kernel, "last_round", inputs, outs, scratch + outs, 8, cost, list(after)
    )


def put_together(info, own, other, query, query_x, query_y, width, wide):
    rows = own.shape[0]
    half = width // 2
    parts = wide // width
    columns = own.shape[1]

    def kernel(ins, outs, scratch, moves):
        info_ref = ins[0]
        sources, results = scratch[:5], scratch[5:]
        got = [moves.fetch(source, to) for source, to in zip(ins[1:], sources)]
        own_v, other_v, query_v, x_v, y_v = sources
        g_qkv, g_out, g_up, g_down = results

        def lanes(at, size, more=0):
            return pl.ds(pl.multiple_of(at * size + more, 128), size if more == 0 else half)

        for copy in got[2:]:
            copy.wait()
        at = 4 * width
        for bit_at, begin, size, arrived, target in (
            (X_BIT, 0, 3 * half, x_v, g_qkv),
            (Y_BIT, at, wide // 2, y_v, g_up),
        ):
            bit = info_ref[bit_at]
            target[0, :, lanes(bit, size)] = query_v[
                :, pl.ds(pl.multiple_of(begin + bit * size, 128), size)
            ]
            target[0, :, lanes(1 - bit, size)] = arrived[...]
        g_out[0] = query_v[:, 3 * width : 4 * width]
        at += wide
        for part in range(parts):
            g_down[0, part * rows : (part + 1) * rows, :] = query_v[
                :, at + part * width : at + (part + 1) * width
            ]
        for copy in got[:2]:
            copy.wait()
        core = info_ref[CORE]
        for source, side in ((own_v, core), (other_v, 1 - core)):
            columns_of = [LAYOUTS[0][at][1] for at in range(4)]
            chunk_width = columns // 2
            begin = [
                LAYOUTS[0][at][0] * chunk_width + columns_of[at] for at in range(4)
            ]
            here = lanes(side, half)
            for part in range(parts):
                g_down[1, part * rows : (part + 1) * rows, here] = source[
                    :, begin[0] + part * half : begin[0] + (part + 1) * half
                ]
            g_up[1, :, lanes(side, wide // 2)] = source[:, begin[1] : begin[1] + wide // 2]
            for third in range(3):
                column = begin[2 + third // 2] + third % 2 * half
                target_lanes = pl.ds(
                    pl.multiple_of(side * 3 * half + third * half, 128), half
                )
                g_qkv[1, :, target_lanes] = source[:, column : column + half]
            g_out[1, :, here] = source[:, begin[3] + half : begin[3] + width]
        for result, to in zip(results, outs):
            moves.store(result, to)
        moves.drain()

    outs = [
        ((2, rows, 3 * width), F32),
        ((2, rows, width), F32),
        ((2, rows, wide), F32),
        ((2, parts * rows, width), F32),
    ]
    arrays = (own, other, query, query_x, query_y)
    inputs = [(SCALARS, info)] + [(ANYWHERE, array) for array in arrays]
    scratch = [(array.shape, F32) for array in arrays]
    return call_kernel(kernel, "put_together", inputs, outs, scratch + outs, 9, 0, [])


def pick_bit(grid, axis, index):
    return lax.dynamic_index_in_dim(grid, index, axis, keepdims=False)


def own_bit(bit):
    return (lax.axis_index("batch") // bit) % 2


def scatter_sum(grid, bits, left):
    left = list(left)
    for bit in bits:
        axis = left.index(bit)
        mine = own_bit(bit)
        sent = pick_bit(grid, axis, 1 - mine)
        kept = pick_bit(grid, axis, mine)
        arrived = flip_swap(sent, bit)
        total = kept.astype(jnp.float32) + arrived.astype(jnp.float32)
        left.remove(bit)
        grid = total if not left else total.astype(grid.dtype)
    return grid


def all_bits(size):
    bits = [1 << i for i in range(size.bit_length() - 1)]
    return bits[::-1]


def to_grid(array, size):
    bits = all_bits(size)
    return array.reshape((2,) * len(bits) + (array.shape[0] // size,) + array.shape[1:])


def gather_all(block, size):
    if size != 16:
        for bit in all_bits(size)[::-1]:
            block = jnp.concatenate([block, flip_swap(block, bit)], 0)
        return block
    block = jnp.concatenate([block] + [flip_swap(block, k) for k in (1, 2, 3)], 0)
    return jnp.concatenate([block] + [flip_swap(block, k) for k in (4, 8, 12)], 0)


def contrast(own_cls, micro, positive, query_count, batch_index, batch_size):
    width = own_cls.shape[1]
    chip_rows = own_cls.shape[0]
    gathered = gather_all(own_cls, batch_size).reshape(batch_size, chip_rows, width)
    all_q = gathered[:, :query_count].reshape(-1, width)
    all_p = gathered[:, query_count:].reshape(-1, width)
    blocks = jnp.arange(batch_size, dtype=jnp.int32) ^ batch_index
    query_ids = (
        blocks[:, None] * query_count + jnp.arange(query_count, dtype=jnp.int32)[None, :]
    ).reshape(-1)
    passage_ids = (
        3 * query_ids[:, None] + jnp.arange(3, dtype=jnp.int32)[None, :]
    ).reshape(-1)
    labels = jnp.take(micro, query_ids)
    wanted = jnp.take(positive, query_ids)
    logit_scale = LOGIT_GAIN * width ** (-0.5)
    logits = mm_nt(all_q, all_p) * logit_scale
    same_group = labels[:, None] == jnp.repeat(labels, 3)[None, :]
    logits = jnp.where(same_group, logits, MASK_FILL)
    row_top = jnp.max(logits, axis=-1, keepdims=True)
    exponent = jnp.exp(logits - row_top)
    totals = jnp.sum(exponent, axis=-1, keepdims=True)
    target = passage_ids[None, :] == wanted[:, None]
    loss_all = (
        row_top[:, 0] + jnp.log(totals[:, 0]) - jnp.sum(jnp.where(target, logits, 0.0), axis=-1)
    )
    coefficient = (exponent / totals - target.astype(jnp.float32)) * logit_scale
    passage_count = 3 * query_count
    d_cls_q = jnp.dot(coefficient[:query_count], all_p.astype(jnp.float32), precision=PRECISE)
    d_cls_p = lax.dot_general(
        coefficient[:, :passage_count],
        all_q.astype(jnp.float32),
        (((0,), (0,)), ((), ())),
        precision=PRECISE,
    )
    return loss_all[:query_count], d_cls_q, d_cls_p


def integers(core, index, size, len_q, len_p):
    blocks = jnp.arange(BLOCKS, dtype=jnp.int32)
    own = index // (size // BLOCKS)
    relative = blocks ^ own
    places = [
        sum(((relative // bit) % 2) * (8 >> at) for at, bit in enumerate(order))
        for order in ORDERS
    ]
    depth = jnp.arange(4, dtype=jnp.int32) ^ (own // 4)
    z_places = (depth % 2) * 2 + depth // 2
    few = jnp.stack([1 - core, core])
    ends = jnp.stack([own % 2, (own // 2) % 2])
    return jnp.concatenate([few, *places, z_places, ends, len_q, len_p]).astype(jnp.int32)


def shards(
    x_q,
    x_p,
    len_q,
    len_p,
    cot_q,
    cot_p,
    positive,
    micro,
    w_qkv,
    w_out,
    w_up,
    w_down,
    norm_gain,
    biases,
    b_up,
):
    core = lax.axis_index("section")
    is_first = core == 0
    batch_index = lax.axis_index("batch")
    size = lax.axis_size("batch")
    bits = all_bits(size)
    query_count, slots_q, model = x_q.shape
    half_count = x_p.shape[0] // 2
    slots_p = x_p.shape[1]
    wide = w_up.shape[-1]
    info = integers(core, batch_index, size, len_q, len_p)
    weights = (w_qkv, w_out, w_up, w_down)
    smalls = (norm_gain, biases, b_up)
    other_p = tuple(core_swap(member[0, 1]) for member in weights)
    small_other = core_swap(
        jnp.concatenate([norm_gain[0, 1], biases[0, 1], b_up[0, 1].reshape(-1, model)], 0)
    )
    tower_q = Tower(0, info, weights, None, smalls, None, query_count, slots_q, LENGTHS)
    tower_p = Tower(
        1, info, weights, other_p, smalls, small_other, half_count, slots_p, LENGTHS + query_count
    )
    flat_q = x_q.reshape(-1, model)
    flat_p = x_p.reshape(-1, model)
    cots_q = cot_q.reshape(-1, model)
    cots_p = cot_p.reshape(-1, model)

    (early_q,) = forward_layers(tower_q, (0,), flat_q, True)
    mid_q = early_q[OUTPUT]
    arrived_q = core_swap(mid_q)
    (late_q,) = forward_layers(tower_q, (1,), arrived_q, True)
    early_p, late_p = forward_layers(tower_p, (0, 1), flat_p, True, (late_q[OUTPUT],))
    mid_p = early_p[OUTPUT]
    top_q, top_p = late_q[OUTPUT], late_p[OUTPUT]

    cls_rows = jnp.concatenate([top_q[::slots_q], top_p[::slots_p]], 0)
    cls_other = core_swap(cls_rows)
    cls_chip = jnp.concatenate(
        [
            jnp.where(is_first, cls_other[:query_count], cls_rows[:query_count]),
            jnp.where(is_first, cls_rows[query_count:], cls_other[query_count:]),
            jnp.where(is_first, cls_other[query_count:], cls_rows[query_count:]),
        ],
        0,
    )
    loss_own, d_cls_q, d_cls_p = contrast(
        cls_chip, micro, positive, query_count, batch_index, size
    )

    def factors(rows, kept, back):
        return (rows, kept[LEFTS], back[4], back[3], back[5], back[6])

    scale = size // BLOCKS

    def core_products(layer, rows, lefts, other_lefts, back, other_rights, after, cost):
        products = passage_products(
            tower_p, layer, rows, lefts, other_lefts, back[4], other_rights, after, cost
        )
        return products

    def chains_of(layer, products):
        return [
            Chain(products[2 * at], products[2 * at + 1], ORDERS[3 * layer + at], scale)
            for at in range(len(products) // 2)
        ]

    late_back_q = backward_layer(
        tower_q, 1, cots_q, d_cls_q, late_q, True, cost=0
    )
    late_sent_q = late_back_q[0]
    grad_mid_q = core_swap(late_sent_q)
    early_back_q = backward_layer(
        tower_q,
        0,
        grad_mid_q,
        None,
        early_q,
        False,
        cost=0,
        through=(late_p[LEFTS], early_p[LEFTS], jnp.where(is_first, top_p, mid_p)),
    )
    *early_back_q, late_left, early_left, hidden_sent = early_back_q
    late_left_other, early_left_other = core_swap(late_left), core_swap(early_left)
    hidden_other = core_swap(hidden_sent)
    packs = pack_first(
        info,
        factors(flat_q, early_q, early_back_q),
        factors(arrived_q, late_q, late_back_q),
        cost=0,
    )
    keeps, sends = packs[0::2], packs[1::2]
    arrivals = [flip_swap(sends[0], scale), flip_swap(sends[1], 2 * scale)]
    late_back_p = backward_layer(
        tower_p, 1, cots_p, d_cls_p, late_p, True, tuple(sends), cost=0
    )
    late_sent_p = late_back_p[0]
    late_other = core_swap(late_back_p[3])
    packs = pack_second(
        info,
        keeps,
        sends,
        arrivals,
        model,
        (late_sent_p, late_left_other, early_left_other, hidden_other),
        cost=40,
    )
    keeps, sends = packs[0::2], packs[1::2]
    arrivals = [flip_swap(sends[0], 2 * scale), flip_swap(sends[1], scale)]
    products = core_products(
        1, None, late_left, late_left_other, late_back_p, late_other, tuple(sends), 0
    )
    a1, b1 = chains_of(1, products)
    early_back_p = backward_layer(
        tower_p, 0, late_sent_p, None, early_p, False, tuple(products[:1]), cost=0
    )
    early_grad_p = early_back_p[0]
    early_other = core_swap(early_back_p[3])
    send, keep = query_products(
        info, keeps, sends, arrivals, model, wide, (early_grad_p,), cost=40
    )
    query = Chain(send, keep, (4, 8), scale)
    products = core_products(
        0, flat_p, early_left, early_left_other, early_back_p, early_other, (send,), 0
    )
    vectors = (*early_back_q[1:3], *late_back_q[1:3], *early_back_p[1:3], *late_back_p[1:3])
    others = (
        early_grad_p,
        late_sent_p,
        early_back_q[0],
        late_sent_q,
        mid_q,
        top_q,
        mid_p,
        top_p,
        hidden_other,
        loss_own[None],
    )
    vectors = (*early_back_q[1:3], *late_back_q[1:3], *early_back_p[1:3], *late_back_p[1:3])
    pieces = vector_pieces(info, 0, vectors, wide, (products[0],))
    vector = Chain(*pieces, (1, 2, 4, 8), scale, True)
    passed = play_round([[a1], [b1]], (pieces[0],), 40, tuple(products))
    a0, b0 = chains_of(0, passed[-len(products) :])
    seen = passed[: -len(products)]
    for step, (groups, cost) in enumerate((
        ([[query]], 0),
        ([[a1, b1], "v"], 15),
        ([[a0], [b0]], 0),
        ([[query], "v"], 0),
        ([[a1]], 12),
        ([[a0, b0], "v"], 12),
        ([[a1]], 0),
        ([[a0], "v"], 0),
    )):
        held = others if step == 4 else ()
        passed = play_round([[vector] if group == "v" else group for group in groups], seen, cost, held)
        seen = passed[: len(passed) - len(held)]
        if step == 4:
            others = passed[-10:]
    early_grad_p, late_sent_p, early_grad_q, late_sent_q = others[:4]
    mid_q, top_q, mid_p, top_p, hidden_other, loss_own = others[4:]
    loss_own = loss_own[0]
    early_grad_other = core_swap(jnp.where(is_first, late_sent_p.astype(F32), early_grad_p))

    total_q = query.total

    def other_half(begin, columns, bit):
        mine = (batch_index // (bit * scale)) % 2
        sent = lax.dynamic_slice_in_dim(total_q, begin + (1 - mine) * columns, columns, 1)
        return flip_swap(sent, bit * scale)

    query_x = other_half(0, 3 * model // 2, 1)
    query_y = other_half(4 * model, wide // 2, 2)
    own, sent, total_v = last_round(info, a0, a1.total, vector, seen)
    sums = put_together(info, own, core_swap(sent), total_q, query_x, query_y, model, wide)
    if scale > 1:
        left = all_bits(scale)
        sums = [
            jnp.stack([scatter_sum(to_grid(tower.astype(LOW), scale), left, left) for tower in item])
            for item in sums
        ]
    g_qkv, g_out, g_up, g_down = sums

    total_v = total_v.reshape(2, 16, 128)
    eight = total_v[:, :8, : model // BLOCKS]
    g_bup = total_v[:, 8:10].reshape(2, -1)[:, : wide // BLOCKS]
    if scale > 1:
        left = all_bits(scale)
        eight = scatter_sum(
            to_grid(jnp.moveaxis(eight, 2, 0).reshape(-1, 16), scale), left, left
        )
        eight = jnp.moveaxis(eight.reshape(-1, 2, 8), 0, 2)
        g_bup = scatter_sum(to_grid(g_bup.T, scale), left, left).T
    g_gain = jnp.stack([eight[:, 3], eight[:, 0]], 1)
    g_bias = jnp.stack([eight[:, at] for at in (6, 7, 5, 4, 2, 1)], 1)

    pairs = (
        jnp.where(is_first, mid_p, hidden_other),
        jnp.where(is_first, hidden_other, top_p),
    )
    hidden_p = jnp.concatenate(pairs, 0).reshape(x_p.shape)
    pairs = (
        jnp.where(is_first, early_grad_p, early_grad_other),
        jnp.where(is_first, early_grad_other, late_sent_p.astype(F32)),
    )
    grad_p = jnp.concatenate(pairs, 0).reshape(x_p.shape)
    hidden_q = jnp.where(is_first, mid_q, top_q).reshape(x_q.shape)
    grad_q = jnp.where(is_first, early_grad_q, late_sent_q.astype(F32)).reshape(x_q.shape)
    return (
        hidden_q[None],
        hidden_p[None],
        grad_q[None],
        grad_p[None],
        loss_own,
        g_qkv[None],
        g_out[None],
        g_up[None],
        g_down[None],
        g_gain[None],
        g_bias[None],
        g_bup[None],
        g_bias[None, :, 0, :],
    )


def solution(mesh):
    return jax.shard_map(
        shards,
        mesh=mesh,
        in_specs=(
            P("batch", None, None),
            P("batch", None, None),
            P("batch"),
            P("batch"),
            P("batch", None, None),
            P("batch", None, None),
            P(),
            P(),
            P("section", None, None, None),
            P("section", None, None, None),
            P("section", None, None, None),
            P("section", None, None, None),
            P("section", None, None, None),
            P("section", None, None, None),
            P("section", None, None),
        ),
        out_specs=(
            P("section", "batch", None, None),
            P("section", "batch", None, None),
            P("section", "batch", None, None),
            P("section", "batch", None, None),
            P("batch"),
            P("section", None, "batch", None),
            P("section", None, "batch", None),
            P("section", None, "batch", None),
            P("section", None, "batch", None),
            P("section", None, None, "batch"),
            P("section", None, None, "batch"),
            P("section", None, "batch"),
            P("section", None, "batch"),
        ),
        check_vma=False,
    )
```

```python
import jax
import jax.numpy as jnp
from jax import lax
from jax.experimental import pallas as pl
from jax.experimental.pallas import tpu as pltpu
from jax.sharding import PartitionSpec as P

HEADS = 12
HEAD_DIM = 64


NORM_EPS = 1e-05
SQRT_HALF = 0.7071067811865476
ROOT_TAU_INV = 0.3989422804014327
MASK_FILL = -1e30
LOGIT_GAIN = 2.5
PRECISE = lax.Precision.HIGHEST


def core_swap(block):
    return lax.ppermute(block, "section", [(0, 1), (1, 0)])


def flip_swap(block, bit):
    size = lax.axis_size("batch")
    return lax.ppermute(block, "batch", [(i, i ^ bit) for i in range(size)])


F32 = jnp.float32
LOW = jnp.bfloat16
VMEM_LIMIT = 58 * 1024 * 1024
BLOCKS = 16
COST = 1 << 30
IS_FIRST, CORE, PLACES, Z_PLACES, X_BIT, Y_BIT, LENGTHS = 0, 1, 2, 98, 102, 103, 104
ORDERS = (
    (1, 2, 4, 8),
    (2, 1, 4, 8),
    (2, 1, 4, 8),
    (1, 2, 4, 8),
    (2, 1, 4, 8),
    (2, 1, 4, 8),
)

LAYOUTS = (((0, 0), (1, 0), (0, 1536), (1, 1536)), ((0, 0), (1, 0), (0, 1536), (1, 1536)))


def mm(left, right):
    return lax.dot_general(left, right, (((1,), (0,)), ((), ())), preferred_element_type=F32)


def mm_nt(left, right):
    return lax.dot_general(left, right, (((1,), (1,)), ((), ())), preferred_element_type=F32)


def mm_tn(left, right):
    return lax.dot_general(left, right, (((0,), (0,)), ((), ())), preferred_element_type=F32)


def row_mean(values):
    return jnp.sum(values, axis=-1, keepdims=True) * (1.0 / values.shape[-1])


def normed_rows(values):
    center = values - row_mean(values)
    inverse = lax.rsqrt(row_mean(center * center) + NORM_EPS)
    return center * inverse, inverse


def norm_pull(upstream, normed, inverse, gain):
    scaled = upstream * gain
    return inverse * (scaled - row_mean(scaled) - normed * row_mean(scaled * normed))


def col_sum(values):
    return jnp.sum(values, axis=0, keepdims=True)


class Moves:
    def __init__(self, sems):
        self.sems = sems
        self.used = 0
        self.open = []

    def slot(self):
        self.used += 1
        return self.sems.at[self.used - 1]

    def fetch(self, source, target):
        copy = pltpu.make_async_copy(source, target, self.slot())
        copy.start()
        return copy

    def fetch_either(self, flag, first, second, target):
        sem = self.slot()
        copy = pltpu.make_async_copy(first, target, sem)
        if second is None:
            copy.start()
            return copy
        other = pltpu.make_async_copy(second, target, sem)

        @pl.when(flag)
        def _():
            copy.start()

        @pl.when(jnp.logical_not(flag))
        def _():
            other.start()

        return copy

    def store(self, source, target):
        self.open.append(self.fetch(source, target))

    def drain(self):
        for copy in self.open:
            copy.wait()


class Tower:
    def __init__(self, index, info, weights, others, small, small_other, seqs, slots, first_len):
        self.index = index
        self.info = info
        self.weights = weights
        self.others = others
        self.small = small
        self.small_other = small_other
        self.seqs = seqs
        self.slots = slots
        self.first_len = first_len
        self.count = seqs * slots
        self.width = weights[1].shape[-1]
        self.wide = weights[2].shape[-1]
        self.group = self.count if self.count <= 128 else slots
        self.shared = others is not None

    def given(self, which):
        own = [self.weights[at] for at in which]
        return own + ([self.others[at] for at in which] if self.shared else [])

    def given_small(self):
        return list(self.small) + ([self.small_other] if self.shared else [])

    def use_own(self, info, layer):
        return info[IS_FIRST] == (1 if layer == 0 else 0)

    def lengths_at(self, info):
        return self.first_len + (info[CORE] * self.seqs if self.shared else 0)

    def row_start(self, info):
        return pl.multiple_of(info[CORE] * self.count, self.count) if self.shared else 0

    def small_rows(self, refs, flag):
        own = [refs[0][0, self.index], refs[1][0, self.index]]
        if self.shared:
            other = refs[3]
            own = [
                jnp.where(flag, own[0], other[0:2, :]),
                jnp.where(flag, own[1], other[2:8, :]),
            ]
        return own

    def hidden_bias(self, refs, flag, step, tile):
        own = refs[2][0, self.index : self.index + 1, step * tile : (step + 1) * tile]
        if self.shared:
            own = jnp.where(flag, own, refs[3][8 + step : 9 + step, :])
        return own


ANYWHERE = pl.BlockSpec(memory_space=pl.ANY)
SCALARS = pl.BlockSpec(memory_space=pltpu.SMEM)
INSIDE = pl.BlockSpec(memory_space=pltpu.VMEM)


def call_kernel(kernel, name, inputs, outs, scratch, copies, micros, after, through=()):
    count = len(inputs)
    given = list(after) + list(through)
    extra = len(given)

    def body(*refs):
        refs = list(refs)
        kernel(
            refs[:count],
            refs[count + extra : count + extra + len(outs)]
            or refs[count + extra : count + extra + len(through)],
            refs[count + extra + len(outs) + len(through) : -1],
            Moves(refs[-1]),
        )

    return pl.pallas_call(
        body,
        out_shape=[jax.ShapeDtypeStruct(shape, kind) for shape, kind in outs]
        + [jax.ShapeDtypeStruct(array.shape, array.dtype) for array in through],
        in_specs=[spec for spec, _ in inputs] + [ANYWHERE] * extra,
        out_specs=[ANYWHERE] * (len(outs) + len(through)),
        input_output_aliases={
            count + len(after) + at: len(outs) + at for at in range(len(through))
        },
        scratch_shapes=[pltpu.VMEM(shape, kind) for shape, kind in scratch]
        + [pltpu.SemaphoreType.DMA((copies,))],
        compiler_params=pltpu.CompilerParams(vmem_limit_bytes=VMEM_LIMIT),
        cost_estimate=pl.CostEstimate(
            flops=int(COST * micros) + 1024, bytes_accessed=1024, transcendentals=0
        ),
        name=name,
    )(*[array for _, array in inputs], *given)


def pair_masks(dtype):
    lanes = lax.broadcasted_iota(jnp.int32, (1, 128), 1)
    low = jnp.where(lanes < HEAD_DIM, 1.0, 0.0)
    return low.astype(dtype), (1.0 - low).astype(dtype)


def stacked_pair(block, low, high):
    return jnp.concatenate([block * low, block * high], axis=0)


def joined_pair(stacked, group):
    lanes = lax.broadcasted_iota(jnp.int32, (1, 128), 1)
    return jnp.where(lanes < HEAD_DIM, stacked[:group], stacked[group:])


def pair_softmax(query_stack, key_block, valid):
    scores = mm_nt(key_block, query_stack) * HEAD_DIM ** (-0.5)
    scores = jnp.where(valid, scores, MASK_FILL)
    exponent = jnp.exp(scores - jnp.max(scores, axis=0, keepdims=True))
    return exponent * (1.0 / jnp.sum(exponent, axis=0, keepdims=True))


def valid_keys(info, first_len, group, slots):
    keys = lax.broadcasted_iota(jnp.int32, (group, 2 * group), 0)
    queries = lax.broadcasted_iota(jnp.int32, (group, 2 * group), 1)
    seqs = group // slots
    if seqs == 1:
        return keys < info[first_len]
    queries = jnp.where(queries >= group, queries - group, queries)
    valid = None
    for j in range(seqs):
        low = j * slots
        inside = (
            (queries >= low)
            & (queries < low + slots)
            & (keys >= low)
            & (keys < low + info[first_len + j])
        )
        valid = inside if valid is None else valid | inside
    return valid


def weight_shapes(tower):
    width, steps = tower.width, tower.wide // tower.width
    return [
        ((3, width, width), LOW),
        ((width, width), LOW),
        ((steps, width, width), LOW),
        ((steps, width, width), LOW),
    ]


def fetch_narrow(tower, flag, own, other, targets, moves, order=(0, 1, 2, 3)):
    width = tower.width
    got = {}
    for part in order:
        if part == 3:
            got[3] = moves.fetch_either(flag, own[1].at[0, tower.index], other[1], targets[1])
            continue
        cols = pl.ds(part * width, width)
        second = other[0].at[:, cols] if tower.shared else None
        got[part] = moves.fetch_either(
            flag, own[0].at[0, tower.index, :, cols], second, targets[0].at[part]
        )
    return got


def fetch_step(tower, flag, own, other, targets, moves, step, at):
    width = tower.width
    part = pl.ds(pl.multiple_of(at * width, width), width)
    up, down = (other[0].at[:, part], other[1].at[part]) if tower.shared else (None, None)
    return (
        moves.fetch_either(flag, own[1].at[0, tower.index, part], down, targets[1].at[step]),
        moves.fetch_either(flag, own[0].at[0, tower.index, :, part], up, targets[0].at[step]),
    )


def kept_scratch(tower):
    count, width, wide = tower.count, tower.width, tower.wide
    steps = wide // width
    return [
        ((count, width), LOW),
        ((count, 3 * width), LOW),
        ((count, width), LOW),
        ((count, width), LOW),
        ((steps, count, width), LOW),
        ((steps, count, width), LOW),
        ((count, width), LOW),
        ((count, width), LOW),
        ((2, count, 128), F32),
        ((width // 128, count, 2 * tower.group), LOW),
    ]


OUTPUT, LEFTS, PROJECTED, SLOPE, HAT1, HAT2, INVERSES, SOFT = range(8)


def kept_shapes(tower, inner):
    count, width, wide = tower.count, tower.width, tower.wide
    steps = wide // width
    return [
        ((count, width), LOW),
        ((count, 2 * width + wide + (width if inner else 0)), LOW),
        ((count, 3 * width), LOW),
        ((steps, count, width), LOW),
        ((count, width), LOW),
        ((count, width), LOW),
        ((2, count, 128), F32),
        ((width // 128, count, 2 * tower.group), LOW),
    ]


def forward_body(
    tower, layer, info, x_v, got, weights, smalls, acc_v, kept, outs, moves, first_out=None
):
    count, width, group = tower.count, tower.width, tower.group
    w_qkv, w_out, w_up, w_down = weights
    out_v, qkv_v, mix_v, low_v, act_v, slope_v, hat1_v, hat2_v, inv_v, soft_v = kept
    use_own = tower.use_own(info, layer)
    gains, bias = tower.small_rows(smalls, use_own)
    x = x_v[...]
    for part in range(3):
        got[part].wait()
        block = mm(x, w_qkv[part])
        if part == 0:
            block = block + bias[0:1, :]
        if part == 2:
            block = block + bias[1:2, :]
        qkv_v[:, part * width : (part + 1) * width] = block.astype(LOW)
    moves.store(qkv_v, outs[PROJECTED])
    low, high = pair_masks(LOW)
    for g in range(count // group):
        at = slice(g * group, (g + 1) * group)
        valid = valid_keys(
            info, tower.lengths_at(info) + g * (group // tower.slots), group, tower.slots
        )
        for pair in range(width // 128):
            lane = pair * 128
            q2 = qkv_v[at, lane : lane + 128]
            k2 = qkv_v[at, width + lane : width + lane + 128]
            v2 = qkv_v[at, 2 * width + lane : 2 * width + lane + 128]
            soft = pair_softmax(stacked_pair(q2, low, high), k2, valid).astype(LOW)
            soft_v[pair, at, :] = soft
            mix_v[at, lane : lane + 128] = joined_pair(mm_tn(soft, v2), group).astype(LOW)
    moves.store(soft_v, outs[SOFT])
    moves.store(mix_v, outs[LEFTS].at[:, pl.ds(0, width)])
    got[3].wait()
    summed = x.astype(F32) + (mm(mix_v[...], w_out[...]) + bias[2:3, :])
    hat, inverse = normed_rows(summed)
    hat1_v[...] = hat.astype(LOW)
    inv_v[0] = jnp.broadcast_to(inverse, (count, 128))
    moves.store(hat1_v, outs[HAT1])
    first = hat * gains[0:1, :] + bias[3:4, :]
    low_v[...] = first.astype(LOW)
    moves.store(low_v, outs[LEFTS].at[:, pl.ds(width, width)])
    acc_v[...] = first + bias[4:5, :]
    for step in range(tower.wide // width):
        for copy in got[4 + step]:
            copy.wait()
        hidden = mm(low_v[...], w_up[step]) + tower.hidden_bias(smalls, use_own, step, width)
        cdf = 0.5 * (1.0 + lax.erf(hidden * SQRT_HALF))
        act = (hidden * cdf).astype(LOW)
        act_v[step] = act
        slope_v[step] = (
            cdf + hidden * (jnp.exp(-0.5 * hidden * hidden) * ROOT_TAU_INV)
        ).astype(LOW)
        moves.store(act_v.at[step], outs[LEFTS].at[:, pl.ds((2 + step) * width, width)])
        moves.store(slope_v.at[step], outs[SLOPE].at[step])
        acc_v[...] += mm(act, w_down[step])
    hat, inverse = normed_rows(acc_v[...])
    hat2_v[...] = hat.astype(LOW)
    moves.store(hat2_v, outs[HAT2])
    inv_v[1] = jnp.broadcast_to(inverse, (count, 128))
    moves.store(inv_v, outs[INVERSES])
    output = hat * gains[1:2, :] + bias[5:6, :]
    out_v[...] = output.astype(LOW)
    moves.store(out_v, outs[OUTPUT])
    if first_out is not None:
        first_v, to, above = first_out
        firsts = [output[at * tower.slots : at * tower.slots + 1, :] for at in range(tower.seqs)]
        spare = jnp.zeros((16 - len(firsts) - sum(item.shape[0] for item in above), width), F32)
        first_v[...] = jnp.concatenate([*above, *firsts, spare], axis=0).astype(LOW)
        moves.store(first_v, to)


def forward_layers(tower, layers, rows, whole_rows, ahead, after=(), cost=0):
    count, width = tower.count, tower.width
    steps = tower.wide // width
    shapes = [kept_shapes(tower, at > 0) for at in range(len(layers))]
    kinds = len(shapes[0])
    held = kept_scratch(tower)

    def kernel(ins, outs, scratch, moves):
        info, x_any = ins[0], ins[1]
        own = ins[2:6]
        other = ins[6:10] if tower.shared else [None] * 4
        smalls = ins[10:] if tower.shared else ins[6:]
        above = []
        if ahead is not None:
            above = [smalls[-1][0 : ahead[1], :].astype(F32)]
            smalls = smalls[:-1]
        x_v, acc_v = scratch[:2]
        if whole_rows:
            x_any = x_any.at[pl.ds(tower.row_start(info), count)]
        x_got = moves.fetch(x_any, x_v)
        weights, got = [], []
        for at, layer in enumerate(layers):
            targets = scratch[2 + 4 * at : 6 + 4 * at]
            flag = tower.use_own(info, layer)
            arrivals = fetch_narrow(tower, flag, own[:2], other[:2], targets[:2], moves)
            for step in range(steps):
                arrivals[4 + step] = fetch_step(
                    tower, flag, own[2:], other[2:], targets[2:], moves, step, step
                )
            weights.append(targets)
            got.append(arrivals)
        x_got.wait()
        for at, layer in enumerate(layers):
            begin = 2 + 4 * len(layers) + len(held) * at
            kept = scratch[begin : begin + len(held)]
            forward_body(
                tower,
                layer,
                info,
                x_v,
                got[at],
                weights[at],
                smalls,
                acc_v,
                kept,
                outs[kinds * at : kinds * (at + 1)],
                moves,
                (scratch[-1], outs[-1], above) if at + 1 == len(layers) else None,
            )
            x_v = kept[0]
            if at + 1 < len(layers):
                inner = outs[kinds * (at + 1) + LEFTS]
                moves.store(x_v, inner.at[:, pl.ds(2 * width + tower.wide, width)])
        moves.drain()

    outs = [shape for layer_shapes in shapes for shape in layer_shapes] + [((16, width), LOW)]
    scratch = [((count, width), LOW), ((count, width), F32)] + weight_shapes(tower) * len(layers)
    inputs = [(SCALARS, tower.info), (ANYWHERE, rows)]
    inputs += [(ANYWHERE, array) for array in tower.given((0, 1, 2, 3))]
    inputs += [(INSIDE, array) for array in tower.given_small()]
    if ahead is not None:
        inputs.append((INSIDE, ahead[0]))
    results = call_kernel(
        kernel,
        "layer_forward",
        inputs,
        outs,
        scratch + held * len(layers) + outs[-1:],
        2 + len(layers) * (4 + 2 * steps + 9 + 2 * steps),
        cost,
        list(after),
    )
    return [results[kinds * at : kinds * (at + 1)] for at in range(len(layers))] + [results[-1]]


def place_rows(target, block, info, first, size, columns):
    for piece in range(block.shape[0] // size):
        at = pl.multiple_of(info[first + piece] * size, size)
        target[pl.ds(at, size), columns] = block[piece * size : (piece + 1) * size].astype(LOW)


def wide_scratch(tower, upstream):
    count, width = tower.count, tower.width
    steps = tower.wide // width
    return weight_shapes(tower)[2:] + [
        ((count, width), upstream.dtype),
        ((count, width), LOW),
        ((count, 128), F32),
        ((steps, count, width), LOW),
        ((count, width), F32),
        ((count, width), LOW),
        ((steps, count, width), LOW),
        ((8, width), F32),
    ]


def store_sides(source, side_width, outs, column, core_at, moves):
    for side, to in ((1 - core_at, outs[0]), (core_at, outs[1])):
        lanes = pl.ds(pl.multiple_of(side * side_width, 128), side_width)
        moves.store(source.at[:, lanes], to.at[:, pl.ds(column, side_width)])


def wide_tiles(tower, info):
    steps = tower.wide // tower.width
    if not tower.shared:
        return list(range(steps))
    return [lax.rem(step + (1 - info[CORE]) * (steps // 2), steps) for step in range(steps)]


def wide_fetch(tower, layer, info, ins, seeded, scratch, moves):
    up_any, own, other, slope_any, hat_any, inv_any = ins
    w_up, w_down, up_v, hat_v, inv_v, slope_v = scratch[:6]
    use_own = tower.use_own(info, layer)
    if seeded:
        up_any = up_any.at[pl.ds(tower.row_start(info), tower.count)]
    first_got = [
        moves.fetch(up_any, up_v),
        moves.fetch(hat_any, hat_v),
        moves.fetch(inv_any.at[1], inv_v),
    ]
    got = []
    for step, at in enumerate(wide_tiles(tower, info)):
        pieces = [moves.fetch(slope_any.at[at], slope_v.at[step])]
        pieces += fetch_step(tower, use_own, own, other, (w_up, w_down), moves, step, at)
        got.append(pieces)
    return first_got, got


def wide_body(tower, layer, info, fetched, first_ref, smalls, scratch, outs, moves):
    count, width = tower.count, tower.width
    steps = tower.wide // width
    w_up, w_down, up_v, hat_v, inv_v, slope_v, da_v, df_v, dh_v, vec_v = scratch
    use_own = tower.use_own(info, layer)
    core_at = info[CORE]
    first_got, got = fetched
    tiles = wide_tiles(tower, info)
    gains, _ = tower.small_rows(smalls, use_own)
    for copy in first_got:
        copy.wait()
    upward = up_v[...].astype(F32)
    if first_ref is not None:
        row_at = lax.broadcasted_iota(jnp.int32, (count, 1), 0)
        lengths = tower.lengths_at(info)
        first_seq = lengths - tower.first_len
        seen = jnp.zeros((count, 1), F32)
        for seq in range(tower.seqs):
            start = seq * tower.slots
            inside_seq = (row_at >= start) & (row_at < start + info[lengths + seq])
            seen = jnp.where(inside_seq, 1.0, seen)
        upward = upward * seen
        for seq in range(tower.seqs):
            upward = upward + jnp.where(
                row_at == seq * tower.slots, first_ref[pl.ds(first_seq + seq, 1), :], 0.0
            )
    hat = hat_v[...].astype(F32)
    vec_v[0:1, :] = col_sum(upward * hat)
    vec_v[1:2, :] = col_sum(upward)
    d_second = norm_pull(upward, hat, inv_v[:, 0:1], gains[1:2, :])
    d_low = d_second.astype(LOW)
    df_v[...] = d_low
    vec_v[2:3, :] = col_sum(d_low.astype(F32))
    vec_v[7:8, :] = jnp.zeros((1, width), F32)
    da_v[...] = d_second
    vec_out, df_out, dh_out = outs
    if tower.shared:
        store_sides(df_v, width // 2, df_out, 0, core_at, moves)
    else:
        moves.store(df_v, df_out[0])
    for step, at in enumerate(tiles):
        for copy in got[step]:
            copy.wait()
        d_hidden = (mm_nt(df_v[...], w_down[step]) * slope_v[step].astype(F32)).astype(LOW)
        vec_v[pl.ds(3 + at, 1), :] = col_sum(d_hidden.astype(F32))
        dh_v[step] = d_hidden
        da_v[...] += mm_nt(d_hidden, w_up[step])
        if tower.shared:
            side, place = divmod(step, steps // 2)
            moves.store(dh_v.at[step], dh_out[side].at[:, pl.ds(place * width, width)])
        else:
            moves.store(dh_v.at[step], dh_out[0].at[step])
    moves.store(vec_v, vec_out)


def narrow_scratch(tower, out_type):
    count, width = tower.count, tower.width
    return weight_shapes(tower)[:2] + [
        ((count, width), LOW),
        ((count, 128), F32),
        ((count, 3 * width), LOW),
        ((width // 128, count, 2 * tower.group), LOW),
        ((count, width), LOW),
        ((count, 3 * width), LOW),
        ((count, width), LOW),
        ((count, width), F32),
        ((count, width), out_type),
        ((8, width), F32),
    ]


def narrow_fetch(tower, layer, info, ins, scratch, moves):
    own, other, qkv_any, hat_any, inv_any, soft_any = ins
    w_qkv, w_out, hat_v, inv_v, qkv_v, soft_v = scratch[:6]
    use_own = tower.use_own(info, layer)
    got = {"hat": [moves.fetch(hat_any, hat_v), moves.fetch(inv_any.at[0], inv_v)]}
    weights = fetch_narrow(tower, use_own, own, other, (w_qkv, w_out), moves, (3,))
    got["heads"] = [moves.fetch(qkv_any, qkv_v), moves.fetch(soft_any, soft_v)]
    weights.update(fetch_narrow(tower, use_own, own, other, (w_qkv, w_out), moves, (0, 1, 2)))
    got["weights"] = weights
    return got


def narrow_body(tower, layer, info, got, da_v, smalls, scratch, outs, moves):
    count, width, group = tower.count, tower.width, tower.group
    w_qkv, w_out, hat_v, inv_v, qkv_v, soft_v, dz_v, dp_v, dmix_v, du_v, dx_v, vec_v = scratch
    use_own = tower.use_own(info, layer)
    core_at = info[CORE]
    dx_out, vec_out, dz_out, dp_out = outs
    gains, _ = tower.small_rows(smalls, use_own)
    for copy in got["hat"]:
        copy.wait()
    upward = da_v[...]
    hat = hat_v[...].astype(F32)
    vec_v[0:1, :] = col_sum(upward * hat)
    vec_v[1:2, :] = col_sum(upward)
    d_summed = norm_pull(upward, hat, inv_v[:, 0:1], gains[0:1, :])
    du_v[...] = d_summed
    d_low = d_summed.astype(LOW)
    dz_v[...] = d_low
    vec_v[2:3, :] = col_sum(d_low.astype(F32))
    vec_v[5:8, :] = jnp.zeros((3, width), F32)
    if tower.shared:
        store_sides(dz_v, width // 2, dz_out, 2 * width, core_at, moves)
    else:
        moves.store(dz_v, dz_out[0])
    got["weights"][3].wait()
    dmix_v[...] = mm_nt(d_low, w_out[...]).astype(LOW)
    for copy in got["heads"]:
        copy.wait()
    low, high = pair_masks(LOW)
    scale = HEAD_DIM ** (-0.5)
    for g in range(count // group):
        at = slice(g * group, (g + 1) * group)
        for pair in range(width // 128):
            lane = pair * 128
            q2 = qkv_v[at, lane : lane + 128]
            k2 = qkv_v[at, width + lane : width + lane + 128]
            v2 = qkv_v[at, 2 * width + lane : 2 * width + lane + 128]
            soft = soft_v[pair, at, :]
            d_stack = stacked_pair(dmix_v[at, lane : lane + 128], low, high)
            d_soft = mm_nt(v2, d_stack)
            soft_wide = soft.astype(F32)
            total = jnp.sum(d_soft * soft_wide, axis=0, keepdims=True)
            d_scores = (soft_wide * (d_soft - total)).astype(LOW)
            dp_v[at, lane : lane + 128] = (
                joined_pair(mm_tn(d_scores, k2), group) * scale
            ).astype(LOW)
            dp_v[at, width + lane : width + lane + 128] = (
                mm(d_scores, stacked_pair(q2, low, high)) * scale
            ).astype(LOW)
            dp_v[at, 2 * width + lane : 2 * width + lane + 128] = mm(soft, d_stack).astype(LOW)
    vec_v[3:4, :] = col_sum(dp_v[:, :width].astype(F32))
    vec_v[4:5, :] = col_sum(dp_v[:, 2 * width :].astype(F32))
    moves.store(vec_v, vec_out)
    if tower.shared:
        store_sides(dp_v, 3 * width // 2, dp_out, width // 2, core_at, moves)
    else:
        moves.store(dp_v, dp_out[0])
    d_input = du_v[...]
    for part in range(3):
        got["weights"][part].wait()
        d_input = d_input + mm_nt(dp_v[:, part * width : (part + 1) * width], w_qkv[part])
    dx_v[...] = d_input.astype(dx_v.dtype)
    moves.store(dx_v, dx_out)


def backward_layer(
    tower, layer, upstream, first_rows, kept, low_out, after=(), cost=0, through=()
):
    count, width, wide = tower.count, tower.width, tower.wide
    steps = wide // width
    seeded = first_rows is not None
    out_type = LOW if low_out else F32
    wide_shapes = wide_scratch(tower, upstream)

    def kernel(ins, outs, scratch, moves):
        ins = list(ins)
        info, up_any = ins.pop(0), ins.pop(0)
        first_ref = ins.pop(0) if seeded else None
        own = [ins.pop(0) for _ in range(4)]
        other = [ins.pop(0) for _ in range(4)] if tower.shared else [None] * 4
        slope_any, hat2_any, inv_any, qkv_any, hat1_any, soft_any = (
            ins.pop(0) for _ in range(6)
        )
        first, second = scratch[: len(wide_shapes)], scratch[len(wide_shapes) :]
        dx, vec1, vec2 = outs[:3]
        if tower.shared:
            dh, df = outs[3:5], outs[5:7]
            dz = dp = df
        else:
            df, dh, dz, dp = (outs[at : at + 1] for at in range(3, 7))
        given = (up_any, own[2:], other[2:], slope_any, hat2_any, inv_any)
        wide_got = wide_fetch(tower, layer, info, given, seeded, first, moves)
        given = (own[:2], other[:2], qkv_any, hat1_any, inv_any, soft_any)
        got = narrow_fetch(tower, layer, info, given, second, moves)
        wide_body(
            tower, layer, info, wide_got, first_ref, ins, first, (vec1, df, dh), moves
        )
        narrow_body(
            tower, layer, info, got, first[6], ins, second, (dx, vec2, dz, dp), moves
        )
        moves.drain()

    outs = [((count, width), out_type), ((8, width), F32), ((8, width), F32)]
    if tower.shared:
        outs += [((count, wide // 2), LOW)] * 2 + [((count, 5 * width // 2), LOW)] * 2
    else:
        outs += [((count, width), LOW), ((steps, count, width), LOW)]
        outs += [((count, width), LOW), ((count, 3 * width), LOW)]
    inputs = [(SCALARS, tower.info), (ANYWHERE, upstream)]
    if seeded:
        inputs.append((INSIDE, first_rows))
    inputs += [(ANYWHERE, array) for array in tower.given((0, 1, 2, 3))]
    inputs += [(ANYWHERE, kept[at]) for at in (SLOPE, HAT2, INVERSES, PROJECTED, HAT1, SOFT)]
    inputs += [(INSIDE, array) for array in tower.given_small()]
    return call_kernel(
        kernel,
        "backward_layer",
        inputs,
        outs,
        wide_shapes + narrow_scratch(tower, out_type),
        3 + 3 * steps + 8 + 3 + steps + 6,
        cost,
        list(after),
        through,
    )


def place_rows(target, block, info, first, size, columns):
    for piece in range(block.shape[0] // size):
        at = pl.multiple_of(info[first + piece] * size, size)
        target[pl.ds(at, size), columns] = block[piece * size : (piece + 1) * size].astype(LOW)


def passage_products(
    tower, layer, rows, lefts, other_lefts, rights, other_rights, vectors, after=(), cost=0
):
    count, width, wide = tower.count, tower.width, tower.wide
    steps = wide // width
    half = width // 2
    piece = width // BLOCKS
    layout = LAYOUTS[layer]
    chunks = 1 + max(chunk for chunk, _ in layout)
    widths = [
        max(column + (wide // 2 if at < 2 else width) for at, (to, column) in enumerate(layout) if to == chunk)
        for chunk in range(chunks)
    ]
    vector_column = widths[0]
    if vectors:
        widths[0] += 128
    whole = rows is not None

    def kernel(ins, outs, scratch, moves):
        ins = list(ins)
        info = ins.pop(0)
        x_any = ins.pop(0) if whole else None
        vector_refs = [ins.pop() for _ in vectors]
        left, other_left = ins[:2]
        hidden_of, rights_of = (ins[2], ins[4]), (ins[3], ins[5])
        low_v, dh_v, act_v, df_v, x_v, dp_v, mix_v, dz_v = scratch[:8]
        grads = scratch[8:]
        above, below = pl.ds(0, count), pl.ds(count, count)

        def both(sources, column, target):
            columns = pl.ds(column, target.shape[1])
            return [
                moves.fetch(sources[0].at[:, columns], target.at[above]),
                moves.fetch(sources[1].at[:, columns], target.at[below]),
            ]

        lefts_of = (left, other_left)
        got_low = both(lefts_of, width, low_v)
        got_dh = [both(hidden_of, at * width, dh_v.at[at]) for at in range(steps // 2)]
        got_df = both(rights_of, 0, df_v)
        got_act = [both(lefts_of, (2 + at) * width, act_v.at[at]) for at in range(steps)]
        if whole:
            start = tower.row_start(info)
            other_start = pl.multiple_of(count - start, count)
            got_x = [
                moves.fetch(x_any.at[pl.ds(start, count)], x_v.at[above]),
                moves.fetch(x_any.at[pl.ds(other_start, count)], x_v.at[below]),
            ]
        else:
            got_x = both(lefts_of, 2 * width + wide, x_v)
        got_x += both(rights_of, half, dp_v)
        got_mix = both(lefts_of, 0, mix_v) + both(rights_of, 2 * width, dz_v)

        def ready(copies):
            for copy in copies:
                copy.wait()

        def target(part):
            chunk, column = layout[part]
            return grads[chunk], column, PLACES + BLOCKS * (3 * layer + chunk)

        def send(part):
            source, column, _ = target(part)
            cut = source.shape[0] // 2
            columns = pl.ds(column, wide // 2 if part < 2 else width)
            to = 2 * layout[part][0]
            moves.store(source.at[pl.ds(cut, cut), columns], outs[to].at[:, columns])
            moves.store(source.at[pl.ds(0, cut), columns], outs[to + 1].at[:, columns])

        if vectors:
            lane = slice(vector_column, vector_column + 128)
            for block in range(BLOCKS):
                from_rows = slice(block * PIECE_ROWS, (block + 1) * PIECE_ROWS)
                begin = block * piece
                grads[0][begin : begin + PIECE_ROWS, lane] = (
                    vector_refs[0][from_rows, :] + vector_refs[1][from_rows, :]
                ).astype(LOW)
                grads[0][begin + PIECE_ROWS : begin + piece, lane] = jnp.zeros(
                    (piece - PIECE_ROWS, 128), LOW
                )
            cut = width // 2
            columns = pl.ds(vector_column, 128)
            moves.store(grads[0].at[pl.ds(cut, cut), columns], outs[0].at[:, columns])
            moves.store(grads[0].at[pl.ds(0, cut), columns], outs[1].at[:, columns])
        ready(got_low)
        for at in range(steps // 2):
            ready(got_dh[at])
            to, column, first = target(1)
            columns = slice(column + at * width, column + (at + 1) * width)
            place_rows(to, mm_tn(low_v[...], dh_v[at]), info, first, piece, columns)
        send(1)
        ready(got_df)
        parts = wide // width
        for at in range(steps):
            ready(got_act[at])
            product = mm_tn(act_v[at], df_v[...])
            for block in range(width // piece):
                index, part = divmod(at * (width // piece) + block, parts)
                to, column, first = target(0)
                rows_to = pl.ds(pl.multiple_of(info[first + index] * piece, piece), piece)
                column += part * half
                to[rows_to, column : column + half] = product[
                    block * piece : (block + 1) * piece
                ].astype(LOW)
        send(0)
        ready(got_x)
        for part in range(4):
            if part == 3:
                ready(got_mix)
                product = mm_tn(mix_v[...], dz_v[...])
            else:
                product = mm_tn(x_v[...], dp_v[:, part * half : (part + 1) * half])
            to, column, first = target(2 + part // 2)
            column += part % 2 * half
            place_rows(to, product, info, first, piece, slice(column, column + half))
            if part % 2:
                send(2 + part // 2)
        moves.drain()

    outs = [((half, columns), LOW) for columns in widths for _ in range(2)]
    scratch = [
        ((2 * count, width), LOW),
        ((steps // 2, 2 * count, width), LOW),
        ((steps, 2 * count, width), LOW),
        ((2 * count, half), LOW),
        ((2 * count, width), LOW),
        ((2 * count, 3 * half), LOW),
        ((2 * count, width), LOW),
        ((2 * count, half), LOW),
    ] + [((width, columns), LOW) for columns in widths]
    arrays = [rows] if whole else []
    arrays += [lefts, other_lefts, *rights, *other_rights]
    inputs = [(SCALARS, tower.info)] + [(ANYWHERE, array) for array in arrays]
    inputs += [(INSIDE, array) for array in vectors]
    return call_kernel(
        kernel,
        "passage_products",
        inputs,
        outs,
        scratch,
        2 * (1 + steps // 2 + 1 + steps + 4) + 10,
        cost,
        list(after),
    )


def block_chooser(rows, columns, valid, size, bit):
    at = lax.broadcasted_iota(jnp.int32, (1, columns), 1)
    piece = jnp.floor((at.astype(F32) + 0.5) * (1.0 / size)).astype(jnp.int32)
    wanted = jnp.where(at < valid, at + (piece + bit) * size, -1)
    row_at = lax.broadcasted_iota(jnp.int32, (rows, columns), 0)
    return jnp.where(row_at == wanted, 1.0, 0.0).astype(LOW)


def pack_first(info, early, late, after=(), cost=0):
    count, width = early[0].shape
    steps = early[2].shape[0]
    wide = steps * width
    half = width // 2
    piece = width // BLOCKS
    keeps = (half + 3 * half, 2 * wide // 2)
    wholes = (2 * width, 2 * width)

    def kernel(ins, outs, scratch, moves):
        info_ref = ins[0]
        first, second = ins[1:7], ins[7:13]
        x_v, left_v, dh_v, df_v, dz_v, dp_v = scratch[:6]
        results = scratch[6:]
        flag = info_ref[IS_FIRST] == 1
        got = [moves.fetch_either(flag, a, b, to) for a, b, to in zip(first, second, scratch)]
        bits = [(info_ref[at], 1 - info_ref[at]) for at in (X_BIT, Y_BIT)]
        for copy in got:
            copy.wait()

        def lanes(bit, size):
            return pl.ds(pl.multiple_of(bit * size, 128), size)

        for which in range(2):
            first_to, second_to = results[which], results[2 + which]
            bit = bits[0][which]
            choose = block_chooser(width, half, half, piece, bit)
            first_to[:, :half] = mm(left_v[:, :width], choose).astype(LOW)
            first_to[:, half : 4 * half] = dp_v[:, lanes(bit, 3 * half)]
            bit = bits[1][which]
            for step in range(steps):
                start = (2 + step) * width + bit * half
                second_to[:, step * half : (step + 1) * half] = left_v[
                    :, pl.ds(pl.multiple_of(start, 128), half)
                ]
            for step in range(steps // 2):
                begin = wide // 2 + step * width
                second_to[:, begin : begin + width] = dh_v[bit * (steps // 2) + step]
        results[1][:, keeps[0] : keeps[0] + width] = x_v[...]
        results[1][:, keeps[0] + width :] = dz_v[...]
        results[3][:, keeps[1] : keeps[1] + width] = left_v[:, width : 2 * width]
        results[3][:, keeps[1] + width :] = df_v[...]
        for at in range(4):
            moves.store(results[at], outs[at])
        moves.drain()

    outs = []
    for keep, rest in zip(keeps, wholes):
        outs += [((count, keep), LOW), ((count, keep + rest), LOW)]
    inputs = [(SCALARS, info)] + [(ANYWHERE, array) for array in tuple(early) + tuple(late)]
    scratch = [(array.shape, LOW) for array in early]
    return call_kernel(
        kernel, "pack_first", inputs, outs, scratch + outs, 12, cost, list(after)
    )


def pack_second(info, keeps, sends, arrivals, width, after=(), cost=0):
    count = keeps[0].shape[0]
    wide = keeps[1].shape[1]
    half, quarter, third = width // 2, width // 4, 256
    piece = width // BLOCKS
    chosen = (third + half, half + wide // 4)
    wholes = (3 * half + width, wide // 2 + width)

    def kernel(ins, outs, scratch, moves):
        info_ref = ins[0]
        got = [moves.fetch(source, to) for source, to in zip(ins[1:], scratch)]
        bits = [(info_ref[at], 1 - info_ref[at]) for at in (Y_BIT, X_BIT)]
        for copy in got:
            copy.wait()
        for lot in range(2):
            keep_v, send_v, arrived_v = scratch[lot], scratch[2 + lot], scratch[4 + lot]
            cut = keep_v.shape[1]
            sources = (
                (slice(0, count), keep_v, send_v),
                (slice(count, 2 * count), arrived_v, arrived_v),
            )
            for which in range(2):
                target = scratch[6 + 2 * lot + which]
                bit = bits[lot][which]
                for rows, halved, whole in sources:
                    if lot == 0:
                        choose = block_chooser(half, third, quarter, piece, bit)
                        target[rows, :third] = mm(halved[:, :half], choose).astype(LOW)
                        choose = block_chooser(width, half, half, 2 * piece, bit)
                        target[rows, third:chosen[0]] = mm(
                            whole[:, cut : cut + width], choose
                        ).astype(LOW)
                        continue
                    choose = block_chooser(width, half, half, piece, bit)
                    target[rows, :half] = mm(whole[:, cut : cut + width], choose).astype(LOW)
                    choose = block_chooser(2 * half, half, half, quarter, bit)
                    for part in range(wide // 2 // width):
                        target[rows, half + part * half : half + (part + 1) * half] = mm(
                            halved[:, part * width : (part + 1) * width], choose
                        ).astype(LOW)
            target = scratch[6 + 2 * lot + 1]
            begin = chosen[lot]
            first = half if lot == 0 else wide // 2
            for rows, halved, whole in sources:
                target[rows, begin : begin + cut - first] = halved[:, first:cut]
                target[rows, begin + cut - first :] = whole[:, cut + width :]
        for at in range(4):
            moves.store(scratch[6 + at], outs[at])
        moves.drain()

    outs = []
    for left, right in zip(chosen, wholes):
        outs += [((2 * count, left), LOW), ((2 * count, left + right), LOW)]
    arrays = tuple(keeps) + tuple(sends) + tuple(arrivals)
    inputs = [(SCALARS, info)] + [(ANYWHERE, array) for array in arrays]
    scratch = [(array.shape, LOW) for array in arrays]
    return call_kernel(
        kernel, "pack_second", inputs, outs, scratch + outs, 10, cost, list(after)
    )


def query_products(info, keeps, sends, arrivals, width, wide, after=(), cost=0):
    count = keeps[0].shape[0]
    half, third = width // 2, 256
    piece = width // BLOCKS
    packed = [keep.shape[1] for keep in keeps]
    rights = [send.shape[1] - left for send, left in zip(sends, packed)]
    columns = 4 * width + 2 * wide

    def kernel(ins, outs, scratch, moves):
        info_ref = ins[0]
        keep_any, send_any, arrived_any = ins[1:3], ins[3:5], ins[5:7]
        left_v, right_v, result = scratch[0:2], scratch[2:4], scratch[4]
        got = []
        for lot in range(2):
            cut = packed[lot]
            below = pl.ds(count, count)
            got.append(
                [
                    moves.fetch(keep_any[lot], left_v[lot].at[pl.ds(0, count)]),
                    moves.fetch(arrived_any[lot].at[:, pl.ds(0, cut)], left_v[lot].at[below]),
                    moves.fetch(
                        send_any[lot].at[:, pl.ds(cut, rights[lot])],
                        right_v[lot].at[pl.ds(0, count)],
                    ),
                    moves.fetch(
                        arrived_any[lot].at[:, pl.ds(cut, rights[lot])], right_v[lot].at[below]
                    ),
                ]
            )

        def place(z, rows, column):
            row = pl.multiple_of(info_ref[Z_PLACES + z] * piece, piece)
            result[pl.ds(row, piece), column : column + rows.shape[1]] = rows.astype(LOW)

        for copy in got[0]:
            copy.wait()
        for part in range(3):
            product = mm_tn(
                left_v[0][:, third:], right_v[0][:, part * half : (part + 1) * half]
            )
            for block in range(8):
                z, bit = divmod(block, 2)
                place(
                    z,
                    product[block * piece : (block + 1) * piece],
                    bit * 3 * half + part * half,
                )
        product = mm_tn(left_v[0][:, :third], right_v[0][:, 3 * half :])
        for z in range(4):
            place(z, product[z * piece : (z + 1) * piece], 3 * width)
        for copy in got[1]:
            copy.wait()
        at = 4 * width
        for part in range(wide // 2 // width):
            product = mm_tn(
                left_v[1][:, :half], right_v[1][:, part * width : (part + 1) * width]
            )
            for block in range(8):
                z, bit = divmod(block, 2)
                place(
                    z,
                    product[block * piece : (block + 1) * piece],
                    at + bit * (wide // 2) + part * width,
                )
        at += wide
        product = mm_tn(left_v[1][:, half:], right_v[1][:, wide // 2 :])
        per = wide // width
        for z in range(4):
            for part in range(per):
                begin = (z * per + part) * piece
                place(z, product[begin : begin + piece], at + part * width)
        moves.store(result.at[pl.ds(2 * piece, 2 * piece)], outs[0])
        moves.store(result.at[pl.ds(0, 2 * piece)], outs[1])
        moves.drain()

    outs = [((2 * piece, columns), LOW)] * 2
    arrays = tuple(keeps) + tuple(sends) + tuple(arrivals)
    inputs = [(SCALARS, info)] + [(ANYWHERE, array) for array in arrays]
    scratch = [((2 * count, cut), LOW) for cut in packed]
    scratch += [((2 * count, cut), LOW) for cut in rights]
    scratch += [((4 * piece, columns), LOW)]
    return call_kernel(
        kernel, "query_products", inputs, outs, scratch, 10, cost, list(after)
    )


PIECE_ROWS = 32


def vector_pieces(info, first, parts, wide, after=(), cost=0):
    width = parts[0].shape[1]
    cut = width // BLOCKS
    big = wide // BLOCKS

    def kernel(ins, outs, scratch, moves):
        info_ref = ins[0]
        refs = ins[1:]
        early = info_ref[IS_FIRST] == 1
        for target in scratch:
            target[...] = jnp.zeros_like(target)

        def lay(target, tower_at, wide_rows, narrow_rows):
            eight = jnp.concatenate([wide_rows[0:3], narrow_rows[0:5]], axis=0)
            for block in range(BLOCKS):
                at = info_ref[PLACES + first + block] * PIECE_ROWS + 16 * tower_at
                at = pl.multiple_of(at, 16)
                target[pl.ds(at, 8), 0:cut] = eight[:, block * cut : (block + 1) * cut]
                row, column = divmod(block * big, width)
                bias = wide_rows[3 + row : 4 + row, column : column + big]
                target[pl.ds(at + 8, 1), 0:128] = bias[:, 0:128]
                target[pl.ds(at + 9, 1), 0 : big - 128] = bias[:, 128:big]

        send, keep = scratch
        eq1, eq2, lq1, lq2, ep1, ep2, lp1, lp2 = (ref[...] for ref in refs)
        lay(keep, 0, jnp.where(early, eq1, lq1), jnp.where(early, eq2, lq2))
        lay(keep, 1, jnp.where(early, ep1, lp1), jnp.where(early, ep2, lp2))
        lay(send, 1, jnp.where(early, lp1, ep1), jnp.where(early, lp2, ep2))
        moves.store(send, outs[0])
        moves.store(keep, outs[1])
        moves.drain()

    outs = [((BLOCKS * PIECE_ROWS, 128), F32)] * 2
    inputs = [(SCALARS, info)] + [(INSIDE, array) for array in parts]
    return call_kernel(kernel, "vector_pieces", inputs, outs, outs, 2, cost, list(after))


def take_in(items, after=(), cost=0, through=()):
    def kernel(ins, outs, scratch, moves):
        ins, scratch = list(ins), list(scratch)
        taken = []
        for pairs, last in items:
            got = []
            for _ in pairs:
                held = [scratch.pop(0), scratch.pop(0)]
                got.append((held, [moves.fetch(ins.pop(0), to) for to in held]))
            taken.append((got, [scratch.pop(0) for _ in range(1 if last else 2)]))
        out_at = 0
        for (got, results), (_, last) in zip(taken, items):
            for held, copies in got:
                for copy in copies:
                    copy.wait()
            for which, result in enumerate(results):
                part_rows = result.shape[0]
                start = 0 if last else (1 - which) * part_rows
                column = 0
                for (keep_v, arrived_v), _ in got:
                    columns = keep_v.shape[1]
                    chunk = 48 if columns <= 1536 and part_rows % 48 == 0 else 16

                    def one(step, carry, keep_v=keep_v, arrived_v=arrived_v, column=column):
                        to = pl.ds(pl.multiple_of(step * chunk, 16), chunk)
                        of = pl.ds(pl.multiple_of(start + step * chunk, 16), chunk)
                        total = keep_v[of, :].astype(F32) + arrived_v[of, :].astype(F32)
                        result[to, column : column + keep_v.shape[1]] = total.astype(result.dtype)
                        return carry

                    lax.fori_loop(0, part_rows // chunk, one, 0)
                    column += columns
                moves.store(result, outs[out_at])
                out_at += 1
        moves.drain()

    outs, scratch = [], []
    for pairs, last in items:
        rows = pairs[0][0].shape[0]
        columns = sum(keep.shape[1] for keep, _ in pairs)
        kind = pairs[0][0].dtype
        mine = [((rows, columns), F32)] if last else [((rows // 2, columns), kind)] * 2
        outs += mine
        for keep, arrived in pairs:
            scratch += [(keep.shape, kind), (arrived.shape, kind)]
        scratch += mine
    inputs = [(ANYWHERE, array) for pairs, _ in items for pair in pairs for array in pair]
    return call_kernel(
        kernel, "take_in", inputs, outs, scratch, len(inputs) + len(outs), cost, list(after), through
    )


def take_in_quarters(pairs, after=(), cost=0):
    rows = pairs[0][0].shape[0] // 4
    columns = sum(keep.shape[1] for keep, _ in pairs)

    def kernel(ins, outs, scratch, moves):
        held = scratch[: len(ins)]
        results = scratch[len(ins) :]
        got = [moves.fetch(source, to) for source, to in zip(ins, held)]
        for copy in got:
            copy.wait()
        for quarter in (1, 2, 3, 0):
            result = results[quarter]
            column = 0
            for at in range(len(pairs)):
                keep_v, arrived_v = held[2 * at : 2 * at + 2]
                wide = keep_v.shape[1]

                def one(step, carry, keep_v=keep_v, arrived_v=arrived_v, column=column, wide=wide):
                    to = pl.ds(pl.multiple_of(step * 16, 16), 16)
                    of = pl.ds(pl.multiple_of(quarter * rows + step * 16, 16), 16)
                    total = keep_v[of, :].astype(F32) + arrived_v[of, :].astype(F32)
                    result[to, column : column + wide] = total.astype(LOW)
                    return carry

                lax.fori_loop(0, rows // 16, one, 0)
                column += wide
            moves.store(result, outs[quarter])
        moves.drain()

    outs = [((rows, columns), LOW)] * 4
    arrays = [array for pair in pairs for array in pair]
    inputs = [(ANYWHERE, array) for array in arrays]
    scratch = [(array.shape, LOW) for array in arrays]
    return call_kernel(
        kernel, "take_in_quarters", inputs, outs, scratch + outs, len(arrays) + 4, cost, list(after)
    )


class Chain:
    def __init__(self, send, keep, order, scale, from_core=False):
        self.order = list(order)
        self.scale = scale
        self.keep = keep
        self.total = None
        self.arrived = core_swap(send) if from_core else self.swap(send)

    def swap(self, block):
        return flip_swap(block, self.order.pop(0) * self.scale)


def play_round(groups, after=(), cost=0, through=()):
    items = [
        ([(chain.keep, chain.arrived) for chain in group], not group[0].order) for group in groups
    ]
    results = list(take_in(items, after, cost, through))
    seen = []
    for group in groups:
        chain = group[0]
        assert all(other.order == chain.order for other in group)
        if not chain.order:
            chain.total = results.pop(0)
            seen.append(chain.total)
            continue
        sent, chain.keep = results.pop(0), results.pop(0)
        chain.arrived = chain.swap(sent)
        seen.append(sent)
    return tuple(seen + results)


def last_round(info, quarters, other_total, vector_column, after=(), cost=0):
    rows, columns = other_total.shape
    begin = vector_column

    def kernel(ins, outs, scratch, moves):
        info_ref = ins[0]
        parts, late_v = scratch[:4], scratch[4]
        own_v, send_v, vec_v = scratch[5:]
        got = [moves.fetch(source, to) for source, to in zip(ins[1:], scratch)]
        for copy in got:
            copy.wait()
        flag = info_ref[IS_FIRST] == 1

        def total(part, lanes):
            values = [ref[part, lanes].astype(F32) for ref in parts]
            return (values[0] + values[1]) + (values[2] + values[3])

        vec_v[...] = total(slice(0, rows), slice(begin, begin + 128))
        moves.store(vec_v, outs[2])
        for row in range(0, rows, 16):
            part = slice(row, row + 16)
            for lanes, of in (
                (slice(0, begin), slice(0, begin)),
                (slice(begin, columns), slice(begin + 128, columns + 128)),
            ):
                early = total(part, of)
                late = late_v[part, lanes]
                send_v[part, lanes] = jnp.where(flag, late, early)
                own_v[part, lanes] = jnp.where(flag, early, late)
        moves.store(send_v, outs[1])
        moves.store(own_v, outs[0])
        moves.drain()

    outs = [((rows, columns), F32)] * 2 + [((rows, 128), F32)]
    arrays = (*quarters, other_total)
    inputs = [(SCALARS, info)] + [(ANYWHERE, array) for array in arrays]
    scratch = [(array.shape, array.dtype) for array in arrays]
    return call_kernel(
        kernel, "last_round", inputs, outs, scratch + outs, 8, cost, list(after)
    )


def output_shapes(rows, width, wide):
    return [
        ((2, rows, 3 * width), F32),
        ((2, rows, width), F32),
        ((2, rows, wide), F32),
        ((2, wide // width * rows, width), F32),
    ]


def query_outputs(info, query, query_x, query_y, width, wide, after=(), cost=0):
    rows = query.shape[0]
    half = width // 2
    parts = wide // width

    def kernel(ins, outs, scratch, moves):
        info_ref = ins[0]
        sources, results = scratch[:3], scratch[3:]
        got = [moves.fetch(source, to) for source, to in zip(ins[1:], sources)]
        query_v, x_v, y_v = sources
        g_qkv, g_out, g_up, g_down = results
        for copy in got:
            copy.wait()
        at = 4 * width
        for bit_at, begin, size, arrived, target in (
            (X_BIT, 0, 3 * half, x_v, g_qkv),
            (Y_BIT, at, wide // 2, y_v, g_up),
        ):
            bit = info_ref[bit_at]
            mine = pl.ds(pl.multiple_of(bit * size, 128), size)
            others = pl.ds(pl.multiple_of((1 - bit) * size, 128), size)
            target[:, mine] = query_v[:, pl.ds(pl.multiple_of(begin + bit * size, 128), size)]
            target[:, others] = arrived[...]
        g_out[...] = query_v[:, 3 * width : 4 * width]
        at += wide
        for part in range(parts):
            g_down[part * rows : (part + 1) * rows, :] = query_v[
                :, at + part * width : at + (part + 1) * width
            ]
        for result, to in zip(results, outs):
            moves.store(result, to.at[0])
        moves.drain()

    outs = output_shapes(rows, width, wide)
    arrays = (query, query_x, query_y)
    inputs = [(SCALARS, info)] + [(ANYWHERE, array) for array in arrays]
    scratch = [(array.shape, F32) for array in arrays] + [(shape[1:], F32) for shape, _ in outs]
    return call_kernel(
        kernel, "query_outputs", inputs, outs, scratch, 7, cost, list(after)
    )


def passage_outputs(info, own, other, outputs, width, wide):
    rows, columns = own.shape
    half = width // 2
    parts = wide // width
    chunk_width = columns // 2
    begin = [to * chunk_width + column for to, column in LAYOUTS[0]]

    def kernel(ins, outs, scratch, moves):
        info_ref = ins[0]
        sources, results = scratch[:2], scratch[2:]
        got = [moves.fetch(source, to) for source, to in zip(ins[1:], sources)]
        g_qkv, g_out, g_up, g_down = results
        core = info_ref[CORE]
        for at, side in ((0, core), (1, 1 - core)):
            got[at].wait()
            source = sources[at]
            here = pl.ds(pl.multiple_of(side * half, 128), half)
            for part in range(parts):
                g_down[part * rows : (part + 1) * rows, here] = source[
                    :, begin[0] + part * half : begin[0] + (part + 1) * half
                ]
            up = pl.ds(pl.multiple_of(side * (wide // 2), 128), wide // 2)
            g_up[:, up] = source[:, begin[1] : begin[1] + wide // 2]
            for third in range(3):
                column = begin[2 + third // 2] + third % 2 * half
                to = pl.ds(pl.multiple_of(side * 3 * half + third * half, 128), half)
                g_qkv[:, to] = source[:, column : column + half]
            g_out[:, here] = source[:, begin[3] + half : begin[3] + width]
        for result, to in zip(results, outs):
            moves.store(result, to.at[1])
        moves.drain()

    shapes = output_shapes(rows, width, wide)
    arrays = (own, other)
    inputs = [(SCALARS, info)] + [(ANYWHERE, array) for array in arrays]
    scratch = [(array.shape, F32) for array in arrays] + [(shape[1:], F32) for shape, _ in shapes]
    return call_kernel(
        kernel, "passage_outputs", inputs, [], scratch, 6, 0, [], tuple(outputs)
    )


def pick_bit(grid, axis, index):
    return lax.dynamic_index_in_dim(grid, index, axis, keepdims=False)


def own_bit(bit):
    return (lax.axis_index("batch") // bit) % 2


def scatter_sum(grid, bits, left):
    left = list(left)
    for bit in bits:
        axis = left.index(bit)
        mine = own_bit(bit)
        sent = pick_bit(grid, axis, 1 - mine)
        kept = pick_bit(grid, axis, mine)
        arrived = flip_swap(sent, bit)
        total = kept.astype(jnp.float32) + arrived.astype(jnp.float32)
        left.remove(bit)
        grid = total if not left else total.astype(grid.dtype)
    return grid


def all_bits(size):
    bits = [1 << i for i in range(size.bit_length() - 1)]
    return bits[::-1]


def to_grid(array, size):
    bits = all_bits(size)
    return array.reshape((2,) * len(bits) + (array.shape[0] // size,) + array.shape[1:])


def gather_all(block, size):
    if size != 16:
        for bit in all_bits(size)[::-1]:
            block = jnp.concatenate([block, flip_swap(block, bit)], 0)
        return block
    block = jnp.concatenate([block] + [flip_swap(block, k) for k in (1, 2, 3)], 0)
    return jnp.concatenate([block] + [flip_swap(block, k) for k in (4, 8, 12)], 0)


def contrast(own_cls, micro, positive, query_count, batch_index, batch_size):
    width = own_cls.shape[1]
    chip_rows = own_cls.shape[0]
    gathered = gather_all(own_cls, batch_size).reshape(batch_size, chip_rows, width)
    all_q = gathered[:, :query_count].reshape(-1, width)
    all_p = gathered[:, query_count:].reshape(-1, width)
    blocks = jnp.arange(batch_size, dtype=jnp.int32) ^ batch_index
    query_ids = (
        blocks[:, None] * query_count + jnp.arange(query_count, dtype=jnp.int32)[None, :]
    ).reshape(-1)
    passage_ids = (
        3 * query_ids[:, None] + jnp.arange(3, dtype=jnp.int32)[None, :]
    ).reshape(-1)
    labels = jnp.take(micro, query_ids)
    wanted = jnp.take(positive, query_ids)
    logit_scale = LOGIT_GAIN * width ** (-0.5)
    logits = mm_nt(all_q, all_p) * logit_scale
    same_group = labels[:, None] == jnp.repeat(labels, 3)[None, :]
    logits = jnp.where(same_group, logits, MASK_FILL)
    row_top = jnp.max(logits, axis=-1, keepdims=True)
    exponent = jnp.exp(logits - row_top)
    totals = jnp.sum(exponent, axis=-1, keepdims=True)
    target = passage_ids[None, :] == wanted[:, None]
    loss_all = (
        row_top[:, 0] + jnp.log(totals[:, 0]) - jnp.sum(jnp.where(target, logits, 0.0), axis=-1)
    )
    coefficient = (exponent / totals - target.astype(jnp.float32)) * logit_scale
    passage_count = 3 * query_count
    d_cls_q = jnp.dot(coefficient[:query_count], all_p.astype(jnp.float32), precision=PRECISE)
    d_cls_p = lax.dot_general(
        coefficient[:, :passage_count],
        all_q.astype(jnp.float32),
        (((0,), (0,)), ((), ())),
        precision=PRECISE,
    )
    return loss_all[:query_count], d_cls_q, d_cls_p


def integers(core, index, size, len_q, len_p):
    blocks = jnp.arange(BLOCKS, dtype=jnp.int32)
    own = index // (size // BLOCKS)
    relative = blocks ^ own
    places = [
        sum(((relative // bit) % 2) * (8 >> at) for at, bit in enumerate(order))
        for order in ORDERS
    ]
    depth = jnp.arange(4, dtype=jnp.int32) ^ (own // 4)
    z_places = (depth % 2) * 2 + depth // 2
    few = jnp.stack([1 - core, core])
    ends = jnp.stack([own % 2, (own // 2) % 2])
    return jnp.concatenate([few, *places, z_places, ends, len_q, len_p]).astype(jnp.int32)


def shards(
    x_q,
    x_p,
    len_q,
    len_p,
    cot_q,
    cot_p,
    positive,
    micro,
    w_qkv,
    w_out,
    w_up,
    w_down,
    norm_gain,
    biases,
    b_up,
):
    core = lax.axis_index("section")
    is_first = core == 0
    batch_index = lax.axis_index("batch")
    size = lax.axis_size("batch")
    bits = all_bits(size)
    query_count, slots_q, model = x_q.shape
    half_count = x_p.shape[0] // 2
    slots_p = x_p.shape[1]
    wide = w_up.shape[-1]
    info = integers(core, batch_index, size, len_q, len_p)
    weights = (w_qkv, w_out, w_up, w_down)
    smalls = (norm_gain, biases, b_up)
    other_p = tuple(core_swap(member[0, 1]) for member in weights)
    small_other = core_swap(
        jnp.concatenate([norm_gain[0, 1], biases[0, 1], b_up[0, 1].reshape(-1, model)], 0)
    )
    tower_q = Tower(0, info, weights, None, smalls, None, query_count, slots_q, LENGTHS)
    tower_p = Tower(
        1, info, weights, other_p, smalls, small_other, half_count, slots_p, LENGTHS + query_count
    )
    flat_q = x_q.reshape(-1, model)
    flat_p = x_p.reshape(-1, model)
    cots_q = cot_q.reshape(-1, model)
    cots_p = cot_p.reshape(-1, model)

    early_q, _ = forward_layers(tower_q, (0,), flat_q, True, None)
    mid_q = early_q[OUTPUT]
    arrived_q = core_swap(mid_q)
    late_q, first_q = forward_layers(tower_q, (1,), arrived_q, True, None)
    early_p, late_p, cls_rows = forward_layers(
        tower_p, (0, 1), flat_p, True, (first_q, query_count)
    )
    mid_p = early_p[OUTPUT]
    top_q, top_p = late_q[OUTPUT], late_p[OUTPUT]

    last = query_count + half_count
    cls_other = core_swap(cls_rows)
    cls_chip = jnp.concatenate(
        [
            jnp.where(is_first, cls_other[:query_count], cls_rows[:query_count]),
            jnp.where(is_first, cls_rows[query_count:last], cls_other[query_count:last]),
            jnp.where(is_first, cls_other[query_count:last], cls_rows[query_count:last]),
        ],
        0,
    )
    loss_own, d_cls_q, d_cls_p = contrast(
        cls_chip, micro, positive, query_count, batch_index, size
    )

    def factors(rows, kept, back):
        return (rows, kept[LEFTS], back[4], back[3], back[5], back[6])

    scale = size // BLOCKS

    def core_products(
        layer, rows, lefts, other_lefts, back, other_rights, vectors, after, cost
    ):
        products = passage_products(
            tower_p, layer, rows, lefts, other_lefts, back[4::2], other_rights, vectors, after, cost
        )
        return products

    def chains_of(layer, products):
        return [
            Chain(products[2 * at], products[2 * at + 1], ORDERS[3 * layer + at], scale)
            for at in range(len(products) // 2)
        ]

    late_back_q = backward_layer(
        tower_q, 1, cots_q, d_cls_q, late_q, True, cost=0
    )
    late_sent_q = late_back_q[0]
    grad_mid_q = core_swap(late_sent_q)
    early_back_q = backward_layer(
        tower_q,
        0,
        grad_mid_q,
        None,
        early_q,
        False,
        cost=0,
        through=(late_p[LEFTS], early_p[LEFTS], jnp.where(is_first, top_p, mid_p)),
    )
    *early_back_q, late_left, early_left, hidden_sent = early_back_q
    late_left_other, early_left_other = core_swap(late_left), core_swap(early_left)
    hidden_other = core_swap(hidden_sent)
    packs = pack_first(
        info,
        factors(flat_q, early_q, early_back_q),
        factors(arrived_q, late_q, late_back_q),
        cost=0,
    )
    keeps, sends = packs[0::2], packs[1::2]
    arrivals = [flip_swap(sends[0], scale), flip_swap(sends[1], 2 * scale)]
    late_back_p = backward_layer(
        tower_p, 1, cots_p, d_cls_p, late_p, True, tuple(sends), cost=0
    )
    late_sent_p = late_back_p[0]
    late_other = [core_swap(array) for array in late_back_p[3::2]]
    packs = pack_second(
        info,
        keeps,
        sends,
        arrivals,
        model,
        (late_sent_p, late_left_other, early_left_other, hidden_other),
        cost=40,
    )
    keeps, sends = packs[0::2], packs[1::2]
    arrivals = [flip_swap(sends[0], 2 * scale), flip_swap(sends[1], scale)]
    products = core_products(
        1, None, late_left, late_left_other, late_back_p, late_other, (), tuple(sends), 0
    )
    a1, b1 = chains_of(1, products)
    send, keep = query_products(
        info, keeps, sends, arrivals, model, wide, tuple(products[:1]), cost=4
    )
    query = Chain(send, keep, (4, 8), scale)
    early_back_p = backward_layer(
        tower_p, 0, late_sent_p, None, early_p, False, (send,), cost=0
    )
    early_grad_p = early_back_p[0]
    early_other = [core_swap(array) for array in early_back_p[3::2]]
    vectors = (*early_back_q[1:3], *late_back_q[1:3], *early_back_p[1:3], *late_back_p[1:3])
    pieces = vector_pieces(info, 0, vectors, wide, (early_grad_p,), 0)
    vectors = (pieces[1], core_swap(pieces[0]))
    seen = play_round([[a1], [b1]], pieces[:1], 4)
    seen = play_round([[query]], seen, 40)
    products = core_products(
        0, flat_p, early_left, early_left_other, early_back_p, early_other, vectors, seen, 4
    )
    a0, b0 = chains_of(0, products)
    seen = (products[0],)
    others = (
        early_grad_p,
        late_sent_p,
        early_back_q[0],
        late_sent_q,
        mid_q,
        top_q,
        mid_p,
        top_p,
        hidden_other,
        loss_own[None],
    )
    for step, (groups, cost) in enumerate((
        ([[a1, b1]], 40),
        ([[query]], 4),
        ([[a0], [b0]], 0),
        ([[a1]], 40),
        ("z", 4),
        ([[a1]], 12),
    )):
        held = others if step == 2 else ()
        if groups == "z":
            parts = take_in_quarters([(chain.keep, chain.arrived) for chain in (a0, b0)], seen, cost)
            low, high = a0.order[0] * scale, a0.order[1] * scale
            quarters = (
                parts[0],
                flip_swap(parts[1], high),
                flip_swap(parts[2], low),
                flip_swap(parts[3], low + high),
            )
            seen = tuple(parts[1:])
            continue
        passed = play_round(groups, seen, cost, held)
        seen = passed[: len(passed) - len(held)]
        if step == 2:
            others = passed[-10:]
    early_grad_p, late_sent_p, early_grad_q, late_sent_q = others[:4]
    mid_q, top_q, mid_p, top_p, hidden_other, loss_own = others[4:]
    loss_own = loss_own[0]
    early_grad_other = core_swap(jnp.where(is_first, late_sent_p.astype(F32), early_grad_p))

    total_q = query.total

    def other_half(begin, columns, bit):
        mine = (batch_index // (bit * scale)) % 2
        sent = lax.dynamic_slice_in_dim(total_q, begin + (1 - mine) * columns, columns, 1)
        return flip_swap(sent, bit * scale)

    query_x = other_half(0, 3 * model // 2, 1)
    query_y = other_half(4 * model, wide // 2, 2)
    outputs = query_outputs(info, total_q, query_x, query_y, model, wide, seen)
    own, sent, total_v = last_round(info, quarters, a1.total, model + wide // 2, seen)
    sums = passage_outputs(info, own, core_swap(sent), outputs, model, wide)
    if scale > 1:
        left = all_bits(scale)
        sums = [
            jnp.stack([scatter_sum(to_grid(tower.astype(LOW), scale), left, left) for tower in item])
            for item in sums
        ]
    g_qkv, g_out, g_up, g_down = sums

    total_v = total_v[:32].reshape(2, 16, 128)
    eight = total_v[:, :8, : model // BLOCKS]
    g_bup = total_v[:, 8:10].reshape(2, -1)[:, : wide // BLOCKS]
    if scale > 1:
        left = all_bits(scale)
        eight = scatter_sum(
            to_grid(jnp.moveaxis(eight, 2, 0).reshape(-1, 16), scale), left, left
        )
        eight = jnp.moveaxis(eight.reshape(-1, 2, 8), 0, 2)
        g_bup = scatter_sum(to_grid(g_bup.T, scale), left, left).T
    g_gain = jnp.stack([eight[:, 3], eight[:, 0]], 1)
    g_bias = jnp.stack([eight[:, at] for at in (6, 7, 5, 4, 2, 1)], 1)

    pairs = (
        jnp.where(is_first, mid_p, hidden_other),
        jnp.where(is_first, hidden_other, top_p),
    )
    hidden_p = jnp.concatenate(pairs, 0).reshape(x_p.shape)
    pairs = (
        jnp.where(is_first, early_grad_p, early_grad_other),
        jnp.where(is_first, early_grad_other, late_sent_p.astype(F32)),
    )
    grad_p = jnp.concatenate(pairs, 0).reshape(x_p.shape)
    hidden_q = jnp.where(is_first, mid_q, top_q).reshape(x_q.shape)
    grad_q = jnp.where(is_first, early_grad_q, late_sent_q.astype(F32)).reshape(x_q.shape)
    return (
        hidden_q[None],
        hidden_p[None],
        grad_q[None],
        grad_p[None],
        loss_own,
        g_qkv[None],
        g_out[None],
        g_up[None],
        g_down[None],
        g_gain[None],
        g_bias[None],
        g_bup[None],
        g_bias[None, :, 0, :],
    )


def solution(mesh):
    return jax.shard_map(
        shards,
        mesh=mesh,
        in_specs=(
            P("batch", None, None),
            P("batch", None, None),
            P("batch"),
            P("batch"),
            P("batch", None, None),
            P("batch", None, None),
            P(),
            P(),
            P("section", None, None, None),
            P("section", None, None, None),
            P("section", None, None, None),
            P("section", None, None, None),
            P("section", None, None, None),
            P("section", None, None, None),
            P("section", None, None),
        ),
        out_specs=(
            P("section", "batch", None, None),
            P("section", "batch", None, None),
            P("section", "batch", None, None),
            P("section", "batch", None, None),
            P("batch"),
            P("section", None, "batch", None),
            P("section", None, "batch", None),
            P("section", None, "batch", None),
            P("section", None, "batch", None),
            P("section", None, None, "batch"),
            P("section", None, None, "batch"),
            P("section", None, "batch"),
            P("section", None, "batch"),
        ),
        check_vma=False,
    )
```

```python
import jax
import jax.numpy as jnp
from jax import lax
from jax.experimental import pallas as pl
from jax.experimental.pallas import tpu as pltpu
from jax.sharding import PartitionSpec as P

HEADS = 12
HEAD_DIM = 64


NORM_EPS = 1e-05
SQRT_HALF = 0.7071067811865476
ROOT_TAU_INV = 0.3989422804014327
MASK_FILL = -1e30
LOGIT_GAIN = 2.5
PRECISE = lax.Precision.HIGHEST


def core_swap(block):
    return lax.ppermute(block, "section", [(0, 1), (1, 0)])


def flip_swap(block, bit):
    size = lax.axis_size("batch")
    return lax.ppermute(block, "batch", [(i, i ^ bit) for i in range(size)])


F32 = jnp.float32
LOW = jnp.bfloat16
VMEM_LIMIT = 63 * 1024 * 1024 + 512 * 1024
BLOCKS = 16
COST = 1 << 30
IS_FIRST, CORE, PLACES, Z_PLACES, X_BIT, Y_BIT, LENGTHS = 0, 1, 2, 98, 102, 103, 104
ORDERS = (
    (1, 2, 4, 8),
    (2, 1, 4, 8),
    (2, 1, 4, 8),
    (1, 2, 4, 8),
    (2, 1, 4, 8),
    (2, 1, 4, 8),
)

LAYOUTS = (((0, 0), (1, 0), (0, 1536), (1, 1536)), ((0, 0), (1, 0), (0, 1536), (1, 1536)))


def mm(left, right):
    return lax.dot_general(left, right, (((1,), (0,)), ((), ())), preferred_element_type=F32)


def mm_nt(left, right):
    return lax.dot_general(left, right, (((1,), (1,)), ((), ())), preferred_element_type=F32)


def mm_tn(left, right):
    return lax.dot_general(left, right, (((0,), (0,)), ((), ())), preferred_element_type=F32)


def row_mean(values):
    return jnp.sum(values, axis=-1, keepdims=True) * (1.0 / values.shape[-1])


def normed_rows(values):
    center = values - row_mean(values)
    inverse = lax.rsqrt(row_mean(center * center) + NORM_EPS)
    return center * inverse, inverse


def norm_pull(upstream, normed, inverse, gain):
    scaled = upstream * gain
    return inverse * (scaled - row_mean(scaled) - normed * row_mean(scaled * normed))


def col_sum(values):
    return jnp.sum(values, axis=0, keepdims=True)


class Moves:
    def __init__(self, sems):
        self.sems = sems
        self.used = 0
        self.open = []

    def slot(self):
        self.used += 1
        return self.sems.at[self.used - 1]

    def fetch(self, source, target):
        copy = pltpu.make_async_copy(source, target, self.slot())
        copy.start()
        return copy

    def fetch_either(self, flag, first, second, target):
        sem = self.slot()
        copy = pltpu.make_async_copy(first, target, sem)
        if second is None:
            copy.start()
            return copy
        other = pltpu.make_async_copy(second, target, sem)

        @pl.when(flag)
        def _():
            copy.start()

        @pl.when(jnp.logical_not(flag))
        def _():
            other.start()

        return copy

    def store(self, source, target):
        self.open.append(self.fetch(source, target))

    def drain(self):
        for copy in self.open:
            copy.wait()


class Tower:
    def __init__(self, index, info, weights, others, small, small_other, seqs, slots, first_len):
        self.index = index
        self.info = info
        self.weights = weights
        self.others = others
        self.small = small
        self.small_other = small_other
        self.seqs = seqs
        self.slots = slots
        self.first_len = first_len
        self.count = seqs * slots
        self.width = weights[1].shape[-1]
        self.wide = weights[2].shape[-1]
        self.group = self.count if self.count <= 128 else slots
        self.shared = others is not None

    def given(self, which):
        own = [self.weights[at] for at in which]
        return own + ([self.others[at] for at in which] if self.shared else [])

    def given_small(self):
        return list(self.small) + ([self.small_other] if self.shared else [])

    def use_own(self, info, layer):
        return info[IS_FIRST] == (1 if layer == 0 else 0)

    def lengths_at(self, info):
        return self.first_len + (info[CORE] * self.seqs if self.shared else 0)

    def row_start(self, info):
        return pl.multiple_of(info[CORE] * self.count, self.count) if self.shared else 0

    def small_rows(self, refs, flag):
        own = [refs[0][0, self.index], refs[1][0, self.index]]
        if self.shared:
            other = refs[3]
            own = [
                jnp.where(flag, own[0], other[0:2, :]),
                jnp.where(flag, own[1], other[2:8, :]),
            ]
        return own

    def hidden_bias(self, refs, flag, step, tile):
        own = refs[2][0, self.index : self.index + 1, step * tile : (step + 1) * tile]
        if self.shared:
            own = jnp.where(flag, own, refs[3][8 + step : 9 + step, :])
        return own


ANYWHERE = pl.BlockSpec(memory_space=pltpu.HBM)
SCALARS = pl.BlockSpec(memory_space=pltpu.SMEM)
INSIDE = pl.BlockSpec(memory_space=pltpu.VMEM)


def call_kernel(kernel, name, inputs, outs, scratch, copies, micros, after, through=()):
    count = len(inputs)
    given = list(after) + list(through)
    extra = len(given)

    def body(*refs):
        refs = list(refs)
        kernel(
            refs[:count],
            refs[count + extra : count + extra + len(outs)]
            or refs[count + extra : count + extra + len(through)],
            refs[count + extra + len(outs) + len(through) : -1],
            Moves(refs[-1]),
        )

    return pl.pallas_call(
        body,
        out_shape=[jax.ShapeDtypeStruct(shape, kind) for shape, kind in outs]
        + [jax.ShapeDtypeStruct(array.shape, array.dtype) for array in through],
        in_specs=[spec for spec, _ in inputs] + [ANYWHERE] * extra,
        out_specs=[ANYWHERE] * (len(outs) + len(through)),
        input_output_aliases={
            count + len(after) + at: len(outs) + at for at in range(len(through))
        },
        scratch_shapes=[pltpu.VMEM(shape, kind) for shape, kind in scratch]
        + [pltpu.SemaphoreType.DMA((copies,))],
        compiler_params=pltpu.CompilerParams(vmem_limit_bytes=VMEM_LIMIT),
        cost_estimate=pl.CostEstimate(
            flops=int(COST * micros) + 1024, bytes_accessed=1024, transcendentals=0
        ),
        name=name,
    )(*[array for _, array in inputs], *given)


def pair_masks(dtype):
    lanes = lax.broadcasted_iota(jnp.int32, (1, 128), 1)
    low = jnp.where(lanes < HEAD_DIM, 1.0, 0.0)
    return low.astype(dtype), (1.0 - low).astype(dtype)


def stacked_pair(block, low, high):
    return jnp.concatenate([block * low, block * high], axis=0)


def joined_pair(stacked, group):
    lanes = lax.broadcasted_iota(jnp.int32, (1, 128), 1)
    return jnp.where(lanes < HEAD_DIM, stacked[:group], stacked[group:])


def pair_softmax(query_stack, key_block, valid):
    scores = mm_nt(key_block, query_stack) * HEAD_DIM ** (-0.5)
    scores = jnp.where(valid, scores, MASK_FILL)
    exponent = jnp.exp(scores - jnp.max(scores, axis=0, keepdims=True))
    return exponent * (1.0 / jnp.sum(exponent, axis=0, keepdims=True))


def valid_keys(info, first_len, group, slots):
    keys = lax.broadcasted_iota(jnp.int32, (group, 2 * group), 0)
    queries = lax.broadcasted_iota(jnp.int32, (group, 2 * group), 1)
    seqs = group // slots
    if seqs == 1:
        return keys < info[first_len]
    queries = jnp.where(queries >= group, queries - group, queries)
    valid = None
    for j in range(seqs):
        low = j * slots
        inside = (
            (queries >= low)
            & (queries < low + slots)
            & (keys >= low)
            & (keys < low + info[first_len + j])
        )
        valid = inside if valid is None else valid | inside
    return valid


def weight_shapes(tower):
    width, steps = tower.width, tower.wide // tower.width
    return [
        ((3, width, width), LOW),
        ((width, width), LOW),
        ((steps, width, width), LOW),
        ((steps, width, width), LOW),
    ]


def fetch_narrow(tower, flag, own, other, targets, moves, order=(0, 1, 2, 3)):
    width = tower.width
    got = {}
    for part in order:
        if part == 3:
            got[3] = moves.fetch_either(flag, own[1].at[0, tower.index], other[1], targets[1])
            continue
        cols = pl.ds(part * width, width)
        second = other[0].at[:, cols] if tower.shared else None
        got[part] = moves.fetch_either(
            flag, own[0].at[0, tower.index, :, cols], second, targets[0].at[part]
        )
    return got


def fetch_step(tower, flag, own, other, targets, moves, step, at):
    width = tower.width
    part = pl.ds(pl.multiple_of(at * width, width), width)
    up, down = (other[0].at[:, part], other[1].at[part]) if tower.shared else (None, None)
    return (
        moves.fetch_either(flag, own[1].at[0, tower.index, part], down, targets[1].at[step]),
        moves.fetch_either(flag, own[0].at[0, tower.index, :, part], up, targets[0].at[step]),
    )


def kept_scratch(tower):
    count, width, wide = tower.count, tower.width, tower.wide
    steps = wide // width
    return [
        ((count, width), LOW),
        ((count, 3 * width), LOW),
        ((count, width), LOW),
        ((count, width), LOW),
        ((steps, count, width), LOW),
        ((steps, count, width), LOW),
        ((count, width), LOW),
        ((count, width), LOW),
        ((2, count, 128), F32),
        ((width // 128, count, 2 * tower.group), LOW),
    ]


OUTPUT, LEFTS, PROJECTED, SLOPE, HAT1, HAT2, INVERSES, SOFT = range(8)


def kept_shapes(tower, inner):
    count, width, wide = tower.count, tower.width, tower.wide
    steps = wide // width
    return [
        ((count, width), LOW),
        ((count, 2 * width + wide + (width if inner else 0)), LOW),
        ((count, 3 * width), LOW),
        ((steps, count, width), LOW),
        ((count, width), LOW),
        ((count, width), LOW),
        ((2, count, 128), F32),
        ((width // 128, count, 2 * tower.group), LOW),
    ]


def forward_body(
    tower, layer, info, x_v, got, weights, smalls, acc_v, kept, outs, moves, first_out=None
):
    count, width, group = tower.count, tower.width, tower.group
    w_qkv, w_out, w_up, w_down = weights
    out_v, qkv_v, mix_v, low_v, act_v, slope_v, hat1_v, hat2_v, inv_v, soft_v = kept
    use_own = tower.use_own(info, layer)
    gains, bias = tower.small_rows(smalls, use_own)
    x = x_v[...]
    for part in range(3):
        got[part].wait()
        block = mm(x, w_qkv[part])
        if part == 0:
            block = block + bias[0:1, :]
        if part == 2:
            block = block + bias[1:2, :]
        qkv_v[:, part * width : (part + 1) * width] = block.astype(LOW)
    moves.store(qkv_v, outs[PROJECTED])
    low, high = pair_masks(LOW)
    for g in range(count // group):
        at = slice(g * group, (g + 1) * group)
        valid = valid_keys(
            info, tower.lengths_at(info) + g * (group // tower.slots), group, tower.slots
        )
        for pair in range(width // 128):
            lane = pair * 128
            q2 = qkv_v[at, lane : lane + 128]
            k2 = qkv_v[at, width + lane : width + lane + 128]
            v2 = qkv_v[at, 2 * width + lane : 2 * width + lane + 128]
            soft = pair_softmax(stacked_pair(q2, low, high), k2, valid).astype(LOW)
            soft_v[pair, at, :] = soft
            mix_v[at, lane : lane + 128] = joined_pair(mm_tn(soft, v2), group).astype(LOW)
    moves.store(soft_v, outs[SOFT])
    moves.store(mix_v, outs[LEFTS].at[:, pl.ds(0, width)])
    got[3].wait()
    summed = x.astype(F32) + (mm(mix_v[...], w_out[...]) + bias[2:3, :])
    hat, inverse = normed_rows(summed)
    hat1_v[...] = hat.astype(LOW)
    inv_v[0] = jnp.broadcast_to(inverse, (count, 128))
    moves.store(hat1_v, outs[HAT1])
    first = hat * gains[0:1, :] + bias[3:4, :]
    low_v[...] = first.astype(LOW)
    moves.store(low_v, outs[LEFTS].at[:, pl.ds(width, width)])
    acc_v[...] = first + bias[4:5, :]
    for step in range(tower.wide // width):
        for copy in got[4 + step]:
            copy.wait()
        hidden = mm(low_v[...], w_up[step]) + tower.hidden_bias(smalls, use_own, step, width)
        cdf = 0.5 * (1.0 + lax.erf(hidden * SQRT_HALF))
        act = (hidden * cdf).astype(LOW)
        act_v[step] = act
        slope_v[step] = (
            cdf + hidden * (jnp.exp(-0.5 * hidden * hidden) * ROOT_TAU_INV)
        ).astype(LOW)
        moves.store(act_v.at[step], outs[LEFTS].at[:, pl.ds((2 + step) * width, width)])
        moves.store(slope_v.at[step], outs[SLOPE].at[step])
        acc_v[...] += mm(act, w_down[step])
    hat, inverse = normed_rows(acc_v[...])
    hat2_v[...] = hat.astype(LOW)
    moves.store(hat2_v, outs[HAT2])
    inv_v[1] = jnp.broadcast_to(inverse, (count, 128))
    moves.store(inv_v, outs[INVERSES])
    output = hat * gains[1:2, :] + bias[5:6, :]
    out_v[...] = output.astype(LOW)
    moves.store(out_v, outs[OUTPUT])
    if first_out is not None:
        first_v, to, above = first_out
        firsts = [output[at * tower.slots : at * tower.slots + 1, :] for at in range(tower.seqs)]
        spare = jnp.zeros((16 - len(firsts) - sum(item.shape[0] for item in above), width), F32)
        first_v[...] = jnp.concatenate([*above, *firsts, spare], axis=0).astype(LOW)
        moves.store(first_v, to)


def forward_layers(tower, layers, rows, whole_rows, ahead, after=(), cost=0):
    count, width = tower.count, tower.width
    steps = tower.wide // width
    shapes = [kept_shapes(tower, at > 0) for at in range(len(layers))]
    kinds = len(shapes[0])
    held = kept_scratch(tower)

    def kernel(ins, outs, scratch, moves):
        info, x_any = ins[0], ins[1]
        own = ins[2:6]
        other = ins[6:10] if tower.shared else [None] * 4
        smalls = ins[10:] if tower.shared else ins[6:]
        above = []
        if ahead is not None:
            above = [smalls[-1][0 : ahead[1], :].astype(F32)]
            smalls = smalls[:-1]
        x_v, acc_v = scratch[:2]
        if whole_rows:
            x_any = x_any.at[pl.ds(tower.row_start(info), count)]
        x_got = moves.fetch(x_any, x_v)
        weights, got = [], []
        for at, layer in enumerate(layers):
            targets = scratch[2 + 4 * at : 6 + 4 * at]
            flag = tower.use_own(info, layer)
            arrivals = fetch_narrow(tower, flag, own[:2], other[:2], targets[:2], moves)
            for step in range(steps):
                arrivals[4 + step] = fetch_step(
                    tower, flag, own[2:], other[2:], targets[2:], moves, step, step
                )
            weights.append(targets)
            got.append(arrivals)
        x_got.wait()
        for at, layer in enumerate(layers):
            begin = 2 + 4 * len(layers) + len(held) * at
            kept = scratch[begin : begin + len(held)]
            forward_body(
                tower,
                layer,
                info,
                x_v,
                got[at],
                weights[at],
                smalls,
                acc_v,
                kept,
                outs[kinds * at : kinds * (at + 1)],
                moves,
                (scratch[-1], outs[-1], above) if at + 1 == len(layers) else None,
            )
            x_v = kept[0]
            if at + 1 < len(layers):
                inner = outs[kinds * (at + 1) + LEFTS]
                moves.store(x_v, inner.at[:, pl.ds(2 * width + tower.wide, width)])
        moves.drain()

    outs = [shape for layer_shapes in shapes for shape in layer_shapes] + [((16, width), LOW)]
    scratch = [((count, width), LOW), ((count, width), F32)] + weight_shapes(tower) * len(layers)
    inputs = [(SCALARS, tower.info), (ANYWHERE, rows)]
    inputs += [(ANYWHERE, array) for array in tower.given((0, 1, 2, 3))]
    inputs += [(INSIDE, array) for array in tower.given_small()]
    if ahead is not None:
        inputs.append((INSIDE, ahead[0]))
    results = call_kernel(
        kernel,
        "layer_forward",
        inputs,
        outs,
        scratch + held * len(layers) + outs[-1:],
        2 + len(layers) * (4 + 2 * steps + 9 + 2 * steps),
        cost,
        list(after),
    )
    return [results[kinds * at : kinds * (at + 1)] for at in range(len(layers))] + [results[-1]]


def place_rows(target, block, info, first, size, columns):
    for piece in range(block.shape[0] // size):
        at = pl.multiple_of(info[first + piece] * size, size)
        target[pl.ds(at, size), columns] = block[piece * size : (piece + 1) * size].astype(LOW)


def wide_scratch(tower, upstream):
    count, width = tower.count, tower.width
    steps = tower.wide // width
    return weight_shapes(tower)[2:] + [
        ((count, width), upstream.dtype),
        ((count, width), LOW),
        ((count, 128), F32),
        ((steps, count, width), LOW),
        ((count, width), F32),
        ((count, width), LOW),
        ((steps, count, width), LOW),
        ((8, width), F32),
    ]


def store_sides(source, side_width, outs, column, core_at, moves):
    for side, to in ((1 - core_at, outs[0]), (core_at, outs[1])):
        lanes = pl.ds(pl.multiple_of(side * side_width, 128), side_width)
        moves.store(source.at[:, lanes], to.at[:, pl.ds(column, side_width)])


def wide_tiles(tower, info):
    steps = tower.wide // tower.width
    if not tower.shared:
        return list(range(steps))
    return [lax.rem(step + (1 - info[CORE]) * (steps // 2), steps) for step in range(steps)]


def wide_fetch(tower, layer, info, ins, seeded, scratch, moves):
    up_any, own, other, slope_any, hat_any, inv_any = ins
    w_up, w_down, up_v, hat_v, inv_v, slope_v = scratch[:6]
    use_own = tower.use_own(info, layer)
    if seeded:
        up_any = up_any.at[pl.ds(tower.row_start(info), tower.count)]
    first_got = [
        moves.fetch(up_any, up_v),
        moves.fetch(hat_any, hat_v),
        moves.fetch(inv_any.at[1], inv_v),
    ]
    got = []
    for step, at in enumerate(wide_tiles(tower, info)):
        pieces = [moves.fetch(slope_any.at[at], slope_v.at[step])]
        pieces += fetch_step(tower, use_own, own, other, (w_up, w_down), moves, step, at)
        got.append(pieces)
    return first_got, got


def wide_body(tower, layer, info, fetched, first_ref, smalls, scratch, outs, moves):
    count, width = tower.count, tower.width
    steps = tower.wide // width
    w_up, w_down, up_v, hat_v, inv_v, slope_v, da_v, df_v, dh_v, vec_v = scratch
    use_own = tower.use_own(info, layer)
    core_at = info[CORE]
    first_got, got = fetched
    tiles = wide_tiles(tower, info)
    gains, _ = tower.small_rows(smalls, use_own)
    for copy in first_got:
        copy.wait()
    upward = up_v[...].astype(F32)
    if first_ref is not None:
        row_at = lax.broadcasted_iota(jnp.int32, (count, 1), 0)
        lengths = tower.lengths_at(info)
        first_seq = lengths - tower.first_len
        seen = jnp.zeros((count, 1), F32)
        for seq in range(tower.seqs):
            start = seq * tower.slots
            inside_seq = (row_at >= start) & (row_at < start + info[lengths + seq])
            seen = jnp.where(inside_seq, 1.0, seen)
        upward = upward * seen
        for seq in range(tower.seqs):
            upward = upward + jnp.where(
                row_at == seq * tower.slots, first_ref[pl.ds(first_seq + seq, 1), :], 0.0
            )
    hat = hat_v[...].astype(F32)
    vec_v[0:1, :] = col_sum(upward * hat)
    vec_v[1:2, :] = col_sum(upward)
    d_second = norm_pull(upward, hat, inv_v[:, 0:1], gains[1:2, :])
    d_low = d_second.astype(LOW)
    df_v[...] = d_low
    vec_v[2:3, :] = col_sum(d_low.astype(F32))
    vec_v[7:8, :] = jnp.zeros((1, width), F32)
    da_v[...] = d_second
    vec_out, df_out, dh_out = outs
    if tower.shared:
        store_sides(df_v, width // 2, df_out, 0, core_at, moves)
    else:
        moves.store(df_v, df_out[0])
    for step, at in enumerate(tiles):
        for copy in got[step]:
            copy.wait()
        d_hidden = (mm_nt(df_v[...], w_down[step]) * slope_v[step].astype(F32)).astype(LOW)
        vec_v[pl.ds(3 + at, 1), :] = col_sum(d_hidden.astype(F32))
        dh_v[step] = d_hidden
        da_v[...] += mm_nt(d_hidden, w_up[step])
        if tower.shared:
            side, place = divmod(step, steps // 2)
            moves.store(dh_v.at[step], dh_out[side].at[:, pl.ds(place * width, width)])
        else:
            moves.store(dh_v.at[step], dh_out[0].at[step])
    moves.store(vec_v, vec_out)


def narrow_scratch(tower, out_type):
    count, width = tower.count, tower.width
    return weight_shapes(tower)[:2] + [
        ((count, width), LOW),
        ((count, 128), F32),
        ((count, 3 * width), LOW),
        ((width // 128, count, 2 * tower.group), LOW),
        ((count, width), LOW),
        ((count, 3 * width), LOW),
        ((count, width), LOW),
        ((count, width), F32),
        ((count, width), out_type),
        ((8, width), F32),
    ]


def narrow_fetch(tower, layer, info, ins, scratch, moves):
    own, other, qkv_any, hat_any, inv_any, soft_any = ins
    w_qkv, w_out, hat_v, inv_v, qkv_v, soft_v = scratch[:6]
    use_own = tower.use_own(info, layer)
    got = {"hat": [moves.fetch(hat_any, hat_v), moves.fetch(inv_any.at[0], inv_v)]}
    weights = fetch_narrow(tower, use_own, own, other, (w_qkv, w_out), moves, (3,))
    got["heads"] = [moves.fetch(qkv_any, qkv_v), moves.fetch(soft_any, soft_v)]
    weights.update(fetch_narrow(tower, use_own, own, other, (w_qkv, w_out), moves, (0, 1, 2)))
    got["weights"] = weights
    return got


def narrow_body(tower, layer, info, got, da_v, smalls, scratch, outs, moves):
    count, width, group = tower.count, tower.width, tower.group
    w_qkv, w_out, hat_v, inv_v, qkv_v, soft_v, dz_v, dp_v, dmix_v, du_v, dx_v, vec_v = scratch
    use_own = tower.use_own(info, layer)
    core_at = info[CORE]
    dx_out, vec_out, dz_out, dp_out = outs
    gains, _ = tower.small_rows(smalls, use_own)
    for copy in got["hat"]:
        copy.wait()
    upward = da_v[...]
    hat = hat_v[...].astype(F32)
    vec_v[0:1, :] = col_sum(upward * hat)
    vec_v[1:2, :] = col_sum(upward)
    d_summed = norm_pull(upward, hat, inv_v[:, 0:1], gains[0:1, :])
    du_v[...] = d_summed
    d_low = d_summed.astype(LOW)
    dz_v[...] = d_low
    vec_v[2:3, :] = col_sum(d_low.astype(F32))
    vec_v[5:8, :] = jnp.zeros((3, width), F32)
    if tower.shared:
        store_sides(dz_v, width // 2, dz_out, 2 * width, core_at, moves)
    else:
        moves.store(dz_v, dz_out[0])
    got["weights"][3].wait()
    dmix_v[...] = mm_nt(d_low, w_out[...]).astype(LOW)
    for copy in got["heads"]:
        copy.wait()
    low, high = pair_masks(LOW)
    scale = HEAD_DIM ** (-0.5)
    for g in range(count // group):
        at = slice(g * group, (g + 1) * group)
        for pair in range(width // 128):
            lane = pair * 128
            q2 = qkv_v[at, lane : lane + 128]
            k2 = qkv_v[at, width + lane : width + lane + 128]
            v2 = qkv_v[at, 2 * width + lane : 2 * width + lane + 128]
            soft = soft_v[pair, at, :]
            d_stack = stacked_pair(dmix_v[at, lane : lane + 128], low, high)
            d_soft = mm_nt(v2, d_stack)
            soft_wide = soft.astype(F32)
            total = jnp.sum(d_soft * soft_wide, axis=0, keepdims=True)
            d_scores = (soft_wide * (d_soft - total)).astype(LOW)
            dp_v[at, lane : lane + 128] = (
                joined_pair(mm_tn(d_scores, k2), group) * scale
            ).astype(LOW)
            dp_v[at, width + lane : width + lane + 128] = (
                mm(d_scores, stacked_pair(q2, low, high)) * scale
            ).astype(LOW)
            dp_v[at, 2 * width + lane : 2 * width + lane + 128] = mm(soft, d_stack).astype(LOW)
    vec_v[3:4, :] = col_sum(dp_v[:, :width].astype(F32))
    vec_v[4:5, :] = col_sum(dp_v[:, 2 * width :].astype(F32))
    moves.store(vec_v, vec_out)
    if tower.shared:
        store_sides(dp_v, 3 * width // 2, dp_out, width // 2, core_at, moves)
    else:
        moves.store(dp_v, dp_out[0])
    d_input = du_v[...]
    for part in range(3):
        got["weights"][part].wait()
        d_input = d_input + mm_nt(dp_v[:, part * width : (part + 1) * width], w_qkv[part])
    dx_v[...] = d_input.astype(dx_v.dtype)
    moves.store(dx_v, dx_out)


def backward_layer(
    tower, layer, upstream, first_rows, kept, low_out, after=(), cost=0, through=()
):
    count, width, wide = tower.count, tower.width, tower.wide
    steps = wide // width
    seeded = first_rows is not None
    out_type = LOW if low_out else F32
    wide_shapes = wide_scratch(tower, upstream)

    def kernel(ins, outs, scratch, moves):
        ins = list(ins)
        info, up_any = ins.pop(0), ins.pop(0)
        first_ref = ins.pop(0) if seeded else None
        own = [ins.pop(0) for _ in range(4)]
        other = [ins.pop(0) for _ in range(4)] if tower.shared else [None] * 4
        slope_any, hat2_any, inv_any, qkv_any, hat1_any, soft_any = (
            ins.pop(0) for _ in range(6)
        )
        first, second = scratch[: len(wide_shapes)], scratch[len(wide_shapes) :]
        dx, vec1, vec2 = outs[:3]
        if tower.shared:
            dh, df = outs[3:5], outs[5:7]
            dz = dp = df
        else:
            df, dh, dz, dp = (outs[at : at + 1] for at in range(3, 7))
        given = (up_any, own[2:], other[2:], slope_any, hat2_any, inv_any)
        wide_got = wide_fetch(tower, layer, info, given, seeded, first, moves)
        given = (own[:2], other[:2], qkv_any, hat1_any, inv_any, soft_any)
        got = narrow_fetch(tower, layer, info, given, second, moves)
        wide_body(
            tower, layer, info, wide_got, first_ref, ins, first, (vec1, df, dh), moves
        )
        narrow_body(
            tower, layer, info, got, first[6], ins, second, (dx, vec2, dz, dp), moves
        )
        moves.drain()

    outs = [((count, width), out_type), ((8, width), F32), ((8, width), F32)]
    if tower.shared:
        outs += [((count, wide // 2), LOW)] * 2 + [((count, 5 * width // 2), LOW)] * 2
    else:
        outs += [((count, width), LOW), ((steps, count, width), LOW)]
        outs += [((count, width), LOW), ((count, 3 * width), LOW)]
    inputs = [(SCALARS, tower.info), (ANYWHERE, upstream)]
    if seeded:
        inputs.append((INSIDE, first_rows))
    inputs += [(ANYWHERE, array) for array in tower.given((0, 1, 2, 3))]
    inputs += [(ANYWHERE, kept[at]) for at in (SLOPE, HAT2, INVERSES, PROJECTED, HAT1, SOFT)]
    inputs += [(INSIDE, array) for array in tower.given_small()]
    return call_kernel(
        kernel,
        "backward_layer",
        inputs,
        outs,
        wide_shapes + narrow_scratch(tower, out_type),
        3 + 3 * steps + 8 + 3 + steps + 6,
        cost,
        list(after),
        through,
    )


def place_rows(target, block, info, first, size, columns):
    for piece in range(block.shape[0] // size):
        at = pl.multiple_of(info[first + piece] * size, size)
        target[pl.ds(at, size), columns] = block[piece * size : (piece + 1) * size].astype(LOW)


def passage_products(
    tower, layer, rows, lefts, other_lefts, rights, other_rights, vectors, after=(), cost=0
):
    count, width, wide = tower.count, tower.width, tower.wide
    steps = wide // width
    half = width // 2
    piece = width // BLOCKS
    layout = LAYOUTS[layer]
    chunks = 1 + max(chunk for chunk, _ in layout)
    widths = [
        max(column + (wide // 2 if at < 2 else width) for at, (to, column) in enumerate(layout) if to == chunk)
        for chunk in range(chunks)
    ]
    vector_column = widths[0]
    if vectors:
        widths[0] += 128
    whole = rows is not None

    def kernel(ins, outs, scratch, moves):
        ins = list(ins)
        info = ins.pop(0)
        x_any = ins.pop(0) if whole else None
        vector_refs = [ins.pop() for _ in vectors]
        left, other_left = ins[:2]
        hidden_of, rights_of = (ins[2], ins[4]), (ins[3], ins[5])
        low_v, dh_v, act_v, df_v, x_v, dp_v, mix_v, dz_v = scratch[:8]
        grads = scratch[8:]
        above, below = pl.ds(0, count), pl.ds(count, count)

        def both(sources, column, target):
            columns = pl.ds(column, target.shape[1])
            return [
                moves.fetch(sources[0].at[:, columns], target.at[above]),
                moves.fetch(sources[1].at[:, columns], target.at[below]),
            ]

        lefts_of = (left, other_left)
        got_low = both(lefts_of, width, low_v)
        got_dh = [both(hidden_of, at * width, dh_v.at[at]) for at in range(steps // 2)]
        got_df = both(rights_of, 0, df_v)
        got_act = [both(lefts_of, (2 + at) * width, act_v.at[at]) for at in range(steps)]
        if whole:
            start = tower.row_start(info)
            other_start = pl.multiple_of(count - start, count)
            got_x = [
                moves.fetch(x_any.at[pl.ds(start, count)], x_v.at[above]),
                moves.fetch(x_any.at[pl.ds(other_start, count)], x_v.at[below]),
            ]
        else:
            got_x = both(lefts_of, 2 * width + wide, x_v)
        got_x += both(rights_of, half, dp_v)
        got_mix = both(lefts_of, 0, mix_v) + both(rights_of, 2 * width, dz_v)

        def ready(copies):
            for copy in copies:
                copy.wait()

        def target(part):
            chunk, column = layout[part]
            return grads[chunk], column, PLACES + BLOCKS * (3 * layer + chunk)

        def send(part):
            source, column, _ = target(part)
            cut = source.shape[0] // 2
            columns = pl.ds(column, wide // 2 if part < 2 else width)
            to = 2 * layout[part][0]
            moves.store(source.at[pl.ds(cut, cut), columns], outs[to].at[:, columns])
            moves.store(source.at[pl.ds(0, cut), columns], outs[to + 1].at[:, columns])

        if vectors:
            lane = slice(vector_column, vector_column + 128)
            for block in range(BLOCKS):
                from_rows = slice(block * PIECE_ROWS, (block + 1) * PIECE_ROWS)
                begin = block * piece
                grads[0][begin : begin + PIECE_ROWS, lane] = (
                    vector_refs[0][from_rows, :] + vector_refs[1][from_rows, :]
                ).astype(LOW)
                grads[0][begin + PIECE_ROWS : begin + piece, lane] = jnp.zeros(
                    (piece - PIECE_ROWS, 128), LOW
                )
            cut = width // 2
            columns = pl.ds(vector_column, 128)
            moves.store(grads[0].at[pl.ds(cut, cut), columns], outs[0].at[:, columns])
            moves.store(grads[0].at[pl.ds(0, cut), columns], outs[1].at[:, columns])
        ready(got_low)
        for at in range(steps // 2):
            ready(got_dh[at])
            to, column, first = target(1)
            columns = slice(column + at * width, column + (at + 1) * width)
            place_rows(to, mm_tn(low_v[...], dh_v[at]), info, first, piece, columns)
        send(1)
        ready(got_df)
        parts = wide // width
        for at in range(steps):
            ready(got_act[at])
            product = mm_tn(act_v[at], df_v[...])
            for block in range(width // piece):
                index, part = divmod(at * (width // piece) + block, parts)
                to, column, first = target(0)
                rows_to = pl.ds(pl.multiple_of(info[first + index] * piece, piece), piece)
                column += part * half
                to[rows_to, column : column + half] = product[
                    block * piece : (block + 1) * piece
                ].astype(LOW)
        send(0)
        ready(got_x)
        for part in range(4):
            if part == 3:
                ready(got_mix)
                product = mm_tn(mix_v[...], dz_v[...])
            else:
                product = mm_tn(x_v[...], dp_v[:, part * half : (part + 1) * half])
            to, column, first = target(2 + part // 2)
            column += part % 2 * half
            place_rows(to, product, info, first, piece, slice(column, column + half))
            if part % 2:
                send(2 + part // 2)
        moves.drain()

    outs = [((half, columns), LOW) for columns in widths for _ in range(2)]
    scratch = [
        ((2 * count, width), LOW),
        ((steps // 2, 2 * count, width), LOW),
        ((steps, 2 * count, width), LOW),
        ((2 * count, half), LOW),
        ((2 * count, width), LOW),
        ((2 * count, 3 * half), LOW),
        ((2 * count, width), LOW),
        ((2 * count, half), LOW),
    ] + [((width, columns), LOW) for columns in widths]
    arrays = [rows] if whole else []
    arrays += [lefts, other_lefts, *rights, *other_rights]
    inputs = [(SCALARS, tower.info)] + [(ANYWHERE, array) for array in arrays]
    inputs += [(INSIDE, array) for array in vectors]
    return call_kernel(
        kernel,
        "passage_products",
        inputs,
        outs,
        scratch,
        2 * (1 + steps // 2 + 1 + steps + 4) + 10,
        cost,
        list(after),
    )


def block_chooser(rows, columns, valid, size, bit):
    at = lax.broadcasted_iota(jnp.int32, (1, columns), 1)
    piece = jnp.floor((at.astype(F32) + 0.5) * (1.0 / size)).astype(jnp.int32)
    wanted = jnp.where(at < valid, at + (piece + bit) * size, -1)
    row_at = lax.broadcasted_iota(jnp.int32, (rows, columns), 0)
    return jnp.where(row_at == wanted, 1.0, 0.0).astype(LOW)


def pack_first(info, early, late, after=(), cost=0):
    count, width = early[0].shape
    steps = early[2].shape[0]
    wide = steps * width
    half = width // 2
    piece = width // BLOCKS
    keeps = (half + 3 * half, 2 * wide // 2)
    wholes = (2 * width, 2 * width)

    def kernel(ins, outs, scratch, moves):
        info_ref = ins[0]
        first, second = ins[1:7], ins[7:13]
        x_v, left_v, dh_v, df_v, dz_v, dp_v = scratch[:6]
        results = scratch[6:]
        flag = info_ref[IS_FIRST] == 1
        got = [moves.fetch_either(flag, a, b, to) for a, b, to in zip(first, second, scratch)]
        bits = [(info_ref[at], 1 - info_ref[at]) for at in (X_BIT, Y_BIT)]
        for copy in got:
            copy.wait()

        def lanes(bit, size):
            return pl.ds(pl.multiple_of(bit * size, 128), size)

        for which in range(2):
            first_to, second_to = results[which], results[2 + which]
            bit = bits[0][which]
            choose = block_chooser(width, half, half, piece, bit)
            first_to[:, :half] = mm(left_v[:, :width], choose).astype(LOW)
            first_to[:, half : 4 * half] = dp_v[:, lanes(bit, 3 * half)]
            bit = bits[1][which]
            for step in range(steps):
                start = (2 + step) * width + bit * half
                second_to[:, step * half : (step + 1) * half] = left_v[
                    :, pl.ds(pl.multiple_of(start, 128), half)
                ]
            for step in range(steps // 2):
                begin = wide // 2 + step * width
                second_to[:, begin : begin + width] = dh_v[bit * (steps // 2) + step]
        results[1][:, keeps[0] : keeps[0] + width] = x_v[...]
        results[1][:, keeps[0] + width :] = dz_v[...]
        results[3][:, keeps[1] : keeps[1] + width] = left_v[:, width : 2 * width]
        results[3][:, keeps[1] + width :] = df_v[...]
        for at in range(4):
            moves.store(results[at], outs[at])
        moves.drain()

    outs = []
    for keep, rest in zip(keeps, wholes):
        outs += [((count, keep), LOW), ((count, keep + rest), LOW)]
    inputs = [(SCALARS, info)] + [(ANYWHERE, array) for array in tuple(early) + tuple(late)]
    scratch = [(array.shape, LOW) for array in early]
    return call_kernel(
        kernel, "pack_first", inputs, outs, scratch + outs, 12, cost, list(after)
    )


def pack_second(info, keeps, sends, arrivals, width, after=(), cost=0):
    count = keeps[0].shape[0]
    wide = keeps[1].shape[1]
    half, quarter, third = width // 2, width // 4, 256
    piece = width // BLOCKS
    chosen = (third + half, half + wide // 4)
    wholes = (3 * half + width, wide // 2 + width)

    def kernel(ins, outs, scratch, moves):
        info_ref = ins[0]
        got = [moves.fetch(source, to) for source, to in zip(ins[1:], scratch)]
        bits = [(info_ref[at], 1 - info_ref[at]) for at in (Y_BIT, X_BIT)]
        for copy in got:
            copy.wait()
        for lot in range(2):
            keep_v, send_v, arrived_v = scratch[lot], scratch[2 + lot], scratch[4 + lot]
            cut = keep_v.shape[1]
            sources = (
                (slice(0, count), keep_v, send_v),
                (slice(count, 2 * count), arrived_v, arrived_v),
            )
            for which in range(2):
                target = scratch[6 + 2 * lot + which]
                bit = bits[lot][which]
                if lot == 0:
                    narrow = block_chooser(half, third, quarter, piece, bit)
                    broad = block_chooser(width, half, half, 2 * piece, bit)
                else:
                    narrow = block_chooser(width, half, half, piece, bit)
                    broad = block_chooser(2 * half, half, half, quarter, bit)
                for rows, halved, whole in sources:
                    if lot == 0:
                        target[rows, :third] = mm(halved[:, :half], narrow).astype(LOW)
                        target[rows, third:chosen[0]] = mm(
                            whole[:, cut : cut + width], broad
                        ).astype(LOW)
                        continue
                    target[rows, :half] = mm(whole[:, cut : cut + width], narrow).astype(LOW)
                    for part in range(wide // 2 // width):
                        target[rows, half + part * half : half + (part + 1) * half] = mm(
                            halved[:, part * width : (part + 1) * width], broad
                        ).astype(LOW)
            target = scratch[6 + 2 * lot + 1]
            begin = chosen[lot]
            first = half if lot == 0 else wide // 2
            for rows, halved, whole in sources:
                target[rows, begin : begin + cut - first] = halved[:, first:cut]
                target[rows, begin + cut - first :] = whole[:, cut + width :]
        for at in range(4):
            moves.store(scratch[6 + at], outs[at])
        moves.drain()

    outs = []
    for left, right in zip(chosen, wholes):
        outs += [((2 * count, left), LOW), ((2 * count, left + right), LOW)]
    arrays = tuple(keeps) + tuple(sends) + tuple(arrivals)
    inputs = [(SCALARS, info)] + [(ANYWHERE, array) for array in arrays]
    scratch = [(array.shape, LOW) for array in arrays]
    return call_kernel(
        kernel, "pack_second", inputs, outs, scratch + outs, 10, cost, list(after)
    )


def query_products(info, keeps, sends, arrivals, width, wide, after=(), cost=0):
    count = keeps[0].shape[0]
    half, third = width // 2, 256
    piece = width // BLOCKS
    packed = [keep.shape[1] for keep in keeps]
    rights = [send.shape[1] - left for send, left in zip(sends, packed)]
    columns = 4 * width + 2 * wide

    def kernel(ins, outs, scratch, moves):
        info_ref = ins[0]
        keep_any, send_any, arrived_any = ins[1:3], ins[3:5], ins[5:7]
        left_v, right_v, result = scratch[0:2], scratch[2:4], scratch[4]
        got = []
        for lot in range(2):
            cut = packed[lot]
            below = pl.ds(count, count)
            got.append(
                [
                    moves.fetch(keep_any[lot], left_v[lot].at[pl.ds(0, count)]),
                    moves.fetch(arrived_any[lot].at[:, pl.ds(0, cut)], left_v[lot].at[below]),
                    moves.fetch(
                        send_any[lot].at[:, pl.ds(cut, rights[lot])],
                        right_v[lot].at[pl.ds(0, count)],
                    ),
                    moves.fetch(
                        arrived_any[lot].at[:, pl.ds(cut, rights[lot])], right_v[lot].at[below]
                    ),
                ]
            )

        def place(z, rows, column):
            row = pl.multiple_of(info_ref[Z_PLACES + z] * piece, piece)
            result[pl.ds(row, piece), column : column + rows.shape[1]] = rows.astype(LOW)

        for copy in got[0]:
            copy.wait()
        for part in range(3):
            product = mm_tn(
                left_v[0][:, third:], right_v[0][:, part * half : (part + 1) * half]
            )
            for block in range(8):
                z, bit = divmod(block, 2)
                place(
                    z,
                    product[block * piece : (block + 1) * piece],
                    bit * 3 * half + part * half,
                )
        product = mm_tn(left_v[0][:, :third], right_v[0][:, 3 * half :])
        for z in range(4):
            place(z, product[z * piece : (z + 1) * piece], 3 * width)
        for copy in got[1]:
            copy.wait()
        at = 4 * width
        for part in range(wide // 2 // width):
            product = mm_tn(
                left_v[1][:, :half], right_v[1][:, part * width : (part + 1) * width]
            )
            for block in range(8):
                z, bit = divmod(block, 2)
                place(
                    z,
                    product[block * piece : (block + 1) * piece],
                    at + bit * (wide // 2) + part * width,
                )
        at += wide
        product = mm_tn(left_v[1][:, half:], right_v[1][:, wide // 2 :])
        per = wide // width
        for z in range(4):
            for part in range(per):
                begin = (z * per + part) * piece
                place(z, product[begin : begin + piece], at + part * width)
        moves.store(result.at[pl.ds(2 * piece, 2 * piece)], outs[0])
        moves.store(result.at[pl.ds(0, 2 * piece)], outs[1])
        moves.drain()

    outs = [((2 * piece, columns), LOW)] * 2
    arrays = tuple(keeps) + tuple(sends) + tuple(arrivals)
    inputs = [(SCALARS, info)] + [(ANYWHERE, array) for array in arrays]
    scratch = [((2 * count, cut), LOW) for cut in packed]
    scratch += [((2 * count, cut), LOW) for cut in rights]
    scratch += [((4 * piece, columns), LOW)]
    return call_kernel(
        kernel, "query_products", inputs, outs, scratch, 10, cost, list(after)
    )


PIECE_ROWS = 32


def vector_pieces(info, first, parts, wide, after=(), cost=0):
    width = parts[0].shape[1]
    cut = width // BLOCKS
    big = wide // BLOCKS

    def kernel(ins, outs, scratch, moves):
        info_ref = ins[0]
        refs = ins[1:]
        early = info_ref[IS_FIRST] == 1
        for target in scratch:
            target[...] = jnp.zeros_like(target)

        def lay(target, tower_at, wide_rows, narrow_rows):
            eight = jnp.concatenate([wide_rows[0:3], narrow_rows[0:5]], axis=0)
            for block in range(BLOCKS):
                at = info_ref[PLACES + first + block] * PIECE_ROWS + 16 * tower_at
                at = pl.multiple_of(at, 16)
                target[pl.ds(at, 8), 0:cut] = eight[:, block * cut : (block + 1) * cut]
                row, column = divmod(block * big, width)
                bias = wide_rows[3 + row : 4 + row, column : column + big]
                target[pl.ds(at + 8, 1), 0:128] = bias[:, 0:128]
                target[pl.ds(at + 9, 1), 0 : big - 128] = bias[:, 128:big]

        send, keep = scratch
        eq1, eq2, lq1, lq2, ep1, ep2, lp1, lp2 = (ref[...] for ref in refs)
        lay(keep, 0, jnp.where(early, eq1, lq1), jnp.where(early, eq2, lq2))
        lay(keep, 1, jnp.where(early, ep1, lp1), jnp.where(early, ep2, lp2))
        lay(send, 1, jnp.where(early, lp1, ep1), jnp.where(early, lp2, ep2))
        moves.store(send, outs[0])
        moves.store(keep, outs[1])
        moves.drain()

    outs = [((BLOCKS * PIECE_ROWS, 128), F32)] * 2
    inputs = [(SCALARS, info)] + [(INSIDE, array) for array in parts]
    return call_kernel(kernel, "vector_pieces", inputs, outs, outs, 2, cost, list(after))


def take_in(items, after=(), cost=0, through=()):
    def kernel(ins, outs, scratch, moves):
        ins, scratch = list(ins), list(scratch)
        taken = []
        for pairs, last in items:
            got = []
            for _ in pairs:
                held = [scratch.pop(0), scratch.pop(0)]
                got.append((held, [moves.fetch(ins.pop(0), to) for to in held]))
            taken.append((got, [scratch.pop(0) for _ in range(1 if last else 2)]))
        out_at = 0
        for (got, results), (_, last) in zip(taken, items):
            for held, copies in got:
                for copy in copies:
                    copy.wait()
            for which, result in enumerate(results):
                part_rows = result.shape[0]
                start = 0 if last else (1 - which) * part_rows
                column = 0
                for (keep_v, arrived_v), _ in got:
                    columns = keep_v.shape[1]
                    chunk = 48 if columns <= 1536 and part_rows % 48 == 0 else 16

                    def one(step, carry, keep_v=keep_v, arrived_v=arrived_v, column=column):
                        to = pl.ds(pl.multiple_of(step * chunk, 16), chunk)
                        of = pl.ds(pl.multiple_of(start + step * chunk, 16), chunk)
                        total = keep_v[of, :].astype(F32) + arrived_v[of, :].astype(F32)
                        result[to, column : column + keep_v.shape[1]] = total.astype(result.dtype)
                        return carry

                    lax.fori_loop(0, part_rows // chunk, one, 0)
                    column += columns
                moves.store(result, outs[out_at])
                out_at += 1
        moves.drain()

    outs, scratch = [], []
    for pairs, last in items:
        rows = pairs[0][0].shape[0]
        columns = sum(keep.shape[1] for keep, _ in pairs)
        kind = pairs[0][0].dtype
        mine = [((rows, columns), F32)] if last else [((rows // 2, columns), kind)] * 2
        outs += mine
        for keep, arrived in pairs:
            scratch += [(keep.shape, kind), (arrived.shape, kind)]
        scratch += mine
    inputs = [(ANYWHERE, array) for pairs, _ in items for pair in pairs for array in pair]
    return call_kernel(
        kernel, "take_in", inputs, outs, scratch, len(inputs) + len(outs), cost, list(after), through
    )


def take_in_quarters(pairs, after=(), cost=0):
    rows = pairs[0][0].shape[0] // 4
    columns = sum(keep.shape[1] for keep, _ in pairs)

    def kernel(ins, outs, scratch, moves):
        held = scratch[: len(ins)]
        results = scratch[len(ins) :]
        got = [moves.fetch(source, to) for source, to in zip(ins, held)]
        for copy in got:
            copy.wait()
        for quarter in (1, 2, 3, 0):
            result = results[quarter]
            column = 0
            for at in range(len(pairs)):
                keep_v, arrived_v = held[2 * at : 2 * at + 2]
                wide = keep_v.shape[1]

                def one(step, carry, keep_v=keep_v, arrived_v=arrived_v, column=column, wide=wide):
                    to = pl.ds(pl.multiple_of(step * 16, 16), 16)
                    of = pl.ds(pl.multiple_of(quarter * rows + step * 16, 16), 16)
                    total = keep_v[of, :].astype(F32) + arrived_v[of, :].astype(F32)
                    result[to, column : column + wide] = total.astype(LOW)
                    return carry

                lax.fori_loop(0, rows // 16, one, 0)
                column += wide
            moves.store(result, outs[quarter])
        moves.drain()

    outs = [((rows, columns), LOW)] * 4
    arrays = [array for pair in pairs for array in pair]
    inputs = [(ANYWHERE, array) for array in arrays]
    scratch = [(array.shape, LOW) for array in arrays]
    return call_kernel(
        kernel, "take_in_quarters", inputs, outs, scratch + outs, len(arrays) + 4, cost, list(after)
    )


class Chain:
    def __init__(self, send, keep, order, scale, from_core=False):
        self.order = list(order)
        self.scale = scale
        self.keep = keep
        self.total = None
        self.arrived = core_swap(send) if from_core else self.swap(send)

    def swap(self, block):
        return flip_swap(block, self.order.pop(0) * self.scale)


def play_round(groups, after=(), cost=0, through=()):
    items = [
        ([(chain.keep, chain.arrived) for chain in group], not group[0].order) for group in groups
    ]
    results = list(take_in(items, after, cost, through))
    seen = []
    for group in groups:
        chain = group[0]
        assert all(other.order == chain.order for other in group)
        if not chain.order:
            chain.total = results.pop(0)
            seen.append(chain.total)
            continue
        sent, chain.keep = results.pop(0), results.pop(0)
        chain.arrived = chain.swap(sent)
        seen.append(sent)
    return tuple(seen + results)


def last_round(info, quarters, other_total, vector_column, after=(), cost=0):
    rows, columns = other_total.shape
    begin = vector_column

    def kernel(ins, outs, scratch, moves):
        info_ref = ins[0]
        parts, late_v = scratch[:4], scratch[4]
        own_v, send_v, vec_v = scratch[5:]
        got = [moves.fetch(source, to) for source, to in zip(ins[1:], scratch)]
        for copy in got:
            copy.wait()
        flag = info_ref[IS_FIRST] == 1

        def total(part, lanes):
            values = [ref[part, lanes].astype(F32) for ref in parts]
            return (values[0] + values[1]) + (values[2] + values[3])

        vec_v[...] = total(slice(0, rows), slice(begin, begin + 128))
        moves.store(vec_v, outs[2])
        for row in range(0, rows, 16):
            part = slice(row, row + 16)
            for lanes, of in (
                (slice(0, begin), slice(0, begin)),
                (slice(begin, columns), slice(begin + 128, columns + 128)),
            ):
                early = total(part, of)
                late = late_v[part, lanes]
                send_v[part, lanes] = jnp.where(flag, late, early).astype(LOW)
                own_v[part, lanes] = jnp.where(flag, early, late)
        moves.store(send_v, outs[1])
        moves.store(own_v, outs[0])
        moves.drain()

    outs = [((rows, columns), F32), ((rows, columns), LOW), ((rows, 128), F32)]
    arrays = (*quarters, other_total)
    inputs = [(SCALARS, info)] + [(ANYWHERE, array) for array in arrays]
    scratch = [(array.shape, array.dtype) for array in arrays]
    return call_kernel(
        kernel, "last_round", inputs, outs, scratch + outs, 8, cost, list(after)
    )


def output_shapes(rows, width, wide):
    return [
        ((2, rows, 3 * width), F32),
        ((2, rows, width), F32),
        ((2, rows, wide), F32),
        ((2, wide // width * rows, width), F32),
    ]


def query_outputs(info, query, query_x, query_y, width, wide, after=(), cost=0):
    rows = query.shape[0]
    half = width // 2
    parts = wide // width

    def kernel(ins, outs, scratch, moves):
        info_ref = ins[0]
        sources, results = scratch[:3], scratch[3:]
        got = [moves.fetch(source, to) for source, to in zip(ins[1:], sources)]
        query_v, x_v, y_v = sources
        g_qkv, g_out, g_up, g_down = results
        for copy in got:
            copy.wait()
        at = 4 * width
        for bit_at, begin, size, arrived, target in (
            (X_BIT, 0, 3 * half, x_v, g_qkv),
            (Y_BIT, at, wide // 2, y_v, g_up),
        ):
            bit = info_ref[bit_at]
            mine = pl.ds(pl.multiple_of(bit * size, 128), size)
            others = pl.ds(pl.multiple_of((1 - bit) * size, 128), size)
            target[:, mine] = query_v[:, pl.ds(pl.multiple_of(begin + bit * size, 128), size)]
            target[:, others] = arrived[...]
        g_out[...] = query_v[:, 3 * width : 4 * width]
        at += wide
        for part in range(parts):
            g_down[part * rows : (part + 1) * rows, :] = query_v[
                :, at + part * width : at + (part + 1) * width
            ]
        for result, to in zip(results, outs):
            moves.store(result, to.at[0])
        moves.drain()

    outs = output_shapes(rows, width, wide)
    arrays = (query, query_x, query_y)
    inputs = [(SCALARS, info)] + [(ANYWHERE, array) for array in arrays]
    scratch = [(array.shape, F32) for array in arrays] + [(shape[1:], F32) for shape, _ in outs]
    return call_kernel(
        kernel, "query_outputs", inputs, outs, scratch, 7, cost, list(after)
    )


def passage_outputs(info, own, other, outputs, width, wide):
    rows, columns = own.shape
    half = width // 2
    parts = wide // width
    chunk_width = columns // 2
    begin = [to * chunk_width + column for to, column in LAYOUTS[0]]

    def kernel(ins, outs, scratch, moves):
        info_ref = ins[0]
        sources, results = scratch[:2], scratch[2:]
        got = [moves.fetch(source, to) for source, to in zip(ins[1:], sources)]
        g_qkv, g_out, g_up, g_down = results
        core = info_ref[CORE]
        for at, side in ((0, core), (1, 1 - core)):
            got[at].wait()
            source = sources[at]
            here = pl.ds(pl.multiple_of(side * half, 128), half)
            for part in range(parts):
                g_down[part * rows : (part + 1) * rows, here] = source[
                    :, begin[0] + part * half : begin[0] + (part + 1) * half
                ].astype(F32)
            up = pl.ds(pl.multiple_of(side * (wide // 2), 128), wide // 2)
            g_up[:, up] = source[:, begin[1] : begin[1] + wide // 2].astype(F32)
            for third in range(3):
                column = begin[2 + third // 2] + third % 2 * half
                to = pl.ds(pl.multiple_of(side * 3 * half + third * half, 128), half)
                g_qkv[:, to] = source[:, column : column + half].astype(F32)
            g_out[:, here] = source[:, begin[3] + half : begin[3] + width].astype(F32)
        for result, to in zip(results, outs):
            moves.store(result, to.at[1])
        moves.drain()

    shapes = output_shapes(rows, width, wide)
    arrays = (own, other)
    inputs = [(SCALARS, info)] + [(ANYWHERE, array) for array in arrays]
    scratch = [(array.shape, array.dtype) for array in arrays]
    scratch += [(shape[1:], F32) for shape, _ in shapes]
    return call_kernel(
        kernel, "passage_outputs", inputs, [], scratch, 6, 0, [], tuple(outputs)
    )


def pick_bit(grid, axis, index):
    return lax.dynamic_index_in_dim(grid, index, axis, keepdims=False)


def own_bit(bit):
    return (lax.axis_index("batch") // bit) % 2


def scatter_sum(grid, bits, left):
    left = list(left)
    for bit in bits:
        axis = left.index(bit)
        mine = own_bit(bit)
        sent = pick_bit(grid, axis, 1 - mine)
        kept = pick_bit(grid, axis, mine)
        arrived = flip_swap(sent, bit)
        total = kept.astype(jnp.float32) + arrived.astype(jnp.float32)
        left.remove(bit)
        grid = total if not left else total.astype(grid.dtype)
    return grid


def all_bits(size):
    bits = [1 << i for i in range(size.bit_length() - 1)]
    return bits[::-1]


def to_grid(array, size):
    bits = all_bits(size)
    return array.reshape((2,) * len(bits) + (array.shape[0] // size,) + array.shape[1:])


def gather_all(block, size):
    if size != 16:
        for bit in all_bits(size)[::-1]:
            block = jnp.concatenate([block, flip_swap(block, bit)], 0)
        return block
    block = jnp.concatenate([block] + [flip_swap(block, k) for k in (1, 2, 3)], 0)
    return jnp.concatenate([block] + [flip_swap(block, k) for k in (4, 8, 12)], 0)


def contrast(own_cls, micro, positive, query_count, batch_index, batch_size):
    width = own_cls.shape[1]
    chip_rows = own_cls.shape[0]
    gathered = gather_all(own_cls, batch_size).reshape(batch_size, chip_rows, width)
    all_q = gathered[:, :query_count].reshape(-1, width)
    all_p = gathered[:, query_count:].reshape(-1, width)
    blocks = jnp.arange(batch_size, dtype=jnp.int32) ^ batch_index
    query_ids = (
        blocks[:, None] * query_count + jnp.arange(query_count, dtype=jnp.int32)[None, :]
    ).reshape(-1)
    passage_ids = (
        3 * query_ids[:, None] + jnp.arange(3, dtype=jnp.int32)[None, :]
    ).reshape(-1)
    labels = jnp.take(micro, query_ids)
    wanted = jnp.take(positive, query_ids)
    logit_scale = LOGIT_GAIN * width ** (-0.5)
    logits = mm_nt(all_q, all_p) * logit_scale
    same_group = labels[:, None] == jnp.repeat(labels, 3)[None, :]
    logits = jnp.where(same_group, logits, MASK_FILL)
    row_top = jnp.max(logits, axis=-1, keepdims=True)
    exponent = jnp.exp(logits - row_top)
    totals = jnp.sum(exponent, axis=-1, keepdims=True)
    target = passage_ids[None, :] == wanted[:, None]
    loss_all = (
        row_top[:, 0] + jnp.log(totals[:, 0]) - jnp.sum(jnp.where(target, logits, 0.0), axis=-1)
    )
    coefficient = (exponent / totals - target.astype(jnp.float32)) * logit_scale
    passage_count = 3 * query_count
    d_cls_q = jnp.dot(coefficient[:query_count], all_p.astype(jnp.float32), precision=PRECISE)
    d_cls_p = lax.dot_general(
        coefficient[:, :passage_count],
        all_q.astype(jnp.float32),
        (((0,), (0,)), ((), ())),
        precision=PRECISE,
    )
    return loss_all[:query_count], d_cls_q, d_cls_p


def integers(core, index, size, len_q, len_p):
    blocks = jnp.arange(BLOCKS, dtype=jnp.int32)
    own = index // (size // BLOCKS)
    relative = blocks ^ own
    places = [
        sum(((relative // bit) % 2) * (8 >> at) for at, bit in enumerate(order))
        for order in ORDERS
    ]
    depth = jnp.arange(4, dtype=jnp.int32) ^ (own // 4)
    z_places = (depth % 2) * 2 + depth // 2
    few = jnp.stack([1 - core, core])
    ends = jnp.stack([own % 2, (own // 2) % 2])
    return jnp.concatenate([few, *places, z_places, ends, len_q, len_p]).astype(jnp.int32)


def shards(
    x_q,
    x_p,
    len_q,
    len_p,
    cot_q,
    cot_p,
    positive,
    micro,
    w_qkv,
    w_out,
    w_up,
    w_down,
    norm_gain,
    biases,
    b_up,
):
    core = lax.axis_index("section")
    is_first = core == 0
    batch_index = lax.axis_index("batch")
    size = lax.axis_size("batch")
    bits = all_bits(size)
    query_count, slots_q, model = x_q.shape
    half_count = x_p.shape[0] // 2
    slots_p = x_p.shape[1]
    wide = w_up.shape[-1]
    info = integers(core, batch_index, size, len_q, len_p)
    weights = (w_qkv, w_out, w_up, w_down)
    smalls = (norm_gain, biases, b_up)
    other_p = tuple(core_swap(member[0, 1]) for member in weights)
    small_other = core_swap(
        jnp.concatenate([norm_gain[0, 1], biases[0, 1], b_up[0, 1].reshape(-1, model)], 0)
    )
    tower_q = Tower(0, info, weights, None, smalls, None, query_count, slots_q, LENGTHS)
    tower_p = Tower(
        1, info, weights, other_p, smalls, small_other, half_count, slots_p, LENGTHS + query_count
    )
    flat_q = x_q.reshape(-1, model)
    flat_p = x_p.reshape(-1, model)
    cots_q = cot_q.reshape(-1, model)
    cots_p = cot_p.reshape(-1, model)

    early_q, _ = forward_layers(tower_q, (0,), flat_q, True, None)
    mid_q = early_q[OUTPUT]
    arrived_q = core_swap(mid_q)
    late_q, first_q = forward_layers(tower_q, (1,), arrived_q, True, None)
    early_p, late_p, cls_rows = forward_layers(
        tower_p, (0, 1), flat_p, True, (first_q, query_count)
    )
    mid_p = early_p[OUTPUT]
    top_q, top_p = late_q[OUTPUT], late_p[OUTPUT]

    last = query_count + half_count
    cls_other = core_swap(cls_rows)
    cls_chip = jnp.concatenate(
        [
            jnp.where(is_first, cls_other[:query_count], cls_rows[:query_count]),
            jnp.where(is_first, cls_rows[query_count:last], cls_other[query_count:last]),
            jnp.where(is_first, cls_other[query_count:last], cls_rows[query_count:last]),
        ],
        0,
    )
    loss_own, d_cls_q, d_cls_p = contrast(
        cls_chip, micro, positive, query_count, batch_index, size
    )

    def factors(rows, kept, back):
        return (rows, kept[LEFTS], back[4], back[3], back[5], back[6])

    scale = size // BLOCKS

    def core_products(
        layer, rows, lefts, other_lefts, back, other_rights, vectors, after, cost
    ):
        products = passage_products(
            tower_p, layer, rows, lefts, other_lefts, back[4::2], other_rights, vectors, after, cost
        )
        return products

    def chains_of(layer, products):
        return [
            Chain(products[2 * at], products[2 * at + 1], ORDERS[3 * layer + at], scale)
            for at in range(len(products) // 2)
        ]

    late_back_q = backward_layer(
        tower_q, 1, cots_q, d_cls_q, late_q, True, cost=0
    )
    late_sent_q = late_back_q[0]
    grad_mid_q = core_swap(late_sent_q)
    early_back_q = backward_layer(
        tower_q,
        0,
        grad_mid_q,
        None,
        early_q,
        False,
        cost=0,
        through=(late_p[LEFTS], early_p[LEFTS], jnp.where(is_first, top_p, mid_p)),
    )
    *early_back_q, late_left, early_left, hidden_sent = early_back_q
    late_left_other, early_left_other = core_swap(late_left), core_swap(early_left)
    hidden_other = core_swap(hidden_sent)
    packs = pack_first(
        info,
        factors(flat_q, early_q, early_back_q),
        factors(arrived_q, late_q, late_back_q),
        cost=0,
    )
    keeps, sends = packs[0::2], packs[1::2]
    arrivals = [flip_swap(sends[0], scale), flip_swap(sends[1], 2 * scale)]
    late_back_p = backward_layer(
        tower_p, 1, cots_p, d_cls_p, late_p, True, tuple(sends), cost=0
    )
    late_sent_p = late_back_p[0]
    late_other = [core_swap(array) for array in late_back_p[3::2]]
    packs = pack_second(
        info,
        keeps,
        sends,
        arrivals,
        model,
        (late_sent_p, late_left_other, early_left_other, hidden_other),
        cost=40,
    )
    keeps, sends = packs[0::2], packs[1::2]
    arrivals = [flip_swap(sends[0], 2 * scale), flip_swap(sends[1], scale)]
    products = core_products(
        1, None, late_left, late_left_other, late_back_p, late_other, (), tuple(sends), 0
    )
    a1, b1 = chains_of(1, products)
    send, keep = query_products(
        info, keeps, sends, arrivals, model, wide, tuple(products[:1]), cost=4
    )
    query = Chain(send, keep, (4, 8), scale)
    early_back_p = backward_layer(
        tower_p, 0, late_sent_p, None, early_p, False, (send,), cost=0
    )
    early_grad_p = early_back_p[0]
    early_other = [core_swap(array) for array in early_back_p[3::2]]
    vectors = (*early_back_q[1:3], *late_back_q[1:3], *early_back_p[1:3], *late_back_p[1:3])
    pieces = vector_pieces(info, 0, vectors, wide, (early_grad_p,), 0)
    vectors = (pieces[1], core_swap(pieces[0]))
    seen = play_round([[a1], [b1]], pieces[:1], 4)
    seen = play_round([[query]], seen, 40)
    products = core_products(
        0, flat_p, early_left, early_left_other, early_back_p, early_other, vectors, seen, 4
    )
    a0, b0 = chains_of(0, products)
    seen = (products[0],)
    others = (
        early_grad_p,
        late_sent_p,
        early_back_q[0],
        late_sent_q,
        mid_q,
        top_q,
        mid_p,
        top_p,
        hidden_other,
        loss_own[None],
    )
    for step, (groups, cost) in enumerate((
        ([[a1, b1]], 40),
        ([[query]], 4),
        ([[a0], [b0]], 0),
        ([[a1]], 40),
        ("z", 4),
        ([[a1]], 12),
    )):
        held = others if step == 2 else ()
        if groups == "z":
            parts = take_in_quarters([(chain.keep, chain.arrived) for chain in (a0, b0)], seen, cost)
            low, high = a0.order[0] * scale, a0.order[1] * scale
            quarters = (
                parts[0],
                flip_swap(parts[1], high),
                flip_swap(parts[2], low),
                flip_swap(parts[3], low + high),
            )
            seen = tuple(parts[1:])
            continue
        passed = play_round(groups, seen, cost, held)
        seen = passed[: len(passed) - len(held)]
        if step == 2:
            others = passed[-10:]
    early_grad_p, late_sent_p, early_grad_q, late_sent_q = others[:4]
    mid_q, top_q, mid_p, top_p, hidden_other, loss_own = others[4:]
    loss_own = loss_own[0]
    early_grad_other = core_swap(jnp.where(is_first, late_sent_p.astype(F32), early_grad_p))

    total_q = query.total

    def other_half(begin, columns, bit):
        mine = (batch_index // (bit * scale)) % 2
        sent = lax.dynamic_slice_in_dim(total_q, begin + (1 - mine) * columns, columns, 1)
        return flip_swap(sent, bit * scale)

    query_x = other_half(0, 3 * model // 2, 1)
    query_y = other_half(4 * model, wide // 2, 2)
    outputs = query_outputs(info, total_q, query_x, query_y, model, wide, seen)
    own, sent, total_v = last_round(info, quarters, a1.total, model + wide // 2, seen)
    sums = passage_outputs(info, own, core_swap(sent), outputs, model, wide)
    if scale > 1:
        left = all_bits(scale)
        sums = [
            jnp.stack([scatter_sum(to_grid(tower.astype(LOW), scale), left, left) for tower in item])
            for item in sums
        ]
    g_qkv, g_out, g_up, g_down = sums

    total_v = total_v[:32].reshape(2, 16, 128)
    eight = total_v[:, :8, : model // BLOCKS]
    g_bup = total_v[:, 8:10].reshape(2, -1)[:, : wide // BLOCKS]
    if scale > 1:
        left = all_bits(scale)
        eight = scatter_sum(
            to_grid(jnp.moveaxis(eight, 2, 0).reshape(-1, 16), scale), left, left
        )
        eight = jnp.moveaxis(eight.reshape(-1, 2, 8), 0, 2)
        g_bup = scatter_sum(to_grid(g_bup.T, scale), left, left).T
    g_gain = jnp.stack([eight[:, 3], eight[:, 0]], 1)
    g_bias = jnp.stack([eight[:, at] for at in (6, 7, 5, 4, 2, 1)], 1)

    pairs = (
        jnp.where(is_first, mid_p, hidden_other),
        jnp.where(is_first, hidden_other, top_p),
    )
    hidden_p = jnp.concatenate(pairs, 0).reshape(x_p.shape)
    pairs = (
        jnp.where(is_first, early_grad_p, early_grad_other),
        jnp.where(is_first, early_grad_other, late_sent_p.astype(F32)),
    )
    grad_p = jnp.concatenate(pairs, 0).reshape(x_p.shape)
    hidden_q = jnp.where(is_first, mid_q, top_q).reshape(x_q.shape)
    grad_q = jnp.where(is_first, early_grad_q, late_sent_q.astype(F32)).reshape(x_q.shape)
    return (
        hidden_q[None],
        hidden_p[None],
        grad_q[None],
        grad_p[None],
        loss_own,
        g_qkv[None],
        g_out[None],
        g_up[None],
        g_down[None],
        g_gain[None],
        g_bias[None],
        g_bup[None],
        g_bias[None, :, 0, :],
    )


def solution(mesh):
    return jax.shard_map(
        shards,
        mesh=mesh,
        in_specs=(
            P("batch", None, None),
            P("batch", None, None),
            P("batch"),
            P("batch"),
            P("batch", None, None),
            P("batch", None, None),
            P(),
            P(),
            P("section", None, None, None),
            P("section", None, None, None),
            P("section", None, None, None),
            P("section", None, None, None),
            P("section", None, None, None),
            P("section", None, None, None),
            P("section", None, None),
        ),
        out_specs=(
            P("section", "batch", None, None),
            P("section", "batch", None, None),
            P("section", "batch", None, None),
            P("section", "batch", None, None),
            P("batch"),
            P("section", None, "batch", None),
            P("section", None, "batch", None),
            P("section", None, "batch", None),
            P("section", None, "batch", None),
            P("section", None, None, "batch"),
            P("section", None, None, "batch"),
            P("section", None, "batch"),
            P("section", None, "batch"),
        ),
        check_vma=False,
    )
```

```python
import jax
import jax.numpy as jnp
from jax import lax
from jax.experimental import pallas as pl
from jax.experimental.pallas import tpu as pltpu
from jax.sharding import PartitionSpec as P

HEADS = 12
HEAD_DIM = 64


NORM_EPS = 1e-05
SQRT_HALF = 0.7071067811865476
ROOT_TAU_INV = 0.3989422804014327
MASK_FILL = -1e30
LOGIT_GAIN = 2.5
PRECISE = lax.Precision.HIGHEST


def core_swap(block):
    return lax.ppermute(block, "section", [(0, 1), (1, 0)])


def flip_swap(block, bit):
    size = lax.axis_size("batch")
    return lax.ppermute(block, "batch", [(i, i ^ bit) for i in range(size)])


F32 = jnp.float32
LOW = jnp.bfloat16
VMEM_LIMIT = 63 * 1024 * 1024 + 512 * 1024
BLOCKS = 16
COST = 1 << 30
IS_FIRST, CORE, PLACES, Z_PLACES, X_BIT, Y_BIT, LENGTHS = 0, 1, 2, 98, 102, 103, 104
ORDERS = (
    (1, 2, 4, 8),
    (2, 1, 4, 8),
    (2, 1, 4, 8),
    (1, 2, 4, 8),
    (2, 1, 4, 8),
    (2, 1, 4, 8),
)

LAYOUTS = (((0, 0), (1, 0), (0, 1536), (1, 1536)), ((0, 0), (1, 0), (0, 1536), (1, 1536)))


def mm(left, right):
    return lax.dot_general(left, right, (((1,), (0,)), ((), ())), preferred_element_type=F32)


def mm_nt(left, right):
    return lax.dot_general(left, right, (((1,), (1,)), ((), ())), preferred_element_type=F32)


def mm_tn(left, right):
    return lax.dot_general(left, right, (((0,), (0,)), ((), ())), preferred_element_type=F32)


def row_mean(values):
    return jnp.sum(values, axis=-1, keepdims=True) * (1.0 / values.shape[-1])


def normed_rows(values):
    center = values - row_mean(values)
    inverse = lax.rsqrt(row_mean(center * center) + NORM_EPS)
    return center * inverse, inverse


def norm_pull(upstream, normed, inverse, gain):
    scaled = upstream * gain
    return inverse * (scaled - row_mean(scaled) - normed * row_mean(scaled * normed))


def col_sum(values):
    return jnp.sum(values, axis=0, keepdims=True)


class Moves:
    def __init__(self, sems):
        self.sems = sems
        self.used = 0
        self.open = []

    def slot(self):
        self.used += 1
        return self.sems.at[self.used - 1]

    def fetch(self, source, target):
        copy = pltpu.make_async_copy(source, target, self.slot())
        copy.start()
        return copy

    def fetch_either(self, flag, first, second, target):
        sem = self.slot()
        copy = pltpu.make_async_copy(first, target, sem)
        if second is None:
            copy.start()
            return copy
        other = pltpu.make_async_copy(second, target, sem)

        @pl.when(flag)
        def _():
            copy.start()

        @pl.when(jnp.logical_not(flag))
        def _():
            other.start()

        return copy

    def store(self, source, target):
        self.open.append(self.fetch(source, target))

    def drain(self):
        for copy in self.open:
            copy.wait()


class Tower:
    def __init__(self, index, info, weights, others, small, small_other, seqs, slots, first_len):
        self.index = index
        self.info = info
        self.weights = weights
        self.others = others
        self.small = small
        self.small_other = small_other
        self.seqs = seqs
        self.slots = slots
        self.first_len = first_len
        self.count = seqs * slots
        self.width = weights[1].shape[-1]
        self.wide = weights[2].shape[-1]
        self.group = self.count if self.count <= 128 else slots
        self.shared = others is not None

    def given(self, which):
        own = [self.weights[at] for at in which]
        return own + ([self.others[at] for at in which] if self.shared else [])

    def given_small(self):
        return list(self.small) + ([self.small_other] if self.shared else [])

    def use_own(self, info, layer):
        return info[IS_FIRST] == (1 if layer == 0 else 0)

    def lengths_at(self, info):
        return self.first_len + (info[CORE] * self.seqs if self.shared else 0)

    def row_start(self, info):
        return pl.multiple_of(info[CORE] * self.count, self.count) if self.shared else 0

    def small_rows(self, refs, flag):
        own = [refs[0][0, self.index], refs[1][0, self.index]]
        if self.shared:
            other = refs[3]
            own = [
                jnp.where(flag, own[0], other[0:2, :]),
                jnp.where(flag, own[1], other[2:8, :]),
            ]
        return own

    def hidden_bias(self, refs, flag, step, tile):
        own = refs[2][0, self.index : self.index + 1, step * tile : (step + 1) * tile]
        if self.shared:
            own = jnp.where(flag, own, refs[3][8 + step : 9 + step, :])
        return own


ANYWHERE = pl.BlockSpec(memory_space=pltpu.HBM)
SCALARS = pl.BlockSpec(memory_space=pltpu.SMEM)
INSIDE = pl.BlockSpec(memory_space=pltpu.VMEM)


def call_kernel(kernel, name, inputs, outs, scratch, copies, micros, after, through=()):
    count = len(inputs)
    given = list(after) + list(through)
    extra = len(given)

    def body(*refs):
        refs = list(refs)
        kernel(
            refs[:count],
            refs[count + extra : count + extra + len(outs)]
            or refs[count + extra : count + extra + len(through)],
            refs[count + extra + len(outs) + len(through) : -1],
            Moves(refs[-1]),
        )

    return pl.pallas_call(
        body,
        out_shape=[jax.ShapeDtypeStruct(shape, kind) for shape, kind in outs]
        + [jax.ShapeDtypeStruct(array.shape, array.dtype) for array in through],
        in_specs=[spec for spec, _ in inputs] + [ANYWHERE] * extra,
        out_specs=[ANYWHERE] * (len(outs) + len(through)),
        input_output_aliases={
            count + len(after) + at: len(outs) + at for at in range(len(through))
        },
        scratch_shapes=[pltpu.VMEM(shape, kind) for shape, kind in scratch]
        + [pltpu.SemaphoreType.DMA((copies,))],
        compiler_params=pltpu.CompilerParams(vmem_limit_bytes=VMEM_LIMIT),
        cost_estimate=pl.CostEstimate(
            flops=int(COST * micros) + 1024, bytes_accessed=1024, transcendentals=0
        ),
        name=name,
    )(*[array for _, array in inputs], *given)


def pair_masks(dtype):
    lanes = lax.broadcasted_iota(jnp.int32, (1, 128), 1)
    low = jnp.where(lanes < HEAD_DIM, 1.0, 0.0)
    return low.astype(dtype), (1.0 - low).astype(dtype)


def stacked_pair(block, low, high):
    return jnp.concatenate([block * low, block * high], axis=0)


def joined_pair(stacked, group):
    lanes = lax.broadcasted_iota(jnp.int32, (1, 128), 1)
    return jnp.where(lanes < HEAD_DIM, stacked[:group], stacked[group:])


def pair_softmax(query_stack, key_block, valid):
    scores = mm_nt(key_block, query_stack) * HEAD_DIM ** (-0.5)
    scores = jnp.where(valid, scores, MASK_FILL)
    exponent = jnp.exp(scores - jnp.max(scores, axis=0, keepdims=True))
    return exponent * (1.0 / jnp.sum(exponent, axis=0, keepdims=True))


def valid_keys(info, first_len, group, slots):
    keys = lax.broadcasted_iota(jnp.int32, (group, 2 * group), 0)
    queries = lax.broadcasted_iota(jnp.int32, (group, 2 * group), 1)
    seqs = group // slots
    if seqs == 1:
        return keys < info[first_len]
    queries = jnp.where(queries >= group, queries - group, queries)
    valid = None
    for j in range(seqs):
        low = j * slots
        inside = (
            (queries >= low)
            & (queries < low + slots)
            & (keys >= low)
            & (keys < low + info[first_len + j])
        )
        valid = inside if valid is None else valid | inside
    return valid


def weight_shapes(tower):
    width, steps = tower.width, tower.wide // tower.width
    return [
        ((3, width, width), LOW),
        ((width, width), LOW),
        ((steps, width, width), LOW),
        ((steps, width, width), LOW),
    ]


def fetch_narrow(tower, flag, own, other, targets, moves, order=(0, 1, 2, 3)):
    width = tower.width
    got = {}
    for part in order:
        if part == 3:
            got[3] = moves.fetch_either(flag, own[1].at[0, tower.index], other[1], targets[1])
            continue
        cols = pl.ds(part * width, width)
        second = other[0].at[:, cols] if tower.shared else None
        got[part] = moves.fetch_either(
            flag, own[0].at[0, tower.index, :, cols], second, targets[0].at[part]
        )
    return got


def fetch_step(tower, flag, own, other, targets, moves, step, at):
    width = tower.width
    part = pl.ds(pl.multiple_of(at * width, width), width)
    up, down = (other[0].at[:, part], other[1].at[part]) if tower.shared else (None, None)
    return (
        moves.fetch_either(flag, own[1].at[0, tower.index, part], down, targets[1].at[step]),
        moves.fetch_either(flag, own[0].at[0, tower.index, :, part], up, targets[0].at[step]),
    )


def kept_scratch(tower):
    count, width, wide = tower.count, tower.width, tower.wide
    steps = wide // width
    return [
        ((count, width), LOW),
        ((count, 3 * width), LOW),
        ((count, width), LOW),
        ((count, width), LOW),
        ((steps, count, width), LOW),
        ((steps, count, width), LOW),
        ((count, width), LOW),
        ((count, width), LOW),
        ((2, count, 128), F32),
        ((width // 128, count, 2 * tower.group), LOW),
    ]


OUTPUT, LEFTS, PROJECTED, SLOPE, HAT1, HAT2, INVERSES, SOFT = range(8)


def kept_shapes(tower, inner):
    count, width, wide = tower.count, tower.width, tower.wide
    steps = wide // width
    return [
        ((count, width), LOW),
        ((count, 2 * width + wide + (width if inner else 0)), LOW),
        ((count, 3 * width), LOW),
        ((steps, count, width), LOW),
        ((count, width), LOW),
        ((count, width), LOW),
        ((2, count, 128), F32),
        ((width // 128, count, 2 * tower.group), LOW),
    ]


def forward_body(
    tower, layer, info, x_v, got, weights, smalls, acc_v, kept, outs, moves, first_out=None
):
    count, width, group = tower.count, tower.width, tower.group
    w_qkv, w_out, w_up, w_down = weights
    out_v, qkv_v, mix_v, low_v, act_v, slope_v, hat1_v, hat2_v, inv_v, soft_v = kept
    use_own = tower.use_own(info, layer)
    gains, bias = tower.small_rows(smalls, use_own)
    x = x_v[...]
    for part in range(3):
        got[part].wait()
        block = mm(x, w_qkv[part])
        if part == 0:
            block = block + bias[0:1, :]
        if part == 2:
            block = block + bias[1:2, :]
        qkv_v[:, part * width : (part + 1) * width] = block.astype(LOW)
    moves.store(qkv_v, outs[PROJECTED])
    low, high = pair_masks(LOW)
    for g in range(count // group):
        at = slice(g * group, (g + 1) * group)
        valid = valid_keys(
            info, tower.lengths_at(info) + g * (group // tower.slots), group, tower.slots
        )
        for pair in range(width // 128):
            lane = pair * 128
            q2 = qkv_v[at, lane : lane + 128]
            k2 = qkv_v[at, width + lane : width + lane + 128]
            v2 = qkv_v[at, 2 * width + lane : 2 * width + lane + 128]
            soft = pair_softmax(stacked_pair(q2, low, high), k2, valid).astype(LOW)
            soft_v[pair, at, :] = soft
            mix_v[at, lane : lane + 128] = joined_pair(mm_tn(soft, v2), group).astype(LOW)
    moves.store(soft_v, outs[SOFT])
    moves.store(mix_v, outs[LEFTS].at[:, pl.ds(0, width)])
    got[3].wait()
    summed = x.astype(F32) + (mm(mix_v[...], w_out[...]) + bias[2:3, :])
    hat, inverse = normed_rows(summed)
    hat1_v[...] = hat.astype(LOW)
    inv_v[0] = jnp.broadcast_to(inverse, (count, 128))
    moves.store(hat1_v, outs[HAT1])
    first = hat * gains[0:1, :] + bias[3:4, :]
    low_v[...] = first.astype(LOW)
    moves.store(low_v, outs[LEFTS].at[:, pl.ds(width, width)])
    acc_v[...] = first + bias[4:5, :]
    for step in range(tower.wide // width):
        for copy in got[4 + step]:
            copy.wait()
        hidden = mm(low_v[...], w_up[step]) + tower.hidden_bias(smalls, use_own, step, width)
        cdf = 0.5 * (1.0 + lax.erf(hidden * SQRT_HALF))
        act = (hidden * cdf).astype(LOW)
        act_v[step] = act
        slope_v[step] = (
            cdf + hidden * (jnp.exp(-0.5 * hidden * hidden) * ROOT_TAU_INV)
        ).astype(LOW)
        moves.store(act_v.at[step], outs[LEFTS].at[:, pl.ds((2 + step) * width, width)])
        moves.store(slope_v.at[step], outs[SLOPE].at[step])
        acc_v[...] += mm(act, w_down[step])
    hat, inverse = normed_rows(acc_v[...])
    hat2_v[...] = hat.astype(LOW)
    moves.store(hat2_v, outs[HAT2])
    inv_v[1] = jnp.broadcast_to(inverse, (count, 128))
    moves.store(inv_v, outs[INVERSES])
    output = hat * gains[1:2, :] + bias[5:6, :]
    out_v[...] = output.astype(LOW)
    moves.store(out_v, outs[OUTPUT])
    if first_out is not None:
        first_v, to, above = first_out
        firsts = [output[at * tower.slots : at * tower.slots + 1, :] for at in range(tower.seqs)]
        spare = jnp.zeros((16 - len(firsts) - sum(item.shape[0] for item in above), width), F32)
        first_v[...] = jnp.concatenate([*above, *firsts, spare], axis=0).astype(LOW)
        moves.store(first_v, to)


def forward_layers(tower, layers, rows, whole_rows, ahead, after=(), cost=0):
    count, width = tower.count, tower.width
    steps = tower.wide // width
    shapes = [kept_shapes(tower, at > 0) for at in range(len(layers))]
    kinds = len(shapes[0])
    held = kept_scratch(tower)

    def kernel(ins, outs, scratch, moves):
        info, x_any = ins[0], ins[1]
        own = ins[2:6]
        other = ins[6:10] if tower.shared else [None] * 4
        smalls = ins[10:] if tower.shared else ins[6:]
        above = []
        if ahead is not None:
            above = [smalls[-1][...].astype(F32)[0 : ahead[1], :]]
            smalls = smalls[:-1]
        x_v, acc_v = scratch[:2]
        if whole_rows:
            x_any = x_any.at[pl.ds(tower.row_start(info), count)]
        x_got = moves.fetch(x_any, x_v)
        weights, got = [], []
        for at, layer in enumerate(layers):
            targets = scratch[2 + 4 * at : 6 + 4 * at]
            flag = tower.use_own(info, layer)
            arrivals = fetch_narrow(tower, flag, own[:2], other[:2], targets[:2], moves)
            for step in range(steps):
                arrivals[4 + step] = fetch_step(
                    tower, flag, own[2:], other[2:], targets[2:], moves, step, step
                )
            weights.append(targets)
            got.append(arrivals)
        x_got.wait()
        for at, layer in enumerate(layers):
            begin = 2 + 4 * len(layers) + len(held) * at
            kept = scratch[begin : begin + len(held)]
            forward_body(
                tower,
                layer,
                info,
                x_v,
                got[at],
                weights[at],
                smalls,
                acc_v,
                kept,
                outs[kinds * at : kinds * (at + 1)],
                moves,
                (scratch[-1], outs[-1], above) if at + 1 == len(layers) else None,
            )
            x_v = kept[0]
            if at + 1 < len(layers):
                inner = outs[kinds * (at + 1) + LEFTS]
                moves.store(x_v, inner.at[:, pl.ds(2 * width + tower.wide, width)])
        moves.drain()

    outs = [shape for layer_shapes in shapes for shape in layer_shapes] + [((16, width), LOW)]
    scratch = [((count, width), LOW), ((count, width), F32)] + weight_shapes(tower) * len(layers)
    inputs = [(SCALARS, tower.info), (ANYWHERE, rows)]
    inputs += [(ANYWHERE, array) for array in tower.given((0, 1, 2, 3))]
    inputs += [(INSIDE, array) for array in tower.given_small()]
    if ahead is not None:
        inputs.append((INSIDE, ahead[0]))
    results = call_kernel(
        kernel,
        "layer_forward",
        inputs,
        outs,
        scratch + held * len(layers) + outs[-1:],
        2 + len(layers) * (4 + 2 * steps + 9 + 2 * steps),
        cost,
        list(after),
    )
    return [results[kinds * at : kinds * (at + 1)] for at in range(len(layers))] + [results[-1]]


def place_rows(target, block, info, first, size, columns):
    for piece in range(block.shape[0] // size):
        at = pl.multiple_of(info[first + piece] * size, size)
        target[pl.ds(at, size), columns] = block[piece * size : (piece + 1) * size].astype(LOW)


def wide_scratch(tower, upstream):
    count, width = tower.count, tower.width
    steps = tower.wide // width
    return weight_shapes(tower)[2:] + [
        ((count, width), upstream.dtype),
        ((count, width), LOW),
        ((count, 128), F32),
        ((steps, count, width), LOW),
        ((count, width), F32),
        ((count, width), LOW),
        ((steps, count, width), LOW),
        ((8, width), F32),
    ]


def store_sides(source, side_width, outs, column, core_at, moves):
    for side, to in ((1 - core_at, outs[0]), (core_at, outs[1])):
        lanes = pl.ds(pl.multiple_of(side * side_width, 128), side_width)
        moves.store(source.at[:, lanes], to.at[:, pl.ds(column, side_width)])


def wide_tiles(tower, info):
    steps = tower.wide // tower.width
    if not tower.shared:
        return list(range(steps))
    return [lax.rem(step + (1 - info[CORE]) * (steps // 2), steps) for step in range(steps)]


def wide_fetch(tower, layer, info, ins, seeded, scratch, moves):
    up_any, own, other, slope_any, hat_any, inv_any = ins
    w_up, w_down, up_v, hat_v, inv_v, slope_v = scratch[:6]
    use_own = tower.use_own(info, layer)
    if seeded:
        up_any = up_any.at[pl.ds(tower.row_start(info), tower.count)]
    first_got = [
        moves.fetch(up_any, up_v),
        moves.fetch(hat_any, hat_v),
        moves.fetch(inv_any.at[1], inv_v),
    ]
    got = []
    for step, at in enumerate(wide_tiles(tower, info)):
        pieces = [moves.fetch(slope_any.at[at], slope_v.at[step])]
        pieces += fetch_step(tower, use_own, own, other, (w_up, w_down), moves, step, at)
        got.append(pieces)
    return first_got, got


def wide_body(tower, layer, info, fetched, first_ref, smalls, scratch, outs, moves):
    count, width = tower.count, tower.width
    steps = tower.wide // width
    w_up, w_down, up_v, hat_v, inv_v, slope_v, da_v, df_v, dh_v, vec_v = scratch
    use_own = tower.use_own(info, layer)
    core_at = info[CORE]
    first_got, got = fetched
    tiles = wide_tiles(tower, info)
    gains, _ = tower.small_rows(smalls, use_own)
    for copy in first_got:
        copy.wait()
    upward = up_v[...].astype(F32)
    if first_ref is not None:
        row_at = lax.broadcasted_iota(jnp.int32, (count, 1), 0)
        lengths = tower.lengths_at(info)
        first_seq = lengths - tower.first_len
        seen = jnp.zeros((count, 1), F32)
        for seq in range(tower.seqs):
            start = seq * tower.slots
            inside_seq = (row_at >= start) & (row_at < start + info[lengths + seq])
            seen = jnp.where(inside_seq, 1.0, seen)
        upward = upward * seen
        for seq in range(tower.seqs):
            upward = upward + jnp.where(
                row_at == seq * tower.slots, first_ref[pl.ds(first_seq + seq, 1), :], 0.0
            )
    hat = hat_v[...].astype(F32)
    vec_v[0:1, :] = col_sum(upward * hat)
    vec_v[1:2, :] = col_sum(upward)
    d_second = norm_pull(upward, hat, inv_v[:, 0:1], gains[1:2, :])
    d_low = d_second.astype(LOW)
    df_v[...] = d_low
    vec_v[2:3, :] = col_sum(d_low.astype(F32))
    vec_v[7:8, :] = jnp.zeros((1, width), F32)
    da_v[...] = d_second
    vec_out, df_out, dh_out = outs
    if tower.shared:
        store_sides(df_v, width // 2, df_out, 0, core_at, moves)
    else:
        moves.store(df_v, df_out[0])
    for step, at in enumerate(tiles):
        for copy in got[step]:
            copy.wait()
        d_hidden = (mm_nt(df_v[...], w_down[step]) * slope_v[step].astype(F32)).astype(LOW)
        vec_v[pl.ds(3 + at, 1), :] = col_sum(d_hidden.astype(F32))
        dh_v[step] = d_hidden
        da_v[...] += mm_nt(d_hidden, w_up[step])
        if tower.shared:
            side, place = divmod(step, steps // 2)
            moves.store(dh_v.at[step], dh_out[side].at[:, pl.ds(place * width, width)])
        else:
            moves.store(dh_v.at[step], dh_out[0].at[step])
    moves.store(vec_v, vec_out)


def narrow_scratch(tower, out_type):
    count, width = tower.count, tower.width
    return weight_shapes(tower)[:2] + [
        ((count, width), LOW),
        ((count, 128), F32),
        ((count, 3 * width), LOW),
        ((width // 128, count, 2 * tower.group), LOW),
        ((count, width), LOW),
        ((count, 3 * width), LOW),
        ((count, width), LOW),
        ((count, width), F32),
        ((count, width), out_type),
        ((8, width), F32),
    ]


def narrow_fetch(tower, layer, info, ins, scratch, moves):
    own, other, qkv_any, hat_any, inv_any, soft_any = ins
    w_qkv, w_out, hat_v, inv_v, qkv_v, soft_v = scratch[:6]
    use_own = tower.use_own(info, layer)
    got = {"hat": [moves.fetch(hat_any, hat_v), moves.fetch(inv_any.at[0], inv_v)]}
    weights = fetch_narrow(tower, use_own, own, other, (w_qkv, w_out), moves, (3,))
    got["heads"] = [moves.fetch(qkv_any, qkv_v), moves.fetch(soft_any, soft_v)]
    weights.update(fetch_narrow(tower, use_own, own, other, (w_qkv, w_out), moves, (0, 1, 2)))
    got["weights"] = weights
    return got


def narrow_body(tower, layer, info, got, da_v, smalls, scratch, outs, moves):
    count, width, group = tower.count, tower.width, tower.group
    w_qkv, w_out, hat_v, inv_v, qkv_v, soft_v, dz_v, dp_v, dmix_v, du_v, dx_v, vec_v = scratch
    use_own = tower.use_own(info, layer)
    core_at = info[CORE]
    dx_out, vec_out, dz_out, dp_out = outs
    gains, _ = tower.small_rows(smalls, use_own)
    for copy in got["hat"]:
        copy.wait()
    upward = da_v[...]
    hat = hat_v[...].astype(F32)
    vec_v[0:1, :] = col_sum(upward * hat)
    vec_v[1:2, :] = col_sum(upward)
    d_summed = norm_pull(upward, hat, inv_v[:, 0:1], gains[0:1, :])
    du_v[...] = d_summed
    d_low = d_summed.astype(LOW)
    dz_v[...] = d_low
    vec_v[2:3, :] = col_sum(d_low.astype(F32))
    vec_v[5:8, :] = jnp.zeros((3, width), F32)
    if tower.shared:
        store_sides(dz_v, width // 2, dz_out, 2 * width, core_at, moves)
    else:
        moves.store(dz_v, dz_out[0])
    got["weights"][3].wait()
    dmix_v[...] = mm_nt(d_low, w_out[...]).astype(LOW)
    for copy in got["heads"]:
        copy.wait()
    low, high = pair_masks(LOW)
    scale = HEAD_DIM ** (-0.5)
    for g in range(count // group):
        at = slice(g * group, (g + 1) * group)
        for pair in range(width // 128):
            lane = pair * 128
            q2 = qkv_v[at, lane : lane + 128]
            k2 = qkv_v[at, width + lane : width + lane + 128]
            v2 = qkv_v[at, 2 * width + lane : 2 * width + lane + 128]
            soft = soft_v[pair, at, :]
            d_stack = stacked_pair(dmix_v[at, lane : lane + 128], low, high)
            d_soft = mm_nt(v2, d_stack)
            soft_wide = soft.astype(F32)
            total = jnp.sum(d_soft * soft_wide, axis=0, keepdims=True)
            d_scores = (soft_wide * (d_soft - total)).astype(LOW)
            dp_v[at, lane : lane + 128] = (
                joined_pair(mm_tn(d_scores, k2), group) * scale
            ).astype(LOW)
            dp_v[at, width + lane : width + lane + 128] = (
                mm(d_scores, stacked_pair(q2, low, high)) * scale
            ).astype(LOW)
            dp_v[at, 2 * width + lane : 2 * width + lane + 128] = mm(soft, d_stack).astype(LOW)
    vec_v[3:4, :] = col_sum(dp_v[:, :width].astype(F32))
    vec_v[4:5, :] = col_sum(dp_v[:, 2 * width :].astype(F32))
    moves.store(vec_v, vec_out)
    if tower.shared:
        store_sides(dp_v, 3 * width // 2, dp_out, width // 2, core_at, moves)
    else:
        moves.store(dp_v, dp_out[0])
    d_input = du_v[...]
    for part in range(3):
        got["weights"][part].wait()
        d_input = d_input + mm_nt(dp_v[:, part * width : (part + 1) * width], w_qkv[part])
    dx_v[...] = d_input.astype(dx_v.dtype)
    moves.store(dx_v, dx_out)


def backward_layer(
    tower, layer, upstream, first_rows, kept, low_out, after=(), cost=0, through=()
):
    count, width, wide = tower.count, tower.width, tower.wide
    steps = wide // width
    seeded = first_rows is not None
    out_type = LOW if low_out else F32
    wide_shapes = wide_scratch(tower, upstream)

    def kernel(ins, outs, scratch, moves):
        ins = list(ins)
        info, up_any = ins.pop(0), ins.pop(0)
        first_ref = ins.pop(0) if seeded else None
        own = [ins.pop(0) for _ in range(4)]
        other = [ins.pop(0) for _ in range(4)] if tower.shared else [None] * 4
        slope_any, hat2_any, inv_any, qkv_any, hat1_any, soft_any = (
            ins.pop(0) for _ in range(6)
        )
        first, second = scratch[: len(wide_shapes)], scratch[len(wide_shapes) :]
        dx, vec1, vec2 = outs[:3]
        if tower.shared:
            dh, df = outs[3:5], outs[5:7]
            dz = dp = df
        else:
            df, dh, dz, dp = (outs[at : at + 1] for at in range(3, 7))
        given = (up_any, own[2:], other[2:], slope_any, hat2_any, inv_any)
        wide_got = wide_fetch(tower, layer, info, given, seeded, first, moves)
        given = (own[:2], other[:2], qkv_any, hat1_any, inv_any, soft_any)
        got = narrow_fetch(tower, layer, info, given, second, moves)
        wide_body(
            tower, layer, info, wide_got, first_ref, ins, first, (vec1, df, dh), moves
        )
        narrow_body(
            tower, layer, info, got, first[6], ins, second, (dx, vec2, dz, dp), moves
        )
        moves.drain()

    outs = [((count, width), out_type), ((8, width), F32), ((8, width), F32)]
    if tower.shared:
        outs += [((count, wide // 2), LOW)] * 2 + [((count, 5 * width // 2), LOW)] * 2
    else:
        outs += [((count, width), LOW), ((steps, count, width), LOW)]
        outs += [((count, width), LOW), ((count, 3 * width), LOW)]
    inputs = [(SCALARS, tower.info), (ANYWHERE, upstream)]
    if seeded:
        inputs.append((INSIDE, first_rows))
    inputs += [(ANYWHERE, array) for array in tower.given((0, 1, 2, 3))]
    inputs += [(ANYWHERE, kept[at]) for at in (SLOPE, HAT2, INVERSES, PROJECTED, HAT1, SOFT)]
    inputs += [(INSIDE, array) for array in tower.given_small()]
    return call_kernel(
        kernel,
        "backward_layer",
        inputs,
        outs,
        wide_shapes + narrow_scratch(tower, out_type),
        3 + 3 * steps + 8 + 3 + steps + 6,
        cost,
        list(after),
        through,
    )


def place_rows(target, block, info, first, size, columns):
    for piece in range(block.shape[0] // size):
        at = pl.multiple_of(info[first + piece] * size, size)
        target[pl.ds(at, size), columns] = block[piece * size : (piece + 1) * size].astype(LOW)


def passage_products(
    tower, layer, rows, lefts, other_lefts, rights, other_rights, vectors, after=(), cost=0
):
    count, width, wide = tower.count, tower.width, tower.wide
    steps = wide // width
    half = width // 2
    piece = width // BLOCKS
    layout = LAYOUTS[layer]
    chunks = 1 + max(chunk for chunk, _ in layout)
    widths = [
        max(column + (wide // 2 if at < 2 else width) for at, (to, column) in enumerate(layout) if to == chunk)
        for chunk in range(chunks)
    ]
    vector_column = widths[0]
    if vectors:
        widths[0] += 128
    whole = rows is not None

    def kernel(ins, outs, scratch, moves):
        ins = list(ins)
        info = ins.pop(0)
        x_any = ins.pop(0) if whole else None
        vector_refs = [ins.pop() for _ in vectors]
        left, other_left = ins[:2]
        hidden_of, rights_of = (ins[2], ins[4]), (ins[3], ins[5])
        low_v, dh_v, act_v, df_v, x_v, dp_v, mix_v, dz_v = scratch[:8]
        grads = scratch[8:]
        above, below = pl.ds(0, count), pl.ds(count, count)

        def both(sources, column, target):
            columns = pl.ds(column, target.shape[1])
            return [
                moves.fetch(sources[0].at[:, columns], target.at[above]),
                moves.fetch(sources[1].at[:, columns], target.at[below]),
            ]

        lefts_of = (left, other_left)
        got_low = both(lefts_of, width, low_v)
        got_dh = [both(hidden_of, at * width, dh_v.at[at]) for at in range(steps // 2)]
        got_df = both(rights_of, 0, df_v)
        got_act = [both(lefts_of, (2 + at) * width, act_v.at[at]) for at in range(steps)]
        if whole:
            start = tower.row_start(info)
            other_start = pl.multiple_of(count - start, count)
            got_x = [
                moves.fetch(x_any.at[pl.ds(start, count)], x_v.at[above]),
                moves.fetch(x_any.at[pl.ds(other_start, count)], x_v.at[below]),
            ]
        else:
            got_x = both(lefts_of, 2 * width + wide, x_v)
        got_x += both(rights_of, half, dp_v)
        got_mix = both(lefts_of, 0, mix_v) + both(rights_of, 2 * width, dz_v)

        def ready(copies):
            for copy in copies:
                copy.wait()

        def target(part):
            chunk, column = layout[part]
            return grads[chunk], column, PLACES + BLOCKS * (3 * layer + chunk)

        def send(part):
            source, column, _ = target(part)
            cut = source.shape[0] // 2
            columns = pl.ds(column, wide // 2 if part < 2 else width)
            to = 2 * layout[part][0]
            moves.store(source.at[pl.ds(cut, cut), columns], outs[to].at[:, columns])
            moves.store(source.at[pl.ds(0, cut), columns], outs[to + 1].at[:, columns])

        if vectors:
            lane = slice(vector_column, vector_column + 128)
            for block in range(BLOCKS):
                from_rows = slice(block * PIECE_ROWS, (block + 1) * PIECE_ROWS)
                begin = block * piece
                grads[0][begin : begin + PIECE_ROWS, lane] = (
                    vector_refs[0][from_rows, :] + vector_refs[1][from_rows, :]
                ).astype(LOW)
                grads[0][begin + PIECE_ROWS : begin + piece, lane] = jnp.zeros(
                    (piece - PIECE_ROWS, 128), LOW
                )
            cut = width // 2
            columns = pl.ds(vector_column, 128)
            moves.store(grads[0].at[pl.ds(cut, cut), columns], outs[0].at[:, columns])
            moves.store(grads[0].at[pl.ds(0, cut), columns], outs[1].at[:, columns])
        ready(got_low)
        for at in range(steps // 2):
            ready(got_dh[at])
            to, column, first = target(1)
            columns = slice(column + at * width, column + (at + 1) * width)
            place_rows(to, mm_tn(low_v[...], dh_v[at]), info, first, piece, columns)
        send(1)
        ready(got_df)
        parts = wide // width
        for at in range(steps):
            ready(got_act[at])
            product = mm_tn(act_v[at], df_v[...])
            for block in range(width // piece):
                index, part = divmod(at * (width // piece) + block, parts)
                to, column, first = target(0)
                rows_to = pl.ds(pl.multiple_of(info[first + index] * piece, piece), piece)
                column += part * half
                to[rows_to, column : column + half] = product[
                    block * piece : (block + 1) * piece
                ].astype(LOW)
        send(0)
        ready(got_x)
        for part in range(4):
            if part == 3:
                ready(got_mix)
                product = mm_tn(mix_v[...], dz_v[...])
            else:
                product = mm_tn(x_v[...], dp_v[:, part * half : (part + 1) * half])
            to, column, first = target(2 + part // 2)
            column += part % 2 * half
            place_rows(to, product, info, first, piece, slice(column, column + half))
            if part % 2:
                send(2 + part // 2)
        moves.drain()

    outs = [((half, columns), LOW) for columns in widths for _ in range(2)]
    scratch = [
        ((2 * count, width), LOW),
        ((steps // 2, 2 * count, width), LOW),
        ((steps, 2 * count, width), LOW),
        ((2 * count, half), LOW),
        ((2 * count, width), LOW),
        ((2 * count, 3 * half), LOW),
        ((2 * count, width), LOW),
        ((2 * count, half), LOW),
    ] + [((width, columns), LOW) for columns in widths]
    arrays = [rows] if whole else []
    arrays += [lefts, other_lefts, *rights, *other_rights]
    inputs = [(SCALARS, tower.info)] + [(ANYWHERE, array) for array in arrays]
    inputs += [(INSIDE, array) for array in vectors]
    return call_kernel(
        kernel,
        "passage_products",
        inputs,
        outs,
        scratch,
        2 * (1 + steps // 2 + 1 + steps + 4) + 10,
        cost,
        list(after),
    )


def block_chooser(rows, columns, valid, size, bit):
    at = lax.broadcasted_iota(jnp.int32, (1, columns), 1)
    piece = jnp.floor((at.astype(F32) + 0.5) * (1.0 / size)).astype(jnp.int32)
    wanted = jnp.where(at < valid, at + (piece + bit) * size, -1)
    row_at = lax.broadcasted_iota(jnp.int32, (rows, columns), 0)
    return jnp.where(row_at == wanted, 1.0, 0.0).astype(LOW)


def pack_first(info, early, late, after=(), cost=0):
    count, width = early[0].shape
    steps = early[2].shape[0]
    wide = steps * width
    half = width // 2
    piece = width // BLOCKS
    keeps = (half + 3 * half, 2 * wide // 2)
    wholes = (2 * width, 2 * width)

    def kernel(ins, outs, scratch, moves):
        info_ref = ins[0]
        first, second = ins[1:7], ins[7:13]
        x_v, left_v, dh_v, df_v, dz_v, dp_v = scratch[:6]
        results = scratch[6:]
        flag = info_ref[IS_FIRST] == 1
        got = [moves.fetch_either(flag, a, b, to) for a, b, to in zip(first, second, scratch)]
        bits = [(info_ref[at], 1 - info_ref[at]) for at in (X_BIT, Y_BIT)]
        for copy in got:
            copy.wait()

        def lanes(bit, size):
            return pl.ds(pl.multiple_of(bit * size, 128), size)

        for which in range(2):
            first_to, second_to = results[which], results[2 + which]
            bit = bits[0][which]
            choose = block_chooser(width, half, half, piece, bit)
            first_to[:, :half] = mm(left_v[:, :width], choose).astype(LOW)
            first_to[:, half : 4 * half] = dp_v[:, lanes(bit, 3 * half)]
            bit = bits[1][which]
            for step in range(steps):
                start = (2 + step) * width + bit * half
                second_to[:, step * half : (step + 1) * half] = left_v[
                    :, pl.ds(pl.multiple_of(start, 128), half)
                ]
            for step in range(steps // 2):
                begin = wide // 2 + step * width
                second_to[:, begin : begin + width] = dh_v[bit * (steps // 2) + step]
        results[1][:, keeps[0] : keeps[0] + width] = x_v[...]
        results[1][:, keeps[0] + width :] = dz_v[...]
        results[3][:, keeps[1] : keeps[1] + width] = left_v[:, width : 2 * width]
        results[3][:, keeps[1] + width :] = df_v[...]
        for at in range(4):
            moves.store(results[at], outs[at])
        moves.drain()

    outs = []
    for keep, rest in zip(keeps, wholes):
        outs += [((count, keep), LOW), ((count, keep + rest), LOW)]
    inputs = [(SCALARS, info)] + [(ANYWHERE, array) for array in tuple(early) + tuple(late)]
    scratch = [(array.shape, LOW) for array in early]
    return call_kernel(
        kernel, "pack_first", inputs, outs, scratch + outs, 12, cost, list(after)
    )


def pack_second(info, keeps, sends, arrivals, width, after=(), cost=0):
    count = keeps[0].shape[0]
    wide = keeps[1].shape[1]
    half, quarter, third = width // 2, width // 4, 256
    piece = width // BLOCKS
    chosen = (third + half, half + wide // 4)
    wholes = (3 * half + width, wide // 2 + width)

    def kernel(ins, outs, scratch, moves):
        info_ref = ins[0]
        got = [moves.fetch(source, to) for source, to in zip(ins[1:], scratch)]
        bits = [(info_ref[at], 1 - info_ref[at]) for at in (Y_BIT, X_BIT)]
        for copy in got:
            copy.wait()
        for lot in range(2):
            keep_v, send_v, arrived_v = scratch[lot], scratch[2 + lot], scratch[4 + lot]
            cut = keep_v.shape[1]
            sources = (
                (slice(0, count), keep_v, send_v),
                (slice(count, 2 * count), arrived_v, arrived_v),
            )
            for which in range(2):
                target = scratch[6 + 2 * lot + which]
                bit = bits[lot][which]
                if lot == 0:
                    narrow = block_chooser(half, third, quarter, piece, bit)
                    broad = block_chooser(width, half, half, 2 * piece, bit)
                else:
                    narrow = block_chooser(width, half, half, piece, bit)
                    broad = block_chooser(2 * half, half, half, quarter, bit)
                for rows, halved, whole in sources:
                    if lot == 0:
                        target[rows, :third] = mm(halved[:, :half], narrow).astype(LOW)
                        target[rows, third:chosen[0]] = mm(
                            whole[:, cut : cut + width], broad
                        ).astype(LOW)
                        continue
                    target[rows, :half] = mm(whole[:, cut : cut + width], narrow).astype(LOW)
                    for part in range(wide // 2 // width):
                        target[rows, half + part * half : half + (part + 1) * half] = mm(
                            halved[:, part * width : (part + 1) * width], broad
                        ).astype(LOW)
            target = scratch[6 + 2 * lot + 1]
            begin = chosen[lot]
            first = half if lot == 0 else wide // 2
            for rows, halved, whole in sources:
                target[rows, begin : begin + cut - first] = halved[:, first:cut]
                target[rows, begin + cut - first :] = whole[:, cut + width :]
        for at in range(4):
            moves.store(scratch[6 + at], outs[at])
        moves.drain()

    outs = []
    for left, right in zip(chosen, wholes):
        outs += [((2 * count, left), LOW), ((2 * count, left + right), LOW)]
    arrays = tuple(keeps) + tuple(sends) + tuple(arrivals)
    inputs = [(SCALARS, info)] + [(ANYWHERE, array) for array in arrays]
    scratch = [(array.shape, LOW) for array in arrays]
    return call_kernel(
        kernel, "pack_second", inputs, outs, scratch + outs, 10, cost, list(after)
    )


def query_products(info, keeps, sends, arrivals, width, wide, after=(), cost=0):
    count = keeps[0].shape[0]
    half, third = width // 2, 256
    piece = width // BLOCKS
    packed = [keep.shape[1] for keep in keeps]
    rights = [send.shape[1] - left for send, left in zip(sends, packed)]
    columns = 4 * width + 2 * wide

    def kernel(ins, outs, scratch, moves):
        info_ref = ins[0]
        keep_any, send_any, arrived_any = ins[1:3], ins[3:5], ins[5:7]
        left_v, right_v, result = scratch[0:2], scratch[2:4], scratch[4]
        got = []
        for lot in range(2):
            cut = packed[lot]
            below = pl.ds(count, count)
            got.append(
                [
                    moves.fetch(keep_any[lot], left_v[lot].at[pl.ds(0, count)]),
                    moves.fetch(arrived_any[lot].at[:, pl.ds(0, cut)], left_v[lot].at[below]),
                    moves.fetch(
                        send_any[lot].at[:, pl.ds(cut, rights[lot])],
                        right_v[lot].at[pl.ds(0, count)],
                    ),
                    moves.fetch(
                        arrived_any[lot].at[:, pl.ds(cut, rights[lot])], right_v[lot].at[below]
                    ),
                ]
            )

        def place(z, rows, column):
            row = pl.multiple_of(info_ref[Z_PLACES + z] * piece, piece)
            result[pl.ds(row, piece), column : column + rows.shape[1]] = rows.astype(LOW)

        for copy in got[0]:
            copy.wait()
        for part in range(3):
            product = mm_tn(
                left_v[0][:, third:], right_v[0][:, part * half : (part + 1) * half]
            )
            for block in range(8):
                z, bit = divmod(block, 2)
                place(
                    z,
                    product[block * piece : (block + 1) * piece],
                    bit * 3 * half + part * half,
                )
        product = mm_tn(left_v[0][:, :third], right_v[0][:, 3 * half :])
        for z in range(4):
            place(z, product[z * piece : (z + 1) * piece], 3 * width)
        for copy in got[1]:
            copy.wait()
        at = 4 * width
        for part in range(wide // 2 // width):
            product = mm_tn(
                left_v[1][:, :half], right_v[1][:, part * width : (part + 1) * width]
            )
            for block in range(8):
                z, bit = divmod(block, 2)
                place(
                    z,
                    product[block * piece : (block + 1) * piece],
                    at + bit * (wide // 2) + part * width,
                )
        at += wide
        product = mm_tn(left_v[1][:, half:], right_v[1][:, wide // 2 :])
        per = wide // width
        for z in range(4):
            for part in range(per):
                begin = (z * per + part) * piece
                place(z, product[begin : begin + piece], at + part * width)
        moves.store(result.at[pl.ds(2 * piece, 2 * piece)], outs[0])
        moves.store(result.at[pl.ds(0, 2 * piece)], outs[1])
        moves.drain()

    outs = [((2 * piece, columns), LOW)] * 2
    arrays = tuple(keeps) + tuple(sends) + tuple(arrivals)
    inputs = [(SCALARS, info)] + [(ANYWHERE, array) for array in arrays]
    scratch = [((2 * count, cut), LOW) for cut in packed]
    scratch += [((2 * count, cut), LOW) for cut in rights]
    scratch += [((4 * piece, columns), LOW)]
    return call_kernel(
        kernel, "query_products", inputs, outs, scratch, 10, cost, list(after)
    )


PIECE_ROWS = 32


def vector_pieces(info, first, parts, wide, after=(), cost=0):
    width = parts[0].shape[1]
    cut = width // BLOCKS
    big = wide // BLOCKS

    def kernel(ins, outs, scratch, moves):
        info_ref = ins[0]
        refs = ins[1:]
        early = info_ref[IS_FIRST] == 1
        for target in scratch:
            target[...] = jnp.zeros_like(target)

        def lay(target, tower_at, wide_rows, narrow_rows):
            eight = jnp.concatenate([wide_rows[0:3], narrow_rows[0:5]], axis=0)
            for block in range(BLOCKS):
                at = info_ref[PLACES + first + block] * PIECE_ROWS + 16 * tower_at
                at = pl.multiple_of(at, 16)
                target[pl.ds(at, 8), 0:cut] = eight[:, block * cut : (block + 1) * cut]
                row, column = divmod(block * big, width)
                bias = wide_rows[3 + row : 4 + row, column : column + big]
                target[pl.ds(at + 8, 1), 0:128] = bias[:, 0:128]
                target[pl.ds(at + 9, 1), 0 : big - 128] = bias[:, 128:big]

        send, keep = scratch
        eq1, eq2, lq1, lq2, ep1, ep2, lp1, lp2 = (ref[...] for ref in refs)
        lay(keep, 0, jnp.where(early, eq1, lq1), jnp.where(early, eq2, lq2))
        lay(keep, 1, jnp.where(early, ep1, lp1), jnp.where(early, ep2, lp2))
        lay(send, 1, jnp.where(early, lp1, ep1), jnp.where(early, lp2, ep2))
        moves.store(send, outs[0])
        moves.store(keep, outs[1])
        moves.drain()

    outs = [((BLOCKS * PIECE_ROWS, 128), F32)] * 2
    inputs = [(SCALARS, info)] + [(INSIDE, array) for array in parts]
    return call_kernel(kernel, "vector_pieces", inputs, outs, outs, 2, cost, list(after))


def take_in(items, after=(), cost=0, through=()):
    def kernel(ins, outs, scratch, moves):
        ins, scratch = list(ins), list(scratch)
        taken = []
        for pairs, last in items:
            got = []
            for _ in pairs:
                held = [scratch.pop(0), scratch.pop(0)]
                got.append((held, [moves.fetch(ins.pop(0), to) for to in held]))
            taken.append((got, [scratch.pop(0) for _ in range(1 if last else 2)]))
        out_at = 0
        for (got, results), (_, last) in zip(taken, items):
            for held, copies in got:
                for copy in copies:
                    copy.wait()
            for which, result in enumerate(results):
                part_rows = result.shape[0]
                start = 0 if last else (1 - which) * part_rows
                column = 0
                for (keep_v, arrived_v), _ in got:
                    columns = keep_v.shape[1]
                    chunk = 48 if columns <= 1536 and part_rows % 48 == 0 else 16

                    def one(step, carry, keep_v=keep_v, arrived_v=arrived_v, column=column):
                        to = pl.ds(pl.multiple_of(step * chunk, 16), chunk)
                        of = pl.ds(pl.multiple_of(start + step * chunk, 16), chunk)
                        total = keep_v[of, :].astype(F32) + arrived_v[of, :].astype(F32)
                        result[to, column : column + keep_v.shape[1]] = total.astype(result.dtype)
                        return carry

                    lax.fori_loop(0, part_rows // chunk, one, 0)
                    column += columns
                moves.store(result, outs[out_at])
                out_at += 1
        moves.drain()

    outs, scratch = [], []
    for pairs, last in items:
        rows = pairs[0][0].shape[0]
        columns = sum(keep.shape[1] for keep, _ in pairs)
        kind = pairs[0][0].dtype
        mine = [((rows, columns), F32)] if last else [((rows // 2, columns), kind)] * 2
        outs += mine
        for keep, arrived in pairs:
            scratch += [(keep.shape, kind), (arrived.shape, kind)]
        scratch += mine
    inputs = [(ANYWHERE, array) for pairs, _ in items for pair in pairs for array in pair]
    return call_kernel(
        kernel, "take_in", inputs, outs, scratch, len(inputs) + len(outs), cost, list(after), through
    )


def take_in_quarters(pairs, after=(), cost=0, through=()):
    rows = pairs[0][0].shape[0] // 4
    columns = sum(keep.shape[1] for keep, _ in pairs)

    def kernel(ins, outs, scratch, moves):
        held = scratch[: len(ins)]
        results = scratch[len(ins) :]
        got = [moves.fetch(source, to) for source, to in zip(ins, held)]
        for copy in got:
            copy.wait()
        for quarter in (1, 2, 3, 0):
            result = results[quarter]
            column = 0
            for at in range(len(pairs)):
                keep_v, arrived_v = held[2 * at : 2 * at + 2]
                wide = keep_v.shape[1]

                def one(step, carry, keep_v=keep_v, arrived_v=arrived_v, column=column, wide=wide):
                    to = pl.ds(pl.multiple_of(step * 16, 16), 16)
                    of = pl.ds(pl.multiple_of(quarter * rows + step * 16, 16), 16)
                    total = keep_v[of, :].astype(F32) + arrived_v[of, :].astype(F32)
                    result[to, column : column + wide] = total.astype(LOW)
                    return carry

                lax.fori_loop(0, rows // 16, one, 0)
                column += wide
            moves.store(result, outs[quarter])
        moves.drain()

    outs = [((rows, columns), LOW)] * 4
    arrays = [array for pair in pairs for array in pair]
    inputs = [(ANYWHERE, array) for array in arrays]
    scratch = [(array.shape, LOW) for array in arrays]
    return call_kernel(
        kernel,
        "take_in_quarters",
        inputs,
        outs,
        scratch + outs,
        len(arrays) + 4,
        cost,
        list(after),
        through,
    )


class Chain:
    def __init__(self, send, keep, order, scale, from_core=False):
        self.order = list(order)
        self.scale = scale
        self.keep = keep
        self.total = None
        self.arrived = core_swap(send) if from_core else self.swap(send)

    def swap(self, block):
        return flip_swap(block, self.order.pop(0) * self.scale)


def play_round(groups, after=(), cost=0, through=()):
    items = [
        ([(chain.keep, chain.arrived) for chain in group], not group[0].order) for group in groups
    ]
    results = list(take_in(items, after, cost, through))
    seen = []
    for group in groups:
        chain = group[0]
        assert all(other.order == chain.order for other in group)
        if not chain.order:
            chain.total = results.pop(0)
            seen.append(chain.total)
            continue
        sent, chain.keep = results.pop(0), results.pop(0)
        chain.arrived = chain.swap(sent)
        seen.append(sent)
    return tuple(seen + results)


def last_round(info, quarters, other_total, vector_column, after=(), cost=0):
    rows, columns = other_total.shape
    begin = vector_column

    def kernel(ins, outs, scratch, moves):
        info_ref = ins[0]
        parts, late_v = scratch[:4], scratch[4]
        own_v, send_v, vec_v = scratch[5:]
        got = [moves.fetch(source, to) for source, to in zip(ins[1:], scratch)]
        for copy in got:
            copy.wait()
        flag = info_ref[IS_FIRST] == 1

        def total(part, lanes):
            values = [ref[part, lanes].astype(F32) for ref in parts]
            return (values[0] + values[1]) + (values[2] + values[3])

        vec_v[...] = total(slice(0, rows), slice(begin, begin + 128))
        moves.store(vec_v, outs[2])
        for row in range(0, rows, 16):
            part = slice(row, row + 16)
            for lanes, of in (
                (slice(0, begin), slice(0, begin)),
                (slice(begin, columns), slice(begin + 128, columns + 128)),
            ):
                early = total(part, of)
                late = late_v[part, lanes]
                send_v[part, lanes] = jnp.where(flag, late, early).astype(LOW)
                own_v[part, lanes] = jnp.where(flag, early, late)
        moves.store(send_v, outs[1])
        moves.store(own_v, outs[0])
        moves.drain()

    outs = [((rows, columns), F32), ((rows, columns), LOW), ((rows, 128), F32)]
    arrays = (*quarters, other_total)
    inputs = [(SCALARS, info)] + [(ANYWHERE, array) for array in arrays]
    scratch = [(array.shape, array.dtype) for array in arrays]
    return call_kernel(
        kernel, "last_round", inputs, outs, scratch + outs, 8, cost, list(after)
    )


def output_shapes(rows, width, wide):
    return [
        ((2, rows, 3 * width), F32),
        ((2, rows, width), F32),
        ((2, rows, wide), F32),
        ((2, wide // width * rows, width), F32),
    ]


def query_outputs(info, query, query_x, query_y, width, wide, after=(), cost=0):
    rows = query.shape[0]
    half = width // 2
    parts = wide // width

    def kernel(ins, outs, scratch, moves):
        info_ref = ins[0]
        sources, results = scratch[:3], scratch[3:]
        got = [moves.fetch(source, to) for source, to in zip(ins[1:], sources)]
        query_v, x_v, y_v = sources
        g_qkv, g_out, g_up, g_down = results
        for copy in got:
            copy.wait()
        at = 4 * width
        for bit_at, begin, size, arrived, target in (
            (X_BIT, 0, 3 * half, x_v, g_qkv),
            (Y_BIT, at, wide // 2, y_v, g_up),
        ):
            bit = info_ref[bit_at]
            mine = pl.ds(pl.multiple_of(bit * size, 128), size)
            others = pl.ds(pl.multiple_of((1 - bit) * size, 128), size)
            target[:, mine] = query_v[:, pl.ds(pl.multiple_of(begin + bit * size, 128), size)]
            target[:, others] = arrived[...]
        g_out[...] = query_v[:, 3 * width : 4 * width]
        at += wide
        for part in range(parts):
            g_down[part * rows : (part + 1) * rows, :] = query_v[
                :, at + part * width : at + (part + 1) * width
            ]
        for result, to in zip(results, outs):
            moves.store(result, to.at[0])
        moves.drain()

    outs = output_shapes(rows, width, wide)
    arrays = (query, query_x, query_y)
    inputs = [(SCALARS, info)] + [(ANYWHERE, array) for array in arrays]
    scratch = [(array.shape, F32) for array in arrays] + [(shape[1:], F32) for shape, _ in outs]
    return call_kernel(
        kernel, "query_outputs", inputs, outs, scratch, 7, cost, list(after)
    )


def passage_outputs(info, own, other, outputs, width, wide):
    rows, columns = own.shape
    half = width // 2
    parts = wide // width
    chunk_width = columns // 2
    begin = [to * chunk_width + column for to, column in LAYOUTS[0]]

    def kernel(ins, outs, scratch, moves):
        info_ref = ins[0]
        sources, results = scratch[:2], scratch[2:]
        got = [moves.fetch(source, to) for source, to in zip(ins[1:], sources)]
        g_qkv, g_out, g_up, g_down = results
        core = info_ref[CORE]
        for at, side in ((0, core), (1, 1 - core)):
            got[at].wait()
            source = sources[at]
            here = pl.ds(pl.multiple_of(side * half, 128), half)
            for part in range(parts):
                g_down[part * rows : (part + 1) * rows, here] = source[
                    :, begin[0] + part * half : begin[0] + (part + 1) * half
                ].astype(F32)
            up = pl.ds(pl.multiple_of(side * (wide // 2), 128), wide // 2)
            g_up[:, up] = source[:, begin[1] : begin[1] + wide // 2].astype(F32)
            for third in range(3):
                column = begin[2 + third // 2] + third % 2 * half
                to = pl.ds(pl.multiple_of(side * 3 * half + third * half, 128), half)
                g_qkv[:, to] = source[:, column : column + half].astype(F32)
            g_out[:, here] = source[:, begin[3] + half : begin[3] + width].astype(F32)
        for result, to in zip(results, outs):
            moves.store(result, to.at[1])
        moves.drain()

    shapes = output_shapes(rows, width, wide)
    arrays = (own, other)
    inputs = [(SCALARS, info)] + [(ANYWHERE, array) for array in arrays]
    scratch = [(array.shape, array.dtype) for array in arrays]
    scratch += [(shape[1:], F32) for shape, _ in shapes]
    return call_kernel(
        kernel, "passage_outputs", inputs, [], scratch, 6, 0, [], tuple(outputs)
    )


def pick_bit(grid, axis, index):
    return lax.dynamic_index_in_dim(grid, index, axis, keepdims=False)


def own_bit(bit):
    return (lax.axis_index("batch") // bit) % 2


def scatter_sum(grid, bits, left):
    left = list(left)
    for bit in bits:
        axis = left.index(bit)
        mine = own_bit(bit)
        sent = pick_bit(grid, axis, 1 - mine)
        kept = pick_bit(grid, axis, mine)
        arrived = flip_swap(sent, bit)
        total = kept.astype(jnp.float32) + arrived.astype(jnp.float32)
        left.remove(bit)
        grid = total if not left else total.astype(grid.dtype)
    return grid


def all_bits(size):
    bits = [1 << i for i in range(size.bit_length() - 1)]
    return bits[::-1]


def to_grid(array, size):
    bits = all_bits(size)
    return array.reshape((2,) * len(bits) + (array.shape[0] // size,) + array.shape[1:])


def gather_all(block, size):
    if size != 16:
        for bit in all_bits(size)[::-1]:
            block = jnp.concatenate([block, flip_swap(block, bit)], 0)
        return block
    block = jnp.concatenate([block] + [flip_swap(block, k) for k in (1, 2, 3)], 0)
    return jnp.concatenate([block] + [flip_swap(block, k) for k in (4, 8, 12)], 0)


def contrast(own_cls, micro, positive, query_count, batch_index, batch_size):
    width = own_cls.shape[1]
    chip_rows = own_cls.shape[0]
    gathered = gather_all(own_cls, batch_size).reshape(batch_size, chip_rows, width)
    all_q = gathered[:, :query_count].reshape(-1, width)
    all_p = gathered[:, query_count:].reshape(-1, width)
    blocks = jnp.arange(batch_size, dtype=jnp.int32) ^ batch_index
    query_ids = (
        blocks[:, None] * query_count + jnp.arange(query_count, dtype=jnp.int32)[None, :]
    ).reshape(-1)
    passage_ids = (
        3 * query_ids[:, None] + jnp.arange(3, dtype=jnp.int32)[None, :]
    ).reshape(-1)
    labels = jnp.take(micro, query_ids)
    wanted = jnp.take(positive, query_ids)
    logit_scale = LOGIT_GAIN * width ** (-0.5)
    logits = mm_nt(all_q, all_p) * logit_scale
    same_group = labels[:, None] == jnp.repeat(labels, 3)[None, :]
    logits = jnp.where(same_group, logits, MASK_FILL)
    row_top = jnp.max(logits, axis=-1, keepdims=True)
    exponent = jnp.exp(logits - row_top)
    totals = jnp.sum(exponent, axis=-1, keepdims=True)
    target = passage_ids[None, :] == wanted[:, None]
    loss_all = (
        row_top[:, 0] + jnp.log(totals[:, 0]) - jnp.sum(jnp.where(target, logits, 0.0), axis=-1)
    )
    coefficient = (exponent / totals - target.astype(jnp.float32)) * logit_scale
    passage_count = 3 * query_count
    d_cls_q = jnp.dot(coefficient[:query_count], all_p.astype(jnp.float32), precision=PRECISE)
    d_cls_p = lax.dot_general(
        coefficient[:, :passage_count],
        all_q.astype(jnp.float32),
        (((0,), (0,)), ((), ())),
        precision=PRECISE,
    )
    return loss_all[:query_count], d_cls_q, d_cls_p


def integers(core, index, size, len_q, len_p):
    blocks = jnp.arange(BLOCKS, dtype=jnp.int32)
    own = index // (size // BLOCKS)
    relative = blocks ^ own
    places = [
        sum(((relative // bit) % 2) * (8 >> at) for at, bit in enumerate(order))
        for order in ORDERS
    ]
    depth = jnp.arange(4, dtype=jnp.int32) ^ (own // 4)
    z_places = (depth % 2) * 2 + depth // 2
    few = jnp.stack([1 - core, core])
    ends = jnp.stack([own % 2, (own // 2) % 2])
    return jnp.concatenate([few, *places, z_places, ends, len_q, len_p]).astype(jnp.int32)


def shards(
    x_q,
    x_p,
    len_q,
    len_p,
    cot_q,
    cot_p,
    positive,
    micro,
    w_qkv,
    w_out,
    w_up,
    w_down,
    norm_gain,
    biases,
    b_up,
):
    core = lax.axis_index("section")
    is_first = core == 0
    batch_index = lax.axis_index("batch")
    size = lax.axis_size("batch")
    bits = all_bits(size)
    query_count, slots_q, model = x_q.shape
    half_count = x_p.shape[0] // 2
    slots_p = x_p.shape[1]
    wide = w_up.shape[-1]
    info = integers(core, batch_index, size, len_q, len_p)
    weights = (w_qkv, w_out, w_up, w_down)
    smalls = (norm_gain, biases, b_up)
    other_p = tuple(core_swap(member[0, 1]) for member in weights)
    small_other = core_swap(
        jnp.concatenate([norm_gain[0, 1], biases[0, 1], b_up[0, 1].reshape(-1, model)], 0)
    )
    tower_q = Tower(0, info, weights, None, smalls, None, query_count, slots_q, LENGTHS)
    tower_p = Tower(
        1, info, weights, other_p, smalls, small_other, half_count, slots_p, LENGTHS + query_count
    )
    flat_q = x_q.reshape(-1, model)
    flat_p = x_p.reshape(-1, model)
    cots_q = cot_q.reshape(-1, model)
    cots_p = cot_p.reshape(-1, model)

    early_q, _ = forward_layers(tower_q, (0,), flat_q, True, None)
    mid_q = early_q[OUTPUT]
    arrived_q = core_swap(mid_q)
    late_q, first_q = forward_layers(tower_q, (1,), arrived_q, True, None)
    early_p, late_p, cls_rows = forward_layers(
        tower_p, (0, 1), flat_p, True, (first_q, query_count)
    )
    mid_p = early_p[OUTPUT]
    top_q, top_p = late_q[OUTPUT], late_p[OUTPUT]

    last = query_count + half_count
    cls_other = core_swap(cls_rows)
    cls_chip = jnp.concatenate(
        [
            jnp.where(is_first, cls_other[:query_count], cls_rows[:query_count]),
            jnp.where(is_first, cls_rows[query_count:last], cls_other[query_count:last]),
            jnp.where(is_first, cls_other[query_count:last], cls_rows[query_count:last]),
        ],
        0,
    )
    loss_own, d_cls_q, d_cls_p = contrast(
        cls_chip, micro, positive, query_count, batch_index, size
    )

    def factors(rows, kept, back):
        return (rows, kept[LEFTS], back[4], back[3], back[5], back[6])

    scale = size // BLOCKS

    def core_products(
        layer, rows, lefts, other_lefts, back, other_rights, vectors, after, cost
    ):
        products = passage_products(
            tower_p, layer, rows, lefts, other_lefts, back[4::2], other_rights, vectors, after, cost
        )
        return products

    def chains_of(layer, products):
        return [
            Chain(products[2 * at], products[2 * at + 1], ORDERS[3 * layer + at], scale)
            for at in range(len(products) // 2)
        ]

    late_back_q = backward_layer(
        tower_q, 1, cots_q, d_cls_q, late_q, True, cost=0
    )
    late_sent_q = late_back_q[0]
    grad_mid_q = core_swap(late_sent_q)
    early_back_q = backward_layer(
        tower_q,
        0,
        grad_mid_q,
        None,
        early_q,
        False,
        cost=0,
        through=(late_p[LEFTS], early_p[LEFTS], jnp.where(is_first, top_p, mid_p)),
    )
    *early_back_q, late_left, early_left, hidden_sent = early_back_q
    late_left_other, early_left_other = core_swap(late_left), core_swap(early_left)
    hidden_other = core_swap(hidden_sent)
    packs = pack_first(
        info,
        factors(flat_q, early_q, early_back_q),
        factors(arrived_q, late_q, late_back_q),
        cost=0,
    )
    keeps, sends = packs[0::2], packs[1::2]
    arrivals = [flip_swap(sends[0], scale), flip_swap(sends[1], 2 * scale)]
    late_back_p = backward_layer(
        tower_p, 1, cots_p, d_cls_p, late_p, True, tuple(sends), cost=0
    )
    late_sent_p = late_back_p[0]
    late_other = [core_swap(array) for array in late_back_p[3::2]]
    packs = pack_second(
        info,
        keeps,
        sends,
        arrivals,
        model,
        (late_sent_p, late_left_other, early_left_other, hidden_other),
        cost=40,
    )
    keeps, sends = packs[0::2], packs[1::2]
    arrivals = [flip_swap(sends[0], 2 * scale), flip_swap(sends[1], scale)]
    products = core_products(
        1, None, late_left, late_left_other, late_back_p, late_other, (), tuple(sends), 0
    )
    a1, b1 = chains_of(1, products)
    send, keep = query_products(
        info, keeps, sends, arrivals, model, wide, tuple(products[:1]), cost=4
    )
    query = Chain(send, keep, (4, 8), scale)
    early_back_p = backward_layer(
        tower_p, 0, late_sent_p, None, early_p, False, (send,), cost=0
    )
    early_grad_p = early_back_p[0]
    early_other = [core_swap(array) for array in early_back_p[3::2]]
    vectors = (*early_back_q[1:3], *late_back_q[1:3], *early_back_p[1:3], *late_back_p[1:3])
    pieces = vector_pieces(info, 0, vectors, wide, (early_grad_p,), 0)
    vectors = (pieces[1], core_swap(pieces[0]))
    seen = play_round([[a1], [b1]], pieces[:1], 4)
    seen = play_round([[query]], seen, 40)
    products = core_products(
        0, flat_p, early_left, early_left_other, early_back_p, early_other, vectors, seen, 4
    )
    a0, b0 = chains_of(0, products)
    seen = (products[0],)
    others = (
        early_grad_p,
        late_sent_p,
        early_back_q[0],
        late_sent_q,
        mid_q,
        top_q,
        mid_p,
        top_p,
        hidden_other,
        loss_own[None],
    )
    rounds = (
        ([[a1, b1]], 40),
        ([[query]], 4),
        ([[a0], [b0]], 0),
        ([[a1]], 40),
        ("z", 4),
        ([[a1]], 12),
    )
    for step, (groups, cost) in enumerate(rounds):
        held = others if step == 2 else (query.total,) if step == len(rounds) - 1 else ()
        if groups == "z":
            parts = take_in_quarters([(chain.keep, chain.arrived) for chain in (a0, b0)], seen, cost)
            low, high = a0.order[0] * scale, a0.order[1] * scale
            quarters = (
                parts[0],
                flip_swap(parts[1], high),
                flip_swap(parts[2], low),
                flip_swap(parts[3], low + high),
            )
            seen = tuple(parts[1:])
            continue
        passed = play_round(groups, seen, cost, held)
        seen = passed[: len(passed) - len(held)]
        if step == 2:
            others = passed[-10:]
    early_grad_p, late_sent_p, early_grad_q, late_sent_q = others[:4]
    mid_q, top_q, mid_p, top_p, hidden_other, loss_own = others[4:]
    loss_own = loss_own[0]
    early_grad_other = core_swap(jnp.where(is_first, late_sent_p.astype(F32), early_grad_p))

    total_q = passed[-1]

    def other_half(begin, columns, bit):
        mine = (batch_index // (bit * scale)) % 2
        sent = lax.dynamic_slice_in_dim(total_q, begin + (1 - mine) * columns, columns, 1)
        return flip_swap(sent, bit * scale)

    query_x = other_half(0, 3 * model // 2, 1)
    query_y = other_half(4 * model, wide // 2, 2)
    outputs = query_outputs(info, total_q, query_x, query_y, model, wide, seen)
    own, sent, total_v = last_round(info, quarters, a1.total, model + wide // 2, seen)
    sums = passage_outputs(info, own, core_swap(sent), outputs, model, wide)
    if scale > 1:
        left = all_bits(scale)
        sums = [
            jnp.stack([scatter_sum(to_grid(tower.astype(LOW), scale), left, left) for tower in item])
            for item in sums
        ]
    g_qkv, g_out, g_up, g_down = sums

    total_v = total_v[:32].reshape(2, 16, 128)
    eight = total_v[:, :8, : model // BLOCKS]
    g_bup = total_v[:, 8:10].reshape(2, -1)[:, : wide // BLOCKS]
    if scale > 1:
        left = all_bits(scale)
        eight = scatter_sum(
            to_grid(jnp.moveaxis(eight, 2, 0).reshape(-1, 16), scale), left, left
        )
        eight = jnp.moveaxis(eight.reshape(-1, 2, 8), 0, 2)
        g_bup = scatter_sum(to_grid(g_bup.T, scale), left, left).T
    g_gain = jnp.stack([eight[:, 3], eight[:, 0]], 1)
    g_bias = jnp.stack([eight[:, at] for at in (6, 7, 5, 4, 2, 1)], 1)

    pairs = (
        jnp.where(is_first, mid_p, hidden_other),
        jnp.where(is_first, hidden_other, top_p),
    )
    hidden_p = jnp.concatenate(pairs, 0).reshape(x_p.shape)
    pairs = (
        jnp.where(is_first, early_grad_p, early_grad_other),
        jnp.where(is_first, early_grad_other, late_sent_p.astype(F32)),
    )
    grad_p = jnp.concatenate(pairs, 0).reshape(x_p.shape)
    hidden_q = jnp.where(is_first, mid_q, top_q).reshape(x_q.shape)
    grad_q = jnp.where(is_first, early_grad_q, late_sent_q.astype(F32)).reshape(x_q.shape)
    return (
        hidden_q[None],
        hidden_p[None],
        grad_q[None],
        grad_p[None],
        loss_own,
        g_qkv[None],
        g_out[None],
        g_up[None],
        g_down[None],
        g_gain[None],
        g_bias[None],
        g_bup[None],
        g_bias[None, :, 0, :],
    )


def solution(mesh):
    return jax.shard_map(
        shards,
        mesh=mesh,
        in_specs=(
            P("batch", None, None),
            P("batch", None, None),
            P("batch"),
            P("batch"),
            P("batch", None, None),
            P("batch", None, None),
            P(),
            P(),
            P("section", None, None, None),
            P("section", None, None, None),
            P("section", None, None, None),
            P("section", None, None, None),
            P("section", None, None, None),
            P("section", None, None, None),
            P("section", None, None),
        ),
        out_specs=(
            P("section", "batch", None, None),
            P("section", "batch", None, None),
            P("section", "batch", None, None),
            P("section", "batch", None, None),
            P("batch"),
            P("section", None, "batch", None),
            P("section", None, "batch", None),
            P("section", None, "batch", None),
            P("section", None, "batch", None),
            P("section", None, None, "batch"),
            P("section", None, None, "batch"),
            P("section", None, "batch"),
            P("section", None, "batch"),
        ),
        check_vma=False,
    )
```

```python
import jax
import jax.numpy as jnp
from jax import lax
from jax.experimental import pallas as pl
from jax.experimental.pallas import tpu as pltpu
from jax.sharding import PartitionSpec as P

HEADS = 12
HEAD_DIM = 64


NORM_EPS = 1e-05
SQRT_HALF = 0.7071067811865476
ROOT_TAU_INV = 0.3989422804014327
MASK_FILL = -1e30
LOGIT_GAIN = 2.5
PRECISE = lax.Precision.HIGHEST


def core_swap(block):
    return lax.ppermute(block, "section", [(0, 1), (1, 0)])


def flip_swap(block, bit):
    size = lax.axis_size("batch")
    return lax.ppermute(block, "batch", [(i, i ^ bit) for i in range(size)])


F32 = jnp.float32
LOW = jnp.bfloat16
VMEM_LIMIT = 63 * 1024 * 1024 + 512 * 1024
BLOCKS = 16
COST = 1 << 30
IS_FIRST, CORE, PLACES, Z_PLACES, X_BIT, Y_BIT, LENGTHS = 0, 1, 2, 98, 102, 103, 104
ORDERS = (
    (1, 2, 4, 8),
    (2, 1, 4, 8),
    (2, 1, 4, 8),
    (1, 2, 4, 8),
    (2, 1, 4, 8),
    (2, 1, 4, 8),
)

LAYOUTS = (((0, 0), (1, 0), (0, 1536), (1, 1536)), ((0, 0), (1, 0), (0, 1536), (1, 1536)))


def mm(left, right):
    return lax.dot_general(left, right, (((1,), (0,)), ((), ())), preferred_element_type=F32)


def mm_nt(left, right):
    return lax.dot_general(left, right, (((1,), (1,)), ((), ())), preferred_element_type=F32)


def mm_tn(left, right):
    return lax.dot_general(left, right, (((0,), (0,)), ((), ())), preferred_element_type=F32)


def row_mean(values):
    return jnp.sum(values, axis=-1, keepdims=True) * (1.0 / values.shape[-1])


def normed_rows(values):
    center = values - row_mean(values)
    inverse = lax.rsqrt(row_mean(center * center) + NORM_EPS)
    return center * inverse, inverse


def norm_pull(upstream, normed, inverse, gain):
    scaled = upstream * gain
    return inverse * (scaled - row_mean(scaled) - normed * row_mean(scaled * normed))


def col_sum(values):
    return jnp.sum(values, axis=0, keepdims=True)


class Moves:
    def __init__(self, sems):
        self.sems = sems
        self.used = 0
        self.open = []

    def slot(self):
        self.used += 1
        return self.sems.at[self.used - 1]

    def fetch(self, source, target):
        copy = pltpu.make_async_copy(source, target, self.slot())
        copy.start()
        return copy

    def fetch_either(self, flag, first, second, target):
        sem = self.slot()
        copy = pltpu.make_async_copy(first, target, sem)
        if second is None:
            copy.start()
            return copy
        other = pltpu.make_async_copy(second, target, sem)

        @pl.when(flag)
        def _():
            copy.start()

        @pl.when(jnp.logical_not(flag))
        def _():
            other.start()

        return copy

    def store(self, source, target):
        self.open.append(self.fetch(source, target))

    def drain(self):
        for copy in self.open:
            copy.wait()


class Tower:
    def __init__(self, index, info, weights, others, small, small_other, seqs, slots, first_len):
        self.index = index
        self.info = info
        self.weights = weights
        self.others = others
        self.small = small
        self.small_other = small_other
        self.seqs = seqs
        self.slots = slots
        self.first_len = first_len
        self.count = seqs * slots
        self.width = weights[1].shape[-1]
        self.wide = weights[2].shape[-1]
        self.group = self.count if self.count <= 128 else slots
        self.shared = others is not None

    def given(self, which):
        own = [self.weights[at] for at in which]
        return own + ([self.others[at] for at in which] if self.shared else [])

    def given_small(self):
        return list(self.small) + ([self.small_other] if self.shared else [])

    def use_own(self, info, layer):
        return info[IS_FIRST] == (1 if layer == 0 else 0)

    def lengths_at(self, info):
        return self.first_len + (info[CORE] * self.seqs if self.shared else 0)

    def row_start(self, info):
        return pl.multiple_of(info[CORE] * self.count, self.count) if self.shared else 0

    def small_rows(self, refs, flag):
        own = [refs[0][0, self.index], refs[1][0, self.index]]
        if self.shared:
            other = refs[3]
            own = [
                jnp.where(flag, own[0], other[0:2, :]),
                jnp.where(flag, own[1], other[2:8, :]),
            ]
        return own

    def hidden_bias(self, refs, flag, step, tile):
        own = refs[2][0, self.index : self.index + 1, step * tile : (step + 1) * tile]
        if self.shared:
            own = jnp.where(flag, own, refs[3][8 + step : 9 + step, :])
        return own


ANYWHERE = pl.BlockSpec(memory_space=pltpu.HBM)
SCALARS = pl.BlockSpec(memory_space=pltpu.SMEM)
INSIDE = pl.BlockSpec(memory_space=pltpu.VMEM)


def call_kernel(kernel, name, inputs, outs, scratch, copies, micros, after, through=()):
    count = len(inputs)
    given = list(after) + list(through)
    extra = len(given)

    def body(*refs):
        refs = list(refs)
        kernel(
            refs[:count],
            refs[count + extra : count + extra + len(outs)]
            or refs[count + extra : count + extra + len(through)],
            refs[count + extra + len(outs) + len(through) : -1],
            Moves(refs[-1]),
        )

    return pl.pallas_call(
        body,
        out_shape=[jax.ShapeDtypeStruct(shape, kind) for shape, kind in outs]
        + [jax.ShapeDtypeStruct(array.shape, array.dtype) for array in through],
        in_specs=[spec for spec, _ in inputs] + [ANYWHERE] * extra,
        out_specs=[ANYWHERE] * (len(outs) + len(through)),
        input_output_aliases={
            count + len(after) + at: len(outs) + at for at in range(len(through))
        },
        scratch_shapes=[pltpu.VMEM(shape, kind) for shape, kind in scratch]
        + [pltpu.SemaphoreType.DMA((copies,))],
        compiler_params=pltpu.CompilerParams(vmem_limit_bytes=VMEM_LIMIT),
        cost_estimate=pl.CostEstimate(
            flops=int(COST * micros) + 1024, bytes_accessed=1024, transcendentals=0
        ),
        name=name,
    )(*[array for _, array in inputs], *given)


def pair_masks(dtype):
    lanes = lax.broadcasted_iota(jnp.int32, (1, 128), 1)
    low = jnp.where(lanes < HEAD_DIM, 1.0, 0.0)
    return low.astype(dtype), (1.0 - low).astype(dtype)


def stacked_pair(block, low, high):
    return jnp.concatenate([block * low, block * high], axis=0)


def joined_pair(stacked, group):
    lanes = lax.broadcasted_iota(jnp.int32, (1, 128), 1)
    return jnp.where(lanes < HEAD_DIM, stacked[:group], stacked[group:])


def pair_softmax(query_stack, key_block, valid):
    scores = mm_nt(key_block, query_stack) * HEAD_DIM ** (-0.5)
    scores = jnp.where(valid, scores, MASK_FILL)
    exponent = jnp.exp(scores - jnp.max(scores, axis=0, keepdims=True))
    return exponent * (1.0 / jnp.sum(exponent, axis=0, keepdims=True))


def valid_keys(info, first_len, group, slots):
    keys = lax.broadcasted_iota(jnp.int32, (group, 2 * group), 0)
    queries = lax.broadcasted_iota(jnp.int32, (group, 2 * group), 1)
    seqs = group // slots
    if seqs == 1:
        return keys < info[first_len]
    queries = jnp.where(queries >= group, queries - group, queries)
    valid = None
    for j in range(seqs):
        low = j * slots
        inside = (
            (queries >= low)
            & (queries < low + slots)
            & (keys >= low)
            & (keys < low + info[first_len + j])
        )
        valid = inside if valid is None else valid | inside
    return valid


def weight_shapes(tower):
    width, steps = tower.width, tower.wide // tower.width
    return [
        ((3, width, width), LOW),
        ((width, width), LOW),
        ((steps, width, width), LOW),
        ((steps, width, width), LOW),
    ]


def fetch_narrow(tower, flag, own, other, targets, moves, order=(0, 1, 2, 3)):
    width = tower.width
    got = {}
    for part in order:
        if part == 3:
            got[3] = moves.fetch_either(flag, own[1].at[0, tower.index], other[1], targets[1])
            continue
        cols = pl.ds(part * width, width)
        second = other[0].at[:, cols] if tower.shared else None
        got[part] = moves.fetch_either(
            flag, own[0].at[0, tower.index, :, cols], second, targets[0].at[part]
        )
    return got


def fetch_step(tower, flag, own, other, targets, moves, step, at):
    width = tower.width
    part = pl.ds(pl.multiple_of(at * width, width), width)
    up, down = (other[0].at[:, part], other[1].at[part]) if tower.shared else (None, None)
    return (
        moves.fetch_either(flag, own[1].at[0, tower.index, part], down, targets[1].at[step]),
        moves.fetch_either(flag, own[0].at[0, tower.index, :, part], up, targets[0].at[step]),
    )


def kept_scratch(tower):
    count, width, wide = tower.count, tower.width, tower.wide
    steps = wide // width
    return [
        ((count, width), LOW),
        ((count, 3 * width), LOW),
        ((count, width), LOW),
        ((count, width), LOW),
        ((steps, count, width), LOW),
        ((steps, count, width), LOW),
        ((count, width), LOW),
        ((count, width), LOW),
        ((2, count, 128), F32),
        ((width // 128, count, 2 * tower.group), LOW),
    ]


OUTPUT, LEFTS, PROJECTED, SLOPE, HAT1, HAT2, INVERSES, SOFT = range(8)


def kept_shapes(tower, inner):
    count, width, wide = tower.count, tower.width, tower.wide
    steps = wide // width
    return [
        ((count, width), LOW),
        ((count, 2 * width + wide + (width if inner else 0)), LOW),
        ((count, 3 * width), LOW),
        ((steps, count, width), LOW),
        ((count, width), LOW),
        ((count, width), LOW),
        ((2, count, 128), F32),
        ((width // 128, count, 2 * tower.group), LOW),
    ]


def forward_body(
    tower, layer, info, x_v, got, weights, smalls, acc_v, kept, outs, moves, first_out=None
):
    count, width, group = tower.count, tower.width, tower.group
    w_qkv, w_out, w_up, w_down = weights
    out_v, qkv_v, mix_v, low_v, act_v, slope_v, hat1_v, hat2_v, inv_v, soft_v = kept
    use_own = tower.use_own(info, layer)
    gains, bias = tower.small_rows(smalls, use_own)
    x = x_v[...]
    for part in range(3):
        got[part].wait()
        block = mm(x, w_qkv[part])
        if part == 0:
            block = block + bias[0:1, :]
        if part == 2:
            block = block + bias[1:2, :]
        qkv_v[:, part * width : (part + 1) * width] = block.astype(LOW)
    moves.store(qkv_v, outs[PROJECTED])
    low, high = pair_masks(LOW)
    for g in range(count // group):
        at = slice(g * group, (g + 1) * group)
        valid = valid_keys(
            info, tower.lengths_at(info) + g * (group // tower.slots), group, tower.slots
        )
        for pair in range(width // 128):
            lane = pair * 128
            q2 = qkv_v[at, lane : lane + 128]
            k2 = qkv_v[at, width + lane : width + lane + 128]
            v2 = qkv_v[at, 2 * width + lane : 2 * width + lane + 128]
            soft = pair_softmax(stacked_pair(q2, low, high), k2, valid).astype(LOW)
            soft_v[pair, at, :] = soft
            mix_v[at, lane : lane + 128] = joined_pair(mm_tn(soft, v2), group).astype(LOW)
    moves.store(soft_v, outs[SOFT])
    moves.store(mix_v, outs[LEFTS].at[:, pl.ds(0, width)])
    got[3].wait()
    summed = x.astype(F32) + (mm(mix_v[...], w_out[...]) + bias[2:3, :])
    hat, inverse = normed_rows(summed)
    hat1_v[...] = hat.astype(LOW)
    inv_v[0] = jnp.broadcast_to(inverse, (count, 128))
    moves.store(hat1_v, outs[HAT1])
    first = hat * gains[0:1, :] + bias[3:4, :]
    low_v[...] = first.astype(LOW)
    moves.store(low_v, outs[LEFTS].at[:, pl.ds(width, width)])
    acc_v[...] = first + bias[4:5, :]
    for step in range(tower.wide // width):
        for copy in got[4 + step]:
            copy.wait()
        hidden = mm(low_v[...], w_up[step]) + tower.hidden_bias(smalls, use_own, step, width)
        cdf = 0.5 * (1.0 + lax.erf(hidden * SQRT_HALF))
        act = (hidden * cdf).astype(LOW)
        act_v[step] = act
        slope_v[step] = (
            cdf + hidden * (jnp.exp(-0.5 * hidden * hidden) * ROOT_TAU_INV)
        ).astype(LOW)
        moves.store(act_v.at[step], outs[LEFTS].at[:, pl.ds((2 + step) * width, width)])
        moves.store(slope_v.at[step], outs[SLOPE].at[step])
        acc_v[...] += mm(act, w_down[step])
    hat, inverse = normed_rows(acc_v[...])
    hat2_v[...] = hat.astype(LOW)
    moves.store(hat2_v, outs[HAT2])
    inv_v[1] = jnp.broadcast_to(inverse, (count, 128))
    moves.store(inv_v, outs[INVERSES])
    output = hat * gains[1:2, :] + bias[5:6, :]
    out_v[...] = output.astype(LOW)
    moves.store(out_v, outs[OUTPUT])
    if first_out is not None:
        first_v, to, above = first_out
        firsts = [output[at * tower.slots : at * tower.slots + 1, :] for at in range(tower.seqs)]
        spare = jnp.zeros((16 - len(firsts) - sum(item.shape[0] for item in above), width), F32)
        first_v[...] = jnp.concatenate([*above, *firsts, spare], axis=0).astype(LOW)
        moves.store(first_v, to)


def forward_layers(tower, layers, rows, whole_rows, ahead, after=(), cost=0):
    count, width = tower.count, tower.width
    steps = tower.wide // width
    shapes = [kept_shapes(tower, at > 0) for at in range(len(layers))]
    kinds = len(shapes[0])
    held = kept_scratch(tower)

    def kernel(ins, outs, scratch, moves):
        info, x_any = ins[0], ins[1]
        own = ins[2:6]
        other = ins[6:10] if tower.shared else [None] * 4
        smalls = ins[10:] if tower.shared else ins[6:]
        above = []
        if ahead is not None:
            above = [smalls[-1][...].astype(F32)[0 : ahead[1], :]]
            smalls = smalls[:-1]
        x_v, acc_v = scratch[:2]
        if whole_rows:
            x_any = x_any.at[pl.ds(tower.row_start(info), count)]
        x_got = moves.fetch(x_any, x_v)
        weights, got = [], []
        for at, layer in enumerate(layers):
            targets = scratch[2 + 4 * at : 6 + 4 * at]
            flag = tower.use_own(info, layer)
            arrivals = fetch_narrow(tower, flag, own[:2], other[:2], targets[:2], moves)
            for step in range(steps):
                arrivals[4 + step] = fetch_step(
                    tower, flag, own[2:], other[2:], targets[2:], moves, step, step
                )
            weights.append(targets)
            got.append(arrivals)
        x_got.wait()
        for at, layer in enumerate(layers):
            begin = 2 + 4 * len(layers) + len(held) * at
            kept = scratch[begin : begin + len(held)]
            forward_body(
                tower,
                layer,
                info,
                x_v,
                got[at],
                weights[at],
                smalls,
                acc_v,
                kept,
                outs[kinds * at : kinds * (at + 1)],
                moves,
                (scratch[-1], outs[-1], above) if at + 1 == len(layers) else None,
            )
            x_v = kept[0]
            if at + 1 < len(layers):
                inner = outs[kinds * (at + 1) + LEFTS]
                moves.store(x_v, inner.at[:, pl.ds(2 * width + tower.wide, width)])
        moves.drain()

    outs = [shape for layer_shapes in shapes for shape in layer_shapes] + [((16, width), LOW)]
    scratch = [((count, width), LOW), ((count, width), F32)] + weight_shapes(tower) * len(layers)
    inputs = [(SCALARS, tower.info), (ANYWHERE, rows)]
    inputs += [(ANYWHERE, array) for array in tower.given((0, 1, 2, 3))]
    inputs += [(INSIDE, array) for array in tower.given_small()]
    if ahead is not None:
        inputs.append((INSIDE, ahead[0]))
    results = call_kernel(
        kernel,
        "layer_forward",
        inputs,
        outs,
        scratch + held * len(layers) + outs[-1:],
        2 + len(layers) * (4 + 2 * steps + 9 + 2 * steps),
        cost,
        list(after),
    )
    return [results[kinds * at : kinds * (at + 1)] for at in range(len(layers))] + [results[-1]]


def place_rows(target, block, info, first, size, columns):
    for piece in range(block.shape[0] // size):
        at = pl.multiple_of(info[first + piece] * size, size)
        target[pl.ds(at, size), columns] = block[piece * size : (piece + 1) * size].astype(LOW)


def wide_scratch(tower, upstream):
    count, width = tower.count, tower.width
    steps = tower.wide // width
    return weight_shapes(tower)[2:] + [
        ((count, width), upstream.dtype),
        ((count, width), LOW),
        ((count, 128), F32),
        ((steps, count, width), LOW),
        ((count, width), F32),
        ((count, width), LOW),
        ((steps, count, width), LOW),
        ((8, width), F32),
    ]


def store_sides(source, side_width, outs, column, core_at, moves):
    for side, to in ((1 - core_at, outs[0]), (core_at, outs[1])):
        lanes = pl.ds(pl.multiple_of(side * side_width, 128), side_width)
        moves.store(source.at[:, lanes], to.at[:, pl.ds(column, side_width)])


def wide_tiles(tower, info):
    steps = tower.wide // tower.width
    if not tower.shared:
        return list(range(steps))
    return [lax.rem(step + (1 - info[CORE]) * (steps // 2), steps) for step in range(steps)]


def wide_fetch(tower, layer, info, ins, seeded, scratch, moves):
    up_any, own, other, slope_any, hat_any, inv_any = ins
    w_up, w_down, up_v, hat_v, inv_v, slope_v = scratch[:6]
    use_own = tower.use_own(info, layer)
    if seeded:
        up_any = up_any.at[pl.ds(tower.row_start(info), tower.count)]
    first_got = [
        moves.fetch(up_any, up_v),
        moves.fetch(hat_any, hat_v),
        moves.fetch(inv_any.at[1], inv_v),
    ]
    got = []
    for step, at in enumerate(wide_tiles(tower, info)):
        pieces = [moves.fetch(slope_any.at[at], slope_v.at[step])]
        pieces += fetch_step(tower, use_own, own, other, (w_up, w_down), moves, step, at)
        got.append(pieces)
    return first_got, got


def wide_body(tower, layer, info, fetched, first_ref, smalls, scratch, outs, moves):
    count, width = tower.count, tower.width
    steps = tower.wide // width
    w_up, w_down, up_v, hat_v, inv_v, slope_v, da_v, df_v, dh_v, vec_v = scratch
    use_own = tower.use_own(info, layer)
    core_at = info[CORE]
    first_got, got = fetched
    tiles = wide_tiles(tower, info)
    gains, _ = tower.small_rows(smalls, use_own)
    for copy in first_got:
        copy.wait()
    upward = up_v[...].astype(F32)
    if first_ref is not None:
        row_at = lax.broadcasted_iota(jnp.int32, (count, 1), 0)
        lengths = tower.lengths_at(info)
        first_seq = lengths - tower.first_len
        seen = jnp.zeros((count, 1), F32)
        for seq in range(tower.seqs):
            start = seq * tower.slots
            inside_seq = (row_at >= start) & (row_at < start + info[lengths + seq])
            seen = jnp.where(inside_seq, 1.0, seen)
        upward = upward * seen
        for seq in range(tower.seqs):
            upward = upward + jnp.where(
                row_at == seq * tower.slots, first_ref[pl.ds(first_seq + seq, 1), :], 0.0
            )
    hat = hat_v[...].astype(F32)
    vec_v[0:1, :] = col_sum(upward * hat)
    vec_v[1:2, :] = col_sum(upward)
    d_second = norm_pull(upward, hat, inv_v[:, 0:1], gains[1:2, :])
    d_low = d_second.astype(LOW)
    df_v[...] = d_low
    vec_v[2:3, :] = col_sum(d_low.astype(F32))
    vec_v[7:8, :] = jnp.zeros((1, width), F32)
    da_v[...] = d_second
    vec_out, df_out, dh_out = outs
    if tower.shared:
        store_sides(df_v, width // 2, df_out, 0, core_at, moves)
    else:
        moves.store(df_v, df_out[0])
    for step, at in enumerate(tiles):
        for copy in got[step]:
            copy.wait()
        d_hidden = (mm_nt(df_v[...], w_down[step]) * slope_v[step].astype(F32)).astype(LOW)
        vec_v[pl.ds(3 + at, 1), :] = col_sum(d_hidden.astype(F32))
        dh_v[step] = d_hidden
        da_v[...] += mm_nt(d_hidden, w_up[step])
        if tower.shared:
            side, place = divmod(step, steps // 2)
            moves.store(dh_v.at[step], dh_out[side].at[:, pl.ds(place * width, width)])
        else:
            moves.store(dh_v.at[step], dh_out[0].at[step])
    moves.store(vec_v, vec_out)


def narrow_scratch(tower, out_type):
    count, width = tower.count, tower.width
    return weight_shapes(tower)[:2] + [
        ((count, width), LOW),
        ((count, 128), F32),
        ((count, 3 * width), LOW),
        ((width // 128, count, 2 * tower.group), LOW),
        ((count, width), LOW),
        ((count, 3 * width), LOW),
        ((count, width), LOW),
        ((count, width), F32),
        ((count, width), out_type),
        ((8, width), F32),
    ]


def narrow_fetch(tower, layer, info, ins, scratch, moves):
    own, other, qkv_any, hat_any, inv_any, soft_any = ins
    w_qkv, w_out, hat_v, inv_v, qkv_v, soft_v = scratch[:6]
    use_own = tower.use_own(info, layer)
    got = {"hat": [moves.fetch(hat_any, hat_v), moves.fetch(inv_any.at[0], inv_v)]}
    weights = fetch_narrow(tower, use_own, own, other, (w_qkv, w_out), moves, (3,))
    got["heads"] = [moves.fetch(qkv_any, qkv_v), moves.fetch(soft_any, soft_v)]
    weights.update(fetch_narrow(tower, use_own, own, other, (w_qkv, w_out), moves, (0, 1, 2)))
    got["weights"] = weights
    return got


def narrow_body(tower, layer, info, got, da_v, smalls, scratch, outs, moves):
    count, width, group = tower.count, tower.width, tower.group
    w_qkv, w_out, hat_v, inv_v, qkv_v, soft_v, dz_v, dp_v, dmix_v, du_v, dx_v, vec_v = scratch
    use_own = tower.use_own(info, layer)
    core_at = info[CORE]
    dx_out, vec_out, dz_out, dp_out = outs
    gains, _ = tower.small_rows(smalls, use_own)
    for copy in got["hat"]:
        copy.wait()
    upward = da_v[...]
    hat = hat_v[...].astype(F32)
    vec_v[0:1, :] = col_sum(upward * hat)
    vec_v[1:2, :] = col_sum(upward)
    d_summed = norm_pull(upward, hat, inv_v[:, 0:1], gains[0:1, :])
    du_v[...] = d_summed
    d_low = d_summed.astype(LOW)
    dz_v[...] = d_low
    vec_v[2:3, :] = col_sum(d_low.astype(F32))
    vec_v[5:8, :] = jnp.zeros((3, width), F32)
    if tower.shared:
        store_sides(dz_v, width // 2, dz_out, 2 * width, core_at, moves)
    else:
        moves.store(dz_v, dz_out[0])
    got["weights"][3].wait()
    dmix_v[...] = mm_nt(d_low, w_out[...]).astype(LOW)
    for copy in got["heads"]:
        copy.wait()
    low, high = pair_masks(LOW)
    scale = HEAD_DIM ** (-0.5)
    for g in range(count // group):
        at = slice(g * group, (g + 1) * group)
        for pair in range(width // 128):
            lane = pair * 128
            q2 = qkv_v[at, lane : lane + 128]
            k2 = qkv_v[at, width + lane : width + lane + 128]
            v2 = qkv_v[at, 2 * width + lane : 2 * width + lane + 128]
            soft = soft_v[pair, at, :]
            d_stack = stacked_pair(dmix_v[at, lane : lane + 128], low, high)
            d_soft = mm_nt(v2, d_stack)
            soft_wide = soft.astype(F32)
            total = jnp.sum(d_soft * soft_wide, axis=0, keepdims=True)
            d_scores = (soft_wide * (d_soft - total)).astype(LOW)
            dp_v[at, lane : lane + 128] = (
                joined_pair(mm_tn(d_scores, k2), group) * scale
            ).astype(LOW)
            dp_v[at, width + lane : width + lane + 128] = (
                mm(d_scores, stacked_pair(q2, low, high)) * scale
            ).astype(LOW)
            dp_v[at, 2 * width + lane : 2 * width + lane + 128] = mm(soft, d_stack).astype(LOW)
    vec_v[3:4, :] = col_sum(dp_v[:, :width].astype(F32))
    vec_v[4:5, :] = col_sum(dp_v[:, 2 * width :].astype(F32))
    moves.store(vec_v, vec_out)
    if tower.shared:
        store_sides(dp_v, 3 * width // 2, dp_out, width // 2, core_at, moves)
    else:
        moves.store(dp_v, dp_out[0])
    d_input = du_v[...]
    for part in range(3):
        got["weights"][part].wait()
        d_input = d_input + mm_nt(dp_v[:, part * width : (part + 1) * width], w_qkv[part])
    dx_v[...] = d_input.astype(dx_v.dtype)
    moves.store(dx_v, dx_out)


def backward_layer(
    tower, layer, upstream, first_rows, kept, low_out, after=(), cost=0, through=()
):
    count, width, wide = tower.count, tower.width, tower.wide
    steps = wide // width
    seeded = first_rows is not None
    out_type = LOW if low_out else F32
    wide_shapes = wide_scratch(tower, upstream)

    def kernel(ins, outs, scratch, moves):
        ins = list(ins)
        info, up_any = ins.pop(0), ins.pop(0)
        first_ref = ins.pop(0) if seeded else None
        own = [ins.pop(0) for _ in range(4)]
        other = [ins.pop(0) for _ in range(4)] if tower.shared else [None] * 4
        slope_any, hat2_any, inv_any, qkv_any, hat1_any, soft_any = (
            ins.pop(0) for _ in range(6)
        )
        first, second = scratch[: len(wide_shapes)], scratch[len(wide_shapes) :]
        dx, vec1, vec2 = outs[:3]
        if tower.shared:
            dh, df = outs[3:5], outs[5:7]
            dz = dp = df
        else:
            df, dh, dz, dp = (outs[at : at + 1] for at in range(3, 7))
        given = (up_any, own[2:], other[2:], slope_any, hat2_any, inv_any)
        wide_got = wide_fetch(tower, layer, info, given, seeded, first, moves)
        given = (own[:2], other[:2], qkv_any, hat1_any, inv_any, soft_any)
        got = narrow_fetch(tower, layer, info, given, second, moves)
        wide_body(
            tower, layer, info, wide_got, first_ref, ins, first, (vec1, df, dh), moves
        )
        narrow_body(
            tower, layer, info, got, first[6], ins, second, (dx, vec2, dz, dp), moves
        )
        moves.drain()

    outs = [((count, width), out_type), ((8, width), F32), ((8, width), F32)]
    if tower.shared:
        outs += [((count, wide // 2), LOW)] * 2 + [((count, 5 * width // 2), LOW)] * 2
    else:
        outs += [((count, width), LOW), ((steps, count, width), LOW)]
        outs += [((count, width), LOW), ((count, 3 * width), LOW)]
    inputs = [(SCALARS, tower.info), (ANYWHERE, upstream)]
    if seeded:
        inputs.append((INSIDE, first_rows))
    inputs += [(ANYWHERE, array) for array in tower.given((0, 1, 2, 3))]
    inputs += [(ANYWHERE, kept[at]) for at in (SLOPE, HAT2, INVERSES, PROJECTED, HAT1, SOFT)]
    inputs += [(INSIDE, array) for array in tower.given_small()]
    return call_kernel(
        kernel,
        "backward_layer",
        inputs,
        outs,
        wide_shapes + narrow_scratch(tower, out_type),
        3 + 3 * steps + 8 + 3 + steps + 6,
        cost,
        list(after),
        through,
    )


def place_rows(target, block, info, first, size, columns):
    for piece in range(block.shape[0] // size):
        at = pl.multiple_of(info[first + piece] * size, size)
        target[pl.ds(at, size), columns] = block[piece * size : (piece + 1) * size].astype(LOW)


def passage_products(
    tower, layer, rows, lefts, other_lefts, rights, other_rights, vectors, after=(), cost=0
):
    count, width, wide = tower.count, tower.width, tower.wide
    steps = wide // width
    half = width // 2
    piece = width // BLOCKS
    layout = LAYOUTS[layer]
    chunks = 1 + max(chunk for chunk, _ in layout)
    widths = [
        max(column + (wide // 2 if at < 2 else width) for at, (to, column) in enumerate(layout) if to == chunk)
        for chunk in range(chunks)
    ]
    vector_column = widths[0]
    if vectors:
        widths[0] += 128
    whole = rows is not None

    def kernel(ins, outs, scratch, moves):
        ins = list(ins)
        info = ins.pop(0)
        x_any = ins.pop(0) if whole else None
        vector_refs = [ins.pop() for _ in vectors]
        left, other_left = ins[:2]
        hidden_of, rights_of = (ins[2], ins[4]), (ins[3], ins[5])
        low_v, dh_v, act_v, df_v, x_v, dp_v, mix_v, dz_v = scratch[:8]
        grads = scratch[8:]
        above, below = pl.ds(0, count), pl.ds(count, count)

        def both(sources, column, target):
            columns = pl.ds(column, target.shape[1])
            return [
                moves.fetch(sources[0].at[:, columns], target.at[above]),
                moves.fetch(sources[1].at[:, columns], target.at[below]),
            ]

        lefts_of = (left, other_left)
        got_low = both(lefts_of, width, low_v)
        got_dh = [both(hidden_of, at * width, dh_v.at[at]) for at in range(steps // 2)]
        got_df = both(rights_of, 0, df_v)
        got_act = [both(lefts_of, (2 + at) * width, act_v.at[at]) for at in range(steps)]
        if whole:
            start = tower.row_start(info)
            other_start = pl.multiple_of(count - start, count)
            got_x = [
                moves.fetch(x_any.at[pl.ds(start, count)], x_v.at[above]),
                moves.fetch(x_any.at[pl.ds(other_start, count)], x_v.at[below]),
            ]
        else:
            got_x = both(lefts_of, 2 * width + wide, x_v)
        got_x += both(rights_of, half, dp_v)
        got_mix = both(lefts_of, 0, mix_v) + both(rights_of, 2 * width, dz_v)

        def ready(copies):
            for copy in copies:
                copy.wait()

        def target(part):
            chunk, column = layout[part]
            return grads[chunk], column, PLACES + BLOCKS * (3 * layer + chunk)

        def send(part):
            source, column, _ = target(part)
            cut = source.shape[0] // 2
            columns = pl.ds(column, wide // 2 if part < 2 else width)
            to = 2 * layout[part][0]
            moves.store(source.at[pl.ds(cut, cut), columns], outs[to].at[:, columns])
            moves.store(source.at[pl.ds(0, cut), columns], outs[to + 1].at[:, columns])

        if vectors:
            lane = slice(vector_column, vector_column + 128)
            for block in range(BLOCKS):
                from_rows = slice(block * PIECE_ROWS, (block + 1) * PIECE_ROWS)
                begin = block * piece
                grads[0][begin : begin + PIECE_ROWS, lane] = (
                    vector_refs[0][from_rows, :] + vector_refs[1][from_rows, :]
                ).astype(LOW)
                grads[0][begin + PIECE_ROWS : begin + piece, lane] = jnp.zeros(
                    (piece - PIECE_ROWS, 128), LOW
                )
            cut = width // 2
            columns = pl.ds(vector_column, 128)
            moves.store(grads[0].at[pl.ds(cut, cut), columns], outs[0].at[:, columns])
            moves.store(grads[0].at[pl.ds(0, cut), columns], outs[1].at[:, columns])
        ready(got_low)
        for at in range(steps // 2):
            ready(got_dh[at])
            to, column, first = target(1)
            columns = slice(column + at * width, column + (at + 1) * width)
            place_rows(to, mm_tn(low_v[...], dh_v[at]), info, first, piece, columns)
        send(1)
        ready(got_df)
        parts = wide // width
        for at in range(steps):
            ready(got_act[at])
            product = mm_tn(act_v[at], df_v[...])
            for block in range(width // piece):
                index, part = divmod(at * (width // piece) + block, parts)
                to, column, first = target(0)
                rows_to = pl.ds(pl.multiple_of(info[first + index] * piece, piece), piece)
                column += part * half
                to[rows_to, column : column + half] = product[
                    block * piece : (block + 1) * piece
                ].astype(LOW)
        send(0)
        ready(got_x)
        for part in range(4):
            if part == 3:
                ready(got_mix)
                product = mm_tn(mix_v[...], dz_v[...])
            else:
                product = mm_tn(x_v[...], dp_v[:, part * half : (part + 1) * half])
            to, column, first = target(2 + part // 2)
            column += part % 2 * half
            place_rows(to, product, info, first, piece, slice(column, column + half))
            if part % 2:
                send(2 + part // 2)
        moves.drain()

    outs = [((half, columns), LOW) for columns in widths for _ in range(2)]
    scratch = [
        ((2 * count, width), LOW),
        ((steps // 2, 2 * count, width), LOW),
        ((steps, 2 * count, width), LOW),
        ((2 * count, half), LOW),
        ((2 * count, width), LOW),
        ((2 * count, 3 * half), LOW),
        ((2 * count, width), LOW),
        ((2 * count, half), LOW),
    ] + [((width, columns), LOW) for columns in widths]
    arrays = [rows] if whole else []
    arrays += [lefts, other_lefts, *rights, *other_rights]
    inputs = [(SCALARS, tower.info)] + [(ANYWHERE, array) for array in arrays]
    inputs += [(INSIDE, array) for array in vectors]
    return call_kernel(
        kernel,
        "passage_products",
        inputs,
        outs,
        scratch,
        2 * (1 + steps // 2 + 1 + steps + 4) + 10,
        cost,
        list(after),
    )


def block_chooser(rows, columns, valid, size, bit):
    at = lax.broadcasted_iota(jnp.int32, (1, columns), 1)
    piece = jnp.floor((at.astype(F32) + 0.5) * (1.0 / size)).astype(jnp.int32)
    wanted = jnp.where(at < valid, at + (piece + bit) * size, -1)
    row_at = lax.broadcasted_iota(jnp.int32, (rows, columns), 0)
    return jnp.where(row_at == wanted, 1.0, 0.0).astype(LOW)


def pack_first(info, early, late, after=(), cost=0):
    count, width = early[0].shape
    steps = early[2].shape[0]
    wide = steps * width
    half = width // 2
    piece = width // BLOCKS
    keeps = (half + 3 * half, 2 * wide // 2)
    wholes = (2 * width, 2 * width)

    def kernel(ins, outs, scratch, moves):
        info_ref = ins[0]
        first, second = ins[1:7], ins[7:13]
        x_v, left_v, dh_v, df_v, dz_v, dp_v = scratch[:6]
        results = scratch[6:]
        flag = info_ref[IS_FIRST] == 1
        got = [moves.fetch_either(flag, a, b, to) for a, b, to in zip(first, second, scratch)]
        bits = [(info_ref[at], 1 - info_ref[at]) for at in (X_BIT, Y_BIT)]
        for copy in got:
            copy.wait()

        def lanes(bit, size):
            return pl.ds(pl.multiple_of(bit * size, 128), size)

        for which in range(2):
            first_to, second_to = results[which], results[2 + which]
            bit = bits[0][which]
            choose = block_chooser(width, half, half, piece, bit)
            first_to[:, :half] = mm(left_v[:, :width], choose).astype(LOW)
            first_to[:, half : 4 * half] = dp_v[:, lanes(bit, 3 * half)]
            bit = bits[1][which]
            for step in range(steps):
                start = (2 + step) * width + bit * half
                second_to[:, step * half : (step + 1) * half] = left_v[
                    :, pl.ds(pl.multiple_of(start, 128), half)
                ]
            for step in range(steps // 2):
                begin = wide // 2 + step * width
                second_to[:, begin : begin + width] = dh_v[bit * (steps // 2) + step]
        results[1][:, keeps[0] : keeps[0] + width] = x_v[...]
        results[1][:, keeps[0] + width :] = dz_v[...]
        results[3][:, keeps[1] : keeps[1] + width] = left_v[:, width : 2 * width]
        results[3][:, keeps[1] + width :] = df_v[...]
        for at in range(4):
            moves.store(results[at], outs[at])
        moves.drain()

    outs = []
    for keep, rest in zip(keeps, wholes):
        outs += [((count, keep), LOW), ((count, keep + rest), LOW)]
    inputs = [(SCALARS, info)] + [(ANYWHERE, array) for array in tuple(early) + tuple(late)]
    scratch = [(array.shape, LOW) for array in early]
    return call_kernel(
        kernel, "pack_first", inputs, outs, scratch + outs, 12, cost, list(after)
    )


def pack_second(info, keeps, sends, arrivals, width, after=(), cost=0):
    count = keeps[0].shape[0]
    wide = keeps[1].shape[1]
    half, quarter, third = width // 2, width // 4, 256
    piece = width // BLOCKS
    chosen = (third + half, half + wide // 4)
    wholes = (3 * half + width, wide // 2 + width)

    def kernel(ins, outs, scratch, moves):
        info_ref = ins[0]
        got = [moves.fetch(source, to) for source, to in zip(ins[1:], scratch)]
        bits = [(info_ref[at], 1 - info_ref[at]) for at in (Y_BIT, X_BIT)]
        for copy in got:
            copy.wait()
        for lot in range(2):
            keep_v, send_v, arrived_v = scratch[lot], scratch[2 + lot], scratch[4 + lot]
            cut = keep_v.shape[1]
            sources = (
                (slice(0, count), keep_v, send_v),
                (slice(count, 2 * count), arrived_v, arrived_v),
            )
            for which in range(2):
                target = scratch[6 + 2 * lot + which]
                bit = bits[lot][which]
                if lot == 0:
                    narrow = block_chooser(half, third, quarter, piece, bit)
                    broad = block_chooser(width, half, half, 2 * piece, bit)
                else:
                    narrow = block_chooser(width, half, half, piece, bit)
                    broad = block_chooser(2 * half, half, half, quarter, bit)
                for rows, halved, whole in sources:
                    if lot == 0:
                        target[rows, :third] = mm(halved[:, :half], narrow).astype(LOW)
                        target[rows, third:chosen[0]] = mm(
                            whole[:, cut : cut + width], broad
                        ).astype(LOW)
                        continue
                    target[rows, :half] = mm(whole[:, cut : cut + width], narrow).astype(LOW)
                    for part in range(wide // 2 // width):
                        target[rows, half + part * half : half + (part + 1) * half] = mm(
                            halved[:, part * width : (part + 1) * width], broad
                        ).astype(LOW)
            target = scratch[6 + 2 * lot + 1]
            begin = chosen[lot]
            first = half if lot == 0 else wide // 2
            for rows, halved, whole in sources:
                target[rows, begin : begin + cut - first] = halved[:, first:cut]
                target[rows, begin + cut - first :] = whole[:, cut + width :]
        for at in range(4):
            moves.store(scratch[6 + at], outs[at])
        moves.drain()

    outs = []
    for left, right in zip(chosen, wholes):
        outs += [((2 * count, left), LOW), ((2 * count, left + right), LOW)]
    arrays = tuple(keeps) + tuple(sends) + tuple(arrivals)
    inputs = [(SCALARS, info)] + [(ANYWHERE, array) for array in arrays]
    scratch = [(array.shape, LOW) for array in arrays]
    return call_kernel(
        kernel, "pack_second", inputs, outs, scratch + outs, 10, cost, list(after)
    )


def query_products(info, keeps, sends, arrivals, width, wide, after=(), cost=0):
    count = keeps[0].shape[0]
    half, third = width // 2, 256
    piece = width // BLOCKS
    packed = [keep.shape[1] for keep in keeps]
    rights = [send.shape[1] - left for send, left in zip(sends, packed)]
    columns = 4 * width + 2 * wide

    def kernel(ins, outs, scratch, moves):
        info_ref = ins[0]
        keep_any, send_any, arrived_any = ins[1:3], ins[3:5], ins[5:7]
        left_v, right_v, result = scratch[0:2], scratch[2:4], scratch[4]
        got = []
        for lot in range(2):
            cut = packed[lot]
            below = pl.ds(count, count)
            got.append(
                [
                    moves.fetch(keep_any[lot], left_v[lot].at[pl.ds(0, count)]),
                    moves.fetch(arrived_any[lot].at[:, pl.ds(0, cut)], left_v[lot].at[below]),
                    moves.fetch(
                        send_any[lot].at[:, pl.ds(cut, rights[lot])],
                        right_v[lot].at[pl.ds(0, count)],
                    ),
                    moves.fetch(
                        arrived_any[lot].at[:, pl.ds(cut, rights[lot])], right_v[lot].at[below]
                    ),
                ]
            )

        def place(z, rows, column):
            row = pl.multiple_of(info_ref[Z_PLACES + z] * piece, piece)
            result[pl.ds(row, piece), column : column + rows.shape[1]] = rows.astype(LOW)

        for copy in got[0]:
            copy.wait()
        for part in range(3):
            product = mm_tn(
                left_v[0][:, third:], right_v[0][:, part * half : (part + 1) * half]
            )
            for block in range(8):
                z, bit = divmod(block, 2)
                place(
                    z,
                    product[block * piece : (block + 1) * piece],
                    bit * 3 * half + part * half,
                )
        product = mm_tn(left_v[0][:, :third], right_v[0][:, 3 * half :])
        for z in range(4):
            place(z, product[z * piece : (z + 1) * piece], 3 * width)
        for copy in got[1]:
            copy.wait()
        at = 4 * width
        for part in range(wide // 2 // width):
            product = mm_tn(
                left_v[1][:, :half], right_v[1][:, part * width : (part + 1) * width]
            )
            for block in range(8):
                z, bit = divmod(block, 2)
                place(
                    z,
                    product[block * piece : (block + 1) * piece],
                    at + bit * (wide // 2) + part * width,
                )
        at += wide
        product = mm_tn(left_v[1][:, half:], right_v[1][:, wide // 2 :])
        per = wide // width
        for z in range(4):
            for part in range(per):
                begin = (z * per + part) * piece
                place(z, product[begin : begin + piece], at + part * width)
        moves.store(result.at[pl.ds(2 * piece, 2 * piece)], outs[0])
        moves.store(result.at[pl.ds(0, 2 * piece)], outs[1])
        moves.drain()

    outs = [((2 * piece, columns), LOW)] * 2
    arrays = tuple(keeps) + tuple(sends) + tuple(arrivals)
    inputs = [(SCALARS, info)] + [(ANYWHERE, array) for array in arrays]
    scratch = [((2 * count, cut), LOW) for cut in packed]
    scratch += [((2 * count, cut), LOW) for cut in rights]
    scratch += [((4 * piece, columns), LOW)]
    return call_kernel(
        kernel, "query_products", inputs, outs, scratch, 10, cost, list(after)
    )


PIECE_ROWS = 32


def vector_pieces(info, first, parts, wide, after=(), cost=0):
    width = parts[0].shape[1]
    cut = width // BLOCKS
    big = wide // BLOCKS

    def kernel(ins, outs, scratch, moves):
        info_ref = ins[0]
        refs = ins[1:]
        early = info_ref[IS_FIRST] == 1
        for target in scratch:
            target[...] = jnp.zeros_like(target)

        def lay(target, tower_at, wide_rows, narrow_rows):
            eight = jnp.concatenate([wide_rows[0:3], narrow_rows[0:5]], axis=0)
            for block in range(BLOCKS):
                at = info_ref[PLACES + first + block] * PIECE_ROWS + 16 * tower_at
                at = pl.multiple_of(at, 16)
                target[pl.ds(at, 8), 0:cut] = eight[:, block * cut : (block + 1) * cut]
                row, column = divmod(block * big, width)
                bias = wide_rows[3 + row : 4 + row, column : column + big]
                target[pl.ds(at + 8, 1), 0:128] = bias[:, 0:128]
                target[pl.ds(at + 9, 1), 0 : big - 128] = bias[:, 128:big]

        send, keep = scratch
        eq1, eq2, lq1, lq2, ep1, ep2, lp1, lp2 = (ref[...] for ref in refs)
        lay(keep, 0, jnp.where(early, eq1, lq1), jnp.where(early, eq2, lq2))
        lay(keep, 1, jnp.where(early, ep1, lp1), jnp.where(early, ep2, lp2))
        lay(send, 1, jnp.where(early, lp1, ep1), jnp.where(early, lp2, ep2))
        moves.store(send, outs[0])
        moves.store(keep, outs[1])
        moves.drain()

    outs = [((BLOCKS * PIECE_ROWS, 128), F32)] * 2
    inputs = [(SCALARS, info)] + [(INSIDE, array) for array in parts]
    return call_kernel(kernel, "vector_pieces", inputs, outs, outs, 2, cost, list(after))


def take_in(items, after=(), cost=0, through=()):
    def kernel(ins, outs, scratch, moves):
        ins, scratch = list(ins), list(scratch)
        taken = []
        for pairs, last in items:
            got = []
            for _ in pairs:
                held = [scratch.pop(0), scratch.pop(0)]
                got.append((held, [moves.fetch(ins.pop(0), to) for to in held]))
            taken.append((got, [scratch.pop(0) for _ in range(1 if last else 2)]))
        out_at = 0
        for (got, results), (_, last) in zip(taken, items):
            for held, copies in got:
                for copy in copies:
                    copy.wait()
            for which, result in enumerate(results):
                part_rows = result.shape[0]
                start = 0 if last else (1 - which) * part_rows
                column = 0
                for (keep_v, arrived_v), _ in got:
                    columns = keep_v.shape[1]
                    chunk = 48 if columns <= 1536 and part_rows % 48 == 0 else 16

                    def one(step, carry, keep_v=keep_v, arrived_v=arrived_v, column=column):
                        to = pl.ds(pl.multiple_of(step * chunk, 16), chunk)
                        of = pl.ds(pl.multiple_of(start + step * chunk, 16), chunk)
                        total = keep_v[of, :].astype(F32) + arrived_v[of, :].astype(F32)
                        result[to, column : column + keep_v.shape[1]] = total.astype(result.dtype)
                        return carry

                    lax.fori_loop(0, part_rows // chunk, one, 0)
                    column += columns
                moves.store(result, outs[out_at])
                out_at += 1
        moves.drain()

    outs, scratch = [], []
    for pairs, last in items:
        rows = pairs[0][0].shape[0]
        columns = sum(keep.shape[1] for keep, _ in pairs)
        kind = pairs[0][0].dtype
        mine = [((rows, columns), F32)] if last else [((rows // 2, columns), kind)] * 2
        outs += mine
        for keep, arrived in pairs:
            scratch += [(keep.shape, kind), (arrived.shape, kind)]
        scratch += mine
    inputs = [(ANYWHERE, array) for pairs, _ in items for pair in pairs for array in pair]
    return call_kernel(
        kernel, "take_in", inputs, outs, scratch, len(inputs) + len(outs), cost, list(after), through
    )


def take_in_quarters(pairs, after=(), cost=0, through=()):
    rows = pairs[0][0].shape[0] // 4
    columns = sum(keep.shape[1] for keep, _ in pairs)

    def kernel(ins, outs, scratch, moves):
        held = scratch[: len(ins)]
        results = scratch[len(ins) :]
        got = [moves.fetch(source, to) for source, to in zip(ins, held)]
        for copy in got:
            copy.wait()
        for quarter in (1, 2, 3, 0):
            result = results[quarter]
            column = 0
            for at in range(len(pairs)):
                keep_v, arrived_v = held[2 * at : 2 * at + 2]
                wide = keep_v.shape[1]

                def one(step, carry, keep_v=keep_v, arrived_v=arrived_v, column=column, wide=wide):
                    to = pl.ds(pl.multiple_of(step * 16, 16), 16)
                    of = pl.ds(pl.multiple_of(quarter * rows + step * 16, 16), 16)
                    total = keep_v[of, :].astype(F32) + arrived_v[of, :].astype(F32)
                    result[to, column : column + wide] = total.astype(LOW)
                    return carry

                lax.fori_loop(0, rows // 16, one, 0)
                column += wide
            moves.store(result, outs[quarter])
        moves.drain()

    outs = [((rows, columns), LOW)] * 4
    arrays = [array for pair in pairs for array in pair]
    inputs = [(ANYWHERE, array) for array in arrays]
    scratch = [(array.shape, LOW) for array in arrays]
    return call_kernel(
        kernel,
        "take_in_quarters",
        inputs,
        outs,
        scratch + outs,
        len(arrays) + 4,
        cost,
        list(after),
        through,
    )


class Chain:
    def __init__(self, send, keep, order, scale, from_core=False):
        self.order = list(order)
        self.scale = scale
        self.keep = keep
        self.total = None
        self.arrived = core_swap(send) if from_core else self.swap(send)

    def swap(self, block):
        return flip_swap(block, self.order.pop(0) * self.scale)


def play_round(groups, after=(), cost=0, through=()):
    items = [
        ([(chain.keep, chain.arrived) for chain in group], not group[0].order) for group in groups
    ]
    results = list(take_in(items, after, cost, through))
    seen = []
    for group in groups:
        chain = group[0]
        assert all(other.order == chain.order for other in group)
        if not chain.order:
            chain.total = results.pop(0)
            seen.append(chain.total)
            continue
        sent, chain.keep = results.pop(0), results.pop(0)
        chain.arrived = chain.swap(sent)
        seen.append(sent)
    return tuple(seen + results)


def last_round(info, quarters, other_total, vector_column, after=(), cost=0):
    rows, columns = other_total.shape
    begin = vector_column

    def kernel(ins, outs, scratch, moves):
        info_ref = ins[0]
        parts, late_v = scratch[:4], scratch[4]
        own_v, send_v, vec_v = scratch[5:]
        got = [moves.fetch(source, to) for source, to in zip(ins[1:], scratch)]
        for copy in got:
            copy.wait()
        flag = info_ref[IS_FIRST] == 1

        def total(part, lanes):
            values = [ref[part, lanes].astype(F32) for ref in parts]
            return (values[0] + values[1]) + (values[2] + values[3])

        vec_v[...] = total(slice(0, rows), slice(begin, begin + 128))
        moves.store(vec_v, outs[2])
        for row in range(0, rows, 16):
            part = slice(row, row + 16)
            for lanes, of in (
                (slice(0, begin), slice(0, begin)),
                (slice(begin, columns), slice(begin + 128, columns + 128)),
            ):
                early = total(part, of)
                late = late_v[part, lanes]
                send_v[part, lanes] = jnp.where(flag, late, early).astype(LOW)
                own_v[part, lanes] = jnp.where(flag, early, late)
            done = pl.ds(row, 16)
            moves.store(send_v.at[done], outs[1].at[done])
            moves.store(own_v.at[done], outs[0].at[done])
        moves.drain()

    outs = [((rows, columns), F32), ((rows, columns), LOW), ((rows, 128), F32)]
    arrays = (*quarters, other_total)
    inputs = [(SCALARS, info)] + [(ANYWHERE, array) for array in arrays]
    scratch = [(array.shape, array.dtype) for array in arrays]
    return call_kernel(
        kernel, "last_round", inputs, outs, scratch + outs, 6 + rows // 8, cost, list(after)
    )


def output_shapes(rows, width, wide):
    return [
        ((2, rows, 3 * width), F32),
        ((2, rows, width), F32),
        ((2, rows, wide), F32),
        ((2, wide // width * rows, width), F32),
    ]


def query_outputs(info, query, query_x, query_y, width, wide, after=(), cost=0):
    rows = query.shape[0]
    half = width // 2
    parts = wide // width

    def kernel(ins, outs, scratch, moves):
        info_ref = ins[0]
        sources, results = scratch[:3], scratch[3:]
        got = [moves.fetch(source, to) for source, to in zip(ins[1:], sources)]
        query_v, x_v, y_v = sources
        g_qkv, g_out, g_up, g_down = results
        for copy in got:
            copy.wait()
        at = 4 * width
        for bit_at, begin, size, arrived, target in (
            (X_BIT, 0, 3 * half, x_v, g_qkv),
            (Y_BIT, at, wide // 2, y_v, g_up),
        ):
            bit = info_ref[bit_at]
            mine = pl.ds(pl.multiple_of(bit * size, 128), size)
            others = pl.ds(pl.multiple_of((1 - bit) * size, 128), size)
            target[:, mine] = query_v[:, pl.ds(pl.multiple_of(begin + bit * size, 128), size)]
            target[:, others] = arrived[...]
        g_out[...] = query_v[:, 3 * width : 4 * width]
        at += wide
        for part in range(parts):
            g_down[part * rows : (part + 1) * rows, :] = query_v[
                :, at + part * width : at + (part + 1) * width
            ]
        for result, to in zip(results, outs):
            moves.store(result, to.at[0])
        moves.drain()

    outs = output_shapes(rows, width, wide)
    arrays = (query, query_x, query_y)
    inputs = [(SCALARS, info)] + [(ANYWHERE, array) for array in arrays]
    scratch = [(array.shape, F32) for array in arrays] + [(shape[1:], F32) for shape, _ in outs]
    return call_kernel(
        kernel, "query_outputs", inputs, outs, scratch, 7, cost, list(after)
    )


def passage_outputs(info, own, other, outputs, width, wide):
    rows, columns = own.shape
    half = width // 2
    parts = wide // width
    chunk_width = columns // 2
    begin = [to * chunk_width + column for to, column in LAYOUTS[0]]

    def kernel(ins, outs, scratch, moves):
        info_ref = ins[0]
        sources, results = scratch[:2], scratch[2:]
        got = [moves.fetch(source, to) for source, to in zip(ins[1:], sources)]
        g_qkv, g_out, g_up, g_down = results
        core = info_ref[CORE]
        for at, side in ((0, core), (1, 1 - core)):
            got[at].wait()
            source = sources[at]
            here = pl.ds(pl.multiple_of(side * half, 128), half)
            for part in range(parts):
                g_down[part * rows : (part + 1) * rows, here] = source[
                    :, begin[0] + part * half : begin[0] + (part + 1) * half
                ].astype(F32)
            up = pl.ds(pl.multiple_of(side * (wide // 2), 128), wide // 2)
            g_up[:, up] = source[:, begin[1] : begin[1] + wide // 2].astype(F32)
            for third in range(3):
                column = begin[2 + third // 2] + third % 2 * half
                to = pl.ds(pl.multiple_of(side * 3 * half + third * half, 128), half)
                g_qkv[:, to] = source[:, column : column + half].astype(F32)
            g_out[:, here] = source[:, begin[3] + half : begin[3] + width].astype(F32)
        for result, to in zip(results, outs):
            moves.store(result, to.at[1])
        moves.drain()

    shapes = output_shapes(rows, width, wide)
    arrays = (own, other)
    inputs = [(SCALARS, info)] + [(ANYWHERE, array) for array in arrays]
    scratch = [(array.shape, array.dtype) for array in arrays]
    scratch += [(shape[1:], F32) for shape, _ in shapes]
    return call_kernel(
        kernel, "passage_outputs", inputs, [], scratch, 6, 0, [], tuple(outputs)
    )


def pick_bit(grid, axis, index):
    return lax.dynamic_index_in_dim(grid, index, axis, keepdims=False)


def own_bit(bit):
    return (lax.axis_index("batch") // bit) % 2


def scatter_sum(grid, bits, left):
    left = list(left)
    for bit in bits:
        axis = left.index(bit)
        mine = own_bit(bit)
        sent = pick_bit(grid, axis, 1 - mine)
        kept = pick_bit(grid, axis, mine)
        arrived = flip_swap(sent, bit)
        total = kept.astype(jnp.float32) + arrived.astype(jnp.float32)
        left.remove(bit)
        grid = total if not left else total.astype(grid.dtype)
    return grid


def all_bits(size):
    bits = [1 << i for i in range(size.bit_length() - 1)]
    return bits[::-1]


def to_grid(array, size):
    bits = all_bits(size)
    return array.reshape((2,) * len(bits) + (array.shape[0] // size,) + array.shape[1:])


def gather_all(block, size):
    if size != 16:
        for bit in all_bits(size)[::-1]:
            block = jnp.concatenate([block, flip_swap(block, bit)], 0)
        return block
    block = jnp.concatenate([block] + [flip_swap(block, k) for k in (1, 2, 3)], 0)
    return jnp.concatenate([block] + [flip_swap(block, k) for k in (4, 8, 12)], 0)


def contrast(own_cls, micro, positive, query_count, batch_index, batch_size):
    width = own_cls.shape[1]
    chip_rows = own_cls.shape[0]
    gathered = gather_all(own_cls, batch_size).reshape(batch_size, chip_rows, width)
    all_q = gathered[:, :query_count].reshape(-1, width)
    all_p = gathered[:, query_count:].reshape(-1, width)
    blocks = jnp.arange(batch_size, dtype=jnp.int32) ^ batch_index
    query_ids = (
        blocks[:, None] * query_count + jnp.arange(query_count, dtype=jnp.int32)[None, :]
    ).reshape(-1)
    passage_ids = (
        3 * query_ids[:, None] + jnp.arange(3, dtype=jnp.int32)[None, :]
    ).reshape(-1)
    labels = jnp.take(micro, query_ids)
    wanted = jnp.take(positive, query_ids)
    logit_scale = LOGIT_GAIN * width ** (-0.5)
    logits = mm_nt(all_q, all_p) * logit_scale
    same_group = labels[:, None] == jnp.repeat(labels, 3)[None, :]
    logits = jnp.where(same_group, logits, MASK_FILL)
    row_top = jnp.max(logits, axis=-1, keepdims=True)
    exponent = jnp.exp(logits - row_top)
    totals = jnp.sum(exponent, axis=-1, keepdims=True)
    target = passage_ids[None, :] == wanted[:, None]
    loss_all = (
        row_top[:, 0] + jnp.log(totals[:, 0]) - jnp.sum(jnp.where(target, logits, 0.0), axis=-1)
    )
    coefficient = (exponent / totals - target.astype(jnp.float32)) * logit_scale
    passage_count = 3 * query_count
    d_cls_q = jnp.dot(coefficient[:query_count], all_p.astype(jnp.float32), precision=PRECISE)
    d_cls_p = lax.dot_general(
        coefficient[:, :passage_count],
        all_q.astype(jnp.float32),
        (((0,), (0,)), ((), ())),
        precision=PRECISE,
    )
    return loss_all[:query_count], d_cls_q, d_cls_p


def integers(core, index, size, len_q, len_p):
    blocks = jnp.arange(BLOCKS, dtype=jnp.int32)
    own = index // (size // BLOCKS)
    relative = blocks ^ own
    places = [
        sum(((relative // bit) % 2) * (8 >> at) for at, bit in enumerate(order))
        for order in ORDERS
    ]
    depth = jnp.arange(4, dtype=jnp.int32) ^ (own // 4)
    z_places = (depth % 2) * 2 + depth // 2
    few = jnp.stack([1 - core, core])
    ends = jnp.stack([own % 2, (own // 2) % 2])
    return jnp.concatenate([few, *places, z_places, ends, len_q, len_p]).astype(jnp.int32)


def shards(
    x_q,
    x_p,
    len_q,
    len_p,
    cot_q,
    cot_p,
    positive,
    micro,
    w_qkv,
    w_out,
    w_up,
    w_down,
    norm_gain,
    biases,
    b_up,
):
    core = lax.axis_index("section")
    is_first = core == 0
    batch_index = lax.axis_index("batch")
    size = lax.axis_size("batch")
    bits = all_bits(size)
    query_count, slots_q, model = x_q.shape
    half_count = x_p.shape[0] // 2
    slots_p = x_p.shape[1]
    wide = w_up.shape[-1]
    info = integers(core, batch_index, size, len_q, len_p)
    weights = (w_qkv, w_out, w_up, w_down)
    smalls = (norm_gain, biases, b_up)
    other_p = tuple(core_swap(member[0, 1]) for member in weights)
    small_other = core_swap(
        jnp.concatenate([norm_gain[0, 1], biases[0, 1], b_up[0, 1].reshape(-1, model)], 0)
    )
    tower_q = Tower(0, info, weights, None, smalls, None, query_count, slots_q, LENGTHS)
    tower_p = Tower(
        1, info, weights, other_p, smalls, small_other, half_count, slots_p, LENGTHS + query_count
    )
    flat_q = x_q.reshape(-1, model)
    flat_p = x_p.reshape(-1, model)
    cots_q = cot_q.reshape(-1, model)
    cots_p = cot_p.reshape(-1, model)

    early_q, _ = forward_layers(tower_q, (0,), flat_q, True, None)
    mid_q = early_q[OUTPUT]
    arrived_q = core_swap(mid_q)
    late_q, first_q = forward_layers(tower_q, (1,), arrived_q, True, None)
    early_p, late_p, cls_rows = forward_layers(
        tower_p, (0, 1), flat_p, True, (first_q, query_count)
    )
    mid_p = early_p[OUTPUT]
    top_q, top_p = late_q[OUTPUT], late_p[OUTPUT]

    last = query_count + half_count
    cls_other = core_swap(cls_rows)
    cls_chip = jnp.concatenate(
        [
            jnp.where(is_first, cls_other[:query_count], cls_rows[:query_count]),
            jnp.where(is_first, cls_rows[query_count:last], cls_other[query_count:last]),
            jnp.where(is_first, cls_other[query_count:last], cls_rows[query_count:last]),
        ],
        0,
    )
    loss_own, d_cls_q, d_cls_p = contrast(
        cls_chip, micro, positive, query_count, batch_index, size
    )

    def factors(rows, kept, back):
        return (rows, kept[LEFTS], back[4], back[3], back[5], back[6])

    scale = size // BLOCKS

    def core_products(
        layer, rows, lefts, other_lefts, back, other_rights, vectors, after, cost
    ):
        products = passage_products(
            tower_p, layer, rows, lefts, other_lefts, back[4::2], other_rights, vectors, after, cost
        )
        return products

    def chains_of(layer, products):
        return [
            Chain(products[2 * at], products[2 * at + 1], ORDERS[3 * layer + at], scale)
            for at in range(len(products) // 2)
        ]

    late_back_q = backward_layer(
        tower_q, 1, cots_q, d_cls_q, late_q, True, cost=0
    )
    late_sent_q = late_back_q[0]
    grad_mid_q = core_swap(late_sent_q)
    early_back_q = backward_layer(
        tower_q,
        0,
        grad_mid_q,
        None,
        early_q,
        False,
        cost=0,
        through=(late_p[LEFTS], early_p[LEFTS], jnp.where(is_first, top_p, mid_p)),
    )
    *early_back_q, late_left, early_left, hidden_sent = early_back_q
    late_left_other, early_left_other = core_swap(late_left), core_swap(early_left)
    hidden_other = core_swap(hidden_sent)
    packs = pack_first(
        info,
        factors(flat_q, early_q, early_back_q),
        factors(arrived_q, late_q, late_back_q),
        cost=0,
    )
    keeps, sends = packs[0::2], packs[1::2]
    arrivals = [flip_swap(sends[0], scale), flip_swap(sends[1], 2 * scale)]
    late_back_p = backward_layer(
        tower_p, 1, cots_p, d_cls_p, late_p, True, tuple(sends), cost=0
    )
    late_sent_p = late_back_p[0]
    late_other = [core_swap(array) for array in late_back_p[3::2]]
    packs = pack_second(
        info,
        keeps,
        sends,
        arrivals,
        model,
        (late_sent_p, late_left_other, early_left_other, hidden_other),
        cost=40,
    )
    keeps, sends = packs[0::2], packs[1::2]
    arrivals = [flip_swap(sends[0], 2 * scale), flip_swap(sends[1], scale)]
    products = core_products(
        1, None, late_left, late_left_other, late_back_p, late_other, (), tuple(sends), 0
    )
    a1, b1 = chains_of(1, products)
    send, keep = query_products(
        info, keeps, sends, arrivals, model, wide, tuple(products[:1]), cost=4
    )
    query = Chain(send, keep, (4, 8), scale)
    early_back_p = backward_layer(
        tower_p, 0, late_sent_p, None, early_p, False, (send,), cost=0
    )
    early_grad_p = early_back_p[0]
    early_other = [core_swap(array) for array in early_back_p[3::2]]
    vectors = (*early_back_q[1:3], *late_back_q[1:3], *early_back_p[1:3], *late_back_p[1:3])
    pieces = vector_pieces(info, 0, vectors, wide, (early_grad_p,), 0)
    vectors = (pieces[1], core_swap(pieces[0]))
    seen = play_round([[a1], [b1]], vectors, 4)
    seen = play_round([[query]], seen, 40)
    products = core_products(
        0, flat_p, early_left, early_left_other, early_back_p, early_other, vectors, seen, 4
    )
    a0, b0 = chains_of(0, products)
    seen = (products[0],)
    others = (
        early_grad_p,
        late_sent_p,
        early_back_q[0],
        late_sent_q,
        mid_q,
        top_q,
        mid_p,
        top_p,
        hidden_other,
        loss_own[None],
    )
    rounds = (
        ([[a1, b1]], 40),
        ([[query]], 4),
        ([[b0]], 0),
        ([[a0]], 0),
        ([[a1]], 40),
        ("z", 4),
        ([[a1]], 12),
    )
    for step, (groups, cost) in enumerate(rounds):
        held = others if step == 3 else (query.total,) if step == len(rounds) - 1 else ()
        if groups == "z":
            parts = take_in_quarters([(chain.keep, chain.arrived) for chain in (a0, b0)], seen, cost)
            low, high = a0.order[0] * scale, a0.order[1] * scale
            quarters = (
                parts[0],
                flip_swap(parts[1], high),
                flip_swap(parts[2], low),
                flip_swap(parts[3], low + high),
            )
            seen = tuple(parts[1:])
            continue
        passed = play_round(groups, seen, cost, held)
        seen = passed[: len(passed) - len(held)]
        if step == 3:
            others = passed[-10:]
    early_grad_p, late_sent_p, early_grad_q, late_sent_q = others[:4]
    mid_q, top_q, mid_p, top_p, hidden_other, loss_own = others[4:]
    loss_own = loss_own[0]
    early_grad_other = core_swap(jnp.where(is_first, late_sent_p.astype(F32), early_grad_p))

    total_q = passed[-1]

    def other_half(begin, columns, bit):
        mine = (batch_index // (bit * scale)) % 2
        sent = lax.dynamic_slice_in_dim(total_q, begin + (1 - mine) * columns, columns, 1)
        return flip_swap(sent, bit * scale)

    query_x = other_half(0, 3 * model // 2, 1)
    query_y = other_half(4 * model, wide // 2, 2)
    outputs = query_outputs(info, total_q, query_x, query_y, model, wide, seen)
    own, sent, total_v = last_round(info, quarters, a1.total, model + wide // 2, seen)
    sums = passage_outputs(info, own, core_swap(sent), outputs, model, wide)
    if scale > 1:
        left = all_bits(scale)
        sums = [
            jnp.stack([scatter_sum(to_grid(tower.astype(LOW), scale), left, left) for tower in item])
            for item in sums
        ]
    g_qkv, g_out, g_up, g_down = sums

    total_v = total_v[:32].reshape(2, 16, 128)
    eight = total_v[:, :8, : model // BLOCKS]
    g_bup = total_v[:, 8:10].reshape(2, -1)[:, : wide // BLOCKS]
    if scale > 1:
        left = all_bits(scale)
        eight = scatter_sum(
            to_grid(jnp.moveaxis(eight, 2, 0).reshape(-1, 16), scale), left, left
        )
        eight = jnp.moveaxis(eight.reshape(-1, 2, 8), 0, 2)
        g_bup = scatter_sum(to_grid(g_bup.T, scale), left, left).T
    g_gain = jnp.stack([eight[:, 3], eight[:, 0]], 1)
    g_bias = jnp.stack([eight[:, at] for at in (6, 7, 5, 4, 2, 1)], 1)

    pairs = (
        jnp.where(is_first, mid_p, hidden_other),
        jnp.where(is_first, hidden_other, top_p),
    )
    hidden_p = jnp.concatenate(pairs, 0).reshape(x_p.shape)
    pairs = (
        jnp.where(is_first, early_grad_p, early_grad_other),
        jnp.where(is_first, early_grad_other, late_sent_p.astype(F32)),
    )
    grad_p = jnp.concatenate(pairs, 0).reshape(x_p.shape)
    hidden_q = jnp.where(is_first, mid_q, top_q).reshape(x_q.shape)
    grad_q = jnp.where(is_first, early_grad_q, late_sent_q.astype(F32)).reshape(x_q.shape)
    return (
        hidden_q[None],
        hidden_p[None],
        grad_q[None],
        grad_p[None],
        loss_own,
        g_qkv[None],
        g_out[None],
        g_up[None],
        g_down[None],
        g_gain[None],
        g_bias[None],
        g_bup[None],
        g_bias[None, :, 0, :],
    )


def solution(mesh):
    return jax.shard_map(
        shards,
        mesh=mesh,
        in_specs=(
            P("batch", None, None),
            P("batch", None, None),
            P("batch"),
            P("batch"),
            P("batch", None, None),
            P("batch", None, None),
            P(),
            P(),
            P("section", None, None, None),
            P("section", None, None, None),
            P("section", None, None, None),
            P("section", None, None, None),
            P("section", None, None, None),
            P("section", None, None, None),
            P("section", None, None),
        ),
        out_specs=(
            P("section", "batch", None, None),
            P("section", "batch", None, None),
            P("section", "batch", None, None),
            P("section", "batch", None, None),
            P("batch"),
            P("section", None, "batch", None),
            P("section", None, "batch", None),
            P("section", None, "batch", None),
            P("section", None, "batch", None),
            P("section", None, None, "batch"),
            P("section", None, None, "batch"),
            P("section", None, "batch"),
            P("section", None, "batch"),
        ),
        check_vma=False,
    )
```
